32 devices in a mesh: groups: 2 (over y), row: 8 (over z, x), col: 2 (over core).
Axes of the slice: x: 2, y: 2, z: 4, core: 2. Of those that a mesh axis runs over, the one named last changes fastest.
Arguments:
- tiles: bfloat16 [16, 2, 96, 128, 128], P(('groups', 'row'), 'col'), parts along dimension 0, may hold values from 0 to 0.023925781
- tile_row: int32 [16, 2, 96], P(('groups', 'row'), 'col'), parts along dimension 0, may hold values from 0 to 3, as said below
- tile_col: int32 [16, 2, 96], P(('groups', 'row'), 'col'), parts along dimension 0, may hold values from 0 to 9
- tile_count: int32 [16, 2], P(('groups', 'row'), 'col'), parts along dimension 0, may hold values from 1 to 96, as said below
- sources: int32 [512], P('groups'), parts along dimension 0, may hold values from 0 to 2303
Outputs:
- scores: float32 [16, 2, 128, 256], P(('groups', 'row'), 'col'), parts along dimension 0
- hub_scores: float32 [512, 256], P(('groups', 'row', 'col')), parts along dimension 0
The draws below stay inside these ranges and needn't reach their ends.
There are 2 independent parts, one for each index of `groups`. The reference program is written for one: setup_inputs(seed, part) draws one part's arguments, and reference() takes and returns one part's arrays. A program takes and returns all parts, laid end to end along the dimension named above; each array names one. Nothing has to cross between parts.
Inputs may be any that keep to these rules, and one draw needn't show every extreme that they name: Slots from tile_count on are padding whose tiles and coordinates are ignored; some device uses all 96 slots. `tile_row`: tile rows from 2 * 128 / 128 on are hub rows.
All inputs are finite; a program needn't handle non-finite values.
Results may differ from the reference program's by a relative error of at most 0.0003.
Values may be sent and summed in bfloat16 or wider, within the bound.
No kernel may reach another device: no remote copies, remote signals or barrier semaphores. Data moves between devices by JAX's collectives and lax.ppermute only.
A program may use at most 64 MiB of HBM per device.

```python
import jax
import jax.numpy as jnp
from jax import lax

TS = 128
S = 256
VB = 128
H = 256
TMAX = 96
ITERS = 2
NTR = 4
NTC = 10
NV = 2304
N_ROW = 8
N_COL = 2


def draw_tile_count(key, part):
    key = jax.random.fold_in(key, 11)
    first, second = jax.random.split(key)
    devices = N_ROW * N_COL
    lowest = max(1, TMAX // 4)
    counts = jax.random.randint(first, (devices,), lowest, TMAX + 1)
    fullest = jax.random.randint(second, (), 0, devices)
    counts = jnp.where(jnp.arange(devices) == fullest, TMAX, counts)
    return counts.reshape(N_ROW, N_COL).astype(jnp.int32)


def draw_tile_row(key, part):
    key = jax.random.fold_in(key, 5)
    first, second, third = jax.random.split(key, 3)
    shape = (N_ROW, N_COL, TMAX)
    own_rows = N_COL * VB // TS
    picker = jax.random.randint(first, shape, 0, N_ROW)
    drawn = jax.random.randint(second, shape, 0, own_rows)
    hubward = jax.random.randint(third, shape, 0, H // TS) + own_rows
    return jnp.where(picker < 4, hubward, drawn).astype(jnp.int32)


def with_ends(drawn, key, low, top_value):
    longest = drawn.shape.index(max(drawn.shape))
    spots = []
    for shift in (0, 1):
        where = [jax.random.randint(jax.random.fold_in(key, axis), (), 0, length) for axis, length in enumerate(drawn.shape)]
        where[longest] = (where[longest] + shift) % drawn.shape[longest]
        spots.append(tuple(where))
    return drawn.at[spots[0]].set(low).at[spots[1]].set(top_value)


def shard_levels(key, shape, cuts, least, top_value):
    loudness, own = 1.0, jax.random.fold_in(key, 6)
    for axis_at, parts in cuts:
        heights = jnp.exp(jax.random.uniform(jax.random.fold_in(own, axis_at), (parts,), jnp.float32, least / len(cuts), top_value / len(cuts)))
        loudness = loudness * jnp.repeat(heights, shape[axis_at] // parts).reshape([-1 if axis == axis_at else 1 for axis in range(len(shape))])
    return loudness


def setup_inputs(seed: int = 0, part: int = 0) -> dict:
    streams_of = jax.random.split(jax.random.key(seed), 6)
    own_keys = jax.random.split(jax.random.fold_in(streams_of[5], part), 6)
    tiles = jnp.clip(0.023925781 * jax.random.uniform(own_keys[0], (N_ROW, N_COL, TMAX, TS, TS), jnp.float32) ** shard_levels(own_keys[0], (N_ROW, N_COL, TMAX, TS, TS), ((0, 8), (1, 2)), -0.2, 0.2), 0.0, 0.023925781).astype(jnp.bfloat16)
    tile_row = draw_tile_row(jax.random.fold_in(jax.random.fold_in(streams_of[5], part), 71), part)
    tile_col = with_ends(jax.random.randint(own_keys[2], (N_ROW, N_COL, TMAX), 0, NTC), jax.random.fold_in(own_keys[2], 1), 0, NTC - 1).astype(jnp.int32)
    tile_count = draw_tile_count(jax.random.fold_in(jax.random.fold_in(streams_of[5], part), 71), part)
    sources = with_ends(jax.random.randint(own_keys[4], (S,), 0, NV), jax.random.fold_in(own_keys[4], 1), 0, NV - 1).astype(jnp.int32)
    return dict(tiles=tiles, tile_row=tile_row, tile_col=tile_col, tile_count=tile_count, sources=sources)


def reference(tiles, tile_row, tile_col, tile_count, sources):
    devices = N_ROW * N_COL
    own_tiles = N_COL * VB // TS
    ids = H + jnp.arange(devices * VB, dtype=jnp.int32)
    tele_reg = (ids[:, None] == sources[None, :]).astype(jnp.float32).reshape(N_ROW, N_COL, VB, S)
    tele_hub = (jnp.arange(H, dtype=jnp.int32)[:, None] == sources[None, :]).astype(jnp.float32)
    x_reg = tele_reg
    x_hub = tele_hub
    for step in range(ITERS):
        xb_reg = x_reg.astype(jnp.bfloat16)
        xb_hub = x_hub.astype(jnp.bfloat16)
        columns = jnp.transpose(xb_reg, (1, 0, 2, 3)).reshape(N_COL, N_ROW * VB, S)
        hubs_all = jnp.broadcast_to(xb_hub[None], (N_COL, H, S))
        panels = jnp.concatenate([columns, hubs_all], axis=1).reshape(N_COL, NTC, TS, S)

        def per_row(r):
            tiles_r = lax.dynamic_index_in_dim(tiles, r, 0, keepdims=False)
            rows_r = lax.dynamic_index_in_dim(tile_row, r, 0, keepdims=False)
            cols_r = lax.dynamic_index_in_dim(tile_col, r, 0, keepdims=False)
            count_r = lax.dynamic_index_in_dim(tile_count, r, 0, keepdims=False)

            def per_col(c):
                panel = lax.dynamic_index_in_dim(panels, c, 0, keepdims=False)
                tile_set = lax.dynamic_index_in_dim(tiles_r, c, 0, keepdims=False)
                rows = lax.dynamic_index_in_dim(rows_r, c, 0, keepdims=False)
                cols = lax.dynamic_index_in_dim(cols_r, c, 0, keepdims=False)
                count = lax.dynamic_index_in_dim(count_r, c, 0, keepdims=False)
                pieces = panel[cols]
                prod = jnp.einsum('tij,tjs->tis', tile_set.astype(jnp.float32), pieces.astype(jnp.float32))
                live = (jnp.arange(TMAX, dtype=jnp.int32) < count).astype(jnp.float32)
                prod = prod * live[:, None, None]
                acc = jnp.zeros((NTR, TS, S), jnp.float32).at[rows].add(prod)
                return acc[:own_tiles].reshape(N_COL, VB, S), acc[own_tiles:].reshape(H, S)

            own, hub = lax.map(per_col, jnp.arange(N_COL, dtype=jnp.int32))
            return jnp.sum(own, axis=0), jnp.sum(hub, axis=0)

        own, hub = lax.map(per_row, jnp.arange(N_ROW, dtype=jnp.int32))
        x_reg = 0.85 * own + 0.15 * tele_reg
        x_hub = 0.85 * jnp.sum(hub, axis=0) + 0.15 * tele_hub
    return x_reg, x_hub
```

```python
import functools

import jax
import jax.numpy as jnp
from jax import lax
from jax.experimental import pallas as pl
from jax.experimental.pallas import tpu as pltpu
from jax.sharding import PartitionSpec as P

VB = 128
H = 256
ITERS = 2
DAMP = 0.85
CHUNK = 16
VMEM_LIMIT = 32 * 1024 * 1024

SMEM = pl.BlockSpec(memory_space=pltpu.SMEM)
VMEM = pl.BlockSpec(memory_space=pltpu.VMEM)
ANY = pl.BlockSpec(memory_space=pl.ANY)


def params():
    return pltpu.CompilerParams(vmem_limit_bytes=VMEM_LIMIT)


def one_hot(first, count, src):
    ids = lax.broadcasted_iota(jnp.int32, (count, src.shape[1]), 0) + first
    return (ids == src).astype(jnp.float32)


def write_terms(dims, where_ref, prod_ref, dense_ref, panel_ref, hub_ref, send_ref, keep_ref):
    n_row, n_col, side = dims
    rows = dense_ref.shape[0] // 2
    own = n_col * VB
    prod = jnp.dot(dense_ref[...], panel_ref[...], preferred_element_type=jnp.float32)
    total = prod[:rows] + prod[rows:]
    prod_ref[...] = total[:own]
    mine = pl.multiple_of(where_ref[1] * VB, VB)
    other = pl.multiple_of((1 - where_ref[1]) * VB, VB)
    keep_ref[...] = prod_ref[pl.ds(mine, VB), :]
    send_ref[...] = prod_ref[pl.ds(other, VB), :]
    hubs = total[own:].reshape(n_row, H // n_row, -1)
    for c in range(n_col):
        hub_ref[:, c] = hubs


def first_kernel(dims, where_ref, count_ref, rows_ref, cols_ref, src_ref, tiles_ref,
                 hub_ref, send_ref, keep_ref, dense_ref,
                 held, total, panel, prod, sems):
    n_row, n_col, side = dims
    slots = tiles_ref.shape[0]
    n_rows = dense_ref.shape[0] // 2
    copies = []
    for i in range(slots // CHUNK):
        part = pl.ds(i * CHUNK, CHUNK)
        copies.append(pltpu.make_async_copy(tiles_ref.at[part], held.at[part], sems.at[i]))
    for copy in copies:
        copy.start()
    total[...] = jnp.zeros_like(total)
    src = src_ref[...]
    for r in range(n_row):
        first = H + (r * n_col + where_ref[1]) * VB
        panel[pl.ds(r * VB, VB), :] = one_hot(first, VB, src).astype(jnp.bfloat16)
    panel[pl.ds(n_row * VB, H), :] = one_hot(0, H, src).astype(jnp.bfloat16)
    count = count_ref[0]

    def add_tile(k, carry):
        live = k < count
        row = pl.multiple_of(jnp.where(live, rows_ref[k] * side, n_rows), side)
        col = pl.multiple_of(jnp.where(live, cols_ref[k] * side, 0), side)
        spot = (pl.ds(row, side), pl.ds(col, side))
        total[spot] += held[k].astype(jnp.float32)
        return carry

    for i, copy in enumerate(copies):
        copy.wait()
        lax.fori_loop(i * CHUNK, (i + 1) * CHUNK, add_tile, 0, unroll=4)
    for r in range(0, n_rows, side):
        whole = total[pl.ds(r, side), :]
        high = whole.astype(jnp.bfloat16)
        dense_ref[pl.ds(r, side), :] = high
        dense_ref[pl.ds(n_rows + r, side), :] = (whole - high.astype(jnp.float32)).astype(jnp.bfloat16)
    write_terms(dims, where_ref, prod, dense_ref, panel, hub_ref, send_ref, keep_ref)


def second_kernel(dims, where_ref, got_ref, dense_ref, hub_ref, send_ref, keep_ref, panel, prod):
    n_row, n_col, side = dims
    share = H // n_row
    for r in range(n_row):
        panel[pl.ds(r * VB, VB), :] = got_ref[r, :VB]
        panel[pl.ds(n_row * VB + r * share, share), :] = got_ref[r, VB:]
    write_terms(dims, where_ref, prod, dense_ref, panel, hub_ref, send_ref, keep_ref)


def new_scores(dims, where_ref, src_ref, keep_ref, came_ref):
    n_row, n_col, side = dims
    src = src_ref[...]
    first = H + (where_ref[0] * n_col + where_ref[1]) * VB
    tele = one_hot(first, VB, src)
    return DAMP * (keep_ref[...] + came_ref[...]) + 0.15 * tele


def new_hubs(dims, where_ref, src_ref, parts_ref):
    n_row = dims[0]
    share = H // n_row
    summed = parts_ref[0]
    for k in range(1, parts_ref.shape[0]):
        summed = summed + parts_ref[k]
    return DAMP * summed + 0.15 * one_hot(where_ref[0] * share, share, src_ref[...])


def middle_kernel(dims, where_ref, src_ref, keep_ref, came_ref, parts_ref, out_ref):
    out_ref[:VB] = new_scores(dims, where_ref, src_ref, keep_ref, came_ref).astype(jnp.bfloat16)
    out_ref[VB:] = new_hubs(dims, where_ref, src_ref, parts_ref).astype(jnp.bfloat16)


def last_kernel(dims, where_ref, src_ref, keep_ref, came_ref, parts_ref, scores_ref, hubs_ref, held):
    scores_ref[...] = new_scores(dims, where_ref, src_ref, keep_ref, came_ref)
    held[...] = new_hubs(dims, where_ref, src_ref, parts_ref)
    piece = hubs_ref.shape[0]
    start = pl.multiple_of(where_ref[1] * piece, piece)
    hubs_ref[...] = held[pl.ds(start, piece), :]


def fast_body(tiles, tile_row, tile_col, tile_count, sources):
    slots, side = tiles.shape[2:4]
    width = sources.shape[0]
    n_row = lax.axis_size("row")
    n_col = lax.axis_size("col")
    devices = n_row * n_col
    share = H // n_row
    dims = (n_row, n_col, side)
    n_rows = n_col * VB + H
    n_cols = n_row * VB + H
    f32 = functools.partial(jax.ShapeDtypeStruct, dtype=jnp.float32)
    bf16 = functools.partial(jax.ShapeDtypeStruct, dtype=jnp.bfloat16)
    where = jnp.stack([lax.axis_index("row"), lax.axis_index("col")]).astype(jnp.int32)
    src = sources.reshape(1, width)
    term_shapes = (f32((n_row, n_col, share, width)), f32((VB, width)), f32((VB, width)))

    hubs, send, keep, dense = pl.pallas_call(
        functools.partial(first_kernel, dims),
        out_shape=term_shapes + (bf16((2 * n_rows, n_cols)),),
        in_specs=[SMEM] * 4 + [VMEM, ANY],
        out_specs=[VMEM] * 4,
        scratch_shapes=[
            pltpu.VMEM((slots, side, side), jnp.bfloat16),
            pltpu.VMEM((n_rows + side, n_cols), jnp.float32),
            pltpu.VMEM((n_cols, width), jnp.bfloat16),
            pltpu.VMEM((n_col * VB, width), jnp.float32),
            pltpu.SemaphoreType.DMA((slots // CHUNK,)),
        ],
        compiler_params=params(),
        name="first_terms",
    )(where, tile_count.reshape(1), tile_row.reshape(slots), tile_col.reshape(slots), src,
      tiles.reshape(slots, side, side))

    def exchange(hubs, send):
        came = lax.ppermute(send, "col", [(0, 1), (1, 0)])
        parts = lax.all_to_all(hubs.reshape(devices, share, width), ("row", "col"), 0, 0, tiled=True)
        return came, parts

    for step in range(ITERS - 1):
        came, parts = exchange(hubs, send)
        mine = pl.pallas_call(
            functools.partial(middle_kernel, dims),
            out_shape=bf16((VB + share, width)),
            in_specs=[SMEM] + [VMEM] * 4,
            out_specs=VMEM,
            compiler_params=params(),
            name="new_panel_rows",
        )(where, src, keep, came, parts)
        got = lax.all_gather(mine, "row", axis=0)
        hubs, send, keep = pl.pallas_call(
            functools.partial(second_kernel, dims),
            out_shape=term_shapes,
            in_specs=[SMEM, VMEM, VMEM],
            out_specs=[VMEM] * 3,
            scratch_shapes=[
                pltpu.VMEM((n_cols, width), jnp.bfloat16),
                pltpu.VMEM((n_col * VB, width), jnp.float32),
            ],
            compiler_params=params(),
            name="later_terms",
        )(where, got, dense)
    came, parts = exchange(hubs, send)
    scores, piece = pl.pallas_call(
        functools.partial(last_kernel, dims),
        out_shape=(f32((VB, width)), f32((H // devices, width))),
        in_specs=[SMEM] + [VMEM] * 4,
        out_specs=[VMEM] * 2,
        scratch_shapes=[pltpu.VMEM((share, width), jnp.float32)],
        compiler_params=params(),
        name="last_scores",
    )(where, src, keep, came, parts)
    return scores.reshape(1, 1, VB, width), piece


def plain_body(tiles, tile_row, tile_col, tile_count, sources):
    slots = tiles.shape[2]
    side = tiles.shape[3]
    width = sources.shape[0]
    tiles = tiles.reshape(slots, side, side)
    rows = tile_row.reshape(slots)
    cols = tile_col.reshape(slots)
    count = tile_count.reshape(())
    n_row = lax.axis_size("row")
    n_col = lax.axis_size("col")
    devices = n_row * n_col
    r_index = lax.axis_index("row")
    c_index = lax.axis_index("col")
    hub_dev = H // devices
    block_rows = n_col * VB
    n_tile_rows = (block_rows + H) // side
    own_base = H + (r_index * n_col + c_index) * VB
    hub_start = (r_index * n_col + c_index) * hub_dev
    own_ids = jnp.arange(VB, dtype=jnp.int32) + own_base
    tele_own = (own_ids[:, None] == sources[None, :]).astype(jnp.float32)
    piece_ids = jnp.arange(hub_dev, dtype=jnp.int32) + hub_start
    tele_piece = (piece_ids[:, None] == sources[None, :]).astype(jnp.float32)
    tele_hubs = (jnp.arange(H, dtype=jnp.int32)[:, None] == sources[None, :]).astype(jnp.float32)
    column_ids = (
        H
        + (jnp.arange(n_row, dtype=jnp.int32)[:, None] * n_col + c_index) * VB
        + jnp.arange(VB, dtype=jnp.int32)[None, :]
    ).reshape(n_row * VB)
    column_panel = (column_ids[:, None] == sources[None, :]).astype(jnp.bfloat16)
    hub_panel = tele_hubs.astype(jnp.bfloat16)
    block = CHUNK
    own_scores = tele_own
    hub_piece = tele_piece
    for step in range(ITERS):
        start_acc = jnp.zeros((n_tile_rows, side, width), jnp.float32)
        if step > 0:
            column_panel = lax.all_gather(
                own_scores.astype(jnp.bfloat16), "row", axis=0, tiled=True
            )
        panel = jnp.concatenate([column_panel, hub_panel], axis=0).reshape(-1, side, width)

        def step_fn(number, total):
            start = number * block
            tile_block = lax.dynamic_slice_in_dim(tiles, start, block, 0)
            col_block = lax.dynamic_slice_in_dim(cols, start, block, 0)
            row_block = lax.dynamic_slice_in_dim(rows, start, block, 0)
            pieces = jnp.take(panel, col_block, axis=0)
            prod = jnp.einsum(
                "tij,tjs->tis", tile_block, pieces, preferred_element_type=jnp.float32
            )
            live = start + jnp.arange(block, dtype=jnp.int32) < count
            prod = jnp.where(live[:, None, None], prod, 0.0)
            return total.at[row_block].add(prod)

        total = lax.fori_loop(0, slots // block, step_fn, start_acc)
        partial_value = total.reshape(n_tile_rows * side, width)
        summed_rows = lax.psum_scatter(
            partial_value[:block_rows], "col", scatter_dimension=0, tiled=True
        )
        own_scores = 0.85 * summed_rows + 0.15 * tele_own
        hub_part = partial_value[block_rows:]
        summed = lax.psum_scatter(hub_part, ("row", "col"), scatter_dimension=0, tiled=True)
        hub_piece = 0.85 * summed + 0.15 * tele_piece
        if step + 1 < ITERS:
            hub_panel = lax.all_gather(
                hub_piece.astype(jnp.bfloat16), ("row", "col"), axis=0, tiled=True
            )
    return (own_scores.reshape(1, 1, VB, width), hub_piece)


def solution(mesh):
    placed = (
        P(("groups", "row"), "col", None, None, None),
        P(("groups", "row"), "col", None),
        P(("groups", "row"), "col", None),
        P(("groups", "row"), "col"),
        P("groups"),
    )

    def body(tiles, *rest):
        n_row, n_col = mesh.shape["row"], mesh.shape["col"]
        slots, side = tiles.shape[2:4]
        blocks = (n_col * VB + H) * (n_row * VB + H) // (side * side)
        if n_col == 2 and blocks <= slots and H // (n_row * n_col) % 16 == 0:
            return fast_body(tiles, *rest)
        return plain_body(tiles, *rest)

    return jax.shard_map(
        body,
        mesh=mesh,
        in_specs=placed,
        out_specs=(P(("groups", "row"), "col", None, None), P(("groups", "row", "col"), None)),
        check_vma=False,
    )
```

```python
import functools

import jax
import jax.numpy as jnp
from jax import lax
from jax.experimental import pallas as pl
from jax.experimental.pallas import tpu as pltpu
from jax.sharding import PartitionSpec as P

VB = 128
H = 256
ITERS = 2
DAMP = 0.85
CHUNK = 16
VMEM_LIMIT = 32 * 1024 * 1024

SMEM = pl.BlockSpec(memory_space=pltpu.SMEM)
VMEM = pl.BlockSpec(memory_space=pltpu.VMEM)
HBM = pl.BlockSpec(memory_space=pltpu.HBM)


def params():
    return pltpu.CompilerParams(vmem_limit_bytes=VMEM_LIMIT)


def one_hot(first, count, src):
    ids = lax.broadcasted_iota(jnp.int32, (count, src.shape[1]), 0) + first
    return (ids == src).astype(jnp.float32)


def write_terms(dims, prod_ref, dense_ref, panel_ref, send_ref, keep_ref):
    n_row, n_col, side = dims
    rows = dense_ref.shape[0] // 2
    piece = H // (n_row * n_col)
    c = lax.axis_index("col")
    prod = jnp.dot(dense_ref[...], panel_ref[...], preferred_element_type=jnp.float32)
    prod_ref[...] = prod[:rows] + prod[rows:]
    for ref, col in ((keep_ref, c), (send_ref, 1 - c)):
        ref[:VB] = prod_ref[pl.ds(pl.multiple_of(col * VB, VB), VB), :]
        for r in range(n_row):
            start = n_col * VB + (r * n_col + col) * piece
            ref[VB + r * piece:VB + (r + 1) * piece] = prod_ref[pl.ds(pl.multiple_of(start, piece), piece), :]


def first_kernel(dims, tiles_ref, rows_hbm, cols_hbm, count_hbm, src_hbm,
                 send_ref, keep_ref, dense_ref,
                 held, rows_ref, cols_ref, count_ref, src_ref, total, panel, prod, sems, small):
    n_row, n_col, side = dims
    slots = tiles_ref.shape[0]
    n_rows = dense_ref.shape[0] // 2
    pairs = ((src_hbm, src_ref), (count_hbm, count_ref), (rows_hbm, rows_ref), (cols_hbm, cols_ref))
    scalars = [pltpu.make_async_copy(a, b, small.at[i]) for i, (a, b) in enumerate(pairs)]
    for copy in scalars:
        copy.start()
    copies = []
    for i in range(slots // CHUNK):
        part = pl.ds(i * CHUNK, CHUNK)
        copies.append(pltpu.make_async_copy(tiles_ref.at[part], held.at[part], sems.at[i]))
    for copy in copies:
        copy.start()
    total[...] = jnp.zeros_like(total)
    for copy in scalars:
        copy.wait()
    src = src_ref[...]
    for r in range(n_row):
        first = H + (r * n_col + lax.axis_index("col")) * VB
        panel[pl.ds(r * VB, VB), :] = one_hot(first, VB, src).astype(jnp.bfloat16)
    panel[pl.ds(n_row * VB, H), :] = one_hot(0, H, src).astype(jnp.bfloat16)
    count = count_ref[0]

    def add_tile(k, carry):
        live = k < count
        row = pl.multiple_of(jnp.where(live, rows_ref[k] * side, n_rows), side)
        col = pl.multiple_of(jnp.where(live, cols_ref[k] * side, 0), side)
        spot = (pl.ds(row, side), pl.ds(col, side))
        total[spot] += held[k].astype(jnp.float32)
        return carry

    for i, copy in enumerate(copies):
        copy.wait()
        lax.fori_loop(i * CHUNK, (i + 1) * CHUNK, add_tile, 0, unroll=4)
    for r in range(0, n_rows, side):
        whole = total[pl.ds(r, side), :]
        high = whole.astype(jnp.bfloat16)
        dense_ref[pl.ds(r, side), :] = high
        dense_ref[pl.ds(n_rows + r, side), :] = (whole - high.astype(jnp.float32)).astype(jnp.bfloat16)
    write_terms(dims, prod, dense_ref, panel, send_ref, keep_ref)


def second_kernel(dims, *refs):
    n_row, n_col, side = dims
    scores, hubs = refs[:n_row], refs[n_row:2 * n_row]
    dense_ref, send_ref, keep_ref, panel, prod = refs[2 * n_row:]
    share = H // n_row
    r = lax.axis_index("row")
    for k in range(n_row):
        owner = lax.rem(r - k + n_row, n_row)
        panel[pl.ds(pl.multiple_of(owner * VB, VB), VB), :] = scores[k][...]
        panel[pl.ds(pl.multiple_of(n_row * VB + owner * share, share), share), :] = hubs[k][...]
    write_terms(dims, prod, dense_ref, panel, send_ref, keep_ref)


def pair_kernel(dims, src_ref, keep_ref, came_ref, scores_ref, *parts):
    n_row, n_col, side = dims
    piece = H // (n_row * n_col)
    r, c = lax.axis_index("row"), lax.axis_index("col")
    tele = one_hot(H + (r * n_col + c) * VB, VB, src_ref[...])
    own = DAMP * (keep_ref[:VB] + came_ref[:VB]) + 0.15 * tele
    scores_ref[...] = own.astype(scores_ref.dtype)
    for k in range(n_row):
        spot = pl.ds(pl.multiple_of(VB + lax.rem(r + k, n_row) * piece, piece), piece)
        parts[k][...] = keep_ref[spot, :] + came_ref[spot, :]


def hub_kernel(dims, src_ref, *refs):
    n_row, n_col, side = dims
    out_ref = refs[n_row]
    piece = out_ref.shape[0]
    summed = refs[0][...]
    for k in range(1, n_row):
        summed = summed + refs[k][...]
    first = (lax.axis_index("row") * n_col + lax.axis_index("col")) * piece
    out_ref[...] = (DAMP * summed + 0.15 * one_hot(first, piece, src_ref[...])).astype(out_ref.dtype)


def fast_body(tiles, tile_row, tile_col, tile_count, sources):
    slots, side = tiles.shape[2:4]
    width = sources.shape[0]
    n_row = lax.axis_size("row")
    n_col = lax.axis_size("col")
    piece = H // (n_row * n_col)
    dims = (n_row, n_col, side)
    n_rows = n_col * VB + H
    n_cols = n_row * VB + H
    f32 = functools.partial(jax.ShapeDtypeStruct, dtype=jnp.float32)
    bf16 = functools.partial(jax.ShapeDtypeStruct, dtype=jnp.bfloat16)
    src = sources.reshape(1, width)
    half = VB + n_row * piece
    product_scratch = [
        pltpu.VMEM((n_cols, width), jnp.bfloat16),
        pltpu.VMEM((n_rows, width), jnp.float32),
    ]

    def other_core(x):
        return lax.ppermute(x, "col", [(0, 1), (1, 0)])

    def along_row(x, k):
        return lax.ppermute(x, "row", [(r, (r + k) % n_row) for r in range(n_row)])

    def pair_sums(keep, send, dtype):
        came = other_core(send)
        scores, *parts = pl.pallas_call(
            functools.partial(pair_kernel, dims),
            out_shape=(jax.ShapeDtypeStruct((VB, width), dtype),) + (f32((piece, width)),) * n_row,
            in_specs=[VMEM] * 3,
            out_specs=[VMEM] * (1 + n_row),
            compiler_params=params(),
            name="pair_sums",
        )(src, keep, came)
        return scores, [parts[0]] + [along_row(parts[k], k) for k in range(1, n_row)]

    def hub_sums(parts, dtype):
        return pl.pallas_call(
            functools.partial(hub_kernel, dims),
            out_shape=jax.ShapeDtypeStruct((piece, width), dtype),
            in_specs=[VMEM] * (1 + n_row),
            out_specs=VMEM,
            compiler_params=params(),
            name="hub_sums",
        )(src, *parts)

    send, keep, dense = pl.pallas_call(
        functools.partial(first_kernel, dims),
        out_shape=(f32((half, width)), f32((half, width)), bf16((2 * n_rows, n_cols))),
        in_specs=[HBM] * 5,
        out_specs=[VMEM] * 3,
        scratch_shapes=[
            pltpu.VMEM((slots, side, side), jnp.bfloat16),
            pltpu.SMEM((slots,), jnp.int32),
            pltpu.SMEM((slots,), jnp.int32),
            pltpu.SMEM((1,), jnp.int32),
            pltpu.VMEM((1, width), jnp.int32),
            pltpu.VMEM((n_rows + side, n_cols), jnp.float32),
        ] + product_scratch + [
            pltpu.SemaphoreType.DMA((slots // CHUNK,)),
            pltpu.SemaphoreType.DMA((4,)),
        ],
        compiler_params=params(),
        name="first_terms",
    )(tiles.reshape(slots, side, side), tile_row.reshape(slots), tile_col.reshape(slots),
      tile_count.reshape(1), src)

    for step in range(ITERS - 1):
        scores, parts = pair_sums(keep, send, jnp.bfloat16)
        got = [scores] + [along_row(scores, k) for k in range(1, n_row)]
        mine = hub_sums(parts, jnp.bfloat16)
        theirs = other_core(mine)
        both = jnp.where(lax.axis_index("col") == 0,
                         jnp.concatenate([mine, theirs]), jnp.concatenate([theirs, mine]))
        hubs = [both] + [along_row(both, k) for k in range(1, n_row)]
        send, keep = pl.pallas_call(
            functools.partial(second_kernel, dims),
            out_shape=(f32((half, width)), f32((half, width))),
            in_specs=[VMEM] * (2 * n_row + 1),
            out_specs=[VMEM] * 2,
            scratch_shapes=product_scratch,
            compiler_params=params(),
            name="later_terms",
        )(*got, *hubs, dense)
    scores, parts = pair_sums(keep, send, jnp.float32)
    return scores.reshape(1, 1, VB, width), hub_sums(parts, jnp.float32)


def plain_body(tiles, tile_row, tile_col, tile_count, sources):
    slots = tiles.shape[2]
    side = tiles.shape[3]
    width = sources.shape[0]
    tiles = tiles.reshape(slots, side, side)
    rows = tile_row.reshape(slots)
    cols = tile_col.reshape(slots)
    count = tile_count.reshape(())
    n_row = lax.axis_size("row")
    n_col = lax.axis_size("col")
    devices = n_row * n_col
    r_index = lax.axis_index("row")
    c_index = lax.axis_index("col")
    hub_dev = H // devices
    block_rows = n_col * VB
    n_tile_rows = (block_rows + H) // side
    own_base = H + (r_index * n_col + c_index) * VB
    hub_start = (r_index * n_col + c_index) * hub_dev
    own_ids = jnp.arange(VB, dtype=jnp.int32) + own_base
    tele_own = (own_ids[:, None] == sources[None, :]).astype(jnp.float32)
    piece_ids = jnp.arange(hub_dev, dtype=jnp.int32) + hub_start
    tele_piece = (piece_ids[:, None] == sources[None, :]).astype(jnp.float32)
    tele_hubs = (jnp.arange(H, dtype=jnp.int32)[:, None] == sources[None, :]).astype(jnp.float32)
    column_ids = (
        H
        + (jnp.arange(n_row, dtype=jnp.int32)[:, None] * n_col + c_index) * VB
        + jnp.arange(VB, dtype=jnp.int32)[None, :]
    ).reshape(n_row * VB)
    column_panel = (column_ids[:, None] == sources[None, :]).astype(jnp.bfloat16)
    hub_panel = tele_hubs.astype(jnp.bfloat16)
    block = CHUNK
    own_scores = tele_own
    hub_piece = tele_piece
    for step in range(ITERS):
        start_acc = jnp.zeros((n_tile_rows, side, width), jnp.float32)
        if step > 0:
            column_panel = lax.all_gather(
                own_scores.astype(jnp.bfloat16), "row", axis=0, tiled=True
            )
        panel = jnp.concatenate([column_panel, hub_panel], axis=0).reshape(-1, side, width)

        def step_fn(number, total):
            start = number * block
            tile_block = lax.dynamic_slice_in_dim(tiles, start, block, 0)
            col_block = lax.dynamic_slice_in_dim(cols, start, block, 0)
            row_block = lax.dynamic_slice_in_dim(rows, start, block, 0)
            pieces = jnp.take(panel, col_block, axis=0)
            prod = jnp.einsum(
                "tij,tjs->tis", tile_block, pieces, preferred_element_type=jnp.float32
            )
            live = start + jnp.arange(block, dtype=jnp.int32) < count
            prod = jnp.where(live[:, None, None], prod, 0.0)
            return total.at[row_block].add(prod)

        total = lax.fori_loop(0, slots // block, step_fn, start_acc)
        partial_value = total.reshape(n_tile_rows * side, width)
        summed_rows = lax.psum_scatter(
            partial_value[:block_rows], "col", scatter_dimension=0, tiled=True
        )
        own_scores = 0.85 * summed_rows + 0.15 * tele_own
        hub_part = partial_value[block_rows:]
        summed = lax.psum_scatter(hub_part, ("row", "col"), scatter_dimension=0, tiled=True)
        hub_piece = 0.85 * summed + 0.15 * tele_piece
        if step + 1 < ITERS:
            hub_panel = lax.all_gather(
                hub_piece.astype(jnp.bfloat16), ("row", "col"), axis=0, tiled=True
            )
    return (own_scores.reshape(1, 1, VB, width), hub_piece)


def solution(mesh):
    placed = (
        P(("groups", "row"), "col", None, None, None),
        P(("groups", "row"), "col", None),
        P(("groups", "row"), "col", None),
        P(("groups", "row"), "col"),
        P("groups"),
    )

    def body(tiles, *rest):
        n_row, n_col = mesh.shape["row"], mesh.shape["col"]
        slots, side = tiles.shape[2:4]
        blocks = (n_col * VB + H) * (n_row * VB + H) // (side * side)
        if n_col == 2 and blocks <= slots and H // (n_row * n_col) % 16 == 0:
            return fast_body(tiles, *rest)
        return plain_body(tiles, *rest)

    return jax.shard_map(
        body,
        mesh=mesh,
        in_specs=placed,
        out_specs=(P(("groups", "row"), "col", None, None), P(("groups", "row", "col"), None)),
        check_vma=False,
    )
```

```python
import functools

import jax
import jax.numpy as jnp
from jax import lax
from jax.experimental import pallas as pl
from jax.experimental.pallas import tpu as pltpu
from jax.sharding import PartitionSpec as P

VB = 128
H = 256
ITERS = 2
DAMP = 0.85
CHUNK = 16
VMEM_LIMIT = 32 * 1024 * 1024

SMEM = pl.BlockSpec(memory_space=pltpu.SMEM)
VMEM = pl.BlockSpec(memory_space=pltpu.VMEM)
HBM = pl.BlockSpec(memory_space=pltpu.HBM)


def params():
    return pltpu.CompilerParams(vmem_limit_bytes=VMEM_LIMIT)


def one_hot(first, count, src):
    ids = lax.broadcasted_iota(jnp.int32, (count, src.shape[1]), 0) + first
    return (ids == src).astype(jnp.float32)


def write_terms(dims, prod_ref, dense_ref, panel_ref, send_ref, keep_ref):
    n_row, n_col, side = dims
    rows = dense_ref.shape[0] // 2
    piece = H // (n_row * n_col)
    c = lax.axis_index("col")
    prod = jnp.dot(dense_ref[...], panel_ref[...], preferred_element_type=jnp.float32)
    prod_ref[...] = prod[:rows] + prod[rows:]
    for ref, col in ((keep_ref, c), (send_ref, 1 - c)):
        ref[:VB] = prod_ref[pl.ds(pl.multiple_of(col * VB, VB), VB), :]
        for r in range(n_row):
            start = n_col * VB + (r * n_col + col) * piece
            ref[VB + r * piece:VB + (r + 1) * piece] = prod_ref[pl.ds(pl.multiple_of(start, piece), piece), :]


def first_kernel(dims, tiles_ref, rows_hbm, cols_hbm, count_hbm, src_hbm,
                 send_ref, keep_ref, dense_ref,
                 held, rows_ref, cols_ref, count_ref, src_ref, total, panel, prod, sems, small):
    n_row, n_col, side = dims
    slots = tiles_ref.shape[0]
    n_rows = dense_ref.shape[0] // 2
    pairs = ((src_hbm, src_ref), (count_hbm, count_ref), (rows_hbm, rows_ref), (cols_hbm, cols_ref))
    scalars = [pltpu.make_async_copy(a, b, small.at[i]) for i, (a, b) in enumerate(pairs)]
    for copy in scalars:
        copy.start()
    copies = []
    for i in range(slots // CHUNK):
        part = pl.ds(i * CHUNK, CHUNK)
        copies.append(pltpu.make_async_copy(tiles_ref.at[part], held.at[part], sems.at[i]))
    for copy in copies:
        copy.start()
    total[...] = jnp.zeros_like(total)
    for copy in scalars:
        copy.wait()
    src = src_ref[...]
    for r in range(n_row):
        first = H + (r * n_col + lax.axis_index("col")) * VB
        panel[pl.ds(r * VB, VB), :] = one_hot(first, VB, src).astype(jnp.bfloat16)
    panel[pl.ds(n_row * VB, H), :] = one_hot(0, H, src).astype(jnp.bfloat16)
    count = count_ref[0]

    def add_tile(k, carry):
        live = k < count
        row = pl.multiple_of(jnp.where(live, rows_ref[k] * side, n_rows), side)
        col = pl.multiple_of(jnp.where(live, cols_ref[k] * side, 0), side)
        spot = (pl.ds(row, side), pl.ds(col, side))
        total[spot] += held[k].astype(jnp.float32)
        return carry

    for i, copy in enumerate(copies):
        copy.wait()
        lax.fori_loop(i * CHUNK, (i + 1) * CHUNK, add_tile, 0, unroll=4)
    for r in range(0, n_rows, side):
        whole = total[pl.ds(r, side), :]
        high = whole.astype(jnp.bfloat16)
        dense_ref[pl.ds(r, side), :] = high
        dense_ref[pl.ds(n_rows + r, side), :] = (whole - high.astype(jnp.float32)).astype(jnp.bfloat16)
    write_terms(dims, prod, dense_ref, panel, send_ref, keep_ref)


def second_kernel(dims, scores_ref, mine_ref, theirs_ref, dense_ref, send_ref, keep_ref, panel, prod):
    n_row, n_col, side = dims
    piece = H // (n_row * n_col)
    c = lax.axis_index("col")
    for r in range(n_row):
        panel[pl.ds(r * VB, VB), :] = scores_ref[r]
        for ref, col in ((mine_ref, c), (theirs_ref, 1 - c)):
            start = n_row * VB + (r * n_col + col) * piece
            panel[pl.ds(pl.multiple_of(start, piece), piece), :] = ref[r]
    write_terms(dims, prod, dense_ref, panel, send_ref, keep_ref)


def pair_kernel(dims, src_ref, keep_ref, came_ref, scores_ref, parts_ref):
    n_row, n_col, side = dims
    piece = H // (n_row * n_col)
    r, c = lax.axis_index("row"), lax.axis_index("col")
    tele = one_hot(H + (r * n_col + c) * VB, VB, src_ref[...])
    own = DAMP * (keep_ref[:VB] + came_ref[:VB]) + 0.15 * tele
    for k in range(scores_ref.shape[0]):
        scores_ref[k] = own.astype(scores_ref.dtype)
    for k in range(n_row):
        spot = slice(VB + k * piece, VB + (k + 1) * piece)
        parts_ref[k] = keep_ref[spot, :] + came_ref[spot, :]


def hub_kernel(dims, src_ref, parts_ref, out_ref):
    n_row, n_col, side = dims
    piece = out_ref.shape[1]
    summed = parts_ref[0]
    for k in range(1, n_row):
        summed = summed + parts_ref[k]
    first = (lax.axis_index("row") * n_col + lax.axis_index("col")) * piece
    new = (DAMP * summed + 0.15 * one_hot(first, piece, src_ref[...])).astype(out_ref.dtype)
    for k in range(out_ref.shape[0]):
        out_ref[k] = new


def fast_body(tiles, tile_row, tile_col, tile_count, sources):
    slots, side = tiles.shape[2:4]
    width = sources.shape[0]
    n_row = lax.axis_size("row")
    n_col = lax.axis_size("col")
    piece = H // (n_row * n_col)
    dims = (n_row, n_col, side)
    n_rows = n_col * VB + H
    n_cols = n_row * VB + H
    f32 = functools.partial(jax.ShapeDtypeStruct, dtype=jnp.float32)
    bf16 = functools.partial(jax.ShapeDtypeStruct, dtype=jnp.bfloat16)
    src = sources.reshape(1, width)
    half = VB + n_row * piece
    product_scratch = [
        pltpu.VMEM((n_cols, width), jnp.bfloat16),
        pltpu.VMEM((n_rows, width), jnp.float32),
    ]

    def other_core(x):
        return lax.ppermute(x, "col", [(0, 1), (1, 0)])

    def to_rows(x):
        return lax.all_to_all(x, "row", 0, 0)

    def pair_sums(keep, send, copies, dtype):
        scores, parts = pl.pallas_call(
            functools.partial(pair_kernel, dims),
            out_shape=(jax.ShapeDtypeStruct((copies, VB, width), dtype), f32((n_row, piece, width))),
            in_specs=[VMEM] * 3,
            out_specs=[VMEM] * 2,
            compiler_params=params(),
            name="pair_sums",
        )(src, keep, other_core(send))
        return scores, to_rows(parts)

    def hub_sums(parts, copies, dtype):
        return pl.pallas_call(
            functools.partial(hub_kernel, dims),
            out_shape=jax.ShapeDtypeStruct((copies, piece, width), dtype),
            in_specs=[VMEM] * 2,
            out_specs=VMEM,
            compiler_params=params(),
            name="hub_sums",
        )(src, parts)

    send, keep, dense = pl.pallas_call(
        functools.partial(first_kernel, dims),
        out_shape=(f32((half, width)), f32((half, width)), bf16((2 * n_rows, n_cols))),
        in_specs=[HBM] * 5,
        out_specs=[VMEM] * 3,
        scratch_shapes=[
            pltpu.VMEM((slots, side, side), jnp.bfloat16),
            pltpu.SMEM((slots,), jnp.int32),
            pltpu.SMEM((slots,), jnp.int32),
            pltpu.SMEM((1,), jnp.int32),
            pltpu.VMEM((1, width), jnp.int32),
            pltpu.VMEM((n_rows + side, n_cols), jnp.float32),
        ] + product_scratch + [
            pltpu.SemaphoreType.DMA((slots // CHUNK,)),
            pltpu.SemaphoreType.DMA((4,)),
        ],
        compiler_params=params(),
        name="first_terms",
    )(tiles.reshape(slots, side, side), tile_row.reshape(slots), tile_col.reshape(slots),
      tile_count.reshape(1), src)

    for step in range(ITERS - 1):
        scores, parts = pair_sums(keep, send, n_row, jnp.bfloat16)
        scores = to_rows(scores)
        mine = to_rows(hub_sums(parts, n_row, jnp.bfloat16))
        send, keep = pl.pallas_call(
            functools.partial(second_kernel, dims),
            out_shape=(f32((half, width)), f32((half, width))),
            in_specs=[VMEM] * 4,
            out_specs=[VMEM] * 2,
            scratch_shapes=product_scratch,
            compiler_params=params(),
            name="later_terms",
        )(scores, mine, other_core(mine), dense)
    scores, parts = pair_sums(keep, send, 1, jnp.float32)
    return scores.reshape(1, 1, VB, width), hub_sums(parts, 1, jnp.float32).reshape(piece, width)


def plain_body(tiles, tile_row, tile_col, tile_count, sources):
    slots = tiles.shape[2]
    side = tiles.shape[3]
    width = sources.shape[0]
    tiles = tiles.reshape(slots, side, side)
    rows = tile_row.reshape(slots)
    cols = tile_col.reshape(slots)
    count = tile_count.reshape(())
    n_row = lax.axis_size("row")
    n_col = lax.axis_size("col")
    devices = n_row * n_col
    r_index = lax.axis_index("row")
    c_index = lax.axis_index("col")
    hub_dev = H // devices
    block_rows = n_col * VB
    n_tile_rows = (block_rows + H) // side
    own_base = H + (r_index * n_col + c_index) * VB
    hub_start = (r_index * n_col + c_index) * hub_dev
    own_ids = jnp.arange(VB, dtype=jnp.int32) + own_base
    tele_own = (own_ids[:, None] == sources[None, :]).astype(jnp.float32)
    piece_ids = jnp.arange(hub_dev, dtype=jnp.int32) + hub_start
    tele_piece = (piece_ids[:, None] == sources[None, :]).astype(jnp.float32)
    tele_hubs = (jnp.arange(H, dtype=jnp.int32)[:, None] == sources[None, :]).astype(jnp.float32)
    column_ids = (
        H
        + (jnp.arange(n_row, dtype=jnp.int32)[:, None] * n_col + c_index) * VB
        + jnp.arange(VB, dtype=jnp.int32)[None, :]
    ).reshape(n_row * VB)
    column_panel = (column_ids[:, None] == sources[None, :]).astype(jnp.bfloat16)
    hub_panel = tele_hubs.astype(jnp.bfloat16)
    block = CHUNK
    own_scores = tele_own
    hub_piece = tele_piece
    for step in range(ITERS):
        start_acc = jnp.zeros((n_tile_rows, side, width), jnp.float32)
        if step > 0:
            column_panel = lax.all_gather(
                own_scores.astype(jnp.bfloat16), "row", axis=0, tiled=True
            )
        panel = jnp.concatenate([column_panel, hub_panel], axis=0).reshape(-1, side, width)

        def step_fn(number, total):
            start = number * block
            tile_block = lax.dynamic_slice_in_dim(tiles, start, block, 0)
            col_block = lax.dynamic_slice_in_dim(cols, start, block, 0)
            row_block = lax.dynamic_slice_in_dim(rows, start, block, 0)
            pieces = jnp.take(panel, col_block, axis=0)
            prod = jnp.einsum(
                "tij,tjs->tis", tile_block, pieces, preferred_element_type=jnp.float32
            )
            live = start + jnp.arange(block, dtype=jnp.int32) < count
            prod = jnp.where(live[:, None, None], prod, 0.0)
            return total.at[row_block].add(prod)

        total = lax.fori_loop(0, slots // block, step_fn, start_acc)
        partial_value = total.reshape(n_tile_rows * side, width)
        summed_rows = lax.psum_scatter(
            partial_value[:block_rows], "col", scatter_dimension=0, tiled=True
        )
        own_scores = 0.85 * summed_rows + 0.15 * tele_own
        hub_part = partial_value[block_rows:]
        summed = lax.psum_scatter(hub_part, ("row", "col"), scatter_dimension=0, tiled=True)
        hub_piece = 0.85 * summed + 0.15 * tele_piece
        if step + 1 < ITERS:
            hub_panel = lax.all_gather(
                hub_piece.astype(jnp.bfloat16), ("row", "col"), axis=0, tiled=True
            )
    return (own_scores.reshape(1, 1, VB, width), hub_piece)


def solution(mesh):
    placed = (
        P(("groups", "row"), "col", None, None, None),
        P(("groups", "row"), "col", None),
        P(("groups", "row"), "col", None),
        P(("groups", "row"), "col"),
        P("groups"),
    )

    def body(tiles, *rest):
        n_row, n_col = mesh.shape["row"], mesh.shape["col"]
        slots, side = tiles.shape[2:4]
        blocks = (n_col * VB + H) * (n_row * VB + H) // (side * side)
        if n_col == 2 and blocks <= slots and H // (n_row * n_col) % 16 == 0:
            return fast_body(tiles, *rest)
        return plain_body(tiles, *rest)

    return jax.shard_map(
        body,
        mesh=mesh,
        in_specs=placed,
        out_specs=(P(("groups", "row"), "col", None, None), P(("groups", "row", "col"), None)),
        check_vma=False,
    )
```

```python
import functools

import jax
import jax.numpy as jnp
from jax import lax
from jax.experimental import pallas as pl
from jax.experimental.pallas import tpu as pltpu
from jax.sharding import PartitionSpec as P

VB = 128
H = 256
ITERS = 2
DAMP = 0.85
CHUNK = 16
X = 2
VMEM_LIMIT = 32 * 1024 * 1024

SMEM = pl.BlockSpec(memory_space=pltpu.SMEM)
VMEM = pl.BlockSpec(memory_space=pltpu.VMEM)
HBM = pl.BlockSpec(memory_space=pltpu.HBM)


def params():
    return pltpu.CompilerParams(vmem_limit_bytes=VMEM_LIMIT)


def one_hot(first, count, src):
    ids = lax.broadcasted_iota(jnp.int32, (count, src.shape[1]), 0) + first
    return (ids == src).astype(jnp.float32)


def write_terms(dims, block, prod_ref, dense_ref, panel_ref, send_ref, keep_ref):
    n_row, n_col, side = dims
    rows = dense_ref.shape[0] // 2
    c = lax.axis_index("col")
    prod = jnp.dot(dense_ref[...], panel_ref[...], preferred_element_type=jnp.float32)
    prod_ref[...] = prod[:rows] + prod[rows:]
    for ref, col in ((keep_ref, c), (send_ref, 1 - c)):
        ref[:VB] = prod_ref[pl.ds(pl.multiple_of(col * VB, VB), VB), :]
        for k in range(H // n_col // block):
            start = n_col * VB + (k * n_col + col) * block
            ref[VB + k * block:VB + (k + 1) * block] = prod_ref[pl.ds(pl.multiple_of(start, block), block), :]


def first_kernel(dims, tiles_ref, rows_hbm, cols_hbm, count_hbm, src_hbm,
                 send_ref, keep_ref, dense_ref,
                 held, rows_ref, cols_ref, count_ref, src_ref, total, panel, prod, sems, small):
    n_row, n_col, side = dims
    slots = tiles_ref.shape[0]
    n_rows = dense_ref.shape[0] // 2
    pairs = ((src_hbm, src_ref), (count_hbm, count_ref), (rows_hbm, rows_ref), (cols_hbm, cols_ref))
    scalars = [pltpu.make_async_copy(a, b, small.at[i]) for i, (a, b) in enumerate(pairs)]
    for copy in scalars:
        copy.start()
    copies = []
    for i in range(slots // CHUNK):
        part = pl.ds(i * CHUNK, CHUNK)
        copies.append(pltpu.make_async_copy(tiles_ref.at[part], held.at[part], sems.at[i]))
    for copy in copies:
        copy.start()
    total[...] = jnp.zeros_like(total)
    for copy in scalars:
        copy.wait()
    src = src_ref[...]
    for r in range(n_row):
        first = H + (r * n_col + lax.axis_index("col")) * VB
        panel[pl.ds(r * VB, VB), :] = one_hot(first, VB, src).astype(jnp.bfloat16)
    panel[pl.ds(n_row * VB, H), :] = one_hot(0, H, src).astype(jnp.bfloat16)
    count = count_ref[0]

    def add_tile(k, carry):
        live = k < count
        row = pl.multiple_of(jnp.where(live, rows_ref[k] * side, n_rows), side)
        col = pl.multiple_of(jnp.where(live, cols_ref[k] * side, 0), side)
        spot = (pl.ds(row, side), pl.ds(col, side))
        total[spot] += held[k].astype(jnp.float32)
        return carry

    for i, copy in enumerate(copies):
        copy.wait()
        lax.fori_loop(i * CHUNK, (i + 1) * CHUNK, add_tile, 0, unroll=4)
    for r in range(0, n_rows, side):
        whole = total[pl.ds(r, side), :]
        high = whole.astype(jnp.bfloat16)
        dense_ref[pl.ds(r, side), :] = high
        dense_ref[pl.ds(n_rows + r, side), :] = (whole - high.astype(jnp.float32)).astype(jnp.bfloat16)
    write_terms(dims, H // n_col, prod, dense_ref, panel, send_ref, keep_ref)


def second_kernel(dims, scores_ref, mine_ref, theirs_ref, dense_ref, send_ref, keep_ref, panel, prod):
    n_row, n_col, side = dims
    half = H // n_col
    c = lax.axis_index("col")
    for r in range(n_row):
        panel[pl.ds(r * VB, VB), :] = scores_ref[r]
    for ref, col in ((mine_ref, c), (theirs_ref, 1 - c)):
        panel[pl.ds(pl.multiple_of(n_row * VB + col * half, half), half), :] = ref[...]
    write_terms(dims, half // n_row, prod, dense_ref, panel, send_ref, keep_ref)


def own_scores(dims, src_ref, keep_ref, came_ref):
    first = H + (lax.axis_index("row") * dims[1] + lax.axis_index("col")) * VB
    tele = one_hot(first, VB, src_ref[...])
    return DAMP * (keep_ref[:VB] + came_ref[:VB]) + 0.15 * tele


def spread_kernel(dims, src_ref, keep_ref, came_ref, scores_ref, hold_ref, pass_ref):
    n_row, n_col, side = dims
    quarter = hold_ref.shape[0]
    x = lax.rem(lax.axis_index("row"), X)
    for ref, place in ((hold_ref, x), (pass_ref, 1 - x)):
        spot = pl.ds(pl.multiple_of(VB + place * quarter, quarter), quarter)
        ref[...] = keep_ref[spot, :] + came_ref[spot, :]
    own = own_scores(dims, src_ref, keep_ref, came_ref).astype(scores_ref.dtype)
    for k in range(n_row):
        scores_ref[k] = own


def plane_kernel(hold_ref, came_ref, out_ref):
    out_ref[...] = hold_ref[...] + came_ref[...]


def hub_kernel(dims, src_ref, *refs):
    n_row, n_col, side = dims
    planes, (out_ref, held) = refs[:-2], refs[-2:]
    quarter = out_ref.shape[0]
    r, c = lax.axis_index("row"), lax.axis_index("col")
    z, x = lax.div(r, X), lax.rem(r, X)
    n_z = len(planes)
    for k in range(n_z):
        held[lax.rem(z - k + n_z, n_z)] = planes[k][...]
    summed = held[0]
    for k in range(1, n_z):
        summed = summed + held[k]
    first = (c * X + x) * quarter
    out_ref[...] = (DAMP * summed + 0.15 * one_hot(first, quarter, src_ref[...])).astype(out_ref.dtype)


def side_kernel(mine_ref, theirs_ref, out_ref):
    quarter = mine_ref.shape[0]
    x = lax.rem(lax.axis_index("row"), X)
    for ref, place in ((mine_ref, x), (theirs_ref, 1 - x)):
        out_ref[pl.ds(pl.multiple_of(place * quarter, quarter), quarter), :] = ref[...]


def pieces_kernel(dims, keep_ref, came_ref, parts_ref):
    piece = parts_ref.shape[1]
    for k in range(parts_ref.shape[0]):
        spot = slice(VB + k * piece, VB + (k + 1) * piece)
        parts_ref[k] = keep_ref[spot, :] + came_ref[spot, :]


def last_scores_kernel(dims, src_ref, keep_ref, came_ref, scores_ref):
    scores_ref[...] = own_scores(dims, src_ref, keep_ref, came_ref)


def last_hubs_kernel(dims, src_ref, parts_ref, out_ref):
    piece = out_ref.shape[0]
    summed = parts_ref[0]
    for k in range(1, parts_ref.shape[0]):
        summed = summed + parts_ref[k]
    first = (lax.axis_index("row") * dims[1] + lax.axis_index("col")) * piece
    out_ref[...] = DAMP * summed + 0.15 * one_hot(first, piece, src_ref[...])


def fast_body(tiles, tile_row, tile_col, tile_count, sources):
    slots, side = tiles.shape[2:4]
    width = sources.shape[0]
    n_row = lax.axis_size("row")
    n_col = lax.axis_size("col")
    piece = H // (n_row * n_col)
    dims = (n_row, n_col, side)
    n_rows = n_col * VB + H
    n_cols = n_row * VB + H
    f32 = functools.partial(jax.ShapeDtypeStruct, dtype=jnp.float32)
    bf16 = functools.partial(jax.ShapeDtypeStruct, dtype=jnp.bfloat16)
    src = sources.reshape(1, width)
    half = VB + n_row * piece
    product_scratch = [
        pltpu.VMEM((n_cols, width), jnp.bfloat16),
        pltpu.VMEM((n_rows, width), jnp.float32),
    ]

    def other_core(x):
        return lax.ppermute(x, "col", [(0, 1), (1, 0)])

    def along_row(x, target):
        return lax.ppermute(x, "row", [(r, target(r)) for r in range(n_row)])

    def other_side(x):
        return along_row(x, lambda r: r ^ 1)

    def call(kernel, name, out_shape, *args, scratch=()):
        return pl.pallas_call(
            kernel,
            out_shape=out_shape,
            in_specs=[VMEM] * len(args),
            out_specs=jax.tree.map(lambda _: VMEM, out_shape),
            scratch_shapes=scratch,
            compiler_params=params(),
            name=name,
        )(*args)

    bind = functools.partial

    send, keep, dense = pl.pallas_call(
        functools.partial(first_kernel, dims),
        out_shape=(f32((half, width)), f32((half, width)), bf16((2 * n_rows, n_cols))),
        in_specs=[HBM] * 5,
        out_specs=[VMEM] * 3,
        scratch_shapes=[
            pltpu.VMEM((slots, side, side), jnp.bfloat16),
            pltpu.SMEM((slots,), jnp.int32),
            pltpu.SMEM((slots,), jnp.int32),
            pltpu.SMEM((1,), jnp.int32),
            pltpu.VMEM((1, width), jnp.int32),
            pltpu.VMEM((n_rows + side, n_cols), jnp.float32),
        ] + product_scratch + [
            pltpu.SemaphoreType.DMA((slots // CHUNK,)),
            pltpu.SemaphoreType.DMA((4,)),
        ],
        compiler_params=params(),
        name="first_terms",
    )(tiles.reshape(slots, side, side), tile_row.reshape(slots), tile_col.reshape(slots),
      tile_count.reshape(1), src)

    quarter = H // n_col // X
    for step in range(ITERS - 1):
        came = other_core(send)
        scores, hold, away = call(
            bind(spread_kernel, dims), "spread",
            (bf16((n_row, VB, width)), f32((quarter, width)), f32((quarter, width))),
            src, keep, came)
        scores = lax.all_to_all(scores, "row", 0, 0)
        plane = call(plane_kernel, "plane_sum", f32((quarter, width)), hold, other_side(away))
        planes = [plane] + [along_row(plane, lambda r: (r + X * k) % n_row) for k in range(1, n_row // X)]
        mine = call(bind(hub_kernel, dims), "hub_sums", bf16((quarter, width)), src, *planes,
                    scratch=[pltpu.VMEM((n_row // X, quarter, width), jnp.float32)])
        mine = call(side_kernel, "join_sides", bf16((H // n_col, width)), mine, other_side(mine))
        send, keep = call(
            bind(second_kernel, dims), "later_terms", (f32((half, width)), f32((half, width))),
            scores, mine, other_core(mine), dense, scratch=product_scratch)
    came = other_core(send)
    parts = call(bind(pieces_kernel, dims), "hub_pieces", f32((n_row, piece, width)), keep, came)
    parts = lax.all_to_all(parts, "row", 0, 0)
    scores = call(bind(last_scores_kernel, dims), "last_scores", f32((VB, width)), src, keep, came)
    hubs = call(bind(last_hubs_kernel, dims), "last_hubs", f32((piece, width)), src, parts)
    return scores.reshape(1, 1, VB, width), hubs


def plain_body(tiles, tile_row, tile_col, tile_count, sources):
    slots = tiles.shape[2]
    side = tiles.shape[3]
    width = sources.shape[0]
    tiles = tiles.reshape(slots, side, side)
    rows = tile_row.reshape(slots)
    cols = tile_col.reshape(slots)
    count = tile_count.reshape(())
    n_row = lax.axis_size("row")
    n_col = lax.axis_size("col")
    devices = n_row * n_col
    r_index = lax.axis_index("row")
    c_index = lax.axis_index("col")
    hub_dev = H // devices
    block_rows = n_col * VB
    n_tile_rows = (block_rows + H) // side
    own_base = H + (r_index * n_col + c_index) * VB
    hub_start = (r_index * n_col + c_index) * hub_dev
    own_ids = jnp.arange(VB, dtype=jnp.int32) + own_base
    tele_own = (own_ids[:, None] == sources[None, :]).astype(jnp.float32)
    piece_ids = jnp.arange(hub_dev, dtype=jnp.int32) + hub_start
    tele_piece = (piece_ids[:, None] == sources[None, :]).astype(jnp.float32)
    tele_hubs = (jnp.arange(H, dtype=jnp.int32)[:, None] == sources[None, :]).astype(jnp.float32)
    column_ids = (
        H
        + (jnp.arange(n_row, dtype=jnp.int32)[:, None] * n_col + c_index) * VB
        + jnp.arange(VB, dtype=jnp.int32)[None, :]
    ).reshape(n_row * VB)
    column_panel = (column_ids[:, None] == sources[None, :]).astype(jnp.bfloat16)
    hub_panel = tele_hubs.astype(jnp.bfloat16)
    block = CHUNK
    own_scores = tele_own
    hub_piece = tele_piece
    for step in range(ITERS):
        start_acc = jnp.zeros((n_tile_rows, side, width), jnp.float32)
        if step > 0:
            column_panel = lax.all_gather(
                own_scores.astype(jnp.bfloat16), "row", axis=0, tiled=True
            )
        panel = jnp.concatenate([column_panel, hub_panel], axis=0).reshape(-1, side, width)

        def step_fn(number, total):
            start = number * block
            tile_block = lax.dynamic_slice_in_dim(tiles, start, block, 0)
            col_block = lax.dynamic_slice_in_dim(cols, start, block, 0)
            row_block = lax.dynamic_slice_in_dim(rows, start, block, 0)
            pieces = jnp.take(panel, col_block, axis=0)
            prod = jnp.einsum(
                "tij,tjs->tis", tile_block, pieces, preferred_element_type=jnp.float32
            )
            live = start + jnp.arange(block, dtype=jnp.int32) < count
            prod = jnp.where(live[:, None, None], prod, 0.0)
            return total.at[row_block].add(prod)

        total = lax.fori_loop(0, slots // block, step_fn, start_acc)
        partial_value = total.reshape(n_tile_rows * side, width)
        summed_rows = lax.psum_scatter(
            partial_value[:block_rows], "col", scatter_dimension=0, tiled=True
        )
        own_scores = 0.85 * summed_rows + 0.15 * tele_own
        hub_part = partial_value[block_rows:]
        summed = lax.psum_scatter(hub_part, ("row", "col"), scatter_dimension=0, tiled=True)
        hub_piece = 0.85 * summed + 0.15 * tele_piece
        if step + 1 < ITERS:
            hub_panel = lax.all_gather(
                hub_piece.astype(jnp.bfloat16), ("row", "col"), axis=0, tiled=True
            )
    return (own_scores.reshape(1, 1, VB, width), hub_piece)


def solution(mesh):
    placed = (
        P(("groups", "row"), "col", None, None, None),
        P(("groups", "row"), "col", None),
        P(("groups", "row"), "col", None),
        P(("groups", "row"), "col"),
        P("groups"),
    )

    def body(tiles, *rest):
        n_row, n_col = mesh.shape["row"], mesh.shape["col"]
        slots, side = tiles.shape[2:4]
        blocks = (n_col * VB + H) * (n_row * VB + H) // (side * side)
        if n_col == 2 and blocks <= slots and H // (n_row * n_col) % 16 == 0:
            return fast_body(tiles, *rest)
        return plain_body(tiles, *rest)

    return jax.shard_map(
        body,
        mesh=mesh,
        in_specs=placed,
        out_specs=(P(("groups", "row"), "col", None, None), P(("groups", "row", "col"), None)),
        check_vma=False,
    )
```

```python
import functools

import jax
import jax.numpy as jnp
from jax import lax
from jax.experimental import pallas as pl
from jax.experimental.pallas import tpu as pltpu
from jax.sharding import PartitionSpec as P

VB = 128
H = 256
ITERS = 2
DAMP = 0.85
CHUNK = 16
X = 2
VMEM_LIMIT = 32 * 1024 * 1024

SMEM = pl.BlockSpec(memory_space=pltpu.SMEM)
VMEM = pl.BlockSpec(memory_space=pltpu.VMEM)
HBM = pl.BlockSpec(memory_space=pltpu.HBM)


def params():
    return pltpu.CompilerParams(vmem_limit_bytes=VMEM_LIMIT)


def one_hot(first, count, src):
    ids = lax.broadcasted_iota(jnp.int32, (count, src.shape[1]), 0) + first
    return (ids == src).astype(jnp.float32)


def write_terms(dims, block, prod_ref, dense_ref, panel_ref, send_ref, keep_ref):
    n_row, n_col, side = dims
    rows = dense_ref.shape[0] // 2
    c = lax.axis_index("col")
    prod = jnp.dot(dense_ref[...], panel_ref[...], preferred_element_type=jnp.float32)
    prod_ref[...] = prod[:rows] + prod[rows:]
    for ref, col in ((keep_ref, c), (send_ref, 1 - c)):
        ref[:VB] = prod_ref[pl.ds(pl.multiple_of(col * VB, VB), VB), :]
        for k in range(H // n_col // block):
            start = n_col * VB + (k * n_col + col) * block
            ref[VB + k * block:VB + (k + 1) * block] = prod_ref[pl.ds(pl.multiple_of(start, block), block), :]


def first_kernel(dims, tiles_ref, rows_hbm, cols_hbm, count_hbm, src_hbm,
                 send_ref, keep_ref, dense_ref,
                 held, rows_ref, cols_ref, count_ref, src_ref, total, panel, prod, sems, small):
    n_row, n_col, side = dims
    slots = tiles_ref.shape[0]
    n_rows = dense_ref.shape[0] // 2
    pairs = ((src_hbm, src_ref), (count_hbm, count_ref), (rows_hbm, rows_ref), (cols_hbm, cols_ref))
    scalars = [pltpu.make_async_copy(a, b, small.at[i]) for i, (a, b) in enumerate(pairs)]
    for copy in scalars:
        copy.start()
    copies = []
    for i in range(slots // CHUNK):
        part = pl.ds(i * CHUNK, CHUNK)
        copies.append(pltpu.make_async_copy(tiles_ref.at[part], held.at[part], sems.at[i]))
    for copy in copies:
        copy.start()
    total[...] = jnp.zeros_like(total)
    for copy in scalars:
        copy.wait()
    src = src_ref[...]
    for r in range(n_row):
        first = H + (r * n_col + lax.axis_index("col")) * VB
        panel[pl.ds(r * VB, VB), :] = one_hot(first, VB, src).astype(jnp.bfloat16)
    panel[pl.ds(n_row * VB, H), :] = one_hot(0, H, src).astype(jnp.bfloat16)
    count = count_ref[0]

    def add_tile(k, carry):
        live = k < count
        row = pl.multiple_of(jnp.where(live, rows_ref[k] * side, n_rows), side)
        col = pl.multiple_of(jnp.where(live, cols_ref[k] * side, 0), side)
        spot = (pl.ds(row, side), pl.ds(col, side))
        total[spot] += held[k].astype(jnp.float32)
        return carry

    for i, copy in enumerate(copies):
        copy.wait()
        lax.fori_loop(i * CHUNK, (i + 1) * CHUNK, add_tile, 0, unroll=4)
    for r in range(0, n_rows, side):
        whole = total[pl.ds(r, side), :]
        high = whole.astype(jnp.bfloat16)
        dense_ref[pl.ds(r, side), :] = high
        dense_ref[pl.ds(n_rows + r, side), :] = (whole - high.astype(jnp.float32)).astype(jnp.bfloat16)
    write_terms(dims, H // n_col, prod, dense_ref, panel, send_ref, keep_ref)


def second_kernel(dims, *refs):
    n_row, n_col, side = dims
    n_z = n_row // X
    own, far, (across, far_across, mine_ref, theirs_ref), rest = refs[0], refs[1:n_z], refs[n_z:n_z + 4], refs[n_z + 4:]
    dense_ref, send_ref, keep_ref, panel, prod = rest
    half = H // n_col
    r, c = lax.axis_index("row"), lax.axis_index("col")

    def put(owner, block):
        panel[pl.ds(pl.multiple_of(owner * VB, VB), VB), :] = block

    put(r, own[...])
    put(r ^ 1, across[...])
    for k in range(1, n_z):
        put(r ^ (X * k), far[k - 1][...])
        put(r ^ (X * k) ^ 1, far_across[k - 1])
    for ref, col in ((mine_ref, c), (theirs_ref, 1 - c)):
        panel[pl.ds(pl.multiple_of(n_row * VB + col * half, half), half), :] = ref[...]
    write_terms(dims, half // n_row, prod, dense_ref, panel, send_ref, keep_ref)


def own_scores(dims, src_ref, keep_ref, came_ref):
    first = H + (lax.axis_index("row") * dims[1] + lax.axis_index("col")) * VB
    tele = one_hot(first, VB, src_ref[...])
    return DAMP * (keep_ref[:VB] + came_ref[:VB]) + 0.15 * tele


def spread_kernel(dims, src_ref, keep_ref, came_ref, scores_ref, hold_ref, pass_ref):
    quarter = hold_ref.shape[0]
    x = lax.axis_index("row") % X
    for ref, place in ((hold_ref, x), (pass_ref, 1 - x)):
        spot = pl.ds(pl.multiple_of(VB + place * quarter, quarter), quarter)
        ref[...] = keep_ref[spot, :] + came_ref[spot, :]
    scores_ref[...] = own_scores(dims, src_ref, keep_ref, came_ref).astype(scores_ref.dtype)


def join_kernel(*refs):
    for k, ref in enumerate(refs[:-1]):
        refs[-1][k] = ref[...]


def plane_kernel(hold_ref, came_ref, out_ref):
    out_ref[...] = hold_ref[...] + came_ref[...]


def sum_planes(planes, held):
    z = lax.axis_index("row") // X
    for k, plane in enumerate(planes):
        held[z ^ k] = plane[...]
    summed = held[0]
    for k in range(1, len(planes)):
        summed = summed + held[k]
    return summed


def hub_kernel(dims, src_ref, *refs):
    planes, (out_ref, held) = refs[:-2], refs[-2:]
    quarter = out_ref.shape[0]
    first = (lax.axis_index("col") * X + lax.axis_index("row") % X) * quarter
    tele = one_hot(first, quarter, src_ref[...])
    out_ref[...] = (DAMP * sum_planes(planes, held) + 0.15 * tele).astype(out_ref.dtype)


def side_kernel(mine_ref, theirs_ref, out_ref):
    quarter = mine_ref.shape[0]
    x = lax.axis_index("row") % X
    for ref, place in ((mine_ref, x), (theirs_ref, 1 - x)):
        out_ref[pl.ds(pl.multiple_of(place * quarter, quarter), quarter), :] = ref[...]


def halves_kernel(dims, keep_ref, came_ref, hold_ref, pass_ref):
    n_row, n_col, side = dims
    piece = H // (n_row * n_col)
    x = lax.axis_index("row") % X
    for ref, place in ((hold_ref, x), (pass_ref, 1 - x)):
        for z in range(n_row // X):
            spot = pl.ds(pl.multiple_of(VB + (z * X + place) * piece, piece), piece)
            ref[z * piece:(z + 1) * piece] = keep_ref[spot, :] + came_ref[spot, :]


def pieces_kernel(hold_ref, came_ref, *outs):
    z = lax.axis_index("row") // X
    piece = outs[0].shape[0]
    for k, out in enumerate(outs):
        spot = pl.ds(pl.multiple_of((z ^ k) * piece, piece), piece)
        out[...] = hold_ref[spot, :] + came_ref[spot, :]


def last_scores_kernel(dims, src_ref, keep_ref, came_ref, scores_ref):
    scores_ref[...] = own_scores(dims, src_ref, keep_ref, came_ref)


def last_hubs_kernel(dims, src_ref, *refs):
    planes, (out_ref, held) = refs[:-2], refs[-2:]
    piece = out_ref.shape[0]
    first = (lax.axis_index("row") * dims[1] + lax.axis_index("col")) * piece
    out_ref[...] = DAMP * sum_planes(planes, held) + 0.15 * one_hot(first, piece, src_ref[...])


def fast_body(tiles, tile_row, tile_col, tile_count, sources):
    slots, side = tiles.shape[2:4]
    width = sources.shape[0]
    n_row = lax.axis_size("row")
    n_col = lax.axis_size("col")
    piece = H // (n_row * n_col)
    dims = (n_row, n_col, side)
    n_rows = n_col * VB + H
    n_cols = n_row * VB + H
    f32 = functools.partial(jax.ShapeDtypeStruct, dtype=jnp.float32)
    bf16 = functools.partial(jax.ShapeDtypeStruct, dtype=jnp.bfloat16)
    src = sources.reshape(1, width)
    half = VB + n_row * piece
    product_scratch = [
        pltpu.VMEM((n_cols, width), jnp.bfloat16),
        pltpu.VMEM((n_rows, width), jnp.float32),
    ]

    def other_core(x):
        return lax.ppermute(x, "col", [(0, 1), (1, 0)])

    def to_partner(x, flip):
        return lax.ppermute(x, "row", [(r, r ^ flip) for r in range(n_row)])

    def other_side(x):
        return to_partner(x, 1)

    def along_z(blocks):
        return [to_partner(block, X * k) for k, block in enumerate(blocks) if k > 0]

    def call(kernel, name, out_shape, *args, scratch=()):
        return pl.pallas_call(
            kernel,
            out_shape=out_shape,
            in_specs=[VMEM] * len(args),
            out_specs=jax.tree.map(lambda _: VMEM, out_shape),
            scratch_shapes=scratch,
            compiler_params=params(),
            name=name,
        )(*args)

    bind = functools.partial

    send, keep, dense = pl.pallas_call(
        functools.partial(first_kernel, dims),
        out_shape=(f32((half, width)), f32((half, width)), bf16((2 * n_rows, n_cols))),
        in_specs=[HBM] * 5,
        out_specs=[VMEM] * 3,
        scratch_shapes=[
            pltpu.VMEM((slots, side, side), jnp.bfloat16),
            pltpu.SMEM((slots,), jnp.int32),
            pltpu.SMEM((slots,), jnp.int32),
            pltpu.SMEM((1,), jnp.int32),
            pltpu.VMEM((1, width), jnp.int32),
            pltpu.VMEM((n_rows + side, n_cols), jnp.float32),
        ] + product_scratch + [
            pltpu.SemaphoreType.DMA((slots // CHUNK,)),
            pltpu.SemaphoreType.DMA((4,)),
        ],
        compiler_params=params(),
        name="first_terms",
    )(tiles.reshape(slots, side, side), tile_row.reshape(slots), tile_col.reshape(slots),
      tile_count.reshape(1), src)

    quarter = H // n_col // X
    n_z = n_row // X
    for step in range(ITERS - 1):
        came = other_core(send)
        own, hold, away = call(
            bind(spread_kernel, dims), "spread",
            (bf16((VB, width)), f32((quarter, width)), f32((quarter, width))),
            src, keep, came)
        away = other_side(away)
        far = along_z([own] * n_z)
        across = other_side(own)
        plane = call(plane_kernel, "plane_sum", f32((quarter, width)), hold, away)
        planes = [plane] + along_z([plane] * n_z)
        far_across = other_side(call(join_kernel, "join_far", bf16((n_z - 1, VB, width)), *far))
        mine = call(bind(hub_kernel, dims), "hub_sums", bf16((quarter, width)), src, *planes,
                    scratch=[pltpu.VMEM((n_z, quarter, width), jnp.float32)])
        mine = call(side_kernel, "join_sides", bf16((H // n_col, width)), mine, other_side(mine))
        send, keep = call(
            bind(second_kernel, dims), "later_terms", (f32((half, width)), f32((half, width))),
            own, *far, across, far_across, mine, other_core(mine), dense, scratch=product_scratch)
    came = other_core(send)
    hold, away = call(bind(halves_kernel, dims), "hub_halves",
                      (f32((quarter, width)), f32((quarter, width))), keep, came)
    pieces = call(pieces_kernel, "hub_pieces", (f32((piece, width)),) * n_z, hold, other_side(away))
    pieces = [pieces[0]] + along_z(pieces)
    scores = call(bind(last_scores_kernel, dims), "last_scores", f32((VB, width)), src, keep, came)
    hubs = call(bind(last_hubs_kernel, dims), "last_hubs", f32((piece, width)), src, *pieces,
                scratch=[pltpu.VMEM((n_z, piece, width), jnp.float32)])
    return scores.reshape(1, 1, VB, width), hubs


def plain_body(tiles, tile_row, tile_col, tile_count, sources):
    slots = tiles.shape[2]
    side = tiles.shape[3]
    width = sources.shape[0]
    tiles = tiles.reshape(slots, side, side)
    rows = tile_row.reshape(slots)
    cols = tile_col.reshape(slots)
    count = tile_count.reshape(())
    n_row = lax.axis_size("row")
    n_col = lax.axis_size("col")
    devices = n_row * n_col
    r_index = lax.axis_index("row")
    c_index = lax.axis_index("col")
    hub_dev = H // devices
    block_rows = n_col * VB
    n_tile_rows = (block_rows + H) // side
    own_base = H + (r_index * n_col + c_index) * VB
    hub_start = (r_index * n_col + c_index) * hub_dev
    own_ids = jnp.arange(VB, dtype=jnp.int32) + own_base
    tele_own = (own_ids[:, None] == sources[None, :]).astype(jnp.float32)
    piece_ids = jnp.arange(hub_dev, dtype=jnp.int32) + hub_start
    tele_piece = (piece_ids[:, None] == sources[None, :]).astype(jnp.float32)
    tele_hubs = (jnp.arange(H, dtype=jnp.int32)[:, None] == sources[None, :]).astype(jnp.float32)
    column_ids = (
        H
        + (jnp.arange(n_row, dtype=jnp.int32)[:, None] * n_col + c_index) * VB
        + jnp.arange(VB, dtype=jnp.int32)[None, :]
    ).reshape(n_row * VB)
    column_panel = (column_ids[:, None] == sources[None, :]).astype(jnp.bfloat16)
    hub_panel = tele_hubs.astype(jnp.bfloat16)
    block = CHUNK
    own_scores = tele_own
    hub_piece = tele_piece
    for step in range(ITERS):
        start_acc = jnp.zeros((n_tile_rows, side, width), jnp.float32)
        if step > 0:
            column_panel = lax.all_gather(
                own_scores.astype(jnp.bfloat16), "row", axis=0, tiled=True
            )
        panel = jnp.concatenate([column_panel, hub_panel], axis=0).reshape(-1, side, width)

        def step_fn(number, total):
            start = number * block
            tile_block = lax.dynamic_slice_in_dim(tiles, start, block, 0)
            col_block = lax.dynamic_slice_in_dim(cols, start, block, 0)
            row_block = lax.dynamic_slice_in_dim(rows, start, block, 0)
            pieces = jnp.take(panel, col_block, axis=0)
            prod = jnp.einsum(
                "tij,tjs->tis", tile_block, pieces, preferred_element_type=jnp.float32
            )
            live = start + jnp.arange(block, dtype=jnp.int32) < count
            prod = jnp.where(live[:, None, None], prod, 0.0)
            return total.at[row_block].add(prod)

        total = lax.fori_loop(0, slots // block, step_fn, start_acc)
        partial_value = total.reshape(n_tile_rows * side, width)
        summed_rows = lax.psum_scatter(
            partial_value[:block_rows], "col", scatter_dimension=0, tiled=True
        )
        own_scores = 0.85 * summed_rows + 0.15 * tele_own
        hub_part = partial_value[block_rows:]
        summed = lax.psum_scatter(hub_part, ("row", "col"), scatter_dimension=0, tiled=True)
        hub_piece = 0.85 * summed + 0.15 * tele_piece
        if step + 1 < ITERS:
            hub_panel = lax.all_gather(
                hub_piece.astype(jnp.bfloat16), ("row", "col"), axis=0, tiled=True
            )
    return (own_scores.reshape(1, 1, VB, width), hub_piece)


def solution(mesh):
    placed = (
        P(("groups", "row"), "col", None, None, None),
        P(("groups", "row"), "col", None),
        P(("groups", "row"), "col", None),
        P(("groups", "row"), "col"),
        P("groups"),
    )

    def body(tiles, *rest):
        n_row, n_col = mesh.shape["row"], mesh.shape["col"]
        slots, side = tiles.shape[2:4]
        blocks = (n_col * VB + H) * (n_row * VB + H) // (side * side)
        if n_col == 2 and n_row in (4, 8, 16) and blocks <= slots and H // (n_row * n_col) % 16 == 0:
            return fast_body(tiles, *rest)
        return plain_body(tiles, *rest)

    return jax.shard_map(
        body,
        mesh=mesh,
        in_specs=placed,
        out_specs=(P(("groups", "row"), "col", None, None), P(("groups", "row", "col"), None)),
        check_vma=False,
    )
```

```python
import functools

import jax
import jax.numpy as jnp
from jax import lax
from jax.experimental import pallas as pl
from jax.experimental.pallas import tpu as pltpu
from jax.sharding import PartitionSpec as P

VB = 128
H = 256
ITERS = 2
DAMP = 0.85
CHUNK = 16
X = 2
MICRO = 10 ** 9
VMEM_LIMIT = 32 * 1024 * 1024

SMEM = pl.BlockSpec(memory_space=pltpu.SMEM)
VMEM = pl.BlockSpec(memory_space=pltpu.VMEM)
HBM = pl.BlockSpec(memory_space=pltpu.HBM)


def params():
    return pltpu.CompilerParams(vmem_limit_bytes=VMEM_LIMIT)


def one_hot(first, count, src):
    ids = lax.broadcasted_iota(jnp.int32, (count, src.shape[1]), 0) + first
    return (ids == src).astype(jnp.float32)


def write_terms(dims, block, prod_ref, dense_ref, panel_ref, send_ref, keep_ref):
    n_row, n_col, side = dims
    rows = dense_ref.shape[0] // 2
    c = lax.axis_index("col")
    prod = jnp.dot(dense_ref[...], panel_ref[...], preferred_element_type=jnp.float32)
    prod_ref[...] = prod[:rows] + prod[rows:]
    for ref, col in ((keep_ref, c), (send_ref, 1 - c)):
        ref[:VB] = prod_ref[pl.ds(pl.multiple_of(col * VB, VB), VB), :]
        for k in range(H // n_col // block):
            start = n_col * VB + (k * n_col + col) * block
            ref[VB + k * block:VB + (k + 1) * block] = prod_ref[pl.ds(pl.multiple_of(start, block), block), :]


def first_kernel(dims, tiles_ref, rows_hbm, cols_hbm, count_hbm, src_hbm,
                 send_ref, keep_ref, dense_ref,
                 held, rows_ref, cols_ref, count_ref, src_ref, total, panel, prod, sems, small):
    n_row, n_col, side = dims
    slots = tiles_ref.shape[0]
    n_rows = dense_ref.shape[0] // 2
    pairs = ((src_hbm, src_ref), (count_hbm, count_ref), (rows_hbm, rows_ref), (cols_hbm, cols_ref))
    scalars = [pltpu.make_async_copy(a, b, small.at[i]) for i, (a, b) in enumerate(pairs)]
    for copy in scalars:
        copy.start()
    copies = []
    for i in range(slots // CHUNK):
        part = pl.ds(i * CHUNK, CHUNK)
        copies.append(pltpu.make_async_copy(tiles_ref.at[part], held.at[part], sems.at[i]))
    for copy in copies:
        copy.start()
    total[...] = jnp.zeros_like(total)
    for copy in scalars:
        copy.wait()
    src = src_ref[...]
    for r in range(n_row):
        first = H + (r * n_col + lax.axis_index("col")) * VB
        panel[pl.ds(r * VB, VB), :] = one_hot(first, VB, src).astype(jnp.bfloat16)
    panel[pl.ds(n_row * VB, H), :] = one_hot(0, H, src).astype(jnp.bfloat16)
    count = count_ref[0]

    def add_tile(k, carry):
        live = k < count
        row = pl.multiple_of(jnp.where(live, rows_ref[k] * side, n_rows), side)
        col = pl.multiple_of(jnp.where(live, cols_ref[k] * side, 0), side)
        spot = (pl.ds(row, side), pl.ds(col, side))
        total[spot] += held[k].astype(jnp.float32)
        return carry

    for i, copy in enumerate(copies):
        copy.wait()
        lax.fori_loop(i * CHUNK, (i + 1) * CHUNK, add_tile, 0, unroll=4)
    for r in range(0, n_rows, side):
        whole = total[pl.ds(r, side), :]
        high = whole.astype(jnp.bfloat16)
        dense_ref[pl.ds(r, side), :] = high
        dense_ref[pl.ds(n_rows + r, side), :] = (whole - high.astype(jnp.float32)).astype(jnp.bfloat16)
    write_terms(dims, H // n_col, prod, dense_ref, panel, send_ref, keep_ref)


def second_kernel(dims, *refs):
    n_row, n_col, side = dims
    n_z = n_row // X
    own, far, (across, far_across, mine_ref, theirs_ref), rest = refs[0], refs[1:n_z], refs[n_z:n_z + 4], refs[n_z + 4:]
    dense_ref, send_ref, keep_ref, panel, prod = rest
    half = H // n_col
    r, c = lax.axis_index("row"), lax.axis_index("col")

    def put(owner, block):
        panel[pl.ds(pl.multiple_of(owner * VB, VB), VB), :] = block

    put(r, own[...])
    put(r ^ 1, across[...])
    for k in range(1, n_z):
        put(r ^ (X * k), far[k - 1][...])
        put(r ^ (X * k) ^ 1, far_across[k - 1])
    for ref, col in ((mine_ref, c), (theirs_ref, 1 - c)):
        panel[pl.ds(pl.multiple_of(n_row * VB + col * half, half), half), :] = ref[...]
    write_terms(dims, half // n_row, prod, dense_ref, panel, send_ref, keep_ref)


def own_scores(dims, src_ref, keep_ref, came_ref):
    first = H + (lax.axis_index("row") * dims[1] + lax.axis_index("col")) * VB
    tele = one_hot(first, VB, src_ref[...])
    return DAMP * (keep_ref[:VB] + came_ref[:VB]) + 0.15 * tele


def spread_kernel(dims, src_ref, keep_ref, came_ref, scores_ref, hold_ref, pass_ref):
    quarter = hold_ref.shape[0]
    x = lax.axis_index("row") % X
    for ref, place in ((hold_ref, x), (pass_ref, 1 - x)):
        spot = pl.ds(pl.multiple_of(VB + place * quarter, quarter), quarter)
        ref[...] = keep_ref[spot, :] + came_ref[spot, :]
    scores_ref[...] = own_scores(dims, src_ref, keep_ref, came_ref).astype(scores_ref.dtype)


def join_kernel(*refs):
    for k, ref in enumerate(refs[:-1]):
        refs[-1][k] = ref[...]


def plane_kernel(hold_ref, came_ref, out_ref):
    out_ref[...] = hold_ref[...] + came_ref[...]


def sum_planes(planes, held):
    z = lax.axis_index("row") // X
    for k, plane in enumerate(planes):
        held[z ^ k] = plane[...]
    summed = held[0]
    for k in range(1, len(planes)):
        summed = summed + held[k]
    return summed


def hub_kernel(dims, src_ref, *refs):
    planes, (out_ref, held) = refs[:-2], refs[-2:]
    quarter = out_ref.shape[0]
    first = (lax.axis_index("col") * X + lax.axis_index("row") % X) * quarter
    tele = one_hot(first, quarter, src_ref[...])
    out_ref[...] = (DAMP * sum_planes(planes, held) + 0.15 * tele).astype(out_ref.dtype)


def side_kernel(mine_ref, theirs_ref, out_ref):
    quarter = mine_ref.shape[0]
    x = lax.axis_index("row") % X
    for ref, place in ((mine_ref, x), (theirs_ref, 1 - x)):
        out_ref[pl.ds(pl.multiple_of(place * quarter, quarter), quarter), :] = ref[...]


def halves_kernel(dims, keep_ref, came_ref, hold_ref, pass_ref):
    n_row, n_col, side = dims
    piece = H // (n_row * n_col)
    x = lax.axis_index("row") % X
    for ref, place in ((hold_ref, x), (pass_ref, 1 - x)):
        for z in range(n_row // X):
            spot = pl.ds(pl.multiple_of(VB + (z * X + place) * piece, piece), piece)
            ref[z * piece:(z + 1) * piece] = keep_ref[spot, :] + came_ref[spot, :]


def pieces_kernel(hold_ref, came_ref, *outs):
    z = lax.axis_index("row") // X
    piece = outs[0].shape[0]
    for k, out in enumerate(outs):
        spot = pl.ds(pl.multiple_of((z ^ k) * piece, piece), piece)
        out[...] = hold_ref[spot, :] + came_ref[spot, :]


def last_scores_kernel(dims, src_ref, keep_ref, came_ref, scores_ref):
    scores_ref[...] = own_scores(dims, src_ref, keep_ref, came_ref)


def last_hubs_kernel(dims, src_ref, *refs):
    planes, (out_ref, held) = refs[:-2], refs[-2:]
    piece = out_ref.shape[0]
    first = (lax.axis_index("row") * dims[1] + lax.axis_index("col")) * piece
    out_ref[...] = DAMP * sum_planes(planes, held) + 0.15 * one_hot(first, piece, src_ref[...])


def fast_body(tiles, tile_row, tile_col, tile_count, sources):
    slots, side = tiles.shape[2:4]
    width = sources.shape[0]
    n_row = lax.axis_size("row")
    n_col = lax.axis_size("col")
    piece = H // (n_row * n_col)
    dims = (n_row, n_col, side)
    n_rows = n_col * VB + H
    n_cols = n_row * VB + H
    f32 = functools.partial(jax.ShapeDtypeStruct, dtype=jnp.float32)
    bf16 = functools.partial(jax.ShapeDtypeStruct, dtype=jnp.bfloat16)
    src = sources.reshape(1, width)
    half = VB + n_row * piece
    product_scratch = [
        pltpu.VMEM((n_cols, width), jnp.bfloat16),
        pltpu.VMEM((n_rows, width), jnp.float32),
    ]

    def other_core(x):
        return lax.ppermute(x, "col", [(0, 1), (1, 0)])

    def to_partner(x, flip):
        return lax.ppermute(x, "row", [(r, r ^ flip) for r in range(n_row)])

    def other_side(x):
        return to_partner(x, 1)

    def along_z(blocks):
        return [to_partner(block, X * k) for k, block in enumerate(blocks) if k > 0]

    def call(kernel, name, out_shape, *args, scratch=(), cost=0):
        return pl.pallas_call(
            kernel,
            out_shape=out_shape,
            in_specs=[VMEM] * len(args),
            out_specs=jax.tree.map(lambda _: VMEM, out_shape),
            scratch_shapes=scratch,
            compiler_params=params(),
            cost_estimate=pl.CostEstimate(flops=cost * MICRO, bytes_accessed=0, transcendentals=0),
            name=name,
        )(*args)

    bind = functools.partial

    send, keep, dense = pl.pallas_call(
        functools.partial(first_kernel, dims),
        out_shape=(f32((half, width)), f32((half, width)), bf16((2 * n_rows, n_cols))),
        in_specs=[HBM] * 5,
        out_specs=[VMEM] * 3,
        scratch_shapes=[
            pltpu.VMEM((slots, side, side), jnp.bfloat16),
            pltpu.SMEM((slots,), jnp.int32),
            pltpu.SMEM((slots,), jnp.int32),
            pltpu.SMEM((1,), jnp.int32),
            pltpu.VMEM((1, width), jnp.int32),
            pltpu.VMEM((n_rows + side, n_cols), jnp.float32),
        ] + product_scratch + [
            pltpu.SemaphoreType.DMA((slots // CHUNK,)),
            pltpu.SemaphoreType.DMA((4,)),
        ],
        compiler_params=params(),
        name="first_terms",
    )(tiles.reshape(slots, side, side), tile_row.reshape(slots), tile_col.reshape(slots),
      tile_count.reshape(1), src)

    quarter = H // n_col // X
    n_z = n_row // X
    for step in range(ITERS - 1):
        came = other_core(send)
        own, hold, away = call(
            bind(spread_kernel, dims), "spread",
            (bf16((VB, width)), f32((quarter, width)), f32((quarter, width))),
            src, keep, came)
        away = other_side(away)
        far = along_z([own] * n_z)
        across = other_side(own)
        plane = call(plane_kernel, "plane_sum", f32((quarter, width)), hold, away, cost=100000)
        planes = [plane] + along_z([plane] * n_z)
        far_across = other_side(call(join_kernel, "join_far", bf16((n_z - 1, VB, width)), *far))
        mine = call(bind(hub_kernel, dims), "hub_sums", bf16((quarter, width)), src, *planes,
                    scratch=[pltpu.VMEM((n_z, quarter, width), jnp.float32)], cost=100000)
        mine = call(side_kernel, "join_sides", bf16((H // n_col, width)), mine, other_side(mine))
        send, keep = call(
            bind(second_kernel, dims), "later_terms", (f32((half, width)), f32((half, width))),
            own, *far, across, far_across, mine, other_core(mine), dense, scratch=product_scratch)
    came = other_core(send)
    hold, away = call(bind(halves_kernel, dims), "hub_halves",
                      (f32((quarter, width)), f32((quarter, width))), keep, came)
    pieces = call(pieces_kernel, "hub_pieces", (f32((piece, width)),) * n_z, hold, other_side(away))
    pieces = [pieces[0]] + along_z(pieces)
    scores = call(bind(last_scores_kernel, dims), "last_scores", f32((VB, width)), src, keep, came)
    hubs = call(bind(last_hubs_kernel, dims), "last_hubs", f32((piece, width)), src, *pieces,
                scratch=[pltpu.VMEM((n_z, piece, width), jnp.float32)])
    return scores.reshape(1, 1, VB, width), hubs


def plain_body(tiles, tile_row, tile_col, tile_count, sources):
    slots = tiles.shape[2]
    side = tiles.shape[3]
    width = sources.shape[0]
    tiles = tiles.reshape(slots, side, side)
    rows = tile_row.reshape(slots)
    cols = tile_col.reshape(slots)
    count = tile_count.reshape(())
    n_row = lax.axis_size("row")
    n_col = lax.axis_size("col")
    devices = n_row * n_col
    r_index = lax.axis_index("row")
    c_index = lax.axis_index("col")
    hub_dev = H // devices
    block_rows = n_col * VB
    n_tile_rows = (block_rows + H) // side
    own_base = H + (r_index * n_col + c_index) * VB
    hub_start = (r_index * n_col + c_index) * hub_dev
    own_ids = jnp.arange(VB, dtype=jnp.int32) + own_base
    tele_own = (own_ids[:, None] == sources[None, :]).astype(jnp.float32)
    piece_ids = jnp.arange(hub_dev, dtype=jnp.int32) + hub_start
    tele_piece = (piece_ids[:, None] == sources[None, :]).astype(jnp.float32)
    tele_hubs = (jnp.arange(H, dtype=jnp.int32)[:, None] == sources[None, :]).astype(jnp.float32)
    column_ids = (
        H
        + (jnp.arange(n_row, dtype=jnp.int32)[:, None] * n_col + c_index) * VB
        + jnp.arange(VB, dtype=jnp.int32)[None, :]
    ).reshape(n_row * VB)
    column_panel = (column_ids[:, None] == sources[None, :]).astype(jnp.bfloat16)
    hub_panel = tele_hubs.astype(jnp.bfloat16)
    block = CHUNK
    own_scores = tele_own
    hub_piece = tele_piece
    for step in range(ITERS):
        start_acc = jnp.zeros((n_tile_rows, side, width), jnp.float32)
        if step > 0:
            column_panel = lax.all_gather(
                own_scores.astype(jnp.bfloat16), "row", axis=0, tiled=True
            )
        panel = jnp.concatenate([column_panel, hub_panel], axis=0).reshape(-1, side, width)

        def step_fn(number, total):
            start = number * block
            tile_block = lax.dynamic_slice_in_dim(tiles, start, block, 0)
            col_block = lax.dynamic_slice_in_dim(cols, start, block, 0)
            row_block = lax.dynamic_slice_in_dim(rows, start, block, 0)
            pieces = jnp.take(panel, col_block, axis=0)
            prod = jnp.einsum(
                "tij,tjs->tis", tile_block, pieces, preferred_element_type=jnp.float32
            )
            live = start + jnp.arange(block, dtype=jnp.int32) < count
            prod = jnp.where(live[:, None, None], prod, 0.0)
            return total.at[row_block].add(prod)

        total = lax.fori_loop(0, slots // block, step_fn, start_acc)
        partial_value = total.reshape(n_tile_rows * side, width)
        summed_rows = lax.psum_scatter(
            partial_value[:block_rows], "col", scatter_dimension=0, tiled=True
        )
        own_scores = 0.85 * summed_rows + 0.15 * tele_own
        hub_part = partial_value[block_rows:]
        summed = lax.psum_scatter(hub_part, ("row", "col"), scatter_dimension=0, tiled=True)
        hub_piece = 0.85 * summed + 0.15 * tele_piece
        if step + 1 < ITERS:
            hub_panel = lax.all_gather(
                hub_piece.astype(jnp.bfloat16), ("row", "col"), axis=0, tiled=True
            )
    return (own_scores.reshape(1, 1, VB, width), hub_piece)


def solution(mesh):
    placed = (
        P(("groups", "row"), "col", None, None, None),
        P(("groups", "row"), "col", None),
        P(("groups", "row"), "col", None),
        P(("groups", "row"), "col"),
        P("groups"),
    )

    def body(tiles, *rest):
        n_row, n_col = mesh.shape["row"], mesh.shape["col"]
        slots, side = tiles.shape[2:4]
        blocks = (n_col * VB + H) * (n_row * VB + H) // (side * side)
        if n_col == 2 and n_row in (4, 8, 16) and blocks <= slots and H // (n_row * n_col) % 16 == 0:
            return fast_body(tiles, *rest)
        return plain_body(tiles, *rest)

    return jax.shard_map(
        body,
        mesh=mesh,
        in_specs=placed,
        out_specs=(P(("groups", "row"), "col", None, None), P(("groups", "row", "col"), None)),
        check_vma=False,
    )
```

```python
import functools

import jax
import jax.numpy as jnp
from jax import lax
from jax.experimental import pallas as pl
from jax.experimental.pallas import tpu as pltpu
from jax.sharding import PartitionSpec as P

VB = 128
H = 256
ITERS = 2
DAMP = 0.85
CHUNK = 16
X = 2
MICRO = 10 ** 9
VMEM_LIMIT = 32 * 1024 * 1024

SMEM = pl.BlockSpec(memory_space=pltpu.SMEM)
VMEM = pl.BlockSpec(memory_space=pltpu.VMEM)
HBM = pl.BlockSpec(memory_space=pltpu.HBM)


def params():
    return pltpu.CompilerParams(vmem_limit_bytes=VMEM_LIMIT)


def one_hot(first, count, src):
    ids = lax.broadcasted_iota(jnp.int32, (count, src.shape[1]), 0) + first
    return (ids == src).astype(jnp.float32)


def write_terms(dims, block, prod_ref, dense_ref, panel_ref, send_ref, keep_ref):
    n_row, n_col, side = dims
    rows = dense_ref.shape[0] // 2
    c = lax.axis_index("col")
    prod = jnp.dot(dense_ref[...], panel_ref[...], preferred_element_type=jnp.float32)
    prod_ref[...] = prod[:rows] + prod[rows:]
    for ref, col in ((keep_ref, c), (send_ref, 1 - c)):
        ref[:VB] = prod_ref[pl.ds(pl.multiple_of(col * VB, VB), VB), :]
        for k in range(H // n_col // block):
            start = n_col * VB + (k * n_col + col) * block
            ref[VB + k * block:VB + (k + 1) * block] = prod_ref[pl.ds(pl.multiple_of(start, block), block), :]


def first_kernel(dims, tiles_ref, rows_hbm, cols_hbm, count_hbm, src_hbm,
                 send_ref, keep_ref, dense_ref,
                 held, rows_ref, cols_ref, count_ref, src_ref, total, panel, prod, sems, small):
    n_row, n_col, side = dims
    slots = tiles_ref.shape[0]
    n_rows = dense_ref.shape[0] // 2
    pairs = ((src_hbm, src_ref), (count_hbm, count_ref), (rows_hbm, rows_ref), (cols_hbm, cols_ref))
    scalars = [pltpu.make_async_copy(a, b, small.at[i]) for i, (a, b) in enumerate(pairs)]
    for copy in scalars:
        copy.start()
    copies = []
    for i in range(slots // CHUNK):
        part = pl.ds(i * CHUNK, CHUNK)
        copies.append(pltpu.make_async_copy(tiles_ref.at[part], held.at[part], sems.at[i]))
    for copy in copies:
        copy.start()
    total[...] = jnp.zeros_like(total)
    for copy in scalars:
        copy.wait()
    src = src_ref[...]
    for r in range(n_row):
        first = H + (r * n_col + lax.axis_index("col")) * VB
        panel[pl.ds(r * VB, VB), :] = one_hot(first, VB, src).astype(jnp.bfloat16)
    panel[pl.ds(n_row * VB, H), :] = one_hot(0, H, src).astype(jnp.bfloat16)
    count = count_ref[0]

    def add_tile(k, carry):
        live = k < count
        row = pl.multiple_of(jnp.where(live, rows_ref[k] * side, n_rows), side)
        col = pl.multiple_of(jnp.where(live, cols_ref[k] * side, 0), side)
        spot = (pl.ds(row, side), pl.ds(col, side))
        total[spot] += held[k].astype(jnp.float32)
        return carry

    for i, copy in enumerate(copies):
        copy.wait()
        lax.fori_loop(i * CHUNK, (i + 1) * CHUNK, add_tile, 0, unroll=4)
    for r in range(0, n_rows, side):
        whole = total[pl.ds(r, side), :]
        high = whole.astype(jnp.bfloat16)
        dense_ref[pl.ds(r, side), :] = high
        dense_ref[pl.ds(n_rows + r, side), :] = (whole - high.astype(jnp.float32)).astype(jnp.bfloat16)
    write_terms(dims, H // n_col, prod, dense_ref, panel, send_ref, keep_ref)


def second_kernel(dims, *refs):
    n_row, n_col, side = dims
    n_z = n_row // X
    own, far, (across, far_across, mine_ref, theirs_ref), rest = refs[0], refs[1:n_z], refs[n_z:n_z + 4], refs[n_z + 4:]
    dense_ref, send_ref, keep_ref, panel, prod = rest
    half = H // n_col
    r, c = lax.axis_index("row"), lax.axis_index("col")

    def put(owner, block):
        panel[pl.ds(pl.multiple_of(owner * VB, VB), VB), :] = block

    put(r, own[...])
    put(r ^ 1, across[...])
    for k in range(1, n_z):
        put(r ^ (X * k), far[k - 1][...])
        put(r ^ (X * k) ^ 1, far_across[k - 1])
    for ref, col in ((mine_ref, c), (theirs_ref, 1 - c)):
        panel[pl.ds(pl.multiple_of(n_row * VB + col * half, half), half), :] = ref[...]
    write_terms(dims, half // n_row, prod, dense_ref, panel, send_ref, keep_ref)


def own_scores(dims, src_ref, keep_ref, came_ref):
    first = H + (lax.axis_index("row") * dims[1] + lax.axis_index("col")) * VB
    tele = one_hot(first, VB, src_ref[...])
    return DAMP * (keep_ref[:VB] + came_ref[:VB]) + 0.15 * tele


def spread_kernel(dims, src_ref, keep_ref, came_ref, scores_ref, hold_ref, pass_ref):
    quarter = hold_ref.shape[0]
    x = lax.axis_index("row") % X
    for ref, place in ((hold_ref, x), (pass_ref, 1 - x)):
        spot = pl.ds(pl.multiple_of(VB + place * quarter, quarter), quarter)
        ref[...] = keep_ref[spot, :] + came_ref[spot, :]
    scores_ref[...] = own_scores(dims, src_ref, keep_ref, came_ref).astype(scores_ref.dtype)


def join_kernel(*refs):
    for k, ref in enumerate(refs[:-1]):
        refs[-1][k] = ref[...]


def plane_kernel(hold_ref, came_ref, out_ref):
    out_ref[...] = hold_ref[...] + came_ref[...]


def sum_planes(planes, held):
    z = lax.axis_index("row") // X
    for k, plane in enumerate(planes):
        held[z ^ k] = plane[...]
    summed = held[0]
    for k in range(1, len(planes)):
        summed = summed + held[k]
    return summed


def hub_kernel(dims, src_ref, *refs):
    planes, (out_ref, held) = refs[:-2], refs[-2:]
    quarter = out_ref.shape[0]
    first = (lax.axis_index("col") * X + lax.axis_index("row") % X) * quarter
    tele = one_hot(first, quarter, src_ref[...])
    out_ref[...] = (DAMP * sum_planes(planes, held) + 0.15 * tele).astype(out_ref.dtype)


def side_kernel(mine_ref, theirs_ref, out_ref):
    quarter = mine_ref.shape[0]
    x = lax.axis_index("row") % X
    for ref, place in ((mine_ref, x), (theirs_ref, 1 - x)):
        out_ref[pl.ds(pl.multiple_of(place * quarter, quarter), quarter), :] = ref[...]


def halves_kernel(dims, keep_ref, came_ref, hold_ref, pass_ref):
    n_row, n_col, side = dims
    piece = H // (n_row * n_col)
    x = lax.axis_index("row") % X
    for ref, place in ((hold_ref, x), (pass_ref, 1 - x)):
        for z in range(n_row // X):
            spot = pl.ds(pl.multiple_of(VB + (z * X + place) * piece, piece), piece)
            ref[z * piece:(z + 1) * piece] = keep_ref[spot, :] + came_ref[spot, :]


def pieces_kernel(hold_ref, came_ref, *outs):
    z = lax.axis_index("row") // X
    piece = outs[0].shape[0]
    for k, out in enumerate(outs):
        spot = pl.ds(pl.multiple_of((z ^ k) * piece, piece), piece)
        out[...] = hold_ref[spot, :] + came_ref[spot, :]


def last_scores_kernel(dims, src_ref, keep_ref, came_ref, scores_ref):
    scores_ref[...] = own_scores(dims, src_ref, keep_ref, came_ref)


def last_hubs_kernel(dims, src_ref, *refs):
    planes, (out_ref, held) = refs[:-2], refs[-2:]
    piece = out_ref.shape[0]
    first = (lax.axis_index("row") * dims[1] + lax.axis_index("col")) * piece
    out_ref[...] = DAMP * sum_planes(planes, held) + 0.15 * one_hot(first, piece, src_ref[...])


def fast_body(tiles, tile_row, tile_col, tile_count, sources):
    slots, side = tiles.shape[2:4]
    width = sources.shape[0]
    n_row = lax.axis_size("row")
    n_col = lax.axis_size("col")
    piece = H // (n_row * n_col)
    dims = (n_row, n_col, side)
    n_rows = n_col * VB + H
    n_cols = n_row * VB + H
    f32 = functools.partial(jax.ShapeDtypeStruct, dtype=jnp.float32)
    bf16 = functools.partial(jax.ShapeDtypeStruct, dtype=jnp.bfloat16)
    src = sources.reshape(1, width)
    half = VB + n_row * piece
    product_scratch = [
        pltpu.VMEM((n_cols, width), jnp.bfloat16),
        pltpu.VMEM((n_rows, width), jnp.float32),
    ]

    def other_core(x):
        return lax.ppermute(x, "col", [(0, 1), (1, 0)])

    def to_partner(x, flip):
        return lax.ppermute(x, "row", [(r, r ^ flip) for r in range(n_row)])

    def other_side(x):
        return to_partner(x, 1)

    def along_z(blocks):
        return [to_partner(block, X * k) for k, block in enumerate(blocks) if k > 0]

    def call(kernel, name, out_shape, *args, scratch=(), cost=0):
        return pl.pallas_call(
            kernel,
            out_shape=out_shape,
            in_specs=[VMEM] * len(args),
            out_specs=jax.tree.map(lambda _: VMEM, out_shape),
            scratch_shapes=scratch,
            compiler_params=params(),
            cost_estimate=pl.CostEstimate(flops=cost * MICRO, bytes_accessed=0, transcendentals=0),
            name=name,
        )(*args)

    bind = functools.partial

    send, keep, dense = pl.pallas_call(
        functools.partial(first_kernel, dims),
        out_shape=(f32((half, width)), f32((half, width)), bf16((2 * n_rows, n_cols))),
        in_specs=[HBM] * 5,
        out_specs=[VMEM] * 3,
        scratch_shapes=[
            pltpu.VMEM((slots, side, side), jnp.bfloat16),
            pltpu.SMEM((slots,), jnp.int32),
            pltpu.SMEM((slots,), jnp.int32),
            pltpu.SMEM((1,), jnp.int32),
            pltpu.VMEM((1, width), jnp.int32),
            pltpu.VMEM((n_rows + side, n_cols), jnp.float32),
        ] + product_scratch + [
            pltpu.SemaphoreType.DMA((slots // CHUNK,)),
            pltpu.SemaphoreType.DMA((4,)),
        ],
        compiler_params=params(),
        name="first_terms",
    )(tiles.reshape(slots, side, side), tile_row.reshape(slots), tile_col.reshape(slots),
      tile_count.reshape(1), src)

    quarter = H // n_col // X
    n_z = n_row // X
    for step in range(ITERS - 1):
        came = other_core(send)
        own, hold, away = call(
            bind(spread_kernel, dims), "spread",
            (bf16((VB, width)), f32((quarter, width)), f32((quarter, width))),
            src, keep, came)
        away = other_side(away)
        far = along_z([own] * n_z)
        across = other_side(own)
        plane = call(plane_kernel, "plane_sum", f32((quarter, width)), hold, away, cost=10)
        planes = [plane] + along_z([plane] * n_z)
        far_across = other_side(call(join_kernel, "join_far", bf16((n_z - 1, VB, width)), *far))
        mine = call(bind(hub_kernel, dims), "hub_sums", bf16((quarter, width)), src, *planes,
                    scratch=[pltpu.VMEM((n_z, quarter, width), jnp.float32)], cost=10)
        mine = call(side_kernel, "join_sides", bf16((H // n_col, width)), mine, other_side(mine))
        send, keep = call(
            bind(second_kernel, dims), "later_terms", (f32((half, width)), f32((half, width))),
            own, *far, across, far_across, mine, other_core(mine), dense, scratch=product_scratch)
    came = other_core(send)
    hold, away = call(bind(halves_kernel, dims), "hub_halves",
                      (f32((quarter, width)), f32((quarter, width))), keep, came)
    pieces = call(pieces_kernel, "hub_pieces", (f32((piece, width)),) * n_z, hold, other_side(away))
    pieces = [pieces[0]] + along_z(pieces)
    scores = call(bind(last_scores_kernel, dims), "last_scores", f32((VB, width)), src, keep, came)
    hubs = call(bind(last_hubs_kernel, dims), "last_hubs", f32((piece, width)), src, *pieces,
                scratch=[pltpu.VMEM((n_z, piece, width), jnp.float32)])
    return scores.reshape(1, 1, VB, width), hubs


def plain_body(tiles, tile_row, tile_col, tile_count, sources):
    slots = tiles.shape[2]
    side = tiles.shape[3]
    width = sources.shape[0]
    tiles = tiles.reshape(slots, side, side)
    rows = tile_row.reshape(slots)
    cols = tile_col.reshape(slots)
    count = tile_count.reshape(())
    n_row = lax.axis_size("row")
    n_col = lax.axis_size("col")
    devices = n_row * n_col
    r_index = lax.axis_index("row")
    c_index = lax.axis_index("col")
    hub_dev = H // devices
    block_rows = n_col * VB
    n_tile_rows = (block_rows + H) // side
    own_base = H + (r_index * n_col + c_index) * VB
    hub_start = (r_index * n_col + c_index) * hub_dev
    own_ids = jnp.arange(VB, dtype=jnp.int32) + own_base
    tele_own = (own_ids[:, None] == sources[None, :]).astype(jnp.float32)
    piece_ids = jnp.arange(hub_dev, dtype=jnp.int32) + hub_start
    tele_piece = (piece_ids[:, None] == sources[None, :]).astype(jnp.float32)
    tele_hubs = (jnp.arange(H, dtype=jnp.int32)[:, None] == sources[None, :]).astype(jnp.float32)
    column_ids = (
        H
        + (jnp.arange(n_row, dtype=jnp.int32)[:, None] * n_col + c_index) * VB
        + jnp.arange(VB, dtype=jnp.int32)[None, :]
    ).reshape(n_row * VB)
    column_panel = (column_ids[:, None] == sources[None, :]).astype(jnp.bfloat16)
    hub_panel = tele_hubs.astype(jnp.bfloat16)
    block = CHUNK
    own_scores = tele_own
    hub_piece = tele_piece
    for step in range(ITERS):
        start_acc = jnp.zeros((n_tile_rows, side, width), jnp.float32)
        if step > 0:
            column_panel = lax.all_gather(
                own_scores.astype(jnp.bfloat16), "row", axis=0, tiled=True
            )
        panel = jnp.concatenate([column_panel, hub_panel], axis=0).reshape(-1, side, width)

        def step_fn(number, total):
            start = number * block
            tile_block = lax.dynamic_slice_in_dim(tiles, start, block, 0)
            col_block = lax.dynamic_slice_in_dim(cols, start, block, 0)
            row_block = lax.dynamic_slice_in_dim(rows, start, block, 0)
            pieces = jnp.take(panel, col_block, axis=0)
            prod = jnp.einsum(
                "tij,tjs->tis", tile_block, pieces, preferred_element_type=jnp.float32
            )
            live = start + jnp.arange(block, dtype=jnp.int32) < count
            prod = jnp.where(live[:, None, None], prod, 0.0)
            return total.at[row_block].add(prod)

        total = lax.fori_loop(0, slots // block, step_fn, start_acc)
        partial_value = total.reshape(n_tile_rows * side, width)
        summed_rows = lax.psum_scatter(
            partial_value[:block_rows], "col", scatter_dimension=0, tiled=True
        )
        own_scores = 0.85 * summed_rows + 0.15 * tele_own
        hub_part = partial_value[block_rows:]
        summed = lax.psum_scatter(hub_part, ("row", "col"), scatter_dimension=0, tiled=True)
        hub_piece = 0.85 * summed + 0.15 * tele_piece
        if step + 1 < ITERS:
            hub_panel = lax.all_gather(
                hub_piece.astype(jnp.bfloat16), ("row", "col"), axis=0, tiled=True
            )
    return (own_scores.reshape(1, 1, VB, width), hub_piece)


def solution(mesh):
    placed = (
        P(("groups", "row"), "col", None, None, None),
        P(("groups", "row"), "col", None),
        P(("groups", "row"), "col", None),
        P(("groups", "row"), "col"),
        P("groups"),
    )

    def body(tiles, *rest):
        n_row, n_col = mesh.shape["row"], mesh.shape["col"]
        slots, side = tiles.shape[2:4]
        blocks = (n_col * VB + H) * (n_row * VB + H) // (side * side)
        if n_col == 2 and n_row in (4, 8, 16) and blocks <= slots and H // (n_row * n_col) % 16 == 0:
            return fast_body(tiles, *rest)
        return plain_body(tiles, *rest)

    return jax.shard_map(
        body,
        mesh=mesh,
        in_specs=placed,
        out_specs=(P(("groups", "row"), "col", None, None), P(("groups", "row", "col"), None)),
        check_vma=False,
    )
```

```python
import functools

import jax
import jax.numpy as jnp
from jax import lax
from jax.experimental import pallas as pl
from jax.experimental.pallas import tpu as pltpu
from jax.sharding import PartitionSpec as P

VB = 128
H = 256
ITERS = 2
DAMP = 0.85
CHUNK = 16
X = 2
MICRO = 10 ** 9
VMEM_LIMIT = 32 * 1024 * 1024
FIRST_VMEM_LIMIT = 60 * 1024 * 1024

SMEM = pl.BlockSpec(memory_space=pltpu.SMEM)
VMEM = pl.BlockSpec(memory_space=pltpu.VMEM)
HBM = pl.BlockSpec(memory_space=pltpu.HBM)


def params():
    return pltpu.CompilerParams(vmem_limit_bytes=VMEM_LIMIT)


def one_hot(first, count, src):
    ids = lax.broadcasted_iota(jnp.int32, (count, src.shape[1]), 0) + first
    return (ids == src).astype(jnp.float32)


def write_terms(dims, block, prod_ref, dense_ref, panel_ref, send_ref, keep_ref):
    n_row, n_col, side = dims
    rows = dense_ref.shape[0] // 2
    c = lax.axis_index("col")
    prod = jnp.dot(dense_ref[...], panel_ref[...], preferred_element_type=jnp.float32)
    prod_ref[...] = prod[:rows] + prod[rows:]
    for ref, col in ((keep_ref, c), (send_ref, 1 - c)):
        ref[:VB] = prod_ref[pl.ds(pl.multiple_of(col * VB, VB), VB), :]
        for k in range(H // n_col // block):
            start = n_col * VB + (k * n_col + col) * block
            ref[VB + k * block:VB + (k + 1) * block] = prod_ref[pl.ds(pl.multiple_of(start, block), block), :]


def start_copies(tiles_ref, held, sems, pairs, small):
    scalars = [pltpu.make_async_copy(a, b, small.at[i]) for i, (a, b) in enumerate(pairs)]
    copies = []
    for i in range(held.shape[0] // CHUNK):
        part = pl.ds(i * CHUNK, CHUNK)
        copies.append(pltpu.make_async_copy(tiles_ref.at[part], held.at[part], sems.at[i]))
    for copy in scalars + copies:
        copy.start()
    return scalars, copies


def sum_tiles(copies, held, rows_ref, cols_ref, count_ref, total, dense_ref):
    side = held.shape[1]
    n_rows = dense_ref.shape[0] // 2
    count = count_ref[0]

    def add_tile(k, carry):
        live = k < count
        row = pl.multiple_of(jnp.where(live, rows_ref[k] * side, n_rows), side)
        col = pl.multiple_of(jnp.where(live, cols_ref[k] * side, 0), side)
        spot = (pl.ds(row, side), pl.ds(col, side))
        total[spot] += held[k].astype(jnp.float32)
        return carry

    for i, copy in enumerate(copies):
        copy.wait()
        lax.fori_loop(i * CHUNK, (i + 1) * CHUNK, add_tile, 0, unroll=4)
    for r in range(0, n_rows, side):
        whole = total[pl.ds(r, side), :]
        high = whole.astype(jnp.bfloat16)
        dense_ref[pl.ds(r, side), :] = high
        dense_ref[pl.ds(n_rows + r, side), :] = (whole - high.astype(jnp.float32)).astype(jnp.bfloat16)


def first_kernel(dims, tiles_ref, rows_hbm, cols_hbm, count_hbm, src_hbm, send_ref, keep_ref,
                 held, rows_ref, cols_ref, count_ref, total, sems, small, src_ref, dense_ref, panel, prod):
    n_row, n_col, side = dims
    pairs = ((rows_hbm, rows_ref), (cols_hbm, cols_ref), (count_hbm, count_ref), (src_hbm, src_ref))
    scalars, copies = start_copies(tiles_ref, held, sems, pairs, small)
    total[...] = jnp.zeros_like(total)
    for copy in scalars:
        copy.wait()
    src = src_ref[...]
    for r in range(n_row):
        first = H + (r * n_col + lax.axis_index("col")) * VB
        panel[pl.ds(r * VB, VB), :] = one_hot(first, VB, src).astype(jnp.bfloat16)
    panel[pl.ds(n_row * VB, H), :] = one_hot(0, H, src).astype(jnp.bfloat16)
    sum_tiles(copies, held, rows_ref, cols_ref, count_ref, total, dense_ref)
    write_terms(dims, H // n_col, prod, dense_ref, panel, send_ref, keep_ref)


def dense_kernel(tiles_ref, rows_hbm, cols_hbm, count_hbm, src_hbm, dense_ref, tele_ref,
                 held, rows_ref, cols_ref, count_ref, total, sems, small, src_ref):
    pairs = ((rows_hbm, rows_ref), (cols_hbm, cols_ref), (count_hbm, count_ref), (src_hbm, src_ref))
    scalars, copies = start_copies(tiles_ref, held, sems, pairs, small)
    total[...] = jnp.zeros_like(total)
    for copy in scalars:
        copy.wait()
    quarter = tele_ref.shape[0]
    first = (lax.axis_index("col") * X + lax.axis_index("row") % X) * quarter
    tele_ref[...] = 0.15 * one_hot(first, quarter, src_ref[...])
    sum_tiles(copies, held, rows_ref, cols_ref, count_ref, total, dense_ref)


def second_kernel(dims, *refs):
    n_row, n_col, side = dims
    n_z = n_row // X
    own, far, (across, far_across, mine_ref, theirs_ref), rest = refs[0], refs[1:n_z], refs[n_z:n_z + 4], refs[n_z + 4:]
    dense_ref, send_ref, keep_ref, panel, prod = rest
    half = H // n_col
    r, c = lax.axis_index("row"), lax.axis_index("col")

    def put(owner, block):
        panel[pl.ds(pl.multiple_of(owner * VB, VB), VB), :] = block

    put(r, own[...])
    put(r ^ 1, across[...])
    for k in range(1, n_z):
        put(r ^ (X * k), far[k - 1][...])
        put(r ^ (X * k) ^ 1, far_across[k - 1])
    for ref, col in ((mine_ref, c), (theirs_ref, 1 - c)):
        panel[pl.ds(pl.multiple_of(n_row * VB + col * half, half), half), :] = ref[...]
    write_terms(dims, half // n_row, prod, dense_ref, panel, send_ref, keep_ref)


def own_scores(dims, src_ref, keep_ref, came_ref):
    first = H + (lax.axis_index("row") * dims[1] + lax.axis_index("col")) * VB
    tele = one_hot(first, VB, src_ref[...])
    return DAMP * (keep_ref[:VB] + came_ref[:VB]) + 0.15 * tele


def spread_kernel(dims, src_ref, keep_ref, came_ref, scores_ref, hold_ref, pass_ref):
    quarter = hold_ref.shape[0]
    x = lax.axis_index("row") % X
    for ref, place in ((hold_ref, x), (pass_ref, 1 - x)):
        spot = pl.ds(pl.multiple_of(VB + place * quarter, quarter), quarter)
        ref[...] = keep_ref[spot, :] + came_ref[spot, :]
    scores_ref[...] = own_scores(dims, src_ref, keep_ref, came_ref).astype(scores_ref.dtype)


def join_kernel(*refs):
    for k, ref in enumerate(refs[:-1]):
        refs[-1][k] = ref[...]


def plane_kernel(hold_ref, came_ref, out_ref):
    out_ref[...] = hold_ref[...] + came_ref[...]


def sum_planes(planes, held):
    z = lax.axis_index("row") // X
    for k, plane in enumerate(planes):
        held[z ^ k] = plane[...]
    summed = held[0]
    for k in range(1, len(planes)):
        summed = summed + held[k]
    return summed


def hub_kernel(tele_ref, *refs):
    planes, (out_ref, held) = refs[:-2], refs[-2:]
    out_ref[...] = (DAMP * sum_planes(planes, held) + tele_ref[...]).astype(out_ref.dtype)


def side_kernel(mine_ref, theirs_ref, out_ref):
    quarter = mine_ref.shape[0]
    x = lax.axis_index("row") % X
    for ref, place in ((mine_ref, x), (theirs_ref, 1 - x)):
        out_ref[pl.ds(pl.multiple_of(place * quarter, quarter), quarter), :] = ref[...]


def halves_kernel(dims, keep_ref, came_ref, hold_ref, pass_ref):
    n_row, n_col, side = dims
    piece = H // (n_row * n_col)
    x = lax.axis_index("row") % X
    for ref, place in ((hold_ref, x), (pass_ref, 1 - x)):
        for z in range(n_row // X):
            spot = pl.ds(pl.multiple_of(VB + (z * X + place) * piece, piece), piece)
            ref[z * piece:(z + 1) * piece] = keep_ref[spot, :] + came_ref[spot, :]


def pieces_kernel(hold_ref, came_ref, *outs):
    z = lax.axis_index("row") // X
    piece = outs[0].shape[0]
    for k, out in enumerate(outs):
        spot = pl.ds(pl.multiple_of((z ^ k) * piece, piece), piece)
        out[...] = hold_ref[spot, :] + came_ref[spot, :]


def last_scores_kernel(dims, src_ref, keep_ref, came_ref, scores_ref):
    scores_ref[...] = own_scores(dims, src_ref, keep_ref, came_ref)


def last_hubs_kernel(dims, src_ref, *refs):
    planes, (out_ref, held) = refs[:-2], refs[-2:]
    piece = out_ref.shape[0]
    first = (lax.axis_index("row") * dims[1] + lax.axis_index("col")) * piece
    out_ref[...] = DAMP * sum_planes(planes, held) + 0.15 * one_hot(first, piece, src_ref[...])


def fast_body(tiles, tile_row, tile_col, tile_count, sources):
    slots, side = tiles.shape[2:4]
    width = sources.shape[0]
    n_row = lax.axis_size("row")
    n_col = lax.axis_size("col")
    piece = H // (n_row * n_col)
    dims = (n_row, n_col, side)
    n_rows = n_col * VB + H
    n_cols = n_row * VB + H
    f32 = functools.partial(jax.ShapeDtypeStruct, dtype=jnp.float32)
    bf16 = functools.partial(jax.ShapeDtypeStruct, dtype=jnp.bfloat16)
    src = sources.reshape(1, width)
    half = VB + n_row * piece
    quarter = H // n_col // X
    product_scratch = [
        pltpu.VMEM((n_cols, width), jnp.bfloat16),
        pltpu.VMEM((n_rows, width), jnp.float32),
    ]

    def other_core(x):
        return lax.ppermute(x, "col", [(0, 1), (1, 0)])

    def to_partner(x, flip):
        return lax.ppermute(x, "row", [(r, r ^ flip) for r in range(n_row)])

    def other_side(x):
        return to_partner(x, 1)

    def along_z(blocks):
        return [to_partner(block, X * k) for k, block in enumerate(blocks) if k > 0]

    def call(kernel, name, out_shape, *args, scratch=(), cost=0):
        return pl.pallas_call(
            kernel,
            out_shape=out_shape,
            in_specs=[VMEM] * len(args),
            out_specs=jax.tree.map(lambda _: VMEM, out_shape),
            scratch_shapes=scratch,
            compiler_params=params(),
            cost_estimate=pl.CostEstimate(flops=cost * MICRO, bytes_accessed=0, transcendentals=0),
            name=name,
        )(*args)

    bind = functools.partial

    sum_scratch = [
        pltpu.VMEM((slots, side, side), jnp.bfloat16),
        pltpu.SMEM((slots,), jnp.int32),
        pltpu.SMEM((slots,), jnp.int32),
        pltpu.SMEM((1,), jnp.int32),
        pltpu.VMEM((n_rows + side, n_cols), jnp.float32),
        pltpu.SemaphoreType.DMA((slots // CHUNK,)),
        pltpu.SemaphoreType.DMA((4,)),
    ]
    slot_args = (tiles.reshape(slots, side, side), tile_row.reshape(slots), tile_col.reshape(slots),
                 tile_count.reshape(1))
    send, keep = pl.pallas_call(
        bind(first_kernel, dims),
        out_shape=(f32((half, width)), f32((half, width))),
        in_specs=[HBM] * 5,
        out_specs=[VMEM] * 2,
        scratch_shapes=sum_scratch + [
            pltpu.VMEM((1, width), jnp.int32),
            pltpu.VMEM((2 * n_rows, n_cols), jnp.bfloat16),
        ] + product_scratch,
        compiler_params=pltpu.CompilerParams(vmem_limit_bytes=FIRST_VMEM_LIMIT),
        name="first_terms",
    )(*slot_args, src)
    dense, tele = pl.pallas_call(
        dense_kernel,
        out_shape=(bf16((2 * n_rows, n_cols)), f32((quarter, width))),
        in_specs=[HBM] * 5,
        out_specs=[VMEM] * 2,
        scratch_shapes=sum_scratch + [pltpu.VMEM((1, width), jnp.int32)],
        compiler_params=params(),
        cost_estimate=pl.CostEstimate(flops=1 * MICRO, bytes_accessed=0, transcendentals=0),
        name="sum_tiles",
    )(*slot_args, src)

    n_z = n_row // X
    for step in range(ITERS - 1):
        came = other_core(send)
        own, hold, away = call(
            bind(spread_kernel, dims), "spread",
            (bf16((VB, width)), f32((quarter, width)), f32((quarter, width))),
            src, keep, came)
        away = other_side(away)
        far = along_z([own] * n_z)
        across = other_side(own)
        plane = call(plane_kernel, "plane_sum", f32((quarter, width)), hold, away, cost=20)
        planes = [plane] + along_z([plane] * n_z)
        far_across = other_side(call(join_kernel, "join_far", bf16((n_z - 1, VB, width)), *far))
        mine = call(hub_kernel, "hub_sums", bf16((quarter, width)), tele, *planes,
                    scratch=[pltpu.VMEM((n_z, quarter, width), jnp.float32)], cost=1)
        mine = call(side_kernel, "join_sides", bf16((H // n_col, width)), mine, other_side(mine))
        send, keep = call(
            bind(second_kernel, dims), "later_terms", (f32((half, width)), f32((half, width))),
            own, *far, across, far_across, mine, other_core(mine), dense, scratch=product_scratch)
    came = other_core(send)
    hold, away = call(bind(halves_kernel, dims), "hub_halves",
                      (f32((quarter, width)), f32((quarter, width))), keep, came)
    pieces = call(pieces_kernel, "hub_pieces", (f32((piece, width)),) * n_z, hold, other_side(away))
    pieces = [pieces[0]] + along_z(pieces)
    scores = call(bind(last_scores_kernel, dims), "last_scores", f32((VB, width)), src, keep, came)
    hubs = call(bind(last_hubs_kernel, dims), "last_hubs", f32((piece, width)), src, *pieces,
                scratch=[pltpu.VMEM((n_z, piece, width), jnp.float32)])
    return scores.reshape(1, 1, VB, width), hubs


def plain_body(tiles, tile_row, tile_col, tile_count, sources):
    slots = tiles.shape[2]
    side = tiles.shape[3]
    width = sources.shape[0]
    tiles = tiles.reshape(slots, side, side)
    rows = tile_row.reshape(slots)
    cols = tile_col.reshape(slots)
    count = tile_count.reshape(())
    n_row = lax.axis_size("row")
    n_col = lax.axis_size("col")
    devices = n_row * n_col
    r_index = lax.axis_index("row")
    c_index = lax.axis_index("col")
    hub_dev = H // devices
    block_rows = n_col * VB
    n_tile_rows = (block_rows + H) // side
    own_base = H + (r_index * n_col + c_index) * VB
    hub_start = (r_index * n_col + c_index) * hub_dev
    own_ids = jnp.arange(VB, dtype=jnp.int32) + own_base
    tele_own = (own_ids[:, None] == sources[None, :]).astype(jnp.float32)
    piece_ids = jnp.arange(hub_dev, dtype=jnp.int32) + hub_start
    tele_piece = (piece_ids[:, None] == sources[None, :]).astype(jnp.float32)
    tele_hubs = (jnp.arange(H, dtype=jnp.int32)[:, None] == sources[None, :]).astype(jnp.float32)
    column_ids = (
        H
        + (jnp.arange(n_row, dtype=jnp.int32)[:, None] * n_col + c_index) * VB
        + jnp.arange(VB, dtype=jnp.int32)[None, :]
    ).reshape(n_row * VB)
    column_panel = (column_ids[:, None] == sources[None, :]).astype(jnp.bfloat16)
    hub_panel = tele_hubs.astype(jnp.bfloat16)
    block = CHUNK
    own_scores = tele_own
    hub_piece = tele_piece
    for step in range(ITERS):
        start_acc = jnp.zeros((n_tile_rows, side, width), jnp.float32)
        if step > 0:
            column_panel = lax.all_gather(
                own_scores.astype(jnp.bfloat16), "row", axis=0, tiled=True
            )
        panel = jnp.concatenate([column_panel, hub_panel], axis=0).reshape(-1, side, width)

        def step_fn(number, total):
            start = number * block
            tile_block = lax.dynamic_slice_in_dim(tiles, start, block, 0)
            col_block = lax.dynamic_slice_in_dim(cols, start, block, 0)
            row_block = lax.dynamic_slice_in_dim(rows, start, block, 0)
            pieces = jnp.take(panel, col_block, axis=0)
            prod = jnp.einsum(
                "tij,tjs->tis", tile_block, pieces, preferred_element_type=jnp.float32
            )
            live = start + jnp.arange(block, dtype=jnp.int32) < count
            prod = jnp.where(live[:, None, None], prod, 0.0)
            return total.at[row_block].add(prod)

        total = lax.fori_loop(0, slots // block, step_fn, start_acc)
        partial_value = total.reshape(n_tile_rows * side, width)
        summed_rows = lax.psum_scatter(
            partial_value[:block_rows], "col", scatter_dimension=0, tiled=True
        )
        own_scores = 0.85 * summed_rows + 0.15 * tele_own
        hub_part = partial_value[block_rows:]
        summed = lax.psum_scatter(hub_part, ("row", "col"), scatter_dimension=0, tiled=True)
        hub_piece = 0.85 * summed + 0.15 * tele_piece
        if step + 1 < ITERS:
            hub_panel = lax.all_gather(
                hub_piece.astype(jnp.bfloat16), ("row", "col"), axis=0, tiled=True
            )
    return (own_scores.reshape(1, 1, VB, width), hub_piece)


def solution(mesh):
    placed = (
        P(("groups", "row"), "col", None, None, None),
        P(("groups", "row"), "col", None),
        P(("groups", "row"), "col", None),
        P(("groups", "row"), "col"),
        P("groups"),
    )

    def body(tiles, *rest):
        n_row, n_col = mesh.shape["row"], mesh.shape["col"]
        slots, side = tiles.shape[2:4]
        blocks = (n_col * VB + H) * (n_row * VB + H) // (side * side)
        if n_col == 2 and n_row in (4, 8, 16) and blocks <= slots and H // (n_row * n_col) % 16 == 0:
            return fast_body(tiles, *rest)
        return plain_body(tiles, *rest)

    return jax.shard_map(
        body,
        mesh=mesh,
        in_specs=placed,
        out_specs=(P(("groups", "row"), "col", None, None), P(("groups", "row", "col"), None)),
        check_vma=False,
    )
```

```python
import functools

import jax
import jax.numpy as jnp
from jax import lax
from jax.experimental import pallas as pl
from jax.experimental.pallas import tpu as pltpu
from jax.sharding import PartitionSpec as P

VB = 128
H = 256
ITERS = 2
DAMP = 0.85
CHUNK = 16
X = 2
MICRO = 10 ** 9
VMEM_LIMIT = 32 * 1024 * 1024

SMEM = pl.BlockSpec(memory_space=pltpu.SMEM)
VMEM = pl.BlockSpec(memory_space=pltpu.VMEM)
HBM = pl.BlockSpec(memory_space=pltpu.HBM)


def params():
    return pltpu.CompilerParams(vmem_limit_bytes=VMEM_LIMIT)


def one_hot(first, count, src):
    ids = lax.broadcasted_iota(jnp.int32, (count, src.shape[1]), 0) + first
    return (ids == src).astype(jnp.float32)


def write_terms(dims, block, prod_ref, dense_ref, panel_ref, send_ref, keep_ref):
    n_row, n_col, side = dims
    rows = dense_ref.shape[0] // 2
    c = lax.axis_index("col")
    prod = jnp.dot(dense_ref[...], panel_ref[...], preferred_element_type=jnp.float32)
    prod_ref[...] = prod[:rows] + prod[rows:]
    for ref, col in ((keep_ref, c), (send_ref, 1 - c)):
        ref[:VB] = prod_ref[pl.ds(pl.multiple_of(col * VB, VB), VB), :]
        for k in range(H // n_col // block):
            start = n_col * VB + (k * n_col + col) * block
            ref[VB + k * block:VB + (k + 1) * block] = prod_ref[pl.ds(pl.multiple_of(start, block), block), :]


def first_kernel(dims, tiles_ref, rows_hbm, cols_hbm, count_hbm, src_hbm, send_ref, keep_ref, dense_ref,
                 held, rows_ref, cols_ref, count_ref, src_ref, total, panel, prod, sems, small):
    n_row, n_col, side = dims
    n_rows = dense_ref.shape[0] // 2
    pairs = ((src_hbm, src_ref), (rows_hbm, rows_ref), (cols_hbm, cols_ref), (count_hbm, count_ref))
    scalars = [pltpu.make_async_copy(a, b, small.at[i]) for i, (a, b) in enumerate(pairs)]
    copies = []
    for i in range(held.shape[0] // CHUNK):
        part = pl.ds(i * CHUNK, CHUNK)
        copies.append(pltpu.make_async_copy(tiles_ref.at[part], held.at[part], sems.at[i]))
    for copy in scalars + copies:
        copy.start()
    total[...] = jnp.zeros_like(total)
    for copy in scalars:
        copy.wait()
    src = src_ref[...]
    for r in range(n_row):
        first = H + (r * n_col + lax.axis_index("col")) * VB
        panel[pl.ds(r * VB, VB), :] = one_hot(first, VB, src).astype(jnp.bfloat16)
    panel[pl.ds(n_row * VB, H), :] = one_hot(0, H, src).astype(jnp.bfloat16)
    count = count_ref[0]

    def add_tile(k, carry):
        live = k < count
        row = pl.multiple_of(jnp.where(live, rows_ref[k] * side, n_rows), side)
        col = pl.multiple_of(jnp.where(live, cols_ref[k] * side, 0), side)
        spot = (pl.ds(row, side), pl.ds(col, side))
        total[spot] += held[k].astype(jnp.float32)
        return carry

    for i, copy in enumerate(copies):
        copy.wait()
        lax.fori_loop(i * CHUNK, (i + 1) * CHUNK, add_tile, 0, unroll=4)
    for r in range(0, n_rows, side):
        whole = total[pl.ds(r, side), :]
        high = whole.astype(jnp.bfloat16)
        dense_ref[pl.ds(r, side), :] = high
        dense_ref[pl.ds(n_rows + r, side), :] = (whole - high.astype(jnp.float32)).astype(jnp.bfloat16)
    write_terms(dims, H // n_col, prod, dense_ref, panel, send_ref, keep_ref)


def second_kernel(dims, *refs):
    n_row, n_col, side = dims
    n_z = n_row // X
    own, far, (across, far_across, mine_ref, theirs_ref), rest = refs[0], refs[1:n_z], refs[n_z:n_z + 4], refs[n_z + 4:]
    dense_ref, send_ref, keep_ref, panel, prod = rest
    half = H // n_col
    r, c = lax.axis_index("row"), lax.axis_index("col")

    def put(owner, block):
        panel[pl.ds(pl.multiple_of(owner * VB, VB), VB), :] = block

    put(r, own[...])
    put(r ^ 1, across[...])
    for k in range(1, n_z):
        put(r ^ (X * k), far[k - 1][...])
        put(r ^ (X * k) ^ 1, far_across[k - 1])
    for ref, col in ((mine_ref, c), (theirs_ref, 1 - c)):
        panel[pl.ds(pl.multiple_of(n_row * VB + col * half, half), half), :] = ref[...]
    write_terms(dims, half // n_row, prod, dense_ref, panel, send_ref, keep_ref)


def own_scores(dims, src_ref, keep_ref, came_ref):
    first = H + (lax.axis_index("row") * dims[1] + lax.axis_index("col")) * VB
    tele = one_hot(first, VB, src_ref[...])
    return DAMP * (keep_ref[:VB] + came_ref[:VB]) + 0.15 * tele


def spread_kernel(dims, src_ref, keep_ref, came_ref, scores_ref, hold_ref, pass_ref):
    quarter = hold_ref.shape[0]
    x = lax.axis_index("row") % X
    for ref, place in ((hold_ref, x), (pass_ref, 1 - x)):
        spot = pl.ds(pl.multiple_of(VB + place * quarter, quarter), quarter)
        ref[...] = keep_ref[spot, :] + came_ref[spot, :]
    scores_ref[...] = own_scores(dims, src_ref, keep_ref, came_ref).astype(scores_ref.dtype)


def join_kernel(*refs):
    for k, ref in enumerate(refs[:-1]):
        refs[-1][k] = ref[...]


def plane_kernel(hold_ref, came_ref, out_ref):
    out_ref[...] = hold_ref[...] + came_ref[...]


def sum_planes(planes, held):
    z = lax.axis_index("row") // X
    for k, plane in enumerate(planes):
        held[z ^ k] = plane[...]
    summed = held[0]
    for k in range(1, len(planes)):
        summed = summed + held[k]
    return summed


def hub_kernel(dims, src_ref, *refs):
    planes, (out_ref, held) = refs[:-2], refs[-2:]
    quarter = out_ref.shape[0]
    first = (lax.axis_index("col") * X + lax.axis_index("row") % X) * quarter
    tele = one_hot(first, quarter, src_ref[...])
    out_ref[...] = (DAMP * sum_planes(planes, held) + 0.15 * tele).astype(out_ref.dtype)


def side_kernel(mine_ref, theirs_ref, out_ref):
    quarter = mine_ref.shape[0]
    x = lax.axis_index("row") % X
    for ref, place in ((mine_ref, x), (theirs_ref, 1 - x)):
        out_ref[pl.ds(pl.multiple_of(place * quarter, quarter), quarter), :] = ref[...]


def halves_kernel(dims, keep_ref, came_ref, hold_ref, pass_ref):
    n_row, n_col, side = dims
    piece = H // (n_row * n_col)
    x = lax.axis_index("row") % X
    for ref, place in ((hold_ref, x), (pass_ref, 1 - x)):
        for z in range(n_row // X):
            spot = pl.ds(pl.multiple_of(VB + (z * X + place) * piece, piece), piece)
            ref[z * piece:(z + 1) * piece] = keep_ref[spot, :] + came_ref[spot, :]


def pieces_kernel(hold_ref, came_ref, *outs):
    z = lax.axis_index("row") // X
    piece = outs[0].shape[0]
    for k, out in enumerate(outs):
        spot = pl.ds(pl.multiple_of((z ^ k) * piece, piece), piece)
        out[...] = hold_ref[spot, :] + came_ref[spot, :]


def last_scores_kernel(dims, src_ref, keep_ref, came_ref, scores_ref):
    scores_ref[...] = own_scores(dims, src_ref, keep_ref, came_ref)


def last_hubs_kernel(dims, src_ref, *refs):
    planes, (out_ref, held) = refs[:-2], refs[-2:]
    piece = out_ref.shape[0]
    first = (lax.axis_index("row") * dims[1] + lax.axis_index("col")) * piece
    out_ref[...] = DAMP * sum_planes(planes, held) + 0.15 * one_hot(first, piece, src_ref[...])


def fast_body(tiles, tile_row, tile_col, tile_count, sources):
    slots, side = tiles.shape[2:4]
    width = sources.shape[0]
    n_row = lax.axis_size("row")
    n_col = lax.axis_size("col")
    piece = H // (n_row * n_col)
    dims = (n_row, n_col, side)
    n_rows = n_col * VB + H
    n_cols = n_row * VB + H
    f32 = functools.partial(jax.ShapeDtypeStruct, dtype=jnp.float32)
    bf16 = functools.partial(jax.ShapeDtypeStruct, dtype=jnp.bfloat16)
    src = sources.reshape(1, width)
    half = VB + n_row * piece
    quarter = H // n_col // X
    product_scratch = [
        pltpu.VMEM((n_cols, width), jnp.bfloat16),
        pltpu.VMEM((n_rows, width), jnp.float32),
    ]

    def other_core(x):
        return lax.ppermute(x, "col", [(0, 1), (1, 0)])

    def to_partner(x, flip):
        return lax.ppermute(x, "row", [(r, r ^ flip) for r in range(n_row)])

    def other_side(x):
        return to_partner(x, 1)

    def along_z(blocks):
        return [to_partner(block, X * k) for k, block in enumerate(blocks) if k > 0]

    def call(kernel, name, out_shape, *args, scratch=(), cost=0):
        return pl.pallas_call(
            kernel,
            out_shape=out_shape,
            in_specs=[VMEM] * len(args),
            out_specs=jax.tree.map(lambda _: VMEM, out_shape),
            scratch_shapes=scratch,
            compiler_params=params(),
            cost_estimate=pl.CostEstimate(flops=cost * MICRO, bytes_accessed=0, transcendentals=0),
            name=name,
        )(*args)

    bind = functools.partial

    in_hbm = [pltpu.with_memory_space_constraint(x, pltpu.HBM) for x in (
        tiles.reshape(slots, side, side), tile_row.reshape(slots), tile_col.reshape(slots), src)]
    send, keep, dense = pl.pallas_call(
        bind(first_kernel, dims),
        out_shape=(f32((half, width)), f32((half, width)), bf16((2 * n_rows, n_cols))),
        in_specs=[HBM] * 5,
        out_specs=[VMEM] * 3,
        scratch_shapes=[
            pltpu.VMEM((slots, side, side), jnp.bfloat16),
            pltpu.SMEM((slots,), jnp.int32),
            pltpu.SMEM((slots,), jnp.int32),
            pltpu.SMEM((1,), jnp.int32),
            pltpu.VMEM((1, width), jnp.int32),
            pltpu.VMEM((n_rows + side, n_cols), jnp.float32),
        ] + product_scratch + [
            pltpu.SemaphoreType.DMA((slots // CHUNK,)),
            pltpu.SemaphoreType.DMA((4,)),
        ],
        compiler_params=params(),
        name="first_terms",
    )(*in_hbm[:3], tile_count.reshape(1), in_hbm[3])

    n_z = n_row // X
    for step in range(ITERS - 1):
        came = other_core(send)
        own, hold, away = call(
            bind(spread_kernel, dims), "spread",
            (bf16((VB, width)), f32((quarter, width)), f32((quarter, width))),
            src, keep, came)
        away = other_side(away)
        far = along_z([own] * n_z)
        across = other_side(own)
        plane = call(plane_kernel, "plane_sum", f32((quarter, width)), hold, away, cost=20)
        planes = [plane] + along_z([plane] * n_z)
        far_across = other_side(call(join_kernel, "join_far", bf16((n_z - 1, VB, width)), *far))
        mine = call(bind(hub_kernel, dims), "hub_sums", bf16((quarter, width)), src, *planes,
                    scratch=[pltpu.VMEM((n_z, quarter, width), jnp.float32)], cost=1)
        mine = call(side_kernel, "join_sides", bf16((H // n_col, width)), mine, other_side(mine))
        send, keep = call(
            bind(second_kernel, dims), "later_terms", (f32((half, width)), f32((half, width))),
            own, *far, across, far_across, mine, other_core(mine), dense, scratch=product_scratch)
    came = other_core(send)
    hold, away = call(bind(halves_kernel, dims), "hub_halves",
                      (f32((quarter, width)), f32((quarter, width))), keep, came)
    pieces = call(pieces_kernel, "hub_pieces", (f32((piece, width)),) * n_z, hold, other_side(away))
    pieces = [pieces[0]] + along_z(pieces)
    scores = call(bind(last_scores_kernel, dims), "last_scores", f32((VB, width)), src, keep, came)
    hubs = call(bind(last_hubs_kernel, dims), "last_hubs", f32((piece, width)), src, *pieces,
                scratch=[pltpu.VMEM((n_z, piece, width), jnp.float32)])
    return scores.reshape(1, 1, VB, width), hubs


def plain_body(tiles, tile_row, tile_col, tile_count, sources):
    slots = tiles.shape[2]
    side = tiles.shape[3]
    width = sources.shape[0]
    tiles = tiles.reshape(slots, side, side)
    rows = tile_row.reshape(slots)
    cols = tile_col.reshape(slots)
    count = tile_count.reshape(())
    n_row = lax.axis_size("row")
    n_col = lax.axis_size("col")
    devices = n_row * n_col
    r_index = lax.axis_index("row")
    c_index = lax.axis_index("col")
    hub_dev = H // devices
    block_rows = n_col * VB
    n_tile_rows = (block_rows + H) // side
    own_base = H + (r_index * n_col + c_index) * VB
    hub_start = (r_index * n_col + c_index) * hub_dev
    own_ids = jnp.arange(VB, dtype=jnp.int32) + own_base
    tele_own = (own_ids[:, None] == sources[None, :]).astype(jnp.float32)
    piece_ids = jnp.arange(hub_dev, dtype=jnp.int32) + hub_start
    tele_piece = (piece_ids[:, None] == sources[None, :]).astype(jnp.float32)
    tele_hubs = (jnp.arange(H, dtype=jnp.int32)[:, None] == sources[None, :]).astype(jnp.float32)
    column_ids = (
        H
        + (jnp.arange(n_row, dtype=jnp.int32)[:, None] * n_col + c_index) * VB
        + jnp.arange(VB, dtype=jnp.int32)[None, :]
    ).reshape(n_row * VB)
    column_panel = (column_ids[:, None] == sources[None, :]).astype(jnp.bfloat16)
    hub_panel = tele_hubs.astype(jnp.bfloat16)
    block = CHUNK
    own_scores = tele_own
    hub_piece = tele_piece
    for step in range(ITERS):
        start_acc = jnp.zeros((n_tile_rows, side, width), jnp.float32)
        if step > 0:
            column_panel = lax.all_gather(
                own_scores.astype(jnp.bfloat16), "row", axis=0, tiled=True
            )
        panel = jnp.concatenate([column_panel, hub_panel], axis=0).reshape(-1, side, width)

        def step_fn(number, total):
            start = number * block
            tile_block = lax.dynamic_slice_in_dim(tiles, start, block, 0)
            col_block = lax.dynamic_slice_in_dim(cols, start, block, 0)
            row_block = lax.dynamic_slice_in_dim(rows, start, block, 0)
            pieces = jnp.take(panel, col_block, axis=0)
            prod = jnp.einsum(
                "tij,tjs->tis", tile_block, pieces, preferred_element_type=jnp.float32
            )
            live = start + jnp.arange(block, dtype=jnp.int32) < count
            prod = jnp.where(live[:, None, None], prod, 0.0)
            return total.at[row_block].add(prod)

        total = lax.fori_loop(0, slots // block, step_fn, start_acc)
        partial_value = total.reshape(n_tile_rows * side, width)
        summed_rows = lax.psum_scatter(
            partial_value[:block_rows], "col", scatter_dimension=0, tiled=True
        )
        own_scores = 0.85 * summed_rows + 0.15 * tele_own
        hub_part = partial_value[block_rows:]
        summed = lax.psum_scatter(hub_part, ("row", "col"), scatter_dimension=0, tiled=True)
        hub_piece = 0.85 * summed + 0.15 * tele_piece
        if step + 1 < ITERS:
            hub_panel = lax.all_gather(
                hub_piece.astype(jnp.bfloat16), ("row", "col"), axis=0, tiled=True
            )
    return (own_scores.reshape(1, 1, VB, width), hub_piece)


def solution(mesh):
    placed = (
        P(("groups", "row"), "col", None, None, None),
        P(("groups", "row"), "col", None),
        P(("groups", "row"), "col", None),
        P(("groups", "row"), "col"),
        P("groups"),
    )

    def body(tiles, *rest):
        n_row, n_col = mesh.shape["row"], mesh.shape["col"]
        slots, side = tiles.shape[2:4]
        blocks = (n_col * VB + H) * (n_row * VB + H) // (side * side)
        if n_col == 2 and n_row in (4, 8, 16) and blocks <= slots and H // (n_row * n_col) % 16 == 0:
            return fast_body(tiles, *rest)
        return plain_body(tiles, *rest)

    return jax.shard_map(
        body,
        mesh=mesh,
        in_specs=placed,
        out_specs=(P(("groups", "row"), "col", None, None), P(("groups", "row", "col"), None)),
        check_vma=False,
    )
```

```python
import functools

import jax
import jax.numpy as jnp
from jax import lax
from jax.experimental import pallas as pl
from jax.experimental.pallas import tpu as pltpu
from jax.sharding import PartitionSpec as P

VB = 128
H = 256
ITERS = 2
DAMP = 0.85
CHUNK = 16
X = 2
HUB_CORE = 1
MICRO = 10 ** 9
VMEM_LIMIT = 32 * 1024 * 1024

SMEM = pl.BlockSpec(memory_space=pltpu.SMEM)
VMEM = pl.BlockSpec(memory_space=pltpu.VMEM)
HBM = pl.BlockSpec(memory_space=pltpu.HBM)


def params():
    return pltpu.CompilerParams(vmem_limit_bytes=VMEM_LIMIT)


def one_hot(first, count, src):
    ids = lax.broadcasted_iota(jnp.int32, (count, src.shape[1]), 0) + first
    return (ids == src).astype(jnp.float32)


def write_terms(dims, prod_ref, dense_ref, panel_ref, send_ref, keep_ref, hubs_ref):
    n_col = dims[1]
    rows = dense_ref.shape[0] // 2
    own = n_col * VB
    c = lax.axis_index("col")
    prod = jnp.dot(dense_ref[...], panel_ref[...], preferred_element_type=jnp.float32)
    prod_ref[...] = prod[:own] + prod[rows:rows + own]
    hubs_ref[...] = prod[own:rows] + prod[rows + own:]
    for ref, col in ((keep_ref, c), (send_ref, 1 - c)):
        ref[...] = prod_ref[pl.ds(pl.multiple_of(col * VB, VB), VB), :]


def first_kernel(dims, tiles_ref, rows_hbm, cols_hbm, count_hbm, src_hbm, send_ref, keep_ref, hubs_ref, dense_ref,
                 held, rows_ref, cols_ref, count_ref, src_ref, total, panel, prod, sems, small):
    n_row, n_col, side = dims
    n_rows = dense_ref.shape[0] // 2
    pairs = ((src_hbm, src_ref), (rows_hbm, rows_ref), (cols_hbm, cols_ref), (count_hbm, count_ref))
    scalars = [pltpu.make_async_copy(a, b, small.at[i]) for i, (a, b) in enumerate(pairs)]
    copies = []
    for i in range(held.shape[0] // CHUNK):
        part = pl.ds(i * CHUNK, CHUNK)
        copies.append(pltpu.make_async_copy(tiles_ref.at[part], held.at[part], sems.at[i]))
    for copy in scalars + copies:
        copy.start()
    total[...] = jnp.zeros_like(total)
    for copy in scalars:
        copy.wait()
    src = src_ref[...]
    for r in range(n_row):
        first = H + (r * n_col + lax.axis_index("col")) * VB
        panel[pl.ds(r * VB, VB), :] = one_hot(first, VB, src).astype(jnp.bfloat16)
    panel[pl.ds(n_row * VB, H), :] = one_hot(0, H, src).astype(jnp.bfloat16)
    count = count_ref[0]

    def add_tile(k, carry):
        live = k < count
        row = pl.multiple_of(jnp.where(live, rows_ref[k] * side, n_rows), side)
        col = pl.multiple_of(jnp.where(live, cols_ref[k] * side, 0), side)
        spot = (pl.ds(row, side), pl.ds(col, side))
        total[spot] += held[k].astype(jnp.float32)
        return carry

    for i, copy in enumerate(copies):
        copy.wait()
        lax.fori_loop(i * CHUNK, (i + 1) * CHUNK, add_tile, 0, unroll=4)
    for r in range(0, n_rows, side):
        whole = total[pl.ds(r, side), :]
        high = whole.astype(jnp.bfloat16)
        dense_ref[pl.ds(r, side), :] = high
        dense_ref[pl.ds(n_rows + r, side), :] = (whole - high.astype(jnp.float32)).astype(jnp.bfloat16)
    write_terms(dims, prod, dense_ref, panel, send_ref, keep_ref, hubs_ref)


def second_kernel(dims, *refs):
    n_row = dims[0]
    n_z = n_row // X
    blocks, (across, mine_ref, theirs_ref) = refs[:n_z], refs[n_z:n_z + 3]
    dense_ref, send_ref, keep_ref, hubs_ref, panel, prod = refs[n_z + 3:]
    r, c = lax.axis_index("row"), lax.axis_index("col")

    def put(owner, block):
        panel[pl.ds(pl.multiple_of(owner * VB, VB), VB), :] = block

    for k in range(n_z):
        put(r ^ (X * k), blocks[k][...])
        put(r ^ (X * k) ^ 1, across[k])
    for ref, core in ((mine_ref, HUB_CORE), (theirs_ref, 1 - HUB_CORE)):
        @pl.when(c == core)
        def _():
            panel[pl.ds(n_row * VB, H), :] = ref[...]
    write_terms(dims, prod, dense_ref, panel, send_ref, keep_ref, hubs_ref)


def own_scores(dims, src_ref, keep_ref, came_ref):
    first = H + (lax.axis_index("row") * dims[1] + lax.axis_index("col")) * VB
    return DAMP * (keep_ref[...] + came_ref[...]) + 0.15 * one_hot(first, VB, src_ref[...])


def scores_kernel(dims, src_ref, keep_ref, came_ref, scores_ref):
    scores_ref[...] = own_scores(dims, src_ref, keep_ref, came_ref).astype(scores_ref.dtype)


def spread_kernel(block, mine_ref, came_ref, hold_ref, pass_ref):
    x = lax.axis_index("row") % X
    for ref, place in ((hold_ref, x), (pass_ref, 1 - x)):
        for k in range(ref.shape[0] // block):
            spot = pl.ds(pl.multiple_of((k * X + place) * block, block), block)
            ref[k * block:(k + 1) * block] = mine_ref[spot, :] + came_ref[spot, :]


def scores_and_spread_kernel(dims, block, src_ref, keep_ref, came_ref, mine_ref, theirs_ref, scores_ref, hold_ref, pass_ref):
    spread_kernel(block, mine_ref, theirs_ref, hold_ref, pass_ref)
    scores_kernel(dims, src_ref, keep_ref, came_ref, scores_ref)


def join_kernel(*refs):
    out_ref = refs[-1]
    for k in range(out_ref.shape[0]):
        out_ref[k] = refs[k][...]


def plane_kernel(hold_ref, came_ref, out_ref):
    out_ref[...] = hold_ref[...] + came_ref[...]


def sum_planes(planes, held):
    z = lax.axis_index("row") // X
    for k, plane in enumerate(planes):
        held[z ^ k] = plane[...]
    summed = held[0]
    for k in range(1, len(planes)):
        summed = summed + held[k]
    return summed


def hub_kernel(first, src_ref, *refs):
    out_ref, held = refs[-2:]
    planes = refs[:held.shape[0]]
    count = out_ref.shape[0]
    tele = one_hot(first(lax.axis_index("row")), count, src_ref[...])
    out_ref[...] = (DAMP * sum_planes(planes, held) + 0.15 * tele).astype(out_ref.dtype)


def side_kernel(mine_ref, theirs_ref, out_ref):
    part = mine_ref.shape[0]
    x = lax.axis_index("row") % X
    for ref, place in ((mine_ref, x), (theirs_ref, 1 - x)):
        out_ref[pl.ds(pl.multiple_of(place * part, part), part), :] = ref[...]


def pieces_kernel(hold_ref, came_ref, *outs):
    z = lax.axis_index("row") // X
    share = outs[0].shape[0]
    for k, out in enumerate(outs):
        spot = pl.ds(pl.multiple_of((z ^ k) * share, share), share)
        out[...] = hold_ref[spot, :] + came_ref[spot, :]


def last_hubs_kernel(mine_ref, theirs_ref, out_ref):
    piece = out_ref.shape[0]
    for ref, core in ((mine_ref, HUB_CORE), (theirs_ref, 1 - HUB_CORE)):
        @pl.when(lax.axis_index("col") == core)
        def _():
            out_ref[...] = ref[core * piece:(core + 1) * piece]


def fast_body(tiles, tile_row, tile_col, tile_count, sources):
    slots, side = tiles.shape[2:4]
    width = sources.shape[0]
    n_row = lax.axis_size("row")
    n_col = lax.axis_size("col")
    n_z = n_row // X
    part = H // X
    share = H // n_row
    dims = (n_row, n_col, side)
    n_rows = n_col * VB + H
    n_cols = n_row * VB + H
    bind = functools.partial
    f32 = bind(jax.ShapeDtypeStruct, dtype=jnp.float32)
    bf16 = bind(jax.ShapeDtypeStruct, dtype=jnp.bfloat16)
    src = sources.reshape(1, width)
    product_scratch = [
        pltpu.VMEM((n_cols, width), jnp.bfloat16),
        pltpu.VMEM((n_col * VB, width), jnp.float32),
    ]
    term_shapes = (f32((VB, width)), f32((VB, width)), f32((H, width)))

    def other_core(x):
        return lax.ppermute(x, "col", [(0, 1), (1, 0)])

    def to_core(x, core):
        return lax.ppermute(x, "col", [(1 - core, core)])

    def to_partner(x, flip):
        return lax.ppermute(x, "row", [(r, r ^ flip) for r in range(n_row)])

    def hub_partner(x, flip):
        pairs = [(r * n_col + HUB_CORE, (r ^ flip) * n_col + HUB_CORE) for r in range(n_row)]
        return lax.ppermute(x, ("row", "col"), pairs)

    def call(kernel, name, out_shape, *args, scratch=(), cost=0):
        return pl.pallas_call(
            kernel,
            out_shape=out_shape,
            in_specs=[VMEM] * len(args),
            out_specs=jax.tree.map(lambda _: VMEM, out_shape),
            scratch_shapes=scratch,
            compiler_params=params(),
            cost_estimate=pl.CostEstimate(flops=cost * MICRO, bytes_accessed=0, transcendentals=0),
            name=name,
        )(*args)

    in_hbm = [pltpu.with_memory_space_constraint(x, pltpu.HBM) for x in (
        tiles.reshape(slots, side, side), tile_row.reshape(slots), tile_col.reshape(slots), src)]
    send, keep, hubs, dense = pl.pallas_call(
        bind(first_kernel, dims),
        out_shape=term_shapes + (bf16((2 * n_rows, n_cols)),),
        in_specs=[HBM] * 5,
        out_specs=[VMEM] * 4,
        scratch_shapes=[
            pltpu.VMEM((slots, side, side), jnp.bfloat16),
            pltpu.SMEM((slots,), jnp.int32),
            pltpu.SMEM((slots,), jnp.int32),
            pltpu.SMEM((1,), jnp.int32),
            pltpu.VMEM((1, width), jnp.int32),
            pltpu.VMEM((n_rows + side, n_cols), jnp.float32),
        ] + product_scratch + [
            pltpu.SemaphoreType.DMA((slots // CHUNK,)),
            pltpu.SemaphoreType.DMA((4,)),
        ],
        compiler_params=params(),
        name="first_terms",
    )(*in_hbm[:3], tile_count.reshape(1), in_hbm[3])

    for step in range(ITERS - 1):
        own, hold, away = call(
            bind(scores_and_spread_kernel, dims, part), "spread",
            (bf16((VB, width)), f32((part, width)), f32((part, width))),
            src, keep, other_core(send), hubs, to_core(hubs, HUB_CORE))
        away = hub_partner(away, 1)
        blocks = [own] + [to_partner(own, X * k) for k in range(1, n_z)]
        plane = call(plane_kernel, "plane_sum", f32((part, width)), hold, away)
        planes = [plane] + [hub_partner(plane, X * k) for k in range(1, n_z)]
        across = to_partner(call(join_kernel, "join_rows", bf16((n_z, VB, width)), *blocks, cost=1), 1)
        mine = call(bind(hub_kernel, lambda r: r % X * part), "hub_sums", bf16((part, width)), src, *planes,
                    scratch=[pltpu.VMEM((n_z, part, width), jnp.float32)], cost=1)
        mine = call(side_kernel, "join_sides", bf16((H, width)), mine, hub_partner(mine, 1))
        send, keep, hubs = call(
            bind(second_kernel, dims), "later_terms", term_shapes,
            *blocks, across, mine, to_core(mine, 1 - HUB_CORE), dense, scratch=product_scratch)
    hold, away = call(bind(spread_kernel, share), "last_spread", (f32((part, width)),) * 2,
                      hubs, to_core(hubs, HUB_CORE))
    pieces = call(pieces_kernel, "hub_pieces", (f32((share, width)),) * n_z, hold, hub_partner(away, 1))
    pieces = [pieces[0]] + [hub_partner(pieces[k], X * k) for k in range(1, n_z)]
    scores = call(bind(scores_kernel, dims), "last_scores", f32((VB, width)), src, keep, other_core(send))
    mine = call(bind(hub_kernel, lambda r: r * share), "last_sums", f32((share, width)), src, *pieces,
                scratch=[pltpu.VMEM((n_z, share, width), jnp.float32)])
    hubs = call(last_hubs_kernel, "last_hubs", f32((share // n_col, width)), mine, to_core(mine, 1 - HUB_CORE))
    return scores.reshape(1, 1, VB, width), hubs


def plain_body(tiles, tile_row, tile_col, tile_count, sources):
    slots = tiles.shape[2]
    side = tiles.shape[3]
    width = sources.shape[0]
    tiles = tiles.reshape(slots, side, side)
    rows = tile_row.reshape(slots)
    cols = tile_col.reshape(slots)
    count = tile_count.reshape(())
    n_row = lax.axis_size("row")
    n_col = lax.axis_size("col")
    devices = n_row * n_col
    r_index = lax.axis_index("row")
    c_index = lax.axis_index("col")
    hub_dev = H // devices
    block_rows = n_col * VB
    n_tile_rows = (block_rows + H) // side
    own_base = H + (r_index * n_col + c_index) * VB
    hub_start = (r_index * n_col + c_index) * hub_dev
    own_ids = jnp.arange(VB, dtype=jnp.int32) + own_base
    tele_own = (own_ids[:, None] == sources[None, :]).astype(jnp.float32)
    piece_ids = jnp.arange(hub_dev, dtype=jnp.int32) + hub_start
    tele_piece = (piece_ids[:, None] == sources[None, :]).astype(jnp.float32)
    tele_hubs = (jnp.arange(H, dtype=jnp.int32)[:, None] == sources[None, :]).astype(jnp.float32)
    column_ids = (
        H
        + (jnp.arange(n_row, dtype=jnp.int32)[:, None] * n_col + c_index) * VB
        + jnp.arange(VB, dtype=jnp.int32)[None, :]
    ).reshape(n_row * VB)
    column_panel = (column_ids[:, None] == sources[None, :]).astype(jnp.bfloat16)
    hub_panel = tele_hubs.astype(jnp.bfloat16)
    block = CHUNK
    own_scores = tele_own
    hub_piece = tele_piece
    for step in range(ITERS):
        start_acc = jnp.zeros((n_tile_rows, side, width), jnp.float32)
        if step > 0:
            column_panel = lax.all_gather(
                own_scores.astype(jnp.bfloat16), "row", axis=0, tiled=True
            )
        panel = jnp.concatenate([column_panel, hub_panel], axis=0).reshape(-1, side, width)

        def step_fn(number, total):
            start = number * block
            tile_block = lax.dynamic_slice_in_dim(tiles, start, block, 0)
            col_block = lax.dynamic_slice_in_dim(cols, start, block, 0)
            row_block = lax.dynamic_slice_in_dim(rows, start, block, 0)
            pieces = jnp.take(panel, col_block, axis=0)
            prod = jnp.einsum(
                "tij,tjs->tis", tile_block, pieces, preferred_element_type=jnp.float32
            )
            live = start + jnp.arange(block, dtype=jnp.int32) < count
            prod = jnp.where(live[:, None, None], prod, 0.0)
            return total.at[row_block].add(prod)

        total = lax.fori_loop(0, slots // block, step_fn, start_acc)
        partial_value = total.reshape(n_tile_rows * side, width)
        summed_rows = lax.psum_scatter(
            partial_value[:block_rows], "col", scatter_dimension=0, tiled=True
        )
        own_scores = 0.85 * summed_rows + 0.15 * tele_own
        hub_part = partial_value[block_rows:]
        summed = lax.psum_scatter(hub_part, ("row", "col"), scatter_dimension=0, tiled=True)
        hub_piece = 0.85 * summed + 0.15 * tele_piece
        if step + 1 < ITERS:
            hub_panel = lax.all_gather(
                hub_piece.astype(jnp.bfloat16), ("row", "col"), axis=0, tiled=True
            )
    return (own_scores.reshape(1, 1, VB, width), hub_piece)


def solution(mesh):
    placed = (
        P(("groups", "row"), "col", None, None, None),
        P(("groups", "row"), "col", None),
        P(("groups", "row"), "col", None),
        P(("groups", "row"), "col"),
        P("groups"),
    )

    def body(tiles, *rest):
        n_row, n_col = mesh.shape["row"], mesh.shape["col"]
        slots, side = tiles.shape[2:4]
        blocks = (n_col * VB + H) * (n_row * VB + H) // (side * side)
        if n_col == 2 and n_row in (4, 8, 16) and blocks <= slots and H // (n_row * n_col) % 16 == 0:
            return fast_body(tiles, *rest)
        return plain_body(tiles, *rest)

    return jax.shard_map(
        body,
        mesh=mesh,
        in_specs=placed,
        out_specs=(P(("groups", "row"), "col", None, None), P(("groups", "row", "col"), None)),
        check_vma=False,
    )
```

```python
import functools

import jax
import jax.numpy as jnp
from jax import lax
from jax.experimental import pallas as pl
from jax.experimental.pallas import tpu as pltpu
from jax.sharding import PartitionSpec as P

VB = 128
H = 256
ITERS = 2
DAMP = 0.85
CHUNK = 16
X = 2
HUB_CORE = 1
MICRO = 10 ** 9
VMEM_LIMIT = 32 * 1024 * 1024

SMEM = pl.BlockSpec(memory_space=pltpu.SMEM)
VMEM = pl.BlockSpec(memory_space=pltpu.VMEM)
HBM = pl.BlockSpec(memory_space=pltpu.HBM)


def params():
    return pltpu.CompilerParams(vmem_limit_bytes=VMEM_LIMIT)


def one_hot(first, count, src):
    ids = lax.broadcasted_iota(jnp.int32, (count, src.shape[1]), 0) + first
    return (ids == src).astype(jnp.float32)


def write_terms(dims, prod_ref, dense_ref, panel_ref, send_ref, keep_ref, hubs_ref):
    n_col = dims[1]
    rows = dense_ref.shape[0] // 2
    own = n_col * VB
    c = lax.axis_index("col")
    prod = jnp.dot(dense_ref[...], panel_ref[...], preferred_element_type=jnp.float32)
    prod_ref[...] = prod[:own] + prod[rows:rows + own]
    hubs_ref[...] = prod[own:rows] + prod[rows + own:]
    for ref, col in ((keep_ref, c), (send_ref, 1 - c)):
        ref[...] = prod_ref[pl.ds(pl.multiple_of(col * VB, VB), VB), :]


def first_kernel(dims, tiles_ref, rows_hbm, cols_hbm, count_hbm, src_hbm, send_ref, keep_ref, hubs_ref, dense_ref,
                 held, rows_ref, cols_ref, count_ref, src_ref, total, panel, prod, sems, small):
    n_row, n_col, side = dims
    n_rows = dense_ref.shape[0] // 2
    pairs = ((src_hbm, src_ref), (rows_hbm, rows_ref), (cols_hbm, cols_ref), (count_hbm, count_ref))
    scalars = [pltpu.make_async_copy(a, b, small.at[i]) for i, (a, b) in enumerate(pairs)]
    copies = []
    for i in range(held.shape[0] // CHUNK):
        part = pl.ds(i * CHUNK, CHUNK)
        copies.append(pltpu.make_async_copy(tiles_ref.at[part], held.at[part], sems.at[i]))
    for copy in scalars + copies:
        copy.start()
    total[...] = jnp.zeros_like(total)
    for copy in scalars:
        copy.wait()
    src = src_ref[...]
    for r in range(n_row):
        first = H + (r * n_col + lax.axis_index("col")) * VB
        panel[pl.ds(r * VB, VB), :] = one_hot(first, VB, src).astype(jnp.bfloat16)
    panel[pl.ds(n_row * VB, H), :] = one_hot(0, H, src).astype(jnp.bfloat16)
    count = count_ref[0]

    def add_tile(k, carry):
        live = k < count
        row = pl.multiple_of(jnp.where(live, rows_ref[k] * side, n_rows), side)
        col = pl.multiple_of(jnp.where(live, cols_ref[k] * side, 0), side)
        spot = (pl.ds(row, side), pl.ds(col, side))
        total[spot] += held[k].astype(jnp.float32)
        return carry

    for i, copy in enumerate(copies):
        copy.wait()
        lax.fori_loop(i * CHUNK, (i + 1) * CHUNK, add_tile, 0, unroll=4)
    for r in range(0, n_rows, side):
        whole = total[pl.ds(r, side), :]
        high = whole.astype(jnp.bfloat16)
        dense_ref[pl.ds(r, side), :] = high
        dense_ref[pl.ds(n_rows + r, side), :] = (whole - high.astype(jnp.float32)).astype(jnp.bfloat16)
    write_terms(dims, prod, dense_ref, panel, send_ref, keep_ref, hubs_ref)


def second_kernel(dims, *refs):
    n_row = dims[0]
    n_z = n_row // X
    blocks, (across, mine_ref, theirs_ref) = refs[:n_z], refs[n_z:n_z + 3]
    dense_ref, send_ref, keep_ref, hubs_ref, panel, prod = refs[n_z + 3:]
    r, c = lax.axis_index("row"), lax.axis_index("col")

    def put(owner, block):
        panel[pl.ds(pl.multiple_of(owner * VB, VB), VB), :] = block

    for k in range(n_z):
        put(r ^ (X * k), blocks[k][...])
        put(r ^ (X * k) ^ 1, across[k])
    for ref, core in ((mine_ref, HUB_CORE), (theirs_ref, 1 - HUB_CORE)):
        @pl.when(c == core)
        def _():
            panel[pl.ds(n_row * VB, H), :] = ref[...]
    write_terms(dims, prod, dense_ref, panel, send_ref, keep_ref, hubs_ref)


def own_scores(dims, src_ref, keep_ref, came_ref):
    first = H + (lax.axis_index("row") * dims[1] + lax.axis_index("col")) * VB
    return DAMP * (keep_ref[...] + came_ref[...]) + 0.15 * one_hot(first, VB, src_ref[...])


def scores_kernel(dims, src_ref, keep_ref, came_ref, scores_ref):
    scores_ref[...] = own_scores(dims, src_ref, keep_ref, came_ref).astype(scores_ref.dtype)


def spread_kernel(block, mine_ref, came_ref, hold_ref, pass_ref):
    x = lax.axis_index("row") % X
    for ref, place in ((hold_ref, x), (pass_ref, 1 - x)):
        for k in range(ref.shape[0] // block):
            spot = pl.ds(pl.multiple_of((k * X + place) * block, block), block)
            ref[k * block:(k + 1) * block] = mine_ref[spot, :] + came_ref[spot, :]


def scores_and_spread_kernel(dims, block, src_ref, keep_ref, came_ref, mine_ref, theirs_ref, scores_ref, hold_ref, pass_ref):
    spread_kernel(block, mine_ref, theirs_ref, hold_ref, pass_ref)
    scores_kernel(dims, src_ref, keep_ref, came_ref, scores_ref)


def join_kernel(*refs):
    out_ref = refs[-1]
    for k in range(out_ref.shape[0]):
        out_ref[k] = refs[k][...]


def plane_kernel(hold_ref, came_ref, out_ref):
    out_ref[...] = hold_ref[...] + came_ref[...]


def sum_planes(planes, held):
    z = lax.axis_index("row") // X
    for k, plane in enumerate(planes):
        held[z ^ k] = plane[...]
    summed = held[0]
    for k in range(1, len(planes)):
        summed = summed + held[k]
    return summed


def hub_kernel(first, src_ref, *refs):
    out_ref, held = refs[-2:]
    planes = refs[:held.shape[0]]
    count = out_ref.shape[0]
    tele = one_hot(first(lax.axis_index("row")), count, src_ref[...])
    out_ref[...] = (DAMP * sum_planes(planes, held) + 0.15 * tele).astype(out_ref.dtype)


def side_kernel(mine_ref, theirs_ref, out_ref):
    part = mine_ref.shape[0]
    x = lax.axis_index("row") % X
    for ref, place in ((mine_ref, x), (theirs_ref, 1 - x)):
        out_ref[pl.ds(pl.multiple_of(place * part, part), part), :] = ref[...]


def pieces_kernel(hold_ref, came_ref, *outs):
    z = lax.axis_index("row") // X
    share = outs[0].shape[0]
    for k, out in enumerate(outs):
        spot = pl.ds(pl.multiple_of((z ^ k) * share, share), share)
        out[...] = hold_ref[spot, :] + came_ref[spot, :]


def last_hubs_kernel(mine_ref, theirs_ref, out_ref):
    piece = out_ref.shape[0]
    for ref, core in ((mine_ref, HUB_CORE), (theirs_ref, 1 - HUB_CORE)):
        @pl.when(lax.axis_index("col") == core)
        def _():
            out_ref[...] = ref[core * piece:(core + 1) * piece]


def fast_body(tiles, tile_row, tile_col, tile_count, sources):
    slots, side = tiles.shape[2:4]
    width = sources.shape[0]
    n_row = lax.axis_size("row")
    n_col = lax.axis_size("col")
    n_z = n_row // X
    part = H // X
    share = H // n_row
    dims = (n_row, n_col, side)
    n_rows = n_col * VB + H
    n_cols = n_row * VB + H
    bind = functools.partial
    f32 = bind(jax.ShapeDtypeStruct, dtype=jnp.float32)
    bf16 = bind(jax.ShapeDtypeStruct, dtype=jnp.bfloat16)
    src = sources.reshape(1, width)
    product_scratch = [
        pltpu.VMEM((n_cols, width), jnp.bfloat16),
        pltpu.VMEM((n_col * VB, width), jnp.float32),
    ]
    term_shapes = (f32((VB, width)), f32((VB, width)), f32((H, width)))

    def other_core(x):
        return lax.ppermute(x, "col", [(0, 1), (1, 0)])

    def to_partner(x, flip):
        return lax.ppermute(x, "row", [(r, r ^ flip) for r in range(n_row)])

    def hub_partner(x, flip):
        devices = [(r, c) for r in range(n_row) for c in range(n_col)]
        pairs = [(r * n_col + c, (r ^ flip if c == HUB_CORE else r) * n_col + c) for r, c in devices]
        return lax.ppermute(x, ("row", "col"), pairs)

    def call(kernel, name, out_shape, *args, scratch=(), cost=0):
        return pl.pallas_call(
            kernel,
            out_shape=out_shape,
            in_specs=[VMEM] * len(args),
            out_specs=jax.tree.map(lambda _: VMEM, out_shape),
            scratch_shapes=scratch,
            compiler_params=params(),
            cost_estimate=pl.CostEstimate(flops=cost * MICRO, bytes_accessed=0, transcendentals=0),
            name=name,
        )(*args)

    in_hbm = [pltpu.with_memory_space_constraint(x, pltpu.HBM) for x in (
        tiles.reshape(slots, side, side), tile_row.reshape(slots), tile_col.reshape(slots), src)]
    send, keep, hubs, dense = pl.pallas_call(
        bind(first_kernel, dims),
        out_shape=term_shapes + (bf16((2 * n_rows, n_cols)),),
        in_specs=[HBM] * 5,
        out_specs=[VMEM] * 4,
        scratch_shapes=[
            pltpu.VMEM((slots, side, side), jnp.bfloat16),
            pltpu.SMEM((slots,), jnp.int32),
            pltpu.SMEM((slots,), jnp.int32),
            pltpu.SMEM((1,), jnp.int32),
            pltpu.VMEM((1, width), jnp.int32),
            pltpu.VMEM((n_rows + side, n_cols), jnp.float32),
        ] + product_scratch + [
            pltpu.SemaphoreType.DMA((slots // CHUNK,)),
            pltpu.SemaphoreType.DMA((4,)),
        ],
        compiler_params=params(),
        name="first_terms",
    )(*in_hbm[:3], tile_count.reshape(1), in_hbm[3])

    for step in range(ITERS - 1):
        own, hold, away = call(
            bind(scores_and_spread_kernel, dims, part), "spread",
            (bf16((VB, width)), f32((part, width)), f32((part, width))),
            src, keep, other_core(send), hubs, other_core(hubs))
        away = hub_partner(away, 1)
        blocks = [own] + [to_partner(own, X * k) for k in range(1, n_z)]
        plane = call(plane_kernel, "plane_sum", f32((part, width)), hold, away)
        planes = [plane] + [hub_partner(plane, X * k) for k in range(1, n_z)]
        across = to_partner(call(join_kernel, "join_rows", bf16((n_z, VB, width)), *blocks, cost=1), 1)
        mine = call(bind(hub_kernel, lambda r: r % X * part), "hub_sums", bf16((part, width)), src, *planes,
                    scratch=[pltpu.VMEM((n_z, part, width), jnp.float32)], cost=1)
        mine = call(side_kernel, "join_sides", bf16((H, width)), mine, hub_partner(mine, 1))
        send, keep, hubs = call(
            bind(second_kernel, dims), "later_terms", term_shapes,
            *blocks, across, mine, other_core(mine), dense, scratch=product_scratch)
    hold, away = call(bind(spread_kernel, share), "last_spread", (f32((part, width)),) * 2,
                      hubs, other_core(hubs))
    pieces = call(pieces_kernel, "hub_pieces", (f32((share, width)),) * n_z, hold, hub_partner(away, 1))
    pieces = [pieces[0]] + [hub_partner(pieces[k], X * k) for k in range(1, n_z)]
    scores = call(bind(scores_kernel, dims), "last_scores", f32((VB, width)), src, keep, other_core(send))
    mine = call(bind(hub_kernel, lambda r: r * share), "last_sums", f32((share, width)), src, *pieces,
                scratch=[pltpu.VMEM((n_z, share, width), jnp.float32)])
    hubs = call(last_hubs_kernel, "last_hubs", f32((share // n_col, width)), mine, other_core(mine))
    return scores.reshape(1, 1, VB, width), hubs


def plain_body(tiles, tile_row, tile_col, tile_count, sources):
    slots = tiles.shape[2]
    side = tiles.shape[3]
    width = sources.shape[0]
    tiles = tiles.reshape(slots, side, side)
    rows = tile_row.reshape(slots)
    cols = tile_col.reshape(slots)
    count = tile_count.reshape(())
    n_row = lax.axis_size("row")
    n_col = lax.axis_size("col")
    devices = n_row * n_col
    r_index = lax.axis_index("row")
    c_index = lax.axis_index("col")
    hub_dev = H // devices
    block_rows = n_col * VB
    n_tile_rows = (block_rows + H) // side
    own_base = H + (r_index * n_col + c_index) * VB
    hub_start = (r_index * n_col + c_index) * hub_dev
    own_ids = jnp.arange(VB, dtype=jnp.int32) + own_base
    tele_own = (own_ids[:, None] == sources[None, :]).astype(jnp.float32)
    piece_ids = jnp.arange(hub_dev, dtype=jnp.int32) + hub_start
    tele_piece = (piece_ids[:, None] == sources[None, :]).astype(jnp.float32)
    tele_hubs = (jnp.arange(H, dtype=jnp.int32)[:, None] == sources[None, :]).astype(jnp.float32)
    column_ids = (
        H
        + (jnp.arange(n_row, dtype=jnp.int32)[:, None] * n_col + c_index) * VB
        + jnp.arange(VB, dtype=jnp.int32)[None, :]
    ).reshape(n_row * VB)
    column_panel = (column_ids[:, None] == sources[None, :]).astype(jnp.bfloat16)
    hub_panel = tele_hubs.astype(jnp.bfloat16)
    block = CHUNK
    own_scores = tele_own
    hub_piece = tele_piece
    for step in range(ITERS):
        start_acc = jnp.zeros((n_tile_rows, side, width), jnp.float32)
        if step > 0:
            column_panel = lax.all_gather(
                own_scores.astype(jnp.bfloat16), "row", axis=0, tiled=True
            )
        panel = jnp.concatenate([column_panel, hub_panel], axis=0).reshape(-1, side, width)

        def step_fn(number, total):
            start = number * block
            tile_block = lax.dynamic_slice_in_dim(tiles, start, block, 0)
            col_block = lax.dynamic_slice_in_dim(cols, start, block, 0)
            row_block = lax.dynamic_slice_in_dim(rows, start, block, 0)
            pieces = jnp.take(panel, col_block, axis=0)
            prod = jnp.einsum(
                "tij,tjs->tis", tile_block, pieces, preferred_element_type=jnp.float32
            )
            live = start + jnp.arange(block, dtype=jnp.int32) < count
            prod = jnp.where(live[:, None, None], prod, 0.0)
            return total.at[row_block].add(prod)

        total = lax.fori_loop(0, slots // block, step_fn, start_acc)
        partial_value = total.reshape(n_tile_rows * side, width)
        summed_rows = lax.psum_scatter(
            partial_value[:block_rows], "col", scatter_dimension=0, tiled=True
        )
        own_scores = 0.85 * summed_rows + 0.15 * tele_own
        hub_part = partial_value[block_rows:]
        summed = lax.psum_scatter(hub_part, ("row", "col"), scatter_dimension=0, tiled=True)
        hub_piece = 0.85 * summed + 0.15 * tele_piece
        if step + 1 < ITERS:
            hub_panel = lax.all_gather(
                hub_piece.astype(jnp.bfloat16), ("row", "col"), axis=0, tiled=True
            )
    return (own_scores.reshape(1, 1, VB, width), hub_piece)


def solution(mesh):
    placed = (
        P(("groups", "row"), "col", None, None, None),
        P(("groups", "row"), "col", None),
        P(("groups", "row"), "col", None),
        P(("groups", "row"), "col"),
        P("groups"),
    )

    def body(tiles, *rest):
        n_row, n_col = mesh.shape["row"], mesh.shape["col"]
        slots, side = tiles.shape[2:4]
        blocks = (n_col * VB + H) * (n_row * VB + H) // (side * side)
        if n_col == 2 and n_row in (4, 8, 16) and blocks <= slots and H // (n_row * n_col) % 16 == 0:
            return fast_body(tiles, *rest)
        return plain_body(tiles, *rest)

    return jax.shard_map(
        body,
        mesh=mesh,
        in_specs=placed,
        out_specs=(P(("groups", "row"), "col", None, None), P(("groups", "row", "col"), None)),
        check_vma=False,
    )
```

```python
import functools

import jax
import jax.numpy as jnp
from jax import lax
from jax.experimental import pallas as pl
from jax.experimental.pallas import tpu as pltpu
from jax.sharding import PartitionSpec as P

VB = 128
H = 256
ITERS = 2
DAMP = 0.85
CHUNK = 16
X = 2
MICRO = 10 ** 9
VMEM_LIMIT = 32 * 1024 * 1024

SMEM = pl.BlockSpec(memory_space=pltpu.SMEM)
VMEM = pl.BlockSpec(memory_space=pltpu.VMEM)
HBM = pl.BlockSpec(memory_space=pltpu.HBM)


def params():
    return pltpu.CompilerParams(vmem_limit_bytes=VMEM_LIMIT)


def one_hot(first, count, src):
    ids = lax.broadcasted_iota(jnp.int32, (count, src.shape[1]), 0) + first
    return (ids == src).astype(jnp.float32)


def write_terms(dims, block, prod_ref, dense_ref, panel_ref, send_ref, keep_ref):
    n_row, n_col, side = dims
    rows = dense_ref.shape[0] // 2
    c = lax.axis_index("col")
    prod = jnp.dot(dense_ref[...], panel_ref[...], preferred_element_type=jnp.float32)
    prod_ref[...] = prod[:rows] + prod[rows:]
    for ref, col in ((keep_ref, c), (send_ref, 1 - c)):
        ref[:VB] = prod_ref[pl.ds(pl.multiple_of(col * VB, VB), VB), :]
        for k in range(H // n_col // block):
            start = n_col * VB + (k * n_col + col) * block
            ref[VB + k * block:VB + (k + 1) * block] = prod_ref[pl.ds(pl.multiple_of(start, block), block), :]


def first_kernel(dims, tiles_ref, rows_hbm, cols_hbm, count_hbm, src_hbm, send_ref, keep_ref, dense_ref,
                 held, rows_ref, cols_ref, count_ref, src_ref, total, panel, prod, sems, small):
    n_row, n_col, side = dims
    n_rows = dense_ref.shape[0] // 2
    pairs = ((src_hbm, src_ref), (rows_hbm, rows_ref), (cols_hbm, cols_ref), (count_hbm, count_ref))
    scalars = [pltpu.make_async_copy(a, b, small.at[i]) for i, (a, b) in enumerate(pairs)]
    copies = []
    for i in range(held.shape[0] // CHUNK):
        part = pl.ds(i * CHUNK, CHUNK)
        copies.append(pltpu.make_async_copy(tiles_ref.at[part], held.at[part], sems.at[i]))
    for copy in scalars + copies:
        copy.start()
    total[...] = jnp.zeros_like(total)
    for copy in scalars:
        copy.wait()
    src = src_ref[...]
    for r in range(n_row):
        first = H + (r * n_col + lax.axis_index("col")) * VB
        panel[pl.ds(r * VB, VB), :] = one_hot(first, VB, src).astype(jnp.bfloat16)
    panel[pl.ds(n_row * VB, H), :] = one_hot(0, H, src).astype(jnp.bfloat16)
    count = count_ref[0]

    def add_tile(k, carry):
        live = k < count
        row = pl.multiple_of(jnp.where(live, rows_ref[k] * side, n_rows), side)
        col = pl.multiple_of(jnp.where(live, cols_ref[k] * side, 0), side)
        spot = (pl.ds(row, side), pl.ds(col, side))
        total[spot] += held[k].astype(jnp.float32)
        return carry

    for i, copy in enumerate(copies):
        copy.wait()
        lax.fori_loop(i * CHUNK, (i + 1) * CHUNK, add_tile, 0, unroll=4)
    for r in range(0, n_rows, side):
        whole = total[pl.ds(r, side), :]
        high = whole.astype(jnp.bfloat16)
        dense_ref[pl.ds(r, side), :] = high
        dense_ref[pl.ds(n_rows + r, side), :] = (whole - high.astype(jnp.float32)).astype(jnp.bfloat16)
    write_terms(dims, H // n_col, prod, dense_ref, panel, send_ref, keep_ref)


def second_kernel(dims, *refs):
    n_row, n_col, side = dims
    n_z = n_row // X
    blocks, (across, mine_ref, theirs_ref) = refs[:n_z], refs[n_z:n_z + 3]
    dense_ref, send_ref, keep_ref, panel, prod = refs[n_z + 3:]
    half = H // n_col
    r, c = lax.axis_index("row"), lax.axis_index("col")

    def put(owner, block):
        panel[pl.ds(pl.multiple_of(owner * VB, VB), VB), :] = block

    for k in range(n_z):
        put(r ^ (X * k), blocks[k][...])
        put(r ^ (X * k) ^ 1, across[k])
    for ref, col in ((mine_ref, c), (theirs_ref, 1 - c)):
        panel[pl.ds(pl.multiple_of(n_row * VB + col * half, half), half), :] = ref[...]
    write_terms(dims, half // n_row, prod, dense_ref, panel, send_ref, keep_ref)


def own_scores(dims, src_ref, keep_ref, came_ref):
    first = H + (lax.axis_index("row") * dims[1] + lax.axis_index("col")) * VB
    tele = one_hot(first, VB, src_ref[...])
    return DAMP * (keep_ref[:VB] + came_ref[:VB]) + 0.15 * tele


def spread_kernel(dims, src_ref, keep_ref, came_ref, scores_ref, hold_ref, pass_ref):
    quarter = hold_ref.shape[0]
    x = lax.axis_index("row") % X
    for ref, place in ((hold_ref, x), (pass_ref, 1 - x)):
        spot = pl.ds(pl.multiple_of(VB + place * quarter, quarter), quarter)
        ref[...] = keep_ref[spot, :] + came_ref[spot, :]
    scores_ref[...] = own_scores(dims, src_ref, keep_ref, came_ref).astype(scores_ref.dtype)


def join_kernel(*refs):
    for k, ref in enumerate(refs[:-1]):
        refs[-1][k] = ref[...]


def plane_kernel(hold_ref, came_ref, out_ref):
    out_ref[...] = hold_ref[...] + came_ref[...]


def sum_planes(planes, held):
    z = lax.axis_index("row") // X
    for k, plane in enumerate(planes):
        held[z ^ k] = plane[...]
    summed = held[0]
    for k in range(1, len(planes)):
        summed = summed + held[k]
    return summed


def hub_kernel(dims, src_ref, *refs):
    planes, (out_ref, held) = refs[:-2], refs[-2:]
    quarter = out_ref.shape[0]
    first = (lax.axis_index("col") * X + lax.axis_index("row") % X) * quarter
    tele = one_hot(first, quarter, src_ref[...])
    out_ref[...] = (DAMP * sum_planes(planes, held) + 0.15 * tele).astype(out_ref.dtype)


def side_kernel(mine_ref, theirs_ref, out_ref):
    quarter = mine_ref.shape[0]
    x = lax.axis_index("row") % X
    for ref, place in ((mine_ref, x), (theirs_ref, 1 - x)):
        out_ref[pl.ds(pl.multiple_of(place * quarter, quarter), quarter), :] = ref[...]


def halves_kernel(dims, keep_ref, came_ref, hold_ref, pass_ref):
    n_row, n_col, side = dims
    piece = H // (n_row * n_col)
    x = lax.axis_index("row") % X
    for ref, place in ((hold_ref, x), (pass_ref, 1 - x)):
        for z in range(n_row // X):
            spot = pl.ds(pl.multiple_of(VB + (z * X + place) * piece, piece), piece)
            ref[z * piece:(z + 1) * piece] = keep_ref[spot, :] + came_ref[spot, :]


def pieces_kernel(hold_ref, came_ref, *outs):
    z = lax.axis_index("row") // X
    piece = outs[0].shape[0]
    for k, out in enumerate(outs):
        spot = pl.ds(pl.multiple_of((z ^ k) * piece, piece), piece)
        out[...] = hold_ref[spot, :] + came_ref[spot, :]


def last_scores_kernel(dims, src_ref, keep_ref, came_ref, scores_ref):
    scores_ref[...] = own_scores(dims, src_ref, keep_ref, came_ref)


def last_hubs_kernel(dims, src_ref, *refs):
    planes, (out_ref, held) = refs[:-2], refs[-2:]
    piece = out_ref.shape[0]
    first = (lax.axis_index("row") * dims[1] + lax.axis_index("col")) * piece
    out_ref[...] = DAMP * sum_planes(planes, held) + 0.15 * one_hot(first, piece, src_ref[...])


def fast_body(tiles, tile_row, tile_col, tile_count, sources):
    slots, side = tiles.shape[2:4]
    width = sources.shape[0]
    n_row = lax.axis_size("row")
    n_col = lax.axis_size("col")
    piece = H // (n_row * n_col)
    dims = (n_row, n_col, side)
    n_rows = n_col * VB + H
    n_cols = n_row * VB + H
    f32 = functools.partial(jax.ShapeDtypeStruct, dtype=jnp.float32)
    bf16 = functools.partial(jax.ShapeDtypeStruct, dtype=jnp.bfloat16)
    src = sources.reshape(1, width)
    half = VB + n_row * piece
    quarter = H // n_col // X
    product_scratch = [
        pltpu.VMEM((n_cols, width), jnp.bfloat16),
        pltpu.VMEM((n_rows, width), jnp.float32),
    ]

    def other_core(x):
        return lax.ppermute(x, "col", [(0, 1), (1, 0)])

    def to_partner(x, flip):
        return lax.ppermute(x, "row", [(r, r ^ flip) for r in range(n_row)])

    def other_side(x):
        return to_partner(x, 1)

    def along_z(blocks):
        return [to_partner(block, X * k) for k, block in enumerate(blocks) if k > 0]

    def call(kernel, name, out_shape, *args, scratch=(), cost=0):
        return pl.pallas_call(
            kernel,
            out_shape=out_shape,
            in_specs=[VMEM] * len(args),
            out_specs=jax.tree.map(lambda _: VMEM, out_shape),
            scratch_shapes=scratch,
            compiler_params=params(),
            cost_estimate=pl.CostEstimate(flops=cost * MICRO, bytes_accessed=0, transcendentals=0),
            name=name,
        )(*args)

    bind = functools.partial

    in_hbm = [pltpu.with_memory_space_constraint(x, pltpu.HBM) for x in (
        tiles.reshape(slots, side, side), tile_row.reshape(slots), tile_col.reshape(slots), src)]
    send, keep, dense = pl.pallas_call(
        bind(first_kernel, dims),
        out_shape=(f32((half, width)), f32((half, width)), bf16((2 * n_rows, n_cols))),
        in_specs=[HBM] * 5,
        out_specs=[VMEM] * 3,
        scratch_shapes=[
            pltpu.VMEM((slots, side, side), jnp.bfloat16),
            pltpu.SMEM((slots,), jnp.int32),
            pltpu.SMEM((slots,), jnp.int32),
            pltpu.SMEM((1,), jnp.int32),
            pltpu.VMEM((1, width), jnp.int32),
            pltpu.VMEM((n_rows + side, n_cols), jnp.float32),
        ] + product_scratch + [
            pltpu.SemaphoreType.DMA((slots // CHUNK,)),
            pltpu.SemaphoreType.DMA((4,)),
        ],
        compiler_params=params(),
        name="first_terms",
    )(*in_hbm[:3], tile_count.reshape(1), in_hbm[3])

    n_z = n_row // X
    for step in range(ITERS - 1):
        came = other_core(send)
        own, hold, away = call(
            bind(spread_kernel, dims), "spread",
            (bf16((VB, width)), f32((quarter, width)), f32((quarter, width))),
            src, keep, came, cost=1)
        away = other_side(away)
        blocks = [own] + along_z([own] * n_z)
        plane = call(plane_kernel, "plane_sum", f32((quarter, width)), hold, away, cost=20)
        planes = [plane] + along_z([plane] * n_z)
        across = other_side(call(join_kernel, "join_rows", bf16((n_z, VB, width)), *blocks, cost=2))
        mine = call(bind(hub_kernel, dims), "hub_sums", bf16((quarter, width)), src, *planes,
                    scratch=[pltpu.VMEM((n_z, quarter, width), jnp.float32)], cost=2)
        mine = call(side_kernel, "join_sides", bf16((H // n_col, width)), mine, other_side(mine), cost=1)
        send, keep = call(
            bind(second_kernel, dims), "later_terms", (f32((half, width)), f32((half, width))),
            *blocks, across, mine, other_core(mine), dense, scratch=product_scratch)
    came = other_core(send)
    hold, away = call(bind(halves_kernel, dims), "hub_halves",
                      (f32((quarter, width)), f32((quarter, width))), keep, came)
    pieces = call(pieces_kernel, "hub_pieces", (f32((piece, width)),) * n_z, hold, other_side(away))
    pieces = [pieces[0]] + along_z(pieces)
    scores = call(bind(last_scores_kernel, dims), "last_scores", f32((VB, width)), src, keep, came)
    hubs = call(bind(last_hubs_kernel, dims), "last_hubs", f32((piece, width)), src, *pieces,
                scratch=[pltpu.VMEM((n_z, piece, width), jnp.float32)])
    return scores.reshape(1, 1, VB, width), hubs


def plain_body(tiles, tile_row, tile_col, tile_count, sources):
    slots = tiles.shape[2]
    side = tiles.shape[3]
    width = sources.shape[0]
    tiles = tiles.reshape(slots, side, side)
    rows = tile_row.reshape(slots)
    cols = tile_col.reshape(slots)
    count = tile_count.reshape(())
    n_row = lax.axis_size("row")
    n_col = lax.axis_size("col")
    devices = n_row * n_col
    r_index = lax.axis_index("row")
    c_index = lax.axis_index("col")
    hub_dev = H // devices
    block_rows = n_col * VB
    n_tile_rows = (block_rows + H) // side
    own_base = H + (r_index * n_col + c_index) * VB
    hub_start = (r_index * n_col + c_index) * hub_dev
    own_ids = jnp.arange(VB, dtype=jnp.int32) + own_base
    tele_own = (own_ids[:, None] == sources[None, :]).astype(jnp.float32)
    piece_ids = jnp.arange(hub_dev, dtype=jnp.int32) + hub_start
    tele_piece = (piece_ids[:, None] == sources[None, :]).astype(jnp.float32)
    tele_hubs = (jnp.arange(H, dtype=jnp.int32)[:, None] == sources[None, :]).astype(jnp.float32)
    column_ids = (
        H
        + (jnp.arange(n_row, dtype=jnp.int32)[:, None] * n_col + c_index) * VB
        + jnp.arange(VB, dtype=jnp.int32)[None, :]
    ).reshape(n_row * VB)
    column_panel = (column_ids[:, None] == sources[None, :]).astype(jnp.bfloat16)
    hub_panel = tele_hubs.astype(jnp.bfloat16)
    block = CHUNK
    own_scores = tele_own
    hub_piece = tele_piece
    for step in range(ITERS):
        start_acc = jnp.zeros((n_tile_rows, side, width), jnp.float32)
        if step > 0:
            column_panel = lax.all_gather(
                own_scores.astype(jnp.bfloat16), "row", axis=0, tiled=True
            )
        panel = jnp.concatenate([column_panel, hub_panel], axis=0).reshape(-1, side, width)

        def step_fn(number, total):
            start = number * block
            tile_block = lax.dynamic_slice_in_dim(tiles, start, block, 0)
            col_block = lax.dynamic_slice_in_dim(cols, start, block, 0)
            row_block = lax.dynamic_slice_in_dim(rows, start, block, 0)
            pieces = jnp.take(panel, col_block, axis=0)
            prod = jnp.einsum(
                "tij,tjs->tis", tile_block, pieces, preferred_element_type=jnp.float32
            )
            live = start + jnp.arange(block, dtype=jnp.int32) < count
            prod = jnp.where(live[:, None, None], prod, 0.0)
            return total.at[row_block].add(prod)

        total = lax.fori_loop(0, slots // block, step_fn, start_acc)
        partial_value = total.reshape(n_tile_rows * side, width)
        summed_rows = lax.psum_scatter(
            partial_value[:block_rows], "col", scatter_dimension=0, tiled=True
        )
        own_scores = 0.85 * summed_rows + 0.15 * tele_own
        hub_part = partial_value[block_rows:]
        summed = lax.psum_scatter(hub_part, ("row", "col"), scatter_dimension=0, tiled=True)
        hub_piece = 0.85 * summed + 0.15 * tele_piece
        if step + 1 < ITERS:
            hub_panel = lax.all_gather(
                hub_piece.astype(jnp.bfloat16), ("row", "col"), axis=0, tiled=True
            )
    return (own_scores.reshape(1, 1, VB, width), hub_piece)


def solution(mesh):
    placed = (
        P(("groups", "row"), "col", None, None, None),
        P(("groups", "row"), "col", None),
        P(("groups", "row"), "col", None),
        P(("groups", "row"), "col"),
        P("groups"),
    )

    def body(tiles, *rest):
        n_row, n_col = mesh.shape["row"], mesh.shape["col"]
        slots, side = tiles.shape[2:4]
        blocks = (n_col * VB + H) * (n_row * VB + H) // (side * side)
        if n_col == 2 and n_row in (4, 8, 16) and blocks <= slots and H // (n_row * n_col) % 16 == 0:
            return fast_body(tiles, *rest)
        return plain_body(tiles, *rest)

    return jax.shard_map(
        body,
        mesh=mesh,
        in_specs=placed,
        out_specs=(P(("groups", "row"), "col", None, None), P(("groups", "row", "col"), None)),
        check_vma=False,
    )
```

```python
import functools

import jax
import jax.numpy as jnp
from jax import lax
from jax.experimental import pallas as pl
from jax.experimental.pallas import tpu as pltpu
from jax.sharding import PartitionSpec as P

VB = 128
H = 256
ITERS = 2
DAMP = 0.85
CHUNK = 16
X = 2
MICRO = 10 ** 9
VMEM_LIMIT = 32 * 1024 * 1024

SMEM = pl.BlockSpec(memory_space=pltpu.SMEM)
VMEM = pl.BlockSpec(memory_space=pltpu.VMEM)
HBM = pl.BlockSpec(memory_space=pltpu.HBM)


def params():
    return pltpu.CompilerParams(vmem_limit_bytes=VMEM_LIMIT)


def one_hot(first, count, src):
    ids = lax.broadcasted_iota(jnp.int32, (count, src.shape[1]), 0) + first
    return (ids == src).astype(jnp.float32)


def write_terms(dims, block, prod_ref, dense_ref, panel_ref, send_ref, keep_ref):
    n_row, n_col, side = dims
    rows = dense_ref.shape[0] // 2
    c = lax.axis_index("col")
    prod = jnp.dot(dense_ref[...], panel_ref[...], preferred_element_type=jnp.float32)
    prod_ref[...] = prod[:rows] + prod[rows:]
    for ref, col in ((keep_ref, c), (send_ref, 1 - c)):
        ref[:VB] = prod_ref[pl.ds(pl.multiple_of(col * VB, VB), VB), :]
        for k in range(H // n_col // block):
            start = n_col * VB + (k * n_col + col) * block
            ref[VB + k * block:VB + (k + 1) * block] = prod_ref[pl.ds(pl.multiple_of(start, block), block), :]


def first_kernel(dims, tiles_ref, rows_hbm, cols_hbm, count_hbm, src_hbm, send_ref, keep_ref, dense_ref,
                 held, rows_ref, cols_ref, count_ref, src_ref, total, panel, prod, sems, small):
    n_row, n_col, side = dims
    n_rows = dense_ref.shape[0] // 2
    pairs = ((src_hbm, src_ref), (rows_hbm, rows_ref), (cols_hbm, cols_ref), (count_hbm, count_ref))
    scalars = [pltpu.make_async_copy(a, b, small.at[i]) for i, (a, b) in enumerate(pairs)]
    copies = []
    for i in range(held.shape[0] // CHUNK):
        part = pl.ds(i * CHUNK, CHUNK)
        copies.append(pltpu.make_async_copy(tiles_ref.at[part], held.at[part], sems.at[i]))
    for copy in scalars + copies:
        copy.start()
    total[...] = jnp.zeros_like(total)
    for copy in scalars:
        copy.wait()
    src = src_ref[...]
    for r in range(n_row):
        first = H + (r * n_col + lax.axis_index("col")) * VB
        panel[pl.ds(r * VB, VB), :] = one_hot(first, VB, src).astype(jnp.bfloat16)
    panel[pl.ds(n_row * VB, H), :] = one_hot(0, H, src).astype(jnp.bfloat16)
    count = count_ref[0]

    def add_tile(k, carry):
        live = k < count
        row = pl.multiple_of(jnp.where(live, rows_ref[k] * side, n_rows), side)
        col = pl.multiple_of(jnp.where(live, cols_ref[k] * side, 0), side)
        spot = (pl.ds(row, side), pl.ds(col, side))
        total[spot] += held[k].astype(jnp.float32)
        return carry

    for i, copy in enumerate(copies):
        copy.wait()
        lax.fori_loop(i * CHUNK, (i + 1) * CHUNK, add_tile, 0, unroll=4)
    for r in range(0, n_rows, side):
        whole = total[pl.ds(r, side), :]
        high = whole.astype(jnp.bfloat16)
        dense_ref[pl.ds(r, side), :] = high
        dense_ref[pl.ds(n_rows + r, side), :] = (whole - high.astype(jnp.float32)).astype(jnp.bfloat16)
    write_terms(dims, H // n_col, prod, dense_ref, panel, send_ref, keep_ref)


def second_kernel(dims, *refs):
    n_row, n_col, side = dims
    n_z = n_row // X
    blocks, (across, mine_ref, theirs_ref) = refs[:n_z], refs[n_z:n_z + 3]
    dense_ref, send_ref, keep_ref, panel, prod = refs[n_z + 3:]
    half = H // n_col
    r, c = lax.axis_index("row"), lax.axis_index("col")

    def put(owner, block):
        panel[pl.ds(pl.multiple_of(owner * VB, VB), VB), :] = block

    for k in range(n_z):
        put(r ^ (X * k), blocks[k][...])
        put(r ^ (X * k) ^ 1, across[k])
    for ref, col in ((mine_ref, c), (theirs_ref, 1 - c)):
        panel[pl.ds(pl.multiple_of(n_row * VB + col * half, half), half), :] = ref[...]
    write_terms(dims, half // n_row, prod, dense_ref, panel, send_ref, keep_ref)


def own_scores(dims, src_ref, keep_ref, came_ref):
    first = H + (lax.axis_index("row") * dims[1] + lax.axis_index("col")) * VB
    tele = one_hot(first, VB, src_ref[...])
    return DAMP * (keep_ref[:VB] + came_ref[:VB]) + 0.15 * tele


def spread_kernel(dims, src_ref, keep_ref, came_ref, scores_ref, hold_ref, pass_ref):
    quarter = hold_ref.shape[0]
    x = lax.axis_index("row") % X
    for ref, place in ((hold_ref, x), (pass_ref, 1 - x)):
        spot = pl.ds(pl.multiple_of(VB + place * quarter, quarter), quarter)
        ref[...] = keep_ref[spot, :] + came_ref[spot, :]
    scores_ref[...] = own_scores(dims, src_ref, keep_ref, came_ref).astype(scores_ref.dtype)


def join_kernel(*refs):
    for k, ref in enumerate(refs[:-1]):
        refs[-1][k] = ref[...]


def plane_kernel(hold_ref, came_ref, out_ref):
    out_ref[...] = hold_ref[...] + came_ref[...]


def sum_planes(planes, held):
    z = lax.axis_index("row") // X
    for k, plane in enumerate(planes):
        held[z ^ k] = plane[...]
    summed = held[0]
    for k in range(1, len(planes)):
        summed = summed + held[k]
    return summed


def hub_kernel(dims, src_ref, *refs):
    planes, (out_ref, held) = refs[:-2], refs[-2:]
    quarter = out_ref.shape[0]
    first = (lax.axis_index("col") * X + lax.axis_index("row") % X) * quarter
    tele = one_hot(first, quarter, src_ref[...])
    out_ref[...] = (DAMP * sum_planes(planes, held) + 0.15 * tele).astype(out_ref.dtype)


def side_kernel(mine_ref, theirs_ref, out_ref):
    quarter = mine_ref.shape[0]
    x = lax.axis_index("row") % X
    for ref, place in ((mine_ref, x), (theirs_ref, 1 - x)):
        out_ref[pl.ds(pl.multiple_of(place * quarter, quarter), quarter), :] = ref[...]


def pieces_kernel(keep_ref, came_ref, parts_ref):
    piece = parts_ref.shape[1]
    for k in range(parts_ref.shape[0]):
        spot = slice(VB + k * piece, VB + (k + 1) * piece)
        parts_ref[k] = keep_ref[spot, :] + came_ref[spot, :]


def last_scores_kernel(dims, src_ref, keep_ref, came_ref, scores_ref):
    scores_ref[...] = own_scores(dims, src_ref, keep_ref, came_ref)


def last_hubs_kernel(dims, src_ref, parts_ref, out_ref):
    piece = out_ref.shape[0]
    summed = parts_ref[0]
    for k in range(1, parts_ref.shape[0]):
        summed = summed + parts_ref[k]
    first = (lax.axis_index("row") * dims[1] + lax.axis_index("col")) * piece
    out_ref[...] = DAMP * summed + 0.15 * one_hot(first, piece, src_ref[...])


def fast_body(tiles, tile_row, tile_col, tile_count, sources):
    slots, side = tiles.shape[2:4]
    width = sources.shape[0]
    n_row = lax.axis_size("row")
    n_col = lax.axis_size("col")
    piece = H // (n_row * n_col)
    dims = (n_row, n_col, side)
    n_rows = n_col * VB + H
    n_cols = n_row * VB + H
    f32 = functools.partial(jax.ShapeDtypeStruct, dtype=jnp.float32)
    bf16 = functools.partial(jax.ShapeDtypeStruct, dtype=jnp.bfloat16)
    src = sources.reshape(1, width)
    half = VB + n_row * piece
    quarter = H // n_col // X
    product_scratch = [
        pltpu.VMEM((n_cols, width), jnp.bfloat16),
        pltpu.VMEM((n_rows, width), jnp.float32),
    ]

    def other_core(x):
        return lax.ppermute(x, "col", [(0, 1), (1, 0)])

    def to_partner(x, flip):
        return lax.ppermute(x, "row", [(r, r ^ flip) for r in range(n_row)])

    def other_side(x):
        return to_partner(x, 1)

    def along_z(blocks):
        return [to_partner(block, X * k) for k, block in enumerate(blocks) if k > 0]

    def call(kernel, name, out_shape, *args, scratch=(), cost=0):
        return pl.pallas_call(
            kernel,
            out_shape=out_shape,
            in_specs=[VMEM] * len(args),
            out_specs=jax.tree.map(lambda _: VMEM, out_shape),
            scratch_shapes=scratch,
            compiler_params=params(),
            cost_estimate=pl.CostEstimate(flops=cost * MICRO, bytes_accessed=0, transcendentals=0),
            name=name,
        )(*args)

    bind = functools.partial

    in_hbm = [pltpu.with_memory_space_constraint(x, pltpu.HBM) for x in (
        tiles.reshape(slots, side, side), tile_row.reshape(slots), tile_col.reshape(slots), src)]
    send, keep, dense = pl.pallas_call(
        bind(first_kernel, dims),
        out_shape=(f32((half, width)), f32((half, width)), bf16((2 * n_rows, n_cols))),
        in_specs=[HBM] * 5,
        out_specs=[VMEM] * 3,
        scratch_shapes=[
            pltpu.VMEM((slots, side, side), jnp.bfloat16),
            pltpu.SMEM((slots,), jnp.int32),
            pltpu.SMEM((slots,), jnp.int32),
            pltpu.SMEM((1,), jnp.int32),
            pltpu.VMEM((1, width), jnp.int32),
            pltpu.VMEM((n_rows + side, n_cols), jnp.float32),
        ] + product_scratch + [
            pltpu.SemaphoreType.DMA((slots // CHUNK,)),
            pltpu.SemaphoreType.DMA((4,)),
        ],
        compiler_params=params(),
        name="first_terms",
    )(*in_hbm[:3], tile_count.reshape(1), in_hbm[3])

    n_z = n_row // X
    for step in range(ITERS - 1):
        came = other_core(send)
        own, hold, away = call(
            bind(spread_kernel, dims), "spread",
            (bf16((VB, width)), f32((quarter, width)), f32((quarter, width))),
            src, keep, came, cost=1)
        away = other_side(away)
        blocks = [own] + along_z([own] * n_z)
        plane = call(plane_kernel, "plane_sum", f32((quarter, width)), hold, away, cost=20)
        planes = [plane] + along_z([plane] * n_z)
        across = other_side(call(join_kernel, "join_rows", bf16((n_z, VB, width)), *blocks, cost=2))
        mine = call(bind(hub_kernel, dims), "hub_sums", bf16((quarter, width)), src, *planes,
                    scratch=[pltpu.VMEM((n_z, quarter, width), jnp.float32)], cost=2)
        mine = call(side_kernel, "join_sides", bf16((H // n_col, width)), mine, other_side(mine), cost=1)
        send, keep = call(
            bind(second_kernel, dims), "later_terms", (f32((half, width)), f32((half, width))),
            *blocks, across, mine, other_core(mine), dense, scratch=product_scratch)
    came = other_core(send)
    parts = call(pieces_kernel, "hub_pieces", f32((n_row, piece, width)), keep, came)
    parts = lax.all_to_all(parts, "row", 0, 0)
    scores = call(bind(last_scores_kernel, dims), "last_scores", f32((VB, width)), src, keep, came)
    hubs = call(bind(last_hubs_kernel, dims), "last_hubs", f32((piece, width)), src, parts)
    return scores.reshape(1, 1, VB, width), hubs


def plain_body(tiles, tile_row, tile_col, tile_count, sources):
    slots = tiles.shape[2]
    side = tiles.shape[3]
    width = sources.shape[0]
    tiles = tiles.reshape(slots, side, side)
    rows = tile_row.reshape(slots)
    cols = tile_col.reshape(slots)
    count = tile_count.reshape(())
    n_row = lax.axis_size("row")
    n_col = lax.axis_size("col")
    devices = n_row * n_col
    r_index = lax.axis_index("row")
    c_index = lax.axis_index("col")
    hub_dev = H // devices
    block_rows = n_col * VB
    n_tile_rows = (block_rows + H) // side
    own_base = H + (r_index * n_col + c_index) * VB
    hub_start = (r_index * n_col + c_index) * hub_dev
    own_ids = jnp.arange(VB, dtype=jnp.int32) + own_base
    tele_own = (own_ids[:, None] == sources[None, :]).astype(jnp.float32)
    piece_ids = jnp.arange(hub_dev, dtype=jnp.int32) + hub_start
    tele_piece = (piece_ids[:, None] == sources[None, :]).astype(jnp.float32)
    tele_hubs = (jnp.arange(H, dtype=jnp.int32)[:, None] == sources[None, :]).astype(jnp.float32)
    column_ids = (
        H
        + (jnp.arange(n_row, dtype=jnp.int32)[:, None] * n_col + c_index) * VB
        + jnp.arange(VB, dtype=jnp.int32)[None, :]
    ).reshape(n_row * VB)
    column_panel = (column_ids[:, None] == sources[None, :]).astype(jnp.bfloat16)
    hub_panel = tele_hubs.astype(jnp.bfloat16)
    block = CHUNK
    own_scores = tele_own
    hub_piece = tele_piece
    for step in range(ITERS):
        start_acc = jnp.zeros((n_tile_rows, side, width), jnp.float32)
        if step > 0:
            column_panel = lax.all_gather(
                own_scores.astype(jnp.bfloat16), "row", axis=0, tiled=True
            )
        panel = jnp.concatenate([column_panel, hub_panel], axis=0).reshape(-1, side, width)

        def step_fn(number, total):
            start = number * block
            tile_block = lax.dynamic_slice_in_dim(tiles, start, block, 0)
            col_block = lax.dynamic_slice_in_dim(cols, start, block, 0)
            row_block = lax.dynamic_slice_in_dim(rows, start, block, 0)
            pieces = jnp.take(panel, col_block, axis=0)
            prod = jnp.einsum(
                "tij,tjs->tis", tile_block, pieces, preferred_element_type=jnp.float32
            )
            live = start + jnp.arange(block, dtype=jnp.int32) < count
            prod = jnp.where(live[:, None, None], prod, 0.0)
            return total.at[row_block].add(prod)

        total = lax.fori_loop(0, slots // block, step_fn, start_acc)
        partial_value = total.reshape(n_tile_rows * side, width)
        summed_rows = lax.psum_scatter(
            partial_value[:block_rows], "col", scatter_dimension=0, tiled=True
        )
        own_scores = 0.85 * summed_rows + 0.15 * tele_own
        hub_part = partial_value[block_rows:]
        summed = lax.psum_scatter(hub_part, ("row", "col"), scatter_dimension=0, tiled=True)
        hub_piece = 0.85 * summed + 0.15 * tele_piece
        if step + 1 < ITERS:
            hub_panel = lax.all_gather(
                hub_piece.astype(jnp.bfloat16), ("row", "col"), axis=0, tiled=True
            )
    return (own_scores.reshape(1, 1, VB, width), hub_piece)


def solution(mesh):
    placed = (
        P(("groups", "row"), "col", None, None, None),
        P(("groups", "row"), "col", None),
        P(("groups", "row"), "col", None),
        P(("groups", "row"), "col"),
        P("groups"),
    )

    def body(tiles, *rest):
        n_row, n_col = mesh.shape["row"], mesh.shape["col"]
        slots, side = tiles.shape[2:4]
        blocks = (n_col * VB + H) * (n_row * VB + H) // (side * side)
        if n_col == 2 and n_row in (4, 8, 16) and blocks <= slots and H // (n_row * n_col) % 16 == 0:
            return fast_body(tiles, *rest)
        return plain_body(tiles, *rest)

    return jax.shard_map(
        body,
        mesh=mesh,
        in_specs=placed,
        out_specs=(P(("groups", "row"), "col", None, None), P(("groups", "row", "col"), None)),
        check_vma=False,
    )
```

```python
import functools

import jax
import jax.numpy as jnp
from jax import lax
from jax.experimental import pallas as pl
from jax.experimental.pallas import tpu as pltpu
from jax.sharding import PartitionSpec as P

VB = 128
H = 256
ITERS = 2
DAMP = 0.85
CHUNK = 16
X = 2
MICRO = 10 ** 9
VMEM_LIMIT = 32 * 1024 * 1024

SMEM = pl.BlockSpec(memory_space=pltpu.SMEM)
VMEM = pl.BlockSpec(memory_space=pltpu.VMEM)
HBM = pl.BlockSpec(memory_space=pltpu.HBM)


def params():
    return pltpu.CompilerParams(vmem_limit_bytes=VMEM_LIMIT)


def one_hot(first, count, src):
    ids = lax.broadcasted_iota(jnp.int32, (count, src.shape[1]), 0) + first
    return (ids == src).astype(jnp.float32)


def write_terms(dims, prod_ref, dense_ref, panel_ref, send_ref, keep_ref):
    n_row, n_col, side = dims
    rows = dense_ref.shape[0] // 2
    half = H // n_col
    c = lax.axis_index("col")
    prod = jnp.dot(dense_ref[...], panel_ref[...], preferred_element_type=jnp.float32)
    prod_ref[...] = prod[:rows] + prod[rows:]
    for ref, col in ((keep_ref, c), (send_ref, 1 - c)):
        ref[:VB] = prod_ref[pl.ds(pl.multiple_of(col * VB, VB), VB), :]
        if ref.shape[0] > VB:
            ref[VB:] = prod_ref[pl.ds(pl.multiple_of(n_col * VB + col * half, half), half), :]


def first_kernel(dims, tiles_ref, rows_hbm, cols_hbm, count_hbm, src_hbm, send_ref, keep_ref, dense_ref,
                 held, rows_ref, cols_ref, count_ref, src_ref, total, panel, prod, sems, small):
    n_row, n_col, side = dims
    n_rows = dense_ref.shape[0] // 2
    pairs = ((src_hbm, src_ref), (rows_hbm, rows_ref), (cols_hbm, cols_ref), (count_hbm, count_ref))
    scalars = [pltpu.make_async_copy(a, b, small.at[i]) for i, (a, b) in enumerate(pairs)]
    copies = []
    for i in range(held.shape[0] // CHUNK):
        part = pl.ds(i * CHUNK, CHUNK)
        copies.append(pltpu.make_async_copy(tiles_ref.at[part], held.at[part], sems.at[i]))
    for copy in scalars + copies:
        copy.start()
    total[...] = jnp.zeros_like(total)
    for copy in scalars:
        copy.wait()
    src = src_ref[...]
    for r in range(n_row):
        first = H + (r * n_col + lax.axis_index("col")) * VB
        panel[pl.ds(r * VB, VB), :] = one_hot(first, VB, src).astype(jnp.bfloat16)
    panel[pl.ds(n_row * VB, H), :] = one_hot(0, H, src).astype(jnp.bfloat16)
    count = count_ref[0]

    def add_tile(k, carry):
        live = k < count
        row = pl.multiple_of(jnp.where(live, rows_ref[k] * side, n_rows), side)
        col = pl.multiple_of(jnp.where(live, cols_ref[k] * side, 0), side)
        spot = (pl.ds(row, side), pl.ds(col, side))
        total[spot] += held[k].astype(jnp.float32)
        return carry

    for i, copy in enumerate(copies):
        copy.wait()
        lax.fori_loop(i * CHUNK, (i + 1) * CHUNK, add_tile, 0, unroll=4)
    for r in range(0, n_rows, side):
        whole = total[pl.ds(r, side), :]
        high = whole.astype(jnp.bfloat16)
        dense_ref[pl.ds(r, side), :] = high
        dense_ref[pl.ds(n_rows + r, side), :] = (whole - high.astype(jnp.float32)).astype(jnp.bfloat16)
    write_terms(dims, prod, dense_ref, panel, send_ref, keep_ref)


def second_kernel(dims, *refs):
    n_row, n_col, side = dims
    n_z = n_row // X
    blocks, (across, mine_ref, theirs_ref) = refs[:n_z], refs[n_z:n_z + 3]
    dense_ref, send_ref, keep_ref, *parts, panel, prod = refs[n_z + 3:]
    half = H // n_col
    r, c = lax.axis_index("row"), lax.axis_index("col")

    def put(owner, block):
        panel[pl.ds(pl.multiple_of(owner * VB, VB), VB), :] = block

    for k in range(n_z):
        put(r ^ (X * k), blocks[k][...])
        put(r ^ (X * k) ^ 1, across[k])
    for ref, col in ((mine_ref, c), (theirs_ref, 1 - c)):
        panel[pl.ds(pl.multiple_of(n_row * VB + col * half, half), half), :] = ref[...]
    write_terms(dims, prod, dense_ref, panel, send_ref, keep_ref)
    for ref in parts:
        ref[...] = prod[n_col * VB:].reshape(ref.shape)


def own_scores(dims, src_ref, keep_ref, came_ref):
    first = H + (lax.axis_index("row") * dims[1] + lax.axis_index("col")) * VB
    tele = one_hot(first, VB, src_ref[...])
    return DAMP * (keep_ref[:VB] + came_ref[:VB]) + 0.15 * tele


def spread_kernel(dims, src_ref, keep_ref, came_ref, scores_ref, hold_ref, pass_ref):
    quarter = hold_ref.shape[0]
    x = lax.axis_index("row") % X
    for ref, place in ((hold_ref, x), (pass_ref, 1 - x)):
        spot = pl.ds(pl.multiple_of(VB + place * quarter, quarter), quarter)
        ref[...] = keep_ref[spot, :] + came_ref[spot, :]
    scores_ref[...] = own_scores(dims, src_ref, keep_ref, came_ref).astype(scores_ref.dtype)


def join_kernel(*refs):
    for k, ref in enumerate(refs[:-1]):
        refs[-1][k] = ref[...]


def plane_kernel(hold_ref, came_ref, out_ref):
    out_ref[...] = hold_ref[...] + came_ref[...]


def sum_planes(planes, held):
    z = lax.axis_index("row") // X
    for k, plane in enumerate(planes):
        held[z ^ k] = plane[...]
    summed = held[0]
    for k in range(1, len(planes)):
        summed = summed + held[k]
    return summed


def hub_kernel(dims, src_ref, *refs):
    planes, (out_ref, held) = refs[:-2], refs[-2:]
    quarter = out_ref.shape[0]
    first = (lax.axis_index("col") * X + lax.axis_index("row") % X) * quarter
    tele = one_hot(first, quarter, src_ref[...])
    out_ref[...] = (DAMP * sum_planes(planes, held) + 0.15 * tele).astype(out_ref.dtype)


def side_kernel(mine_ref, theirs_ref, out_ref):
    quarter = mine_ref.shape[0]
    x = lax.axis_index("row") % X
    for ref, place in ((mine_ref, x), (theirs_ref, 1 - x)):
        out_ref[pl.ds(pl.multiple_of(place * quarter, quarter), quarter), :] = ref[...]


def last_scores_kernel(dims, src_ref, keep_ref, came_ref, scores_ref):
    scores_ref[...] = own_scores(dims, src_ref, keep_ref, came_ref)


def last_hubs_kernel(dims, src_ref, parts_ref, out_ref):
    piece = out_ref.shape[0]
    summed = parts_ref[0]
    for k in range(1, parts_ref.shape[0]):
        summed = summed + parts_ref[k]
    first = (lax.axis_index("row") * dims[1] + lax.axis_index("col")) * piece
    out_ref[...] = DAMP * summed + 0.15 * one_hot(first, piece, src_ref[...])


def fast_body(tiles, tile_row, tile_col, tile_count, sources):
    slots, side = tiles.shape[2:4]
    width = sources.shape[0]
    n_row = lax.axis_size("row")
    n_col = lax.axis_size("col")
    devices = n_row * n_col
    piece = H // devices
    dims = (n_row, n_col, side)
    n_rows = n_col * VB + H
    n_cols = n_row * VB + H
    f32 = functools.partial(jax.ShapeDtypeStruct, dtype=jnp.float32)
    bf16 = functools.partial(jax.ShapeDtypeStruct, dtype=jnp.bfloat16)
    src = sources.reshape(1, width)
    half = VB + n_row * piece
    quarter = H // n_col // X
    product_scratch = [
        pltpu.VMEM((n_cols, width), jnp.bfloat16),
        pltpu.VMEM((n_rows, width), jnp.float32),
    ]

    def other_core(x):
        return lax.ppermute(x, "col", [(0, 1), (1, 0)])

    def to_partner(x, flip):
        return lax.ppermute(x, "row", [(r, r ^ flip) for r in range(n_row)])

    def other_side(x):
        return to_partner(x, 1)

    def along_z(blocks):
        return [to_partner(block, X * k) for k, block in enumerate(blocks) if k > 0]

    def call(kernel, name, out_shape, *args, scratch=(), cost=0):
        return pl.pallas_call(
            kernel,
            out_shape=out_shape,
            in_specs=[VMEM] * len(args),
            out_specs=jax.tree.map(lambda _: VMEM, out_shape),
            scratch_shapes=scratch,
            compiler_params=params(),
            cost_estimate=pl.CostEstimate(flops=cost * MICRO, bytes_accessed=0, transcendentals=0),
            name=name,
        )(*args)

    bind = functools.partial

    in_hbm = [pltpu.with_memory_space_constraint(x, pltpu.HBM) for x in (
        tiles.reshape(slots, side, side), tile_row.reshape(slots), tile_col.reshape(slots), src)]
    send, keep, dense = pl.pallas_call(
        bind(first_kernel, dims),
        out_shape=(f32((half, width)), f32((half, width)), bf16((2 * n_rows, n_cols))),
        in_specs=[HBM] * 5,
        out_specs=[VMEM] * 3,
        scratch_shapes=[
            pltpu.VMEM((slots, side, side), jnp.bfloat16),
            pltpu.SMEM((slots,), jnp.int32),
            pltpu.SMEM((slots,), jnp.int32),
            pltpu.SMEM((1,), jnp.int32),
            pltpu.VMEM((1, width), jnp.int32),
            pltpu.VMEM((n_rows + side, n_cols), jnp.float32),
        ] + product_scratch + [
            pltpu.SemaphoreType.DMA((slots // CHUNK,)),
            pltpu.SemaphoreType.DMA((4,)),
        ],
        compiler_params=params(),
        name="first_terms",
    )(*in_hbm[:3], tile_count.reshape(1), in_hbm[3])

    n_z = n_row // X
    for step in range(ITERS - 1):
        came = other_core(send)
        own, hold, away = call(
            bind(spread_kernel, dims), "spread",
            (bf16((VB, width)), f32((quarter, width)), f32((quarter, width))),
            src, keep, came, cost=1)
        away = other_side(away)
        blocks = [own] + along_z([own] * n_z)
        plane = call(plane_kernel, "plane_sum", f32((quarter, width)), hold, away, cost=20)
        planes = [plane] + along_z([plane] * n_z)
        across = other_side(call(join_kernel, "join_rows", bf16((n_z, VB, width)), *blocks, cost=2))
        mine = call(bind(hub_kernel, dims), "hub_sums", bf16((quarter, width)), src, *planes,
                    scratch=[pltpu.VMEM((n_z, quarter, width), jnp.float32)], cost=2)
        mine = call(side_kernel, "join_sides", bf16((H // n_col, width)), mine, other_side(mine), cost=1)
        last = step + 2 == ITERS
        rows = VB if last else half
        pieces = (f32((devices, piece, width)),) if last else ()
        send, keep, *parts = call(
            bind(second_kernel, dims), "later_terms", (f32((rows, width)),) * 2 + pieces,
            *blocks, across, mine, other_core(mine), dense, scratch=product_scratch)
    parts = lax.all_to_all(parts[0], ("row", "col"), 0, 0)
    scores = call(bind(last_scores_kernel, dims), "last_scores", f32((VB, width)), src, keep, other_core(send))
    hubs = call(bind(last_hubs_kernel, dims), "last_hubs", f32((piece, width)), src, parts)
    return scores.reshape(1, 1, VB, width), hubs


def plain_body(tiles, tile_row, tile_col, tile_count, sources):
    slots = tiles.shape[2]
    side = tiles.shape[3]
    width = sources.shape[0]
    tiles = tiles.reshape(slots, side, side)
    rows = tile_row.reshape(slots)
    cols = tile_col.reshape(slots)
    count = tile_count.reshape(())
    n_row = lax.axis_size("row")
    n_col = lax.axis_size("col")
    devices = n_row * n_col
    r_index = lax.axis_index("row")
    c_index = lax.axis_index("col")
    hub_dev = H // devices
    block_rows = n_col * VB
    n_tile_rows = (block_rows + H) // side
    own_base = H + (r_index * n_col + c_index) * VB
    hub_start = (r_index * n_col + c_index) * hub_dev
    own_ids = jnp.arange(VB, dtype=jnp.int32) + own_base
    tele_own = (own_ids[:, None] == sources[None, :]).astype(jnp.float32)
    piece_ids = jnp.arange(hub_dev, dtype=jnp.int32) + hub_start
    tele_piece = (piece_ids[:, None] == sources[None, :]).astype(jnp.float32)
    tele_hubs = (jnp.arange(H, dtype=jnp.int32)[:, None] == sources[None, :]).astype(jnp.float32)
    column_ids = (
        H
        + (jnp.arange(n_row, dtype=jnp.int32)[:, None] * n_col + c_index) * VB
        + jnp.arange(VB, dtype=jnp.int32)[None, :]
    ).reshape(n_row * VB)
    column_panel = (column_ids[:, None] == sources[None, :]).astype(jnp.bfloat16)
    hub_panel = tele_hubs.astype(jnp.bfloat16)
    block = CHUNK
    own_scores = tele_own
    hub_piece = tele_piece
    for step in range(ITERS):
        start_acc = jnp.zeros((n_tile_rows, side, width), jnp.float32)
        if step > 0:
            column_panel = lax.all_gather(
                own_scores.astype(jnp.bfloat16), "row", axis=0, tiled=True
            )
        panel = jnp.concatenate([column_panel, hub_panel], axis=0).reshape(-1, side, width)

        def step_fn(number, total):
            start = number * block
            tile_block = lax.dynamic_slice_in_dim(tiles, start, block, 0)
            col_block = lax.dynamic_slice_in_dim(cols, start, block, 0)
            row_block = lax.dynamic_slice_in_dim(rows, start, block, 0)
            pieces = jnp.take(panel, col_block, axis=0)
            prod = jnp.einsum(
                "tij,tjs->tis", tile_block, pieces, preferred_element_type=jnp.float32
            )
            live = start + jnp.arange(block, dtype=jnp.int32) < count
            prod = jnp.where(live[:, None, None], prod, 0.0)
            return total.at[row_block].add(prod)

        total = lax.fori_loop(0, slots // block, step_fn, start_acc)
        partial_value = total.reshape(n_tile_rows * side, width)
        summed_rows = lax.psum_scatter(
            partial_value[:block_rows], "col", scatter_dimension=0, tiled=True
        )
        own_scores = 0.85 * summed_rows + 0.15 * tele_own
        hub_part = partial_value[block_rows:]
        summed = lax.psum_scatter(hub_part, ("row", "col"), scatter_dimension=0, tiled=True)
        hub_piece = 0.85 * summed + 0.15 * tele_piece
        if step + 1 < ITERS:
            hub_panel = lax.all_gather(
                hub_piece.astype(jnp.bfloat16), ("row", "col"), axis=0, tiled=True
            )
    return (own_scores.reshape(1, 1, VB, width), hub_piece)


def solution(mesh):
    placed = (
        P(("groups", "row"), "col", None, None, None),
        P(("groups", "row"), "col", None),
        P(("groups", "row"), "col", None),
        P(("groups", "row"), "col"),
        P("groups"),
    )

    def body(tiles, *rest):
        n_row, n_col = mesh.shape["row"], mesh.shape["col"]
        slots, side = tiles.shape[2:4]
        blocks = (n_col * VB + H) * (n_row * VB + H) // (side * side)
        if n_col == 2 and n_row in (4, 8, 16) and blocks <= slots and H // (n_row * n_col) % 16 == 0:
            return fast_body(tiles, *rest)
        return plain_body(tiles, *rest)

    return jax.shard_map(
        body,
        mesh=mesh,
        in_specs=placed,
        out_specs=(P(("groups", "row"), "col", None, None), P(("groups", "row", "col"), None)),
        check_vma=False,
    )
```

```python
import functools

import jax
import jax.numpy as jnp
from jax import lax
from jax.experimental import pallas as pl
from jax.experimental.pallas import tpu as pltpu
from jax.sharding import PartitionSpec as P

VB = 128
H = 256
ITERS = 2
DAMP = 0.85
CHUNK = 16
X = 2
MICRO = 10 ** 9
VMEM_LIMIT = 32 * 1024 * 1024

SMEM = pl.BlockSpec(memory_space=pltpu.SMEM)
VMEM = pl.BlockSpec(memory_space=pltpu.VMEM)
HBM = pl.BlockSpec(memory_space=pltpu.HBM)


def params():
    return pltpu.CompilerParams(vmem_limit_bytes=VMEM_LIMIT)


def one_hot(first, count, src):
    ids = lax.broadcasted_iota(jnp.int32, (count, src.shape[1]), 0) + first
    return (ids == src).astype(jnp.float32)


def write_terms(dims, block, prod_ref, dense_ref, panel_ref, send_ref, keep_ref):
    n_row, n_col, side = dims
    rows = dense_ref.shape[0] // 2
    c = lax.axis_index("col")
    prod = jnp.dot(dense_ref[...], panel_ref[...], preferred_element_type=jnp.float32)
    prod_ref[...] = prod[:rows] + prod[rows:]
    for ref, col in ((keep_ref, c), (send_ref, 1 - c)):
        ref[:VB] = prod_ref[pl.ds(pl.multiple_of(col * VB, VB), VB), :]
        for k in range(H // n_col // block):
            start = n_col * VB + (k * n_col + col) * block
            ref[VB + k * block:VB + (k + 1) * block] = prod_ref[pl.ds(pl.multiple_of(start, block), block), :]


def first_kernel(dims, tiles_ref, rows_hbm, cols_hbm, count_hbm, src_hbm, send_ref, keep_ref, dense_ref,
                 held, rows_ref, cols_ref, count_ref, src_ref, total, panel, prod, sems, small):
    n_row, n_col, side = dims
    n_rows = dense_ref.shape[0] // 2
    pairs = ((src_hbm, src_ref), (rows_hbm, rows_ref), (cols_hbm, cols_ref), (count_hbm, count_ref))
    scalars = [pltpu.make_async_copy(a, b, small.at[i]) for i, (a, b) in enumerate(pairs)]
    copies = []
    for i in range(held.shape[0] // CHUNK):
        part = pl.ds(i * CHUNK, CHUNK)
        copies.append(pltpu.make_async_copy(tiles_ref.at[part], held.at[part], sems.at[i]))
    for copy in scalars + copies:
        copy.start()
    total[...] = jnp.zeros_like(total)
    for copy in scalars:
        copy.wait()
    src = src_ref[...]
    for r in range(n_row):
        first = H + (r * n_col + lax.axis_index("col")) * VB
        panel[pl.ds(r * VB, VB), :] = one_hot(first, VB, src).astype(jnp.bfloat16)
    panel[pl.ds(n_row * VB, H), :] = one_hot(0, H, src).astype(jnp.bfloat16)
    count = count_ref[0]

    def add_tile(k, carry):
        live = k < count
        row = pl.multiple_of(jnp.where(live, rows_ref[k] * side, n_rows), side)
        col = pl.multiple_of(jnp.where(live, cols_ref[k] * side, 0), side)
        spot = (pl.ds(row, side), pl.ds(col, side))
        total[spot] += held[k].astype(jnp.float32)
        return carry

    for i, copy in enumerate(copies):
        copy.wait()
        lax.fori_loop(i * CHUNK, (i + 1) * CHUNK, add_tile, 0, unroll=4)
    for r in range(0, n_rows, side):
        whole = total[pl.ds(r, side), :]
        high = whole.astype(jnp.bfloat16)
        dense_ref[pl.ds(r, side), :] = high
        dense_ref[pl.ds(n_rows + r, side), :] = (whole - high.astype(jnp.float32)).astype(jnp.bfloat16)
    write_terms(dims, H // n_col, prod, dense_ref, panel, send_ref, keep_ref)


def second_kernel(dims, *refs):
    n_row, n_col, side = dims
    n_z = n_row // X
    blocks, across, quarters = refs[:n_z], refs[n_z], refs[n_z + 1:n_z + 1 + X * n_col]
    dense_ref, send_ref, keep_ref, panel, prod = refs[n_z + 1 + X * n_col:]
    half = H // n_col
    r, c = lax.axis_index("row"), lax.axis_index("col")

    def put(owner, block):
        panel[pl.ds(pl.multiple_of(owner * VB, VB), VB), :] = block

    for k in range(n_z):
        put(r ^ (X * k), blocks[k][...])
        put(r ^ (X * k) ^ 1, across[k])
    quarter = quarters[0].shape[0]
    for k, ref in enumerate(quarters):
        place = n_row * VB + ((c ^ (k // X)) * X + (r % X ^ (k % X))) * quarter
        panel[pl.ds(pl.multiple_of(place, quarter), quarter), :] = ref[...]
    write_terms(dims, half // n_row, prod, dense_ref, panel, send_ref, keep_ref)


def own_scores(dims, src_ref, keep_ref, came_ref):
    first = H + (lax.axis_index("row") * dims[1] + lax.axis_index("col")) * VB
    tele = one_hot(first, VB, src_ref[...])
    return DAMP * (keep_ref[:VB] + came_ref[:VB]) + 0.15 * tele


def spread_kernel(dims, src_ref, keep_ref, came_ref, scores_ref, hold_ref, pass_ref):
    quarter = hold_ref.shape[0]
    x = lax.axis_index("row") % X
    for ref, place in ((hold_ref, x), (pass_ref, 1 - x)):
        spot = pl.ds(pl.multiple_of(VB + place * quarter, quarter), quarter)
        ref[...] = keep_ref[spot, :] + came_ref[spot, :]
    scores_ref[...] = own_scores(dims, src_ref, keep_ref, came_ref).astype(scores_ref.dtype)


def join_kernel(*refs):
    for k, ref in enumerate(refs[:-1]):
        refs[-1][k] = ref[...]


def plane_kernel(hold_ref, came_ref, out_ref):
    out_ref[...] = hold_ref[...] + came_ref[...]


def sum_planes(planes, held):
    z = lax.axis_index("row") // X
    for k, plane in enumerate(planes):
        held[z ^ k] = plane[...]
    summed = held[0]
    for k in range(1, len(planes)):
        summed = summed + held[k]
    return summed


def hub_kernel(dims, src_ref, *refs):
    planes, (out_ref, held) = refs[:-2], refs[-2:]
    quarter = out_ref.shape[0]
    first = (lax.axis_index("col") * X + lax.axis_index("row") % X) * quarter
    tele = one_hot(first, quarter, src_ref[...])
    out_ref[...] = (DAMP * sum_planes(planes, held) + 0.15 * tele).astype(out_ref.dtype)


def pieces_kernel(keep_ref, came_ref, parts_ref):
    piece = parts_ref.shape[1]
    for k in range(parts_ref.shape[0]):
        spot = slice(VB + k * piece, VB + (k + 1) * piece)
        parts_ref[k] = keep_ref[spot, :] + came_ref[spot, :]


def last_scores_kernel(dims, src_ref, keep_ref, came_ref, scores_ref):
    scores_ref[...] = own_scores(dims, src_ref, keep_ref, came_ref)


def last_hubs_kernel(dims, src_ref, parts_ref, out_ref):
    piece = out_ref.shape[0]
    summed = parts_ref[0]
    for k in range(1, parts_ref.shape[0]):
        summed = summed + parts_ref[k]
    first = (lax.axis_index("row") * dims[1] + lax.axis_index("col")) * piece
    out_ref[...] = DAMP * summed + 0.15 * one_hot(first, piece, src_ref[...])


def fast_body(tiles, tile_row, tile_col, tile_count, sources):
    slots, side = tiles.shape[2:4]
    width = sources.shape[0]
    n_row = lax.axis_size("row")
    n_col = lax.axis_size("col")
    piece = H // (n_row * n_col)
    dims = (n_row, n_col, side)
    n_rows = n_col * VB + H
    n_cols = n_row * VB + H
    f32 = functools.partial(jax.ShapeDtypeStruct, dtype=jnp.float32)
    bf16 = functools.partial(jax.ShapeDtypeStruct, dtype=jnp.bfloat16)
    src = sources.reshape(1, width)
    half = VB + n_row * piece
    quarter = H // n_col // X
    product_scratch = [
        pltpu.VMEM((n_cols, width), jnp.bfloat16),
        pltpu.VMEM((n_rows, width), jnp.float32),
    ]

    def other_core(x):
        return lax.ppermute(x, "col", [(0, 1), (1, 0)])

    def to_partner(x, flip):
        return lax.ppermute(x, "row", [(r, r ^ flip) for r in range(n_row)])

    def other_side(x):
        return to_partner(x, 1)

    def other_both(x):
        devices = [(r, c) for r in range(n_row) for c in range(n_col)]
        return lax.ppermute(x, ("row", "col"), [(r * n_col + c, (r ^ 1) * n_col + 1 - c) for r, c in devices])

    def along_z(blocks):
        return [to_partner(block, X * k) for k, block in enumerate(blocks) if k > 0]

    def call(kernel, name, out_shape, *args, scratch=(), cost=0):
        return pl.pallas_call(
            kernel,
            out_shape=out_shape,
            in_specs=[VMEM] * len(args),
            out_specs=jax.tree.map(lambda _: VMEM, out_shape),
            scratch_shapes=scratch,
            compiler_params=params(),
            cost_estimate=pl.CostEstimate(flops=cost * MICRO, bytes_accessed=0, transcendentals=0),
            name=name,
        )(*args)

    bind = functools.partial

    in_hbm = [pltpu.with_memory_space_constraint(x, pltpu.HBM) for x in (
        tiles.reshape(slots, side, side), tile_row.reshape(slots), tile_col.reshape(slots), src)]
    send, keep, dense = pl.pallas_call(
        bind(first_kernel, dims),
        out_shape=(f32((half, width)), f32((half, width)), bf16((2 * n_rows, n_cols))),
        in_specs=[HBM] * 5,
        out_specs=[VMEM] * 3,
        scratch_shapes=[
            pltpu.VMEM((slots, side, side), jnp.bfloat16),
            pltpu.SMEM((slots,), jnp.int32),
            pltpu.SMEM((slots,), jnp.int32),
            pltpu.SMEM((1,), jnp.int32),
            pltpu.VMEM((1, width), jnp.int32),
            pltpu.VMEM((n_rows + side, n_cols), jnp.float32),
        ] + product_scratch + [
            pltpu.SemaphoreType.DMA((slots // CHUNK,)),
            pltpu.SemaphoreType.DMA((4,)),
        ],
        compiler_params=params(),
        name="first_terms",
    )(*in_hbm[:3], tile_count.reshape(1), in_hbm[3])

    n_z = n_row // X
    for step in range(ITERS - 1):
        came = other_core(send)
        own, hold, away = call(
            bind(spread_kernel, dims), "spread",
            (bf16((VB, width)), f32((quarter, width)), f32((quarter, width))),
            src, keep, came, cost=1)
        away = other_side(away)
        blocks = [own] + along_z([own] * n_z)
        plane = call(plane_kernel, "plane_sum", f32((quarter, width)), hold, away, cost=20)
        planes = [plane] + along_z([plane] * n_z)
        across = other_side(call(join_kernel, "join_rows", bf16((n_z, VB, width)), *blocks, cost=2))
        mine = call(bind(hub_kernel, dims), "hub_sums", bf16((quarter, width)), src, *planes,
                    scratch=[pltpu.VMEM((n_z, quarter, width), jnp.float32)], cost=2)
        quarters = [mine, other_side(mine), other_core(mine), other_both(mine)]
        send, keep = call(
            bind(second_kernel, dims), "later_terms", (f32((half, width)), f32((half, width))),
            *blocks, across, *quarters, dense, scratch=product_scratch)
    came = other_core(send)
    parts = call(pieces_kernel, "hub_pieces", f32((n_row, piece, width)), keep, came)
    parts = lax.all_to_all(parts, "row", 0, 0)
    scores = call(bind(last_scores_kernel, dims), "last_scores", f32((VB, width)), src, keep, came)
    hubs = call(bind(last_hubs_kernel, dims), "last_hubs", f32((piece, width)), src, parts)
    return scores.reshape(1, 1, VB, width), hubs


def plain_body(tiles, tile_row, tile_col, tile_count, sources):
    slots = tiles.shape[2]
    side = tiles.shape[3]
    width = sources.shape[0]
    tiles = tiles.reshape(slots, side, side)
    rows = tile_row.reshape(slots)
    cols = tile_col.reshape(slots)
    count = tile_count.reshape(())
    n_row = lax.axis_size("row")
    n_col = lax.axis_size("col")
    devices = n_row * n_col
    r_index = lax.axis_index("row")
    c_index = lax.axis_index("col")
    hub_dev = H // devices
    block_rows = n_col * VB
    n_tile_rows = (block_rows + H) // side
    own_base = H + (r_index * n_col + c_index) * VB
    hub_start = (r_index * n_col + c_index) * hub_dev
    own_ids = jnp.arange(VB, dtype=jnp.int32) + own_base
    tele_own = (own_ids[:, None] == sources[None, :]).astype(jnp.float32)
    piece_ids = jnp.arange(hub_dev, dtype=jnp.int32) + hub_start
    tele_piece = (piece_ids[:, None] == sources[None, :]).astype(jnp.float32)
    tele_hubs = (jnp.arange(H, dtype=jnp.int32)[:, None] == sources[None, :]).astype(jnp.float32)
    column_ids = (
        H
        + (jnp.arange(n_row, dtype=jnp.int32)[:, None] * n_col + c_index) * VB
        + jnp.arange(VB, dtype=jnp.int32)[None, :]
    ).reshape(n_row * VB)
    column_panel = (column_ids[:, None] == sources[None, :]).astype(jnp.bfloat16)
    hub_panel = tele_hubs.astype(jnp.bfloat16)
    block = CHUNK
    own_scores = tele_own
    hub_piece = tele_piece
    for step in range(ITERS):
        start_acc = jnp.zeros((n_tile_rows, side, width), jnp.float32)
        if step > 0:
            column_panel = lax.all_gather(
                own_scores.astype(jnp.bfloat16), "row", axis=0, tiled=True
            )
        panel = jnp.concatenate([column_panel, hub_panel], axis=0).reshape(-1, side, width)

        def step_fn(number, total):
            start = number * block
            tile_block = lax.dynamic_slice_in_dim(tiles, start, block, 0)
            col_block = lax.dynamic_slice_in_dim(cols, start, block, 0)
            row_block = lax.dynamic_slice_in_dim(rows, start, block, 0)
            pieces = jnp.take(panel, col_block, axis=0)
            prod = jnp.einsum(
                "tij,tjs->tis", tile_block, pieces, preferred_element_type=jnp.float32
            )
            live = start + jnp.arange(block, dtype=jnp.int32) < count
            prod = jnp.where(live[:, None, None], prod, 0.0)
            return total.at[row_block].add(prod)

        total = lax.fori_loop(0, slots // block, step_fn, start_acc)
        partial_value = total.reshape(n_tile_rows * side, width)
        summed_rows = lax.psum_scatter(
            partial_value[:block_rows], "col", scatter_dimension=0, tiled=True
        )
        own_scores = 0.85 * summed_rows + 0.15 * tele_own
        hub_part = partial_value[block_rows:]
        summed = lax.psum_scatter(hub_part, ("row", "col"), scatter_dimension=0, tiled=True)
        hub_piece = 0.85 * summed + 0.15 * tele_piece
        if step + 1 < ITERS:
            hub_panel = lax.all_gather(
                hub_piece.astype(jnp.bfloat16), ("row", "col"), axis=0, tiled=True
            )
    return (own_scores.reshape(1, 1, VB, width), hub_piece)


def solution(mesh):
    placed = (
        P(("groups", "row"), "col", None, None, None),
        P(("groups", "row"), "col", None),
        P(("groups", "row"), "col", None),
        P(("groups", "row"), "col"),
        P("groups"),
    )

    def body(tiles, *rest):
        n_row, n_col = mesh.shape["row"], mesh.shape["col"]
        slots, side = tiles.shape[2:4]
        blocks = (n_col * VB + H) * (n_row * VB + H) // (side * side)
        if n_col == 2 and n_row in (4, 8, 16) and blocks <= slots and H // (n_row * n_col) % 16 == 0:
            return fast_body(tiles, *rest)
        return plain_body(tiles, *rest)

    return jax.shard_map(
        body,
        mesh=mesh,
        in_specs=placed,
        out_specs=(P(("groups", "row"), "col", None, None), P(("groups", "row", "col"), None)),
        check_vma=False,
    )
```

```python
import functools

import jax
import jax.numpy as jnp
from jax import lax
from jax.experimental import pallas as pl
from jax.experimental.pallas import tpu as pltpu
from jax.sharding import PartitionSpec as P

VB = 128
H = 256
ITERS = 2
DAMP = 0.85
CHUNK = 16
X = 2
NEAR = 2
MICRO = 10 ** 9
VMEM_LIMIT = 32 * 1024 * 1024

SMEM = pl.BlockSpec(memory_space=pltpu.SMEM)
VMEM = pl.BlockSpec(memory_space=pltpu.VMEM)
HBM = pl.BlockSpec(memory_space=pltpu.HBM)


def params():
    return pltpu.CompilerParams(vmem_limit_bytes=VMEM_LIMIT)


def one_hot(first, count, src):
    ids = lax.broadcasted_iota(jnp.int32, (count, src.shape[1]), 0) + first
    return (ids == src).astype(jnp.float32)


def write_terms(dims, block, prod_ref, dense_ref, panel_ref, send_ref, keep_ref):
    n_row, n_col, side = dims
    rows = dense_ref.shape[0] // 2
    c = lax.axis_index("col")
    prod = jnp.dot(dense_ref[...], panel_ref[...], preferred_element_type=jnp.float32)
    prod_ref[...] = prod[:rows] + prod[rows:]
    for ref, col in ((keep_ref, c), (send_ref, 1 - c)):
        ref[:VB] = prod_ref[pl.ds(pl.multiple_of(col * VB, VB), VB), :]
        for k in range(H // n_col // block):
            start = n_col * VB + (k * n_col + col) * block
            ref[VB + k * block:VB + (k + 1) * block] = prod_ref[pl.ds(pl.multiple_of(start, block), block), :]


def first_kernel(dims, tiles_ref, rows_hbm, cols_hbm, count_hbm, src_hbm, send_ref, keep_ref, dense_ref,
                 held, rows_ref, cols_ref, count_ref, src_ref, total, panel, prod, sems, small):
    n_row, n_col, side = dims
    n_rows = dense_ref.shape[0] // 2
    pairs = ((src_hbm, src_ref), (rows_hbm, rows_ref), (cols_hbm, cols_ref), (count_hbm, count_ref))
    scalars = [pltpu.make_async_copy(a, b, small.at[i]) for i, (a, b) in enumerate(pairs)]
    copies = []
    for i in range(held.shape[0] // CHUNK):
        part = pl.ds(i * CHUNK, CHUNK)
        copies.append(pltpu.make_async_copy(tiles_ref.at[part], held.at[part], sems.at[i]))
    for copy in scalars + copies:
        copy.start()
    total[...] = jnp.zeros_like(total)
    for copy in scalars:
        copy.wait()
    src = src_ref[...]
    for r in range(n_row):
        first = H + (r * n_col + lax.axis_index("col")) * VB
        panel[pl.ds(r * VB, VB), :] = one_hot(first, VB, src).astype(jnp.bfloat16)
    panel[pl.ds(n_row * VB, H), :] = one_hot(0, H, src).astype(jnp.bfloat16)
    count = count_ref[0]

    def add_tile(k, carry):
        live = k < count
        row = pl.multiple_of(jnp.where(live, rows_ref[k] * side, n_rows), side)
        col = pl.multiple_of(jnp.where(live, cols_ref[k] * side, 0), side)
        spot = (pl.ds(row, side), pl.ds(col, side))
        total[spot] += held[k].astype(jnp.float32)
        return carry

    for i, copy in enumerate(copies):
        copy.wait()
        lax.fori_loop(i * CHUNK, (i + 1) * CHUNK, add_tile, 0, unroll=4)
    for r in range(0, n_rows, side):
        whole = total[pl.ds(r, side), :]
        high = whole.astype(jnp.bfloat16)
        dense_ref[pl.ds(r, side), :] = high
        dense_ref[pl.ds(n_rows + r, side), :] = (whole - high.astype(jnp.float32)).astype(jnp.bfloat16)
    write_terms(dims, H // n_col, prod, dense_ref, panel, send_ref, keep_ref)


def second_kernel(dims, *refs):
    n_row, n_col, side = dims
    n_z = n_row // X
    blocks, across, quarters = refs[:n_z], refs[n_z:n_z + 2], refs[n_z + 2:n_z + 2 + X * n_col]
    dense_ref, send_ref, keep_ref, panel, prod = refs[n_z + 2 + X * n_col:]
    across = [across[0][k] for k in range(NEAR)] + [across[1][k] for k in range(n_z - NEAR)]
    half = H // n_col
    r, c = lax.axis_index("row"), lax.axis_index("col")

    def put(owner, block):
        panel[pl.ds(pl.multiple_of(owner * VB, VB), VB), :] = block

    for k in range(n_z):
        put(r ^ (X * k), blocks[k][...])
        put(r ^ (X * k) ^ 1, across[k])
    quarter = quarters[0].shape[0]
    for k, ref in enumerate(quarters):
        place = n_row * VB + ((c ^ (k // X)) * X + (r % X ^ (k % X))) * quarter
        panel[pl.ds(pl.multiple_of(place, quarter), quarter), :] = ref[...]
    write_terms(dims, half // n_row, prod, dense_ref, panel, send_ref, keep_ref)


def own_scores(dims, src_ref, keep_ref, came_ref):
    first = H + (lax.axis_index("row") * dims[1] + lax.axis_index("col")) * VB
    tele = one_hot(first, VB, src_ref[...])
    return DAMP * (keep_ref[:VB] + came_ref[:VB]) + 0.15 * tele


def spread_kernel(dims, src_ref, keep_ref, came_ref, scores_ref, hold_ref, pass_ref):
    quarter = hold_ref.shape[0]
    x = lax.axis_index("row") % X
    for ref, place in ((hold_ref, x), (pass_ref, 1 - x)):
        spot = pl.ds(pl.multiple_of(VB + place * quarter, quarter), quarter)
        ref[...] = keep_ref[spot, :] + came_ref[spot, :]
    scores_ref[...] = own_scores(dims, src_ref, keep_ref, came_ref).astype(scores_ref.dtype)


def join_kernel(*refs):
    for k, ref in enumerate(refs[:-1]):
        refs[-1][k] = ref[...]


def plane_kernel(hold_ref, came_ref, out_ref):
    out_ref[...] = hold_ref[...] + came_ref[...]


def sum_planes(planes, held):
    z = lax.axis_index("row") // X
    for k, plane in enumerate(planes):
        held[z ^ k] = plane[...]
    summed = held[0]
    for k in range(1, len(planes)):
        summed = summed + held[k]
    return summed


def hub_kernel(dims, src_ref, *refs):
    out_ref, held = refs[-2:]
    planes = refs[:held.shape[0]]
    quarter = out_ref.shape[0]
    first = (lax.axis_index("col") * X + lax.axis_index("row") % X) * quarter
    tele = one_hot(first, quarter, src_ref[...])
    out_ref[...] = (DAMP * sum_planes(planes, held) + 0.15 * tele).astype(out_ref.dtype)


def pieces_kernel(keep_ref, came_ref, parts_ref):
    piece = parts_ref.shape[1]
    for k in range(parts_ref.shape[0]):
        spot = slice(VB + k * piece, VB + (k + 1) * piece)
        parts_ref[k] = keep_ref[spot, :] + came_ref[spot, :]


def last_scores_kernel(dims, src_ref, keep_ref, came_ref, scores_ref):
    scores_ref[...] = own_scores(dims, src_ref, keep_ref, came_ref)


def last_hubs_kernel(dims, src_ref, parts_ref, out_ref):
    piece = out_ref.shape[0]
    summed = parts_ref[0]
    for k in range(1, parts_ref.shape[0]):
        summed = summed + parts_ref[k]
    first = (lax.axis_index("row") * dims[1] + lax.axis_index("col")) * piece
    out_ref[...] = DAMP * summed + 0.15 * one_hot(first, piece, src_ref[...])


def fast_body(tiles, tile_row, tile_col, tile_count, sources):
    slots, side = tiles.shape[2:4]
    width = sources.shape[0]
    n_row = lax.axis_size("row")
    n_col = lax.axis_size("col")
    piece = H // (n_row * n_col)
    dims = (n_row, n_col, side)
    n_rows = n_col * VB + H
    n_cols = n_row * VB + H
    f32 = functools.partial(jax.ShapeDtypeStruct, dtype=jnp.float32)
    bf16 = functools.partial(jax.ShapeDtypeStruct, dtype=jnp.bfloat16)
    src = sources.reshape(1, width)
    half = VB + n_row * piece
    quarter = H // n_col // X
    product_scratch = [
        pltpu.VMEM((n_cols, width), jnp.bfloat16),
        pltpu.VMEM((n_rows, width), jnp.float32),
    ]

    def other_core(x):
        return lax.ppermute(x, "col", [(0, 1), (1, 0)])

    def to_partner(x, flip):
        return lax.ppermute(x, "row", [(r, r ^ flip) for r in range(n_row)])

    def other_side(x):
        return to_partner(x, 1)

    def other_both(x):
        devices = [(r, c) for r in range(n_row) for c in range(n_col)]
        return lax.ppermute(x, ("row", "col"), [(r * n_col + c, (r ^ 1) * n_col + 1 - c) for r, c in devices])

    def along_z(blocks):
        return [to_partner(block, X * k) for k, block in enumerate(blocks) if k > 0]

    def call(kernel, name, out_shape, *args, scratch=(), cost=0):
        return pl.pallas_call(
            kernel,
            out_shape=out_shape,
            in_specs=[VMEM] * len(args),
            out_specs=jax.tree.map(lambda _: VMEM, out_shape),
            scratch_shapes=scratch,
            compiler_params=params(),
            cost_estimate=pl.CostEstimate(flops=cost * MICRO, bytes_accessed=0, transcendentals=0),
            name=name,
        )(*args)

    bind = functools.partial

    in_hbm = [pltpu.with_memory_space_constraint(x, pltpu.HBM) for x in (
        tiles.reshape(slots, side, side), tile_row.reshape(slots), tile_col.reshape(slots), src)]
    send, keep, dense = pl.pallas_call(
        bind(first_kernel, dims),
        out_shape=(f32((half, width)), f32((half, width)), bf16((2 * n_rows, n_cols))),
        in_specs=[HBM] * 5,
        out_specs=[VMEM] * 3,
        scratch_shapes=[
            pltpu.VMEM((slots, side, side), jnp.bfloat16),
            pltpu.SMEM((slots,), jnp.int32),
            pltpu.SMEM((slots,), jnp.int32),
            pltpu.SMEM((1,), jnp.int32),
            pltpu.VMEM((1, width), jnp.int32),
            pltpu.VMEM((n_rows + side, n_cols), jnp.float32),
        ] + product_scratch + [
            pltpu.SemaphoreType.DMA((slots // CHUNK,)),
            pltpu.SemaphoreType.DMA((4,)),
        ],
        compiler_params=params(),
        name="first_terms",
    )(*in_hbm[:3], tile_count.reshape(1), in_hbm[3])

    n_z = n_row // X
    for step in range(ITERS - 1):
        came = other_core(send)
        own, hold, away = call(
            bind(spread_kernel, dims), "spread",
            (bf16((VB, width)), f32((quarter, width)), f32((quarter, width))),
            src, keep, came, cost=8)
        away = other_side(away)
        blocks = [own] + along_z([own] * n_z)
        plane = call(plane_kernel, "plane_sum", f32((quarter, width)), hold, away, cost=8)
        planes = [plane] + along_z([plane] * n_z)
        near = other_side(call(join_kernel, "join_near", bf16((NEAR, VB, width)), *blocks[:NEAR], cost=0))
        far = other_side(call(join_kernel, "join_far", bf16((n_z - NEAR, VB, width)), *blocks[NEAR:], cost=3))
        mine = call(bind(hub_kernel, dims), "hub_sums", bf16((quarter, width)), src, *planes, near,
                    scratch=[pltpu.VMEM((n_z, quarter, width), jnp.float32)], cost=20)
        quarters = [mine, other_side(mine), other_core(mine), other_both(mine)]
        send, keep = call(
            bind(second_kernel, dims), "later_terms", (f32((half, width)), f32((half, width))),
            *blocks, near, far, *quarters, dense, scratch=product_scratch)
    came = other_core(send)
    parts = call(pieces_kernel, "hub_pieces", f32((n_row, piece, width)), keep, came)
    parts = lax.all_to_all(parts, "row", 0, 0)
    scores = call(bind(last_scores_kernel, dims), "last_scores", f32((VB, width)), src, keep, came)
    hubs = call(bind(last_hubs_kernel, dims), "last_hubs", f32((piece, width)), src, parts)
    return scores.reshape(1, 1, VB, width), hubs


def plain_body(tiles, tile_row, tile_col, tile_count, sources):
    slots = tiles.shape[2]
    side = tiles.shape[3]
    width = sources.shape[0]
    tiles = tiles.reshape(slots, side, side)
    rows = tile_row.reshape(slots)
    cols = tile_col.reshape(slots)
    count = tile_count.reshape(())
    n_row = lax.axis_size("row")
    n_col = lax.axis_size("col")
    devices = n_row * n_col
    r_index = lax.axis_index("row")
    c_index = lax.axis_index("col")
    hub_dev = H // devices
    block_rows = n_col * VB
    n_tile_rows = (block_rows + H) // side
    own_base = H + (r_index * n_col + c_index) * VB
    hub_start = (r_index * n_col + c_index) * hub_dev
    own_ids = jnp.arange(VB, dtype=jnp.int32) + own_base
    tele_own = (own_ids[:, None] == sources[None, :]).astype(jnp.float32)
    piece_ids = jnp.arange(hub_dev, dtype=jnp.int32) + hub_start
    tele_piece = (piece_ids[:, None] == sources[None, :]).astype(jnp.float32)
    tele_hubs = (jnp.arange(H, dtype=jnp.int32)[:, None] == sources[None, :]).astype(jnp.float32)
    column_ids = (
        H
        + (jnp.arange(n_row, dtype=jnp.int32)[:, None] * n_col + c_index) * VB
        + jnp.arange(VB, dtype=jnp.int32)[None, :]
    ).reshape(n_row * VB)
    column_panel = (column_ids[:, None] == sources[None, :]).astype(jnp.bfloat16)
    hub_panel = tele_hubs.astype(jnp.bfloat16)
    block = CHUNK
    own_scores = tele_own
    hub_piece = tele_piece
    for step in range(ITERS):
        start_acc = jnp.zeros((n_tile_rows, side, width), jnp.float32)
        if step > 0:
            column_panel = lax.all_gather(
                own_scores.astype(jnp.bfloat16), "row", axis=0, tiled=True
            )
        panel = jnp.concatenate([column_panel, hub_panel], axis=0).reshape(-1, side, width)

        def step_fn(number, total):
            start = number * block
            tile_block = lax.dynamic_slice_in_dim(tiles, start, block, 0)
            col_block = lax.dynamic_slice_in_dim(cols, start, block, 0)
            row_block = lax.dynamic_slice_in_dim(rows, start, block, 0)
            pieces = jnp.take(panel, col_block, axis=0)
            prod = jnp.einsum(
                "tij,tjs->tis", tile_block, pieces, preferred_element_type=jnp.float32
            )
            live = start + jnp.arange(block, dtype=jnp.int32) < count
            prod = jnp.where(live[:, None, None], prod, 0.0)
            return total.at[row_block].add(prod)

        total = lax.fori_loop(0, slots // block, step_fn, start_acc)
        partial_value = total.reshape(n_tile_rows * side, width)
        summed_rows = lax.psum_scatter(
            partial_value[:block_rows], "col", scatter_dimension=0, tiled=True
        )
        own_scores = 0.85 * summed_rows + 0.15 * tele_own
        hub_part = partial_value[block_rows:]
        summed = lax.psum_scatter(hub_part, ("row", "col"), scatter_dimension=0, tiled=True)
        hub_piece = 0.85 * summed + 0.15 * tele_piece
        if step + 1 < ITERS:
            hub_panel = lax.all_gather(
                hub_piece.astype(jnp.bfloat16), ("row", "col"), axis=0, tiled=True
            )
    return (own_scores.reshape(1, 1, VB, width), hub_piece)


def solution(mesh):
    placed = (
        P(("groups", "row"), "col", None, None, None),
        P(("groups", "row"), "col", None),
        P(("groups", "row"), "col", None),
        P(("groups", "row"), "col"),
        P("groups"),
    )

    def body(tiles, *rest):
        n_row, n_col = mesh.shape["row"], mesh.shape["col"]
        slots, side = tiles.shape[2:4]
        blocks = (n_col * VB + H) * (n_row * VB + H) // (side * side)
        if n_col == 2 and n_row in (4, 8, 16) and blocks <= slots and H // (n_row * n_col) % 16 == 0:
            return fast_body(tiles, *rest)
        return plain_body(tiles, *rest)

    return jax.shard_map(
        body,
        mesh=mesh,
        in_specs=placed,
        out_specs=(P(("groups", "row"), "col", None, None), P(("groups", "row", "col"), None)),
        check_vma=False,
    )
```

```python
import functools

import jax
import jax.numpy as jnp
from jax import lax
from jax.experimental import pallas as pl
from jax.experimental.pallas import tpu as pltpu
from jax.sharding import PartitionSpec as P

VB = 128
H = 256
ITERS = 2
DAMP = 0.85
CHUNK = 16
X = 2
MICRO = 10 ** 9
VMEM_LIMIT = 32 * 1024 * 1024

SMEM = pl.BlockSpec(memory_space=pltpu.SMEM)
VMEM = pl.BlockSpec(memory_space=pltpu.VMEM)
HBM = pl.BlockSpec(memory_space=pltpu.HBM)


def params():
    return pltpu.CompilerParams(vmem_limit_bytes=VMEM_LIMIT)


def one_hot(first, count, src):
    ids = lax.broadcasted_iota(jnp.int32, (count, src.shape[1]), 0) + first
    return (ids == src).astype(jnp.float32)


def write_terms(dims, block, prod_ref, dense_ref, panel_ref, send_ref, keep_ref):
    n_row, n_col, side = dims
    rows = dense_ref.shape[0] // 2
    c = lax.axis_index("col")
    prod = jnp.dot(dense_ref[...], panel_ref[...], preferred_element_type=jnp.float32)
    prod_ref[...] = prod[:rows] + prod[rows:]
    for ref, col in ((keep_ref, c), (send_ref, 1 - c)):
        ref[:VB] = prod_ref[pl.ds(pl.multiple_of(col * VB, VB), VB), :]
        for k in range(H // n_col // block):
            start = n_col * VB + (k * n_col + col) * block
            ref[VB + k * block:VB + (k + 1) * block] = prod_ref[pl.ds(pl.multiple_of(start, block), block), :]


def first_kernel(dims, tiles_ref, rows_hbm, cols_hbm, count_hbm, src_hbm, send_ref, keep_ref, dense_ref,
                 held, rows_ref, cols_ref, count_ref, src_ref, total, panel, prod, sems, small):
    n_row, n_col, side = dims
    n_rows = dense_ref.shape[0] // 2
    pairs = ((src_hbm, src_ref), (rows_hbm, rows_ref), (cols_hbm, cols_ref), (count_hbm, count_ref))
    scalars = [pltpu.make_async_copy(a, b, small.at[i]) for i, (a, b) in enumerate(pairs)]
    copies = []
    for i in range(held.shape[0] // CHUNK):
        part = pl.ds(i * CHUNK, CHUNK)
        copies.append(pltpu.make_async_copy(tiles_ref.at[part], held.at[part], sems.at[i]))
    for copy in scalars + copies:
        copy.start()
    total[...] = jnp.zeros_like(total)
    for copy in scalars:
        copy.wait()
    src = src_ref[...]
    for r in range(n_row):
        first = H + (r * n_col + lax.axis_index("col")) * VB
        panel[pl.ds(r * VB, VB), :] = one_hot(first, VB, src).astype(jnp.bfloat16)
    panel[pl.ds(n_row * VB, H), :] = one_hot(0, H, src).astype(jnp.bfloat16)
    count = count_ref[0]

    def add_tile(k, carry):
        live = k < count
        row = pl.multiple_of(jnp.where(live, rows_ref[k] * side, n_rows), side)
        col = pl.multiple_of(jnp.where(live, cols_ref[k] * side, 0), side)
        spot = (pl.ds(row, side), pl.ds(col, side))
        total[spot] += held[k].astype(jnp.float32)
        return carry

    for i, copy in enumerate(copies):
        copy.wait()
        lax.fori_loop(i * CHUNK, (i + 1) * CHUNK, add_tile, 0, unroll=4)
    for r in range(0, n_rows, side):
        whole = total[pl.ds(r, side), :]
        high = whole.astype(jnp.bfloat16)
        dense_ref[pl.ds(r, side), :] = high
        dense_ref[pl.ds(n_rows + r, side), :] = (whole - high.astype(jnp.float32)).astype(jnp.bfloat16)
    write_terms(dims, H // n_col, prod, dense_ref, panel, send_ref, keep_ref)


def second_kernel(dims, flips, *refs):
    n_row, n_col, side = dims
    n_z = n_row // X
    blocks, quarters = refs[:4], refs[4:4 + X * n_col]
    dense_ref, send_ref, keep_ref, panel, prod = refs[4 + X * n_col:]
    half = H // n_col
    r, c = lax.axis_index("row"), lax.axis_index("col")
    near, far = flips[:n_z // 2], flips[n_z // 2:]
    for ref, group, x in ((blocks[0], near, 0), (blocks[1], far, 0), (blocks[2], near, 1), (blocks[3], far, 1)):
        for k, flip in enumerate(group):
            owner = r ^ (X * flip + x)
            panel[pl.ds(pl.multiple_of(owner * VB, VB), VB), :] = ref[k]
    quarter = quarters[0].shape[0]
    for k, ref in enumerate(quarters):
        place = n_row * VB + ((c ^ (k // X)) * X + (r % X ^ (k % X))) * quarter
        panel[pl.ds(pl.multiple_of(place, quarter), quarter), :] = ref[...]
    write_terms(dims, half // n_row, prod, dense_ref, panel, send_ref, keep_ref)


def own_scores(dims, src_ref, keep_ref, came_ref):
    first = H + (lax.axis_index("row") * dims[1] + lax.axis_index("col")) * VB
    tele = one_hot(first, VB, src_ref[...])
    return DAMP * (keep_ref[:VB] + came_ref[:VB]) + 0.15 * tele


def spread_kernel(dims, src_ref, keep_ref, came_ref, scores_ref, hold_ref, pass_ref):
    quarter = hold_ref.shape[0]
    x = lax.axis_index("row") % X
    for ref, place in ((hold_ref, x), (pass_ref, 1 - x)):
        spot = pl.ds(pl.multiple_of(VB + place * quarter, quarter), quarter)
        ref[...] = keep_ref[spot, :] + came_ref[spot, :]
    scores_ref[0] = own_scores(dims, src_ref, keep_ref, came_ref).astype(scores_ref.dtype)


def join_kernel(held_ref, came_ref, out_ref):
    count = held_ref.shape[0]
    out_ref[:count] = held_ref[...]
    out_ref[count:] = came_ref[...]


def add_kernel(hold_ref, came_ref, out_ref):
    out_ref[...] = hold_ref[...] + came_ref[...]


def hub_kernel(dims, src_ref, held_ref, came_ref, out_ref):
    quarter = out_ref.shape[0]
    first = (lax.axis_index("col") * X + lax.axis_index("row") % X) * quarter
    tele = one_hot(first, quarter, src_ref[...])
    out_ref[...] = (DAMP * (held_ref[...] + came_ref[...]) + 0.15 * tele).astype(out_ref.dtype)


def pieces_kernel(keep_ref, came_ref, parts_ref):
    piece = parts_ref.shape[1]
    for k in range(parts_ref.shape[0]):
        spot = slice(VB + k * piece, VB + (k + 1) * piece)
        parts_ref[k] = keep_ref[spot, :] + came_ref[spot, :]


def last_scores_kernel(dims, src_ref, keep_ref, came_ref, scores_ref):
    scores_ref[...] = own_scores(dims, src_ref, keep_ref, came_ref)


def last_hubs_kernel(dims, src_ref, parts_ref, out_ref):
    piece = out_ref.shape[0]
    summed = parts_ref[0]
    for k in range(1, parts_ref.shape[0]):
        summed = summed + parts_ref[k]
    first = (lax.axis_index("row") * dims[1] + lax.axis_index("col")) * piece
    out_ref[...] = DAMP * summed + 0.15 * one_hot(first, piece, src_ref[...])


def fast_body(tiles, tile_row, tile_col, tile_count, sources):
    slots, side = tiles.shape[2:4]
    width = sources.shape[0]
    n_row = lax.axis_size("row")
    n_col = lax.axis_size("col")
    piece = H // (n_row * n_col)
    dims = (n_row, n_col, side)
    n_rows = n_col * VB + H
    n_cols = n_row * VB + H
    f32 = functools.partial(jax.ShapeDtypeStruct, dtype=jnp.float32)
    bf16 = functools.partial(jax.ShapeDtypeStruct, dtype=jnp.bfloat16)
    src = sources.reshape(1, width)
    half = VB + n_row * piece
    quarter = H // n_col // X
    product_scratch = [
        pltpu.VMEM((n_cols, width), jnp.bfloat16),
        pltpu.VMEM((n_rows, width), jnp.float32),
    ]

    def other_core(x):
        return lax.ppermute(x, "col", [(0, 1), (1, 0)])

    def to_partner(x, flip):
        return lax.ppermute(x, "row", [(r, r ^ flip) for r in range(n_row)])

    def other_side(x):
        return to_partner(x, 1)

    def other_both(x):
        devices = [(r, c) for r in range(n_row) for c in range(n_col)]
        return lax.ppermute(x, ("row", "col"), [(r * n_col + c, (r ^ 1) * n_col + 1 - c) for r, c in devices])

    def call(kernel, name, out_shape, *args, scratch=(), cost=0):
        return pl.pallas_call(
            kernel,
            out_shape=out_shape,
            in_specs=[VMEM] * len(args),
            out_specs=jax.tree.map(lambda _: VMEM, out_shape),
            scratch_shapes=scratch,
            compiler_params=params(),
            cost_estimate=pl.CostEstimate(flops=cost * MICRO, bytes_accessed=0, transcendentals=0),
            name=name,
        )(*args)

    bind = functools.partial

    in_hbm = [pltpu.with_memory_space_constraint(x, pltpu.HBM) for x in (
        tiles.reshape(slots, side, side), tile_row.reshape(slots), tile_col.reshape(slots), src)]
    send, keep, dense = pl.pallas_call(
        bind(first_kernel, dims),
        out_shape=(f32((half, width)), f32((half, width)), bf16((2 * n_rows, n_cols))),
        in_specs=[HBM] * 5,
        out_specs=[VMEM] * 3,
        scratch_shapes=[
            pltpu.VMEM((slots, side, side), jnp.bfloat16),
            pltpu.SMEM((slots,), jnp.int32),
            pltpu.SMEM((slots,), jnp.int32),
            pltpu.SMEM((1,), jnp.int32),
            pltpu.VMEM((1, width), jnp.int32),
            pltpu.VMEM((n_rows + side, n_cols), jnp.float32),
        ] + product_scratch + [
            pltpu.SemaphoreType.DMA((slots // CHUNK,)),
            pltpu.SemaphoreType.DMA((4,)),
        ],
        compiler_params=params(),
        name="first_terms",
    )(*in_hbm[:3], tile_count.reshape(1), in_hbm[3])

    masks = [n_row // X - 1]
    while masks[-1] > 1:
        masks.append(masks[-1] // 2)
    for step in range(ITERS - 1):
        came = other_core(send)
        held, hold, away = call(
            bind(spread_kernel, dims), "spread",
            (bf16((1, VB, width)), f32((quarter, width)), f32((quarter, width))),
            src, keep, came, cost=2)
        away = other_side(away)
        flips = [0]
        for mask in masks[:-1]:
            far = to_partner(held, X * mask)
            held = call(join_kernel, "join_near", bf16((2 * len(flips), VB, width)), held, far, cost=3)
            flips += [flip ^ mask for flip in flips]
        far = to_partner(held, X * masks[-1])
        flips += [flip ^ masks[-1] for flip in flips]
        near_across, far_across = other_side(held), other_side(far)
        sums = call(add_kernel, "plane_sum", f32((quarter, width)), hold, away, cost=20)
        for mask in masks[:0:-1]:
            sums = call(add_kernel, "pair_sum", f32((quarter, width)), sums, to_partner(sums, X * mask), cost=1)
        mine = call(bind(hub_kernel, dims), "hub_sums", bf16((quarter, width)), src, sums, to_partner(sums, X * masks[0]), cost=1)
        quarters = [mine, other_side(mine), other_core(mine), other_both(mine)]
        send, keep = call(
            bind(second_kernel, dims, flips), "later_terms", (f32((half, width)), f32((half, width))),
            held, far, near_across, far_across, *quarters, dense, scratch=product_scratch)
    came = other_core(send)
    parts = call(pieces_kernel, "hub_pieces", f32((n_row, piece, width)), keep, came)
    parts = lax.all_to_all(parts, "row", 0, 0)
    scores = call(bind(last_scores_kernel, dims), "last_scores", f32((VB, width)), src, keep, came)
    hubs = call(bind(last_hubs_kernel, dims), "last_hubs", f32((piece, width)), src, parts)
    return scores.reshape(1, 1, VB, width), hubs


def plain_body(tiles, tile_row, tile_col, tile_count, sources):
    slots = tiles.shape[2]
    side = tiles.shape[3]
    width = sources.shape[0]
    tiles = tiles.reshape(slots, side, side)
    rows = tile_row.reshape(slots)
    cols = tile_col.reshape(slots)
    count = tile_count.reshape(())
    n_row = lax.axis_size("row")
    n_col = lax.axis_size("col")
    devices = n_row * n_col
    r_index = lax.axis_index("row")
    c_index = lax.axis_index("col")
    hub_dev = H // devices
    block_rows = n_col * VB
    n_tile_rows = (block_rows + H) // side
    own_base = H + (r_index * n_col + c_index) * VB
    hub_start = (r_index * n_col + c_index) * hub_dev
    own_ids = jnp.arange(VB, dtype=jnp.int32) + own_base
    tele_own = (own_ids[:, None] == sources[None, :]).astype(jnp.float32)
    piece_ids = jnp.arange(hub_dev, dtype=jnp.int32) + hub_start
    tele_piece = (piece_ids[:, None] == sources[None, :]).astype(jnp.float32)
    tele_hubs = (jnp.arange(H, dtype=jnp.int32)[:, None] == sources[None, :]).astype(jnp.float32)
    column_ids = (
        H
        + (jnp.arange(n_row, dtype=jnp.int32)[:, None] * n_col + c_index) * VB
        + jnp.arange(VB, dtype=jnp.int32)[None, :]
    ).reshape(n_row * VB)
    column_panel = (column_ids[:, None] == sources[None, :]).astype(jnp.bfloat16)
    hub_panel = tele_hubs.astype(jnp.bfloat16)
    block = CHUNK
    own_scores = tele_own
    hub_piece = tele_piece
    for step in range(ITERS):
        start_acc = jnp.zeros((n_tile_rows, side, width), jnp.float32)
        if step > 0:
            column_panel = lax.all_gather(
                own_scores.astype(jnp.bfloat16), "row", axis=0, tiled=True
            )
        panel = jnp.concatenate([column_panel, hub_panel], axis=0).reshape(-1, side, width)

        def step_fn(number, total):
            start = number * block
            tile_block = lax.dynamic_slice_in_dim(tiles, start, block, 0)
            col_block = lax.dynamic_slice_in_dim(cols, start, block, 0)
            row_block = lax.dynamic_slice_in_dim(rows, start, block, 0)
            pieces = jnp.take(panel, col_block, axis=0)
            prod = jnp.einsum(
                "tij,tjs->tis", tile_block, pieces, preferred_element_type=jnp.float32
            )
            live = start + jnp.arange(block, dtype=jnp.int32) < count
            prod = jnp.where(live[:, None, None], prod, 0.0)
            return total.at[row_block].add(prod)

        total = lax.fori_loop(0, slots // block, step_fn, start_acc)
        partial_value = total.reshape(n_tile_rows * side, width)
        summed_rows = lax.psum_scatter(
            partial_value[:block_rows], "col", scatter_dimension=0, tiled=True
        )
        own_scores = 0.85 * summed_rows + 0.15 * tele_own
        hub_part = partial_value[block_rows:]
        summed = lax.psum_scatter(hub_part, ("row", "col"), scatter_dimension=0, tiled=True)
        hub_piece = 0.85 * summed + 0.15 * tele_piece
        if step + 1 < ITERS:
            hub_panel = lax.all_gather(
                hub_piece.astype(jnp.bfloat16), ("row", "col"), axis=0, tiled=True
            )
    return (own_scores.reshape(1, 1, VB, width), hub_piece)


def solution(mesh):
    placed = (
        P(("groups", "row"), "col", None, None, None),
        P(("groups", "row"), "col", None),
        P(("groups", "row"), "col", None),
        P(("groups", "row"), "col"),
        P("groups"),
    )

    def body(tiles, *rest):
        n_row, n_col = mesh.shape["row"], mesh.shape["col"]
        slots, side = tiles.shape[2:4]
        blocks = (n_col * VB + H) * (n_row * VB + H) // (side * side)
        if n_col == 2 and n_row in (8, 16) and blocks <= slots and H // (n_row * n_col) % 16 == 0:
            return fast_body(tiles, *rest)
        return plain_body(tiles, *rest)

    return jax.shard_map(
        body,
        mesh=mesh,
        in_specs=placed,
        out_specs=(P(("groups", "row"), "col", None, None), P(("groups", "row", "col"), None)),
        check_vma=False,
    )
```

```python
import functools

import jax
import jax.numpy as jnp
from jax import lax
from jax.experimental import pallas as pl
from jax.experimental.pallas import tpu as pltpu
from jax.sharding import PartitionSpec as P

VB = 128
H = 256
ITERS = 2
DAMP = 0.85
CHUNK = 16
X = 2
MICRO = 10 ** 9
VMEM_LIMIT = 32 * 1024 * 1024

SMEM = pl.BlockSpec(memory_space=pltpu.SMEM)
VMEM = pl.BlockSpec(memory_space=pltpu.VMEM)
HBM = pl.BlockSpec(memory_space=pltpu.HBM)


def params():
    return pltpu.CompilerParams(vmem_limit_bytes=VMEM_LIMIT)


def one_hot(first, count, src):
    ids = lax.broadcasted_iota(jnp.int32, (count, src.shape[1]), 0) + first
    return (ids == src).astype(jnp.float32)


def first_kernel(dims, tiles_ref, rows_hbm, cols_hbm, count_hbm, src_hbm,
                 send_ref, keep_ref, dense_send_ref, dense_keep_ref,
                 held, rows_ref, cols_ref, count_ref, src_ref, total, panel, sems, small):
    n_row, n_col, side = dims
    n_rows = n_col * VB + H
    piece = H // (n_row * n_col)
    c = lax.axis_index("col")
    pairs = ((src_hbm, src_ref), (rows_hbm, rows_ref), (cols_hbm, cols_ref), (count_hbm, count_ref))
    scalars = [pltpu.make_async_copy(a, b, small.at[i]) for i, (a, b) in enumerate(pairs)]
    copies = []
    for i in range(held.shape[0] // CHUNK):
        part = pl.ds(i * CHUNK, CHUNK)
        copies.append(pltpu.make_async_copy(tiles_ref.at[part], held.at[part], sems.at[i]))
    for copy in scalars + copies:
        copy.start()
    total[...] = jnp.zeros_like(total)
    for copy in scalars:
        copy.wait()
    src = src_ref[...]
    for r in range(n_row):
        first = H + (r * n_col + c) * VB
        panel[pl.ds(r * VB, VB), :] = one_hot(first, VB, src).astype(jnp.bfloat16)
    panel[pl.ds(n_row * VB, H), :] = one_hot(0, H, src).astype(jnp.bfloat16)
    count = count_ref[0]

    def add_tile(k, carry):
        live = k < count
        row = pl.multiple_of(jnp.where(live, rows_ref[k] * side, n_rows), side)
        col = pl.multiple_of(jnp.where(live, cols_ref[k] * side, 0), side)
        spot = (pl.ds(row, side), pl.ds(col, side))
        total[spot] += held[k].astype(jnp.float32)
        return carry

    for i, copy in enumerate(copies):
        copy.wait()
        lax.fori_loop(i * CHUNK, (i + 1) * CHUNK, add_tile, 0, unroll=4)
    half = n_rows // n_col
    for dense, out, core in ((dense_send_ref, send_ref, 1 - c), (dense_keep_ref, keep_ref, c)):
        chunks = [(0, core * VB, VB)]
        for r in range(n_row):
            chunks.append((VB + r * piece, n_col * VB + (r * n_col + core) * piece, piece))
        for at, start, size in chunks:
            whole = total[pl.ds(pl.multiple_of(start, size), size), :]
            high = whole.astype(jnp.bfloat16)
            dense[at:at + size] = high
            dense[half + at:half + at + size] = (whole - high.astype(jnp.float32)).astype(jnp.bfloat16)
        prod = jnp.dot(dense[...], panel[...], preferred_element_type=jnp.float32)
        out[...] = prod[:half] + prod[half:]


def second_kernel(dims, flips, src_ref, *refs):
    n_row, n_col, side = dims
    n_z = n_row // X
    mine, theirs, quarters = refs[:X], refs[X:2 * X], refs[2 * X:2 * X + X * n_col]
    dense_mine, dense_theirs, scores_ref, parts_ref, panel = refs[2 * X + X * n_col:]
    piece = parts_ref.shape[1]
    r, c = lax.axis_index("row"), lax.axis_index("col")
    for at, refs_of in enumerate((mine, theirs)):
        for x, ref in enumerate(refs_of):
            for k, flip in enumerate(flips):
                owner = r ^ (X * flip + x)
                panel[at, pl.ds(pl.multiple_of(owner * VB, VB), VB), :] = ref[k]
        for k, ref in enumerate(quarters):
            for i in range(n_z):
                row = ((r % X ^ (k % X)) * n_z + i) * n_col + (c ^ (k // X))
                place = pl.ds(pl.multiple_of(n_row * VB + row * piece, piece), piece)
                panel[at, place, :] = ref[i * piece:(i + 1) * piece]
    prod = jnp.dot(dense_mine[...], panel[0], preferred_element_type=jnp.float32)
    prod += jnp.dot(dense_theirs[...], panel[1], preferred_element_type=jnp.float32)
    half = prod.shape[0] // 2
    total = prod[:half] + prod[half:]
    tele = one_hot(H + (r * n_col + c) * VB, VB, src_ref[...])
    scores_ref[...] = DAMP * total[:VB] + 0.15 * tele
    parts_ref[...] = total[VB:].reshape(parts_ref.shape)


def spread_kernel(dims, src_ref, keep_ref, came_ref, scores_ref, hold_ref, pass_ref):
    quarter = hold_ref.shape[0]
    r, c = lax.axis_index("row"), lax.axis_index("col")
    for ref, place in ((hold_ref, r % X), (pass_ref, 1 - r % X)):
        spot = pl.ds(pl.multiple_of(VB + place * quarter, quarter), quarter)
        ref[...] = keep_ref[spot, :] + came_ref[spot, :]
    tele = one_hot(H + (r * dims[1] + c) * VB, VB, src_ref[...])
    scores_ref[0] = (DAMP * (keep_ref[:VB] + came_ref[:VB]) + 0.15 * tele).astype(scores_ref.dtype)


def join_kernel(held_ref, came_ref, out_ref):
    count = held_ref.shape[0]
    out_ref[:count] = held_ref[...]
    out_ref[count:] = came_ref[...]


def add_kernel(hold_ref, came_ref, out_ref):
    out_ref[...] = hold_ref[...] + came_ref[...]


def hub_kernel(dims, src_ref, held_ref, came_ref, out_ref):
    n_row, n_col, side = dims
    piece = H // (n_row * n_col)
    r, c = lax.axis_index("row"), lax.axis_index("col")
    at = lax.broadcasted_iota(jnp.int32, out_ref.shape, 0)
    ids = ((r % X * (n_row // X) + at // piece) * n_col + c) * piece + at % piece
    tele = (ids == src_ref[...]).astype(jnp.float32)
    out_ref[...] = (DAMP * (held_ref[...] + came_ref[...]) + 0.15 * tele).astype(out_ref.dtype)


def last_hubs_kernel(dims, src_ref, parts_ref, out_ref):
    piece = out_ref.shape[0]
    summed = parts_ref[0]
    for k in range(1, parts_ref.shape[0]):
        summed = summed + parts_ref[k]
    first = (lax.axis_index("row") * dims[1] + lax.axis_index("col")) * piece
    out_ref[...] = DAMP * summed + 0.15 * one_hot(first, piece, src_ref[...])


def fast_body(tiles, tile_row, tile_col, tile_count, sources):
    slots, side = tiles.shape[2:4]
    width = sources.shape[0]
    n_row = lax.axis_size("row")
    n_col = lax.axis_size("col")
    piece = H // (n_row * n_col)
    dims = (n_row, n_col, side)
    n_rows = n_col * VB + H
    n_cols = n_row * VB + H
    f32 = functools.partial(jax.ShapeDtypeStruct, dtype=jnp.float32)
    bf16 = functools.partial(jax.ShapeDtypeStruct, dtype=jnp.bfloat16)
    src = sources.reshape(1, width)
    half = VB + n_row * piece
    quarter = H // n_col // X
    def other_core(x):
        return lax.ppermute(x, "col", [(0, 1), (1, 0)])

    def to_partner(x, flip):
        return lax.ppermute(x, "row", [(r, r ^ flip) for r in range(n_row)])

    def other_side(x):
        return to_partner(x, 1)

    def other_both(x):
        devices = [(r, c) for r in range(n_row) for c in range(n_col)]
        return lax.ppermute(x, ("row", "col"), [(r * n_col + c, (r ^ 1) * n_col + 1 - c) for r, c in devices])

    def call(kernel, name, out_shape, *args, scratch=(), after=(), cost=0):
        def body(*refs):
            kernel(*refs[:len(args)], *refs[len(args) + len(after):])

        return pl.pallas_call(
            body,
            out_shape=out_shape,
            in_specs=[VMEM] * len(args) + [pl.BlockSpec(memory_space=pl.ANY)] * len(after),
            out_specs=jax.tree.map(lambda _: VMEM, out_shape),
            scratch_shapes=scratch,
            compiler_params=params(),
            cost_estimate=pl.CostEstimate(flops=cost * MICRO, bytes_accessed=0, transcendentals=0),
            name=name,
        )(*args, *after)

    bind = functools.partial

    in_hbm = [pltpu.with_memory_space_constraint(x, pltpu.HBM) for x in (
        tiles.reshape(slots, side, side), tile_row.reshape(slots), tile_col.reshape(slots), src)]
    dense_shape = bf16((2 * half, n_cols))
    send, keep, dense_send, dense_keep = pl.pallas_call(
        bind(first_kernel, dims),
        out_shape=(f32((half, width)), f32((half, width)), dense_shape, dense_shape),
        in_specs=[HBM] * 5,
        out_specs=[VMEM] * 4,
        scratch_shapes=[
            pltpu.VMEM((slots, side, side), jnp.bfloat16),
            pltpu.SMEM((slots,), jnp.int32),
            pltpu.SMEM((slots,), jnp.int32),
            pltpu.SMEM((1,), jnp.int32),
            pltpu.VMEM((1, width), jnp.int32),
            pltpu.VMEM((n_rows + side, n_cols), jnp.float32),
            pltpu.VMEM((n_cols, width), jnp.bfloat16),
            pltpu.SemaphoreType.DMA((slots // CHUNK,)),
            pltpu.SemaphoreType.DMA((4,)),
        ],
        compiler_params=params(),
        name="first_terms",
    )(*in_hbm[:3], tile_count.reshape(1), in_hbm[3])

    masks = [n_row // X - 1]
    while masks[-1] > 1:
        masks.append(masks[-1] // 2)
    held, hold, away = call(
        bind(spread_kernel, dims), "spread",
        (bf16((1, VB, width)), f32((quarter, width)), f32((quarter, width))),
        src, keep, other_core(send), cost=2)
    away = other_side(away)
    flips = [0]
    for mask in masks[:-1]:
        far = to_partner(held, X * mask)
        held = call(join_kernel, "join_near", bf16((2 * len(flips), VB, width)), held, far, cost=3)
        flips += [flip ^ mask for flip in flips]
    far = to_partner(held, X * masks[-1])
    flips += [flip ^ masks[-1] for flip in flips]
    near_across, far_across = other_side(held), other_side(far)
    blocks = bf16((len(flips), VB, width))
    mine = [call(join_kernel, "join_line", blocks, held, far, cost=12)]
    theirs = [other_core(mine[0])]
    mine.append(call(join_kernel, "join_across", blocks, near_across, far_across, cost=12))
    theirs.append(other_core(mine[1]))
    dense_came = other_core(dense_send)
    sums = call(add_kernel, "plane_sum", f32((quarter, width)), hold, away, cost=2)
    for mask in masks[:0:-1]:
        sums = call(add_kernel, "pair_sum", f32((quarter, width)), sums, to_partner(sums, X * mask), cost=8)
    hub = call(bind(hub_kernel, dims), "hub_sums", bf16((quarter, width)), src, sums, to_partner(sums, X * masks[0]),
               after=[dense_came, theirs[0]], cost=5)
    quarters = [hub, other_side(hub), other_core(hub), other_both(hub)]
    scores, parts = call(
        bind(second_kernel, dims, flips), "later_terms", (f32((VB, width)), f32((n_row, piece, width))),
        src, *mine, *theirs, *quarters, dense_keep, dense_came,
        scratch=[pltpu.VMEM((2, n_cols, width), jnp.bfloat16)])
    parts = lax.all_to_all(parts, "row", 0, 0)
    hubs = call(bind(last_hubs_kernel, dims), "last_hubs", f32((piece, width)), src, parts)
    return scores.reshape(1, 1, VB, width), hubs


def plain_body(tiles, tile_row, tile_col, tile_count, sources):
    slots = tiles.shape[2]
    side = tiles.shape[3]
    width = sources.shape[0]
    tiles = tiles.reshape(slots, side, side)
    rows = tile_row.reshape(slots)
    cols = tile_col.reshape(slots)
    count = tile_count.reshape(())
    n_row = lax.axis_size("row")
    n_col = lax.axis_size("col")
    devices = n_row * n_col
    r_index = lax.axis_index("row")
    c_index = lax.axis_index("col")
    hub_dev = H // devices
    block_rows = n_col * VB
    n_tile_rows = (block_rows + H) // side
    own_base = H + (r_index * n_col + c_index) * VB
    hub_start = (r_index * n_col + c_index) * hub_dev
    own_ids = jnp.arange(VB, dtype=jnp.int32) + own_base
    tele_own = (own_ids[:, None] == sources[None, :]).astype(jnp.float32)
    piece_ids = jnp.arange(hub_dev, dtype=jnp.int32) + hub_start
    tele_piece = (piece_ids[:, None] == sources[None, :]).astype(jnp.float32)
    tele_hubs = (jnp.arange(H, dtype=jnp.int32)[:, None] == sources[None, :]).astype(jnp.float32)
    column_ids = (
        H
        + (jnp.arange(n_row, dtype=jnp.int32)[:, None] * n_col + c_index) * VB
        + jnp.arange(VB, dtype=jnp.int32)[None, :]
    ).reshape(n_row * VB)
    column_panel = (column_ids[:, None] == sources[None, :]).astype(jnp.bfloat16)
    hub_panel = tele_hubs.astype(jnp.bfloat16)
    block = CHUNK
    own_scores = tele_own
    hub_piece = tele_piece
    for step in range(ITERS):
        start_acc = jnp.zeros((n_tile_rows, side, width), jnp.float32)
        if step > 0:
            column_panel = lax.all_gather(
                own_scores.astype(jnp.bfloat16), "row", axis=0, tiled=True
            )
        panel = jnp.concatenate([column_panel, hub_panel], axis=0).reshape(-1, side, width)

        def step_fn(number, total):
            start = number * block
            tile_block = lax.dynamic_slice_in_dim(tiles, start, block, 0)
            col_block = lax.dynamic_slice_in_dim(cols, start, block, 0)
            row_block = lax.dynamic_slice_in_dim(rows, start, block, 0)
            pieces = jnp.take(panel, col_block, axis=0)
            prod = jnp.einsum(
                "tij,tjs->tis", tile_block, pieces, preferred_element_type=jnp.float32
            )
            live = start + jnp.arange(block, dtype=jnp.int32) < count
            prod = jnp.where(live[:, None, None], prod, 0.0)
            return total.at[row_block].add(prod)

        total = lax.fori_loop(0, slots // block, step_fn, start_acc)
        partial_value = total.reshape(n_tile_rows * side, width)
        summed_rows = lax.psum_scatter(
            partial_value[:block_rows], "col", scatter_dimension=0, tiled=True
        )
        own_scores = 0.85 * summed_rows + 0.15 * tele_own
        hub_part = partial_value[block_rows:]
        summed = lax.psum_scatter(hub_part, ("row", "col"), scatter_dimension=0, tiled=True)
        hub_piece = 0.85 * summed + 0.15 * tele_piece
        if step + 1 < ITERS:
            hub_panel = lax.all_gather(
                hub_piece.astype(jnp.bfloat16), ("row", "col"), axis=0, tiled=True
            )
    return (own_scores.reshape(1, 1, VB, width), hub_piece)


def solution(mesh):
    placed = (
        P(("groups", "row"), "col", None, None, None),
        P(("groups", "row"), "col", None),
        P(("groups", "row"), "col", None),
        P(("groups", "row"), "col"),
        P("groups"),
    )

    def body(tiles, *rest):
        n_row, n_col = mesh.shape["row"], mesh.shape["col"]
        slots, side = tiles.shape[2:4]
        blocks = (n_col * VB + H) * (n_row * VB + H) // (side * side)
        if ITERS == 2 and n_col == 2 and n_row in (8, 16) and blocks <= slots and H // (n_row * n_col) % 16 == 0:
            return fast_body(tiles, *rest)
        return plain_body(tiles, *rest)

    return jax.shard_map(
        body,
        mesh=mesh,
        in_specs=placed,
        out_specs=(P(("groups", "row"), "col", None, None), P(("groups", "row", "col"), None)),
        check_vma=False,
    )
```

```python
import functools

import jax
import jax.numpy as jnp
from jax import lax
from jax.experimental import pallas as pl
from jax.experimental.pallas import tpu as pltpu
from jax.sharding import PartitionSpec as P

VB = 128
H = 256
ITERS = 2
DAMP = 0.85
CHUNK = 16
X = 2
MICRO = 10 ** 9
VMEM_LIMIT = 32 * 1024 * 1024

SMEM = pl.BlockSpec(memory_space=pltpu.SMEM)
VMEM = pl.BlockSpec(memory_space=pltpu.VMEM)
HBM = pl.BlockSpec(memory_space=pltpu.HBM)


def params():
    return pltpu.CompilerParams(vmem_limit_bytes=VMEM_LIMIT)


def one_hot(first, count, src):
    ids = lax.broadcasted_iota(jnp.int32, (count, src.shape[1]), 0) + first
    return (ids == src).astype(jnp.float32)


def write_terms(dims, block, prod_ref, dense_ref, panel_ref, send_ref, keep_ref):
    n_row, n_col, side = dims
    rows = dense_ref.shape[0] // 2
    c = lax.axis_index("col")
    prod = jnp.dot(dense_ref[...], panel_ref[...], preferred_element_type=jnp.float32)
    prod_ref[...] = prod[:rows] + prod[rows:]
    for ref, col in ((keep_ref, c), (send_ref, 1 - c)):
        ref[:VB] = prod_ref[pl.ds(pl.multiple_of(col * VB, VB), VB), :]
        for k in range(H // n_col // block):
            start = n_col * VB + (k * n_col + col) * block
            ref[VB + k * block:VB + (k + 1) * block] = prod_ref[pl.ds(pl.multiple_of(start, block), block), :]


def first_kernel(dims, tiles_ref, rows_hbm, cols_hbm, count_hbm, src_hbm, send_ref, keep_ref, dense_ref,
                 held, rows_ref, cols_ref, count_ref, src_ref, total, panel, prod, sems, small):
    n_row, n_col, side = dims
    n_rows = dense_ref.shape[0] // 2
    pairs = ((src_hbm, src_ref), (rows_hbm, rows_ref), (cols_hbm, cols_ref), (count_hbm, count_ref))
    scalars = [pltpu.make_async_copy(a, b, small.at[i]) for i, (a, b) in enumerate(pairs)]
    copies = []
    for i in range(held.shape[0] // CHUNK):
        part = pl.ds(i * CHUNK, CHUNK)
        copies.append(pltpu.make_async_copy(tiles_ref.at[part], held.at[part], sems.at[i]))
    for copy in scalars + copies:
        copy.start()
    total[...] = jnp.zeros_like(total)
    for copy in scalars:
        copy.wait()
    src = src_ref[...]
    for r in range(n_row):
        first = H + (r * n_col + lax.axis_index("col")) * VB
        panel[pl.ds(r * VB, VB), :] = one_hot(first, VB, src).astype(jnp.bfloat16)
    panel[pl.ds(n_row * VB, H), :] = one_hot(0, H, src).astype(jnp.bfloat16)
    count = count_ref[0]

    def add_tile(k, carry):
        live = k < count
        row = pl.multiple_of(jnp.where(live, rows_ref[k] * side, n_rows), side)
        col = pl.multiple_of(jnp.where(live, cols_ref[k] * side, 0), side)
        spot = (pl.ds(row, side), pl.ds(col, side))
        total[spot] += held[k].astype(jnp.float32)
        return carry

    for i, copy in enumerate(copies):
        copy.wait()
        lax.fori_loop(i * CHUNK, (i + 1) * CHUNK, add_tile, 0, unroll=4)
    for r in range(0, n_rows, side):
        whole = total[pl.ds(r, side), :]
        high = whole.astype(jnp.bfloat16)
        dense_ref[pl.ds(r, side), :] = high
        dense_ref[pl.ds(n_rows + r, side), :] = (whole - high.astype(jnp.float32)).astype(jnp.bfloat16)
    write_terms(dims, H // n_col, prod, dense_ref, panel, send_ref, keep_ref)


def second_kernel(dims, flips, *refs):
    n_row, n_col, side = dims
    n_z = n_row // X
    blocks, quarters = refs[:4], refs[4:4 + X * n_col]
    dense_ref, send_ref, keep_ref, panel, prod = refs[4 + X * n_col:]
    half = H // n_col
    r, c = lax.axis_index("row"), lax.axis_index("col")
    near, far = flips[:n_z // 2], flips[n_z // 2:]
    for ref, group, x in ((blocks[0], near, 0), (blocks[1], far, 0), (blocks[2], near, 1), (blocks[3], far, 1)):
        for k, flip in enumerate(group):
            owner = r ^ (X * flip + x)
            panel[pl.ds(pl.multiple_of(owner * VB, VB), VB), :] = ref[k]
    quarter = quarters[0].shape[0]
    for k, ref in enumerate(quarters):
        place = n_row * VB + ((c ^ (k // X)) * X + (r % X ^ (k % X))) * quarter
        panel[pl.ds(pl.multiple_of(place, quarter), quarter), :] = ref[...]
    write_terms(dims, half // n_row, prod, dense_ref, panel, send_ref, keep_ref)


def own_scores(dims, src_ref, keep_ref, came_ref):
    first = H + (lax.axis_index("row") * dims[1] + lax.axis_index("col")) * VB
    tele = one_hot(first, VB, src_ref[...])
    return DAMP * (keep_ref[:VB] + came_ref[:VB]) + 0.15 * tele


def spread_kernel(dims, src_ref, keep_ref, came_ref, scores_ref, hold_ref, pass_ref):
    quarter = hold_ref.shape[0]
    x = lax.axis_index("row") % X
    for ref, place in ((hold_ref, x), (pass_ref, 1 - x)):
        spot = pl.ds(pl.multiple_of(VB + place * quarter, quarter), quarter)
        ref[...] = keep_ref[spot, :] + came_ref[spot, :]
    scores_ref[0] = own_scores(dims, src_ref, keep_ref, came_ref).astype(scores_ref.dtype)


def join_kernel(held_ref, came_ref, out_ref):
    count = held_ref.shape[0]
    out_ref[:count] = held_ref[...]
    out_ref[count:] = came_ref[...]


def add_kernel(hold_ref, came_ref, out_ref):
    out_ref[...] = hold_ref[...] + came_ref[...]


def hub_kernel(dims, src_ref, held_ref, came_ref, out_ref):
    quarter = out_ref.shape[0]
    first = (lax.axis_index("col") * X + lax.axis_index("row") % X) * quarter
    tele = one_hot(first, quarter, src_ref[...])
    out_ref[...] = (DAMP * (held_ref[...] + came_ref[...]) + 0.15 * tele).astype(out_ref.dtype)


def pieces_kernel(keep_ref, came_ref, parts_ref):
    piece = parts_ref.shape[1]
    for k in range(parts_ref.shape[0]):
        spot = slice(VB + k * piece, VB + (k + 1) * piece)
        parts_ref[k] = keep_ref[spot, :] + came_ref[spot, :]


def last_kernel(dims, src_ref, keep_ref, came_ref, parts_ref, scores_ref, hubs_ref):
    scores_ref[...] = own_scores(dims, src_ref, keep_ref, came_ref)
    piece = hubs_ref.shape[0]
    summed = parts_ref[0]
    for k in range(1, parts_ref.shape[0]):
        summed = summed + parts_ref[k]
    first = (lax.axis_index("row") * dims[1] + lax.axis_index("col")) * piece
    hubs_ref[...] = DAMP * summed + 0.15 * one_hot(first, piece, src_ref[...])


def fast_body(tiles, tile_row, tile_col, tile_count, sources):
    slots, side = tiles.shape[2:4]
    width = sources.shape[0]
    n_row = lax.axis_size("row")
    n_col = lax.axis_size("col")
    piece = H // (n_row * n_col)
    dims = (n_row, n_col, side)
    n_rows = n_col * VB + H
    n_cols = n_row * VB + H
    f32 = functools.partial(jax.ShapeDtypeStruct, dtype=jnp.float32)
    bf16 = functools.partial(jax.ShapeDtypeStruct, dtype=jnp.bfloat16)
    src = sources.reshape(1, width)
    half = VB + n_row * piece
    quarter = H // n_col // X
    product_scratch = [
        pltpu.VMEM((n_cols, width), jnp.bfloat16),
        pltpu.VMEM((n_rows, width), jnp.float32),
    ]

    def other_core(x):
        return lax.ppermute(x, "col", [(0, 1), (1, 0)])

    def to_partner(x, flip):
        return lax.ppermute(x, "row", [(r, r ^ flip) for r in range(n_row)])

    def other_side(x):
        return to_partner(x, 1)

    def other_both(x):
        devices = [(r, c) for r in range(n_row) for c in range(n_col)]
        return lax.ppermute(x, ("row", "col"), [(r * n_col + c, (r ^ 1) * n_col + 1 - c) for r, c in devices])

    def call(kernel, name, out_shape, *args, scratch=(), cost=0):
        return pl.pallas_call(
            kernel,
            out_shape=out_shape,
            in_specs=[VMEM] * len(args),
            out_specs=jax.tree.map(lambda _: VMEM, out_shape),
            scratch_shapes=scratch,
            compiler_params=params(),
            cost_estimate=pl.CostEstimate(flops=cost * MICRO, bytes_accessed=0, transcendentals=0),
            name=name,
        )(*args)

    bind = functools.partial

    in_hbm = [pltpu.with_memory_space_constraint(x, pltpu.HBM) for x in (
        tiles.reshape(slots, side, side), tile_row.reshape(slots), tile_col.reshape(slots), src)]
    send, keep, dense = pl.pallas_call(
        bind(first_kernel, dims),
        out_shape=(f32((half, width)), f32((half, width)), bf16((2 * n_rows, n_cols))),
        in_specs=[HBM] * 5,
        out_specs=[VMEM] * 3,
        scratch_shapes=[
            pltpu.VMEM((slots, side, side), jnp.bfloat16),
            pltpu.SMEM((slots,), jnp.int32),
            pltpu.SMEM((slots,), jnp.int32),
            pltpu.SMEM((1,), jnp.int32),
            pltpu.VMEM((1, width), jnp.int32),
            pltpu.VMEM((n_rows + side, n_cols), jnp.float32),
        ] + product_scratch + [
            pltpu.SemaphoreType.DMA((slots // CHUNK,)),
            pltpu.SemaphoreType.DMA((4,)),
        ],
        compiler_params=params(),
        name="first_terms",
    )(*in_hbm[:3], tile_count.reshape(1), in_hbm[3])

    masks = [n_row // X - 1]
    while masks[-1] > 1:
        masks.append(masks[-1] // 2)
    for step in range(ITERS - 1):
        came = other_core(send)
        held, hold, away = call(
            bind(spread_kernel, dims), "spread",
            (bf16((1, VB, width)), f32((quarter, width)), f32((quarter, width))),
            src, keep, came, cost=2)
        away = other_side(away)
        flips = [0]
        for mask in masks[:-1]:
            far = to_partner(held, X * mask)
            held = call(join_kernel, "join_near", bf16((2 * len(flips), VB, width)), held, far, cost=3)
            flips += [flip ^ mask for flip in flips]
        far = to_partner(held, X * masks[-1])
        flips += [flip ^ masks[-1] for flip in flips]
        near_across, far_across = other_side(held), other_side(far)
        sums = call(add_kernel, "plane_sum", f32((quarter, width)), hold, away, cost=20)
        for mask in masks[:0:-1]:
            sums = call(add_kernel, "pair_sum", f32((quarter, width)), sums, to_partner(sums, X * mask), cost=1)
        mine = call(bind(hub_kernel, dims), "hub_sums", bf16((quarter, width)), src, sums, to_partner(sums, X * masks[0]), cost=1)
        quarters = [mine, other_side(mine), other_core(mine), other_both(mine)]
        send, keep = call(
            bind(second_kernel, dims, flips), "later_terms", (f32((half, width)), f32((half, width))),
            held, far, near_across, far_across, *quarters, dense, scratch=product_scratch)
    came = other_core(send)
    parts = call(pieces_kernel, "hub_pieces", f32((n_row, piece, width)), keep, came)
    parts = lax.all_to_all(parts, "row", 0, 0)
    scores, hubs = call(bind(last_kernel, dims), "last_sums", (f32((VB, width)), f32((piece, width))),
                        src, keep, came, parts)
    return scores.reshape(1, 1, VB, width), hubs


def plain_body(tiles, tile_row, tile_col, tile_count, sources):
    slots = tiles.shape[2]
    side = tiles.shape[3]
    width = sources.shape[0]
    tiles = tiles.reshape(slots, side, side)
    rows = tile_row.reshape(slots)
    cols = tile_col.reshape(slots)
    count = tile_count.reshape(())
    n_row = lax.axis_size("row")
    n_col = lax.axis_size("col")
    devices = n_row * n_col
    r_index = lax.axis_index("row")
    c_index = lax.axis_index("col")
    hub_dev = H // devices
    block_rows = n_col * VB
    n_tile_rows = (block_rows + H) // side
    own_base = H + (r_index * n_col + c_index) * VB
    hub_start = (r_index * n_col + c_index) * hub_dev
    own_ids = jnp.arange(VB, dtype=jnp.int32) + own_base
    tele_own = (own_ids[:, None] == sources[None, :]).astype(jnp.float32)
    piece_ids = jnp.arange(hub_dev, dtype=jnp.int32) + hub_start
    tele_piece = (piece_ids[:, None] == sources[None, :]).astype(jnp.float32)
    tele_hubs = (jnp.arange(H, dtype=jnp.int32)[:, None] == sources[None, :]).astype(jnp.float32)
    column_ids = (
        H
        + (jnp.arange(n_row, dtype=jnp.int32)[:, None] * n_col + c_index) * VB
        + jnp.arange(VB, dtype=jnp.int32)[None, :]
    ).reshape(n_row * VB)
    column_panel = (column_ids[:, None] == sources[None, :]).astype(jnp.bfloat16)
    hub_panel = tele_hubs.astype(jnp.bfloat16)
    block = CHUNK
    own_scores = tele_own
    hub_piece = tele_piece
    for step in range(ITERS):
        start_acc = jnp.zeros((n_tile_rows, side, width), jnp.float32)
        if step > 0:
            column_panel = lax.all_gather(
                own_scores.astype(jnp.bfloat16), "row", axis=0, tiled=True
            )
        panel = jnp.concatenate([column_panel, hub_panel], axis=0).reshape(-1, side, width)

        def step_fn(number, total):
            start = number * block
            tile_block = lax.dynamic_slice_in_dim(tiles, start, block, 0)
            col_block = lax.dynamic_slice_in_dim(cols, start, block, 0)
            row_block = lax.dynamic_slice_in_dim(rows, start, block, 0)
            pieces = jnp.take(panel, col_block, axis=0)
            prod = jnp.einsum(
                "tij,tjs->tis", tile_block, pieces, preferred_element_type=jnp.float32
            )
            live = start + jnp.arange(block, dtype=jnp.int32) < count
            prod = jnp.where(live[:, None, None], prod, 0.0)
            return total.at[row_block].add(prod)

        total = lax.fori_loop(0, slots // block, step_fn, start_acc)
        partial_value = total.reshape(n_tile_rows * side, width)
        summed_rows = lax.psum_scatter(
            partial_value[:block_rows], "col", scatter_dimension=0, tiled=True
        )
        own_scores = 0.85 * summed_rows + 0.15 * tele_own
        hub_part = partial_value[block_rows:]
        summed = lax.psum_scatter(hub_part, ("row", "col"), scatter_dimension=0, tiled=True)
        hub_piece = 0.85 * summed + 0.15 * tele_piece
        if step + 1 < ITERS:
            hub_panel = lax.all_gather(
                hub_piece.astype(jnp.bfloat16), ("row", "col"), axis=0, tiled=True
            )
    return (own_scores.reshape(1, 1, VB, width), hub_piece)


def solution(mesh):
    placed = (
        P(("groups", "row"), "col", None, None, None),
        P(("groups", "row"), "col", None),
        P(("groups", "row"), "col", None),
        P(("groups", "row"), "col"),
        P("groups"),
    )

    def body(tiles, *rest):
        n_row, n_col = mesh.shape["row"], mesh.shape["col"]
        slots, side = tiles.shape[2:4]
        blocks = (n_col * VB + H) * (n_row * VB + H) // (side * side)
        if n_col == 2 and n_row in (8, 16) and blocks <= slots and H // (n_row * n_col) % 16 == 0:
            return fast_body(tiles, *rest)
        return plain_body(tiles, *rest)

    return jax.shard_map(
        body,
        mesh=mesh,
        in_specs=placed,
        out_specs=(P(("groups", "row"), "col", None, None), P(("groups", "row", "col"), None)),
        check_vma=False,
    )
```

```python
import functools
import math

import jax
import jax.numpy as jnp
from jax import lax
from jax.experimental import pallas as pl
from jax.experimental.pallas import tpu as pltpu
from jax.sharding import PartitionSpec as P

VB = 128
H = 256
ITERS = 2
DAMP = 0.85
CHUNK = 8
AHEAD = 4
X = 2
MICRO = 10 ** 9
VMEM_LIMIT = 32 * 1024 * 1024

SMEM = pl.BlockSpec(memory_space=pltpu.SMEM)
VMEM = pl.BlockSpec(memory_space=pltpu.VMEM)
HBM = pl.BlockSpec(memory_space=pltpu.HBM)


def params():
    return pltpu.CompilerParams(vmem_limit_bytes=VMEM_LIMIT)


def one_hot(first, count, src):
    ids = lax.broadcasted_iota(jnp.int32, (count, src.shape[1]), 0) + first
    return (ids == src).astype(jnp.float32)


def write_terms(dims, block, prod_ref, send_ref, keep_ref):
    n_row, n_col, side = dims
    c = lax.axis_index("col")
    for ref, col in ((keep_ref, c), (send_ref, 1 - c)):
        ref[:VB] = prod_ref[pl.ds(pl.multiple_of(col * VB, VB), VB), :]
        for k in range(H // n_col // block):
            start = n_col * VB + (k * n_col + col) * block
            ref[VB + k * block:VB + (k + 1) * block] = prod_ref[pl.ds(pl.multiple_of(start, block), block), :]


def product(dense, panel):
    prod = jnp.dot(dense, panel, preferred_element_type=jnp.float32)
    rows = prod.shape[0] // 2
    return prod[:rows] + prod[rows:]


def first_kernel(dims, tiles_ref, rows_hbm, cols_hbm, count_hbm, src_hbm, send_ref, keep_ref, dense_ref,
                 held, rows_ref, cols_ref, count_ref, src_ref, total, panel, prod, sems, small):
    n_row, n_col, side = dims
    n_rows = dense_ref.shape[0] // 2
    pairs = ((src_hbm, src_ref), (rows_hbm, rows_ref), (cols_hbm, cols_ref), (count_hbm, count_ref))
    scalars = [pltpu.make_async_copy(a, b, small.at[i]) for i, (a, b) in enumerate(pairs)]
    copies = []
    for i in range(held.shape[0] // CHUNK):
        part = pl.ds(i * CHUNK, CHUNK)
        copies.append(pltpu.make_async_copy(tiles_ref.at[part], held.at[part], sems.at[i]))
    for copy in scalars + copies[:AHEAD]:
        copy.start()
    total[...] = jnp.zeros_like(total)
    for copy in scalars:
        copy.wait()
    src = src_ref[...]
    for r in range(n_row):
        first = H + (r * n_col + lax.axis_index("col")) * VB
        panel[pl.ds(r * VB, VB), :] = one_hot(first, VB, src).astype(jnp.bfloat16)
    panel[pl.ds(n_row * VB, H), :] = one_hot(0, H, src).astype(jnp.bfloat16)
    count = count_ref[0]

    def add_tile(k, carry):
        live = k < count
        row = pl.multiple_of(jnp.where(live, rows_ref[k] * side, n_rows), side)
        col = pl.multiple_of(jnp.where(live, cols_ref[k] * side, 0), side)
        spot = (pl.ds(row, side), pl.ds(col, side))
        total[spot] += held[k].astype(jnp.float32)
        return carry

    for i, copy in enumerate(copies):
        copy.wait()
        if i + AHEAD < len(copies):
            copies[i + AHEAD].start()
        lax.fori_loop(i * CHUNK, (i + 1) * CHUNK, add_tile, 0, unroll=4)
    for r in range(0, n_rows, side):
        whole = total[pl.ds(r, side), :]
        high = whole.astype(jnp.bfloat16)
        dense_ref[pl.ds(r, side), :] = high
        dense_ref[pl.ds(n_rows + r, side), :] = (whole - high.astype(jnp.float32)).astype(jnp.bfloat16)
    prod[...] = product(dense_ref[...], panel[...])
    write_terms(dims, H // n_col, prod, send_ref, keep_ref)


def score_columns_kernel(dims, flips, *refs):
    n_row, n_col, side = dims
    n_z = n_row // X
    blocks, (dense_ref, prod_ref, panel) = refs[:4], refs[4:]
    r = lax.axis_index("row")
    near, far = flips[:n_z // 2], flips[n_z // 2:]
    for ref, group, x in ((blocks[0], near, 0), (blocks[1], far, 0), (blocks[2], near, 1), (blocks[3], far, 1)):
        for k, flip in enumerate(group):
            owner = r ^ (X * flip + x)
            panel[pl.ds(pl.multiple_of(owner * VB, VB), VB), :] = ref[k]
    prod_ref[...] = product(dense_ref[:, :n_row * VB], panel[...])


def hub_columns_kernel(dims, *refs):
    n_row, n_col, side = dims
    quarters, (dense_ref, prod_ref, send_ref, keep_ref, panel, total) = refs[:X * n_col], refs[X * n_col:]
    r, c = lax.axis_index("row"), lax.axis_index("col")
    quarter = quarters[0].shape[0]
    for k, ref in enumerate(quarters):
        place = ((c ^ (k // X)) * X + (r % X ^ (k % X))) * quarter
        panel[pl.ds(pl.multiple_of(place, quarter), quarter), :] = ref[...]
    total[...] = prod_ref[...] + product(dense_ref[:, n_row * VB:], panel[...])
    write_terms(dims, H // (n_row * n_col), total, send_ref, keep_ref)


def own_scores(dims, src_ref, keep_ref, came_ref):
    first = H + (lax.axis_index("row") * dims[1] + lax.axis_index("col")) * VB
    tele = one_hot(first, VB, src_ref[...])
    return DAMP * (keep_ref[:VB] + came_ref[:VB]) + 0.15 * tele


def spread_kernel(dims, src_ref, keep_ref, came_ref, scores_ref, hold_ref, pass_ref):
    quarter = hold_ref.shape[0]
    x = lax.axis_index("row") % X
    for ref, place in ((hold_ref, x), (pass_ref, 1 - x)):
        spot = pl.ds(pl.multiple_of(VB + place * quarter, quarter), quarter)
        ref[...] = keep_ref[spot, :] + came_ref[spot, :]
    scores_ref[0] = own_scores(dims, src_ref, keep_ref, came_ref).astype(scores_ref.dtype)


def join_kernel(held_ref, came_ref, out_ref):
    count = held_ref.shape[0]
    out_ref[:count] = held_ref[...]
    out_ref[count:] = came_ref[...]


def add_kernel(hold_ref, came_ref, out_ref):
    out_ref[...] = hold_ref[...] + came_ref[...]


def hub_kernel(dims, src_ref, held_ref, came_ref, out_ref):
    quarter = out_ref.shape[0]
    first = (lax.axis_index("col") * X + lax.axis_index("row") % X) * quarter
    tele = one_hot(first, quarter, src_ref[...])
    out_ref[...] = (DAMP * (held_ref[...] + came_ref[...]) + 0.15 * tele).astype(out_ref.dtype)


def pieces_kernel(keep_ref, came_ref, parts_ref):
    piece = parts_ref.shape[1]
    for k in range(parts_ref.shape[0]):
        spot = slice(VB + k * piece, VB + (k + 1) * piece)
        parts_ref[k] = keep_ref[spot, :] + came_ref[spot, :]


def last_kernel(dims, src_ref, keep_ref, came_ref, parts_ref, scores_ref, hubs_ref):
    scores_ref[...] = own_scores(dims, src_ref, keep_ref, came_ref)
    piece = hubs_ref.shape[0]
    summed = parts_ref[0]
    for k in range(1, parts_ref.shape[0]):
        summed = summed + parts_ref[k]
    first = (lax.axis_index("row") * dims[1] + lax.axis_index("col")) * piece
    hubs_ref[...] = DAMP * summed + 0.15 * one_hot(first, piece, src_ref[...])


def fast_body(tiles, tile_row, tile_col, tile_count, sources):
    slots, side = tiles.shape[2:4]
    width = sources.shape[0]
    n_row = lax.axis_size("row")
    n_col = lax.axis_size("col")
    piece = H // (n_row * n_col)
    dims = (n_row, n_col, side)
    n_rows = n_col * VB + H
    n_cols = n_row * VB + H
    f32 = functools.partial(jax.ShapeDtypeStruct, dtype=jnp.float32)
    bf16 = functools.partial(jax.ShapeDtypeStruct, dtype=jnp.bfloat16)
    src = sources.reshape(1, width)
    half = VB + n_row * piece
    quarter = H // n_col // X
    def other_core(x):
        return lax.ppermute(x, "col", [(0, 1), (1, 0)])

    def to_partner(x, flip):
        return lax.ppermute(x, "row", [(r, r ^ flip) for r in range(n_row)])

    def other_side(x):
        return to_partner(x, 1)

    def other_both(x):
        devices = [(r, c) for r in range(n_row) for c in range(n_col)]
        return lax.ppermute(x, ("row", "col"), [(r * n_col + c, (r ^ 1) * n_col + 1 - c) for r, c in devices])

    def call(kernel, name, out_shape, *args, scratch=(), cost=0):
        return pl.pallas_call(
            kernel,
            out_shape=out_shape,
            in_specs=[VMEM] * len(args),
            out_specs=jax.tree.map(lambda _: VMEM, out_shape),
            scratch_shapes=scratch,
            compiler_params=params(),
            cost_estimate=pl.CostEstimate(flops=cost * MICRO, bytes_accessed=0, transcendentals=0),
            name=name,
        )(*args)

    bind = functools.partial

    in_hbm = [pltpu.with_memory_space_constraint(x, pltpu.HBM) for x in (
        tiles.reshape(slots, side, side), tile_row.reshape(slots), tile_col.reshape(slots), src)]
    send, keep, dense = pl.pallas_call(
        bind(first_kernel, dims),
        out_shape=(f32((half, width)), f32((half, width)), bf16((2 * n_rows, n_cols))),
        in_specs=[HBM] * 5,
        out_specs=[VMEM] * 3,
        scratch_shapes=[
            pltpu.VMEM((slots, side, side), jnp.bfloat16),
            pltpu.SMEM((slots,), jnp.int32),
            pltpu.SMEM((slots,), jnp.int32),
            pltpu.SMEM((1,), jnp.int32),
            pltpu.VMEM((1, width), jnp.int32),
            pltpu.VMEM((n_rows + side, n_cols), jnp.float32),
            pltpu.VMEM((n_cols, width), jnp.bfloat16),
            pltpu.VMEM((n_rows, width), jnp.float32),
            pltpu.SemaphoreType.DMA((slots // CHUNK,)),
            pltpu.SemaphoreType.DMA((4,)),
        ],
        compiler_params=params(),
        name="first_terms",
    )(*in_hbm[:3], tile_count.reshape(1), in_hbm[3])

    masks = [n_row // X - 1]
    while masks[-1] > 1:
        masks.append(masks[-1] // 2)
    for step in range(ITERS - 1):
        came = other_core(send)
        held, hold, away = call(
            bind(spread_kernel, dims), "spread",
            (bf16((1, VB, width)), f32((quarter, width)), f32((quarter, width))),
            src, keep, came, cost=2)
        away = other_side(away)
        flips = [0]
        for mask in masks[:-1]:
            far = to_partner(held, X * mask)
            held = call(join_kernel, "join_near", bf16((2 * len(flips), VB, width)), held, far, cost=3)
            flips += [flip ^ mask for flip in flips]
        far = to_partner(held, X * masks[-1])
        flips += [flip ^ masks[-1] for flip in flips]
        near_across, far_across = other_side(held), other_side(far)
        sums = call(add_kernel, "plane_sum", f32((quarter, width)), hold, away, cost=20)
        for mask in masks[:0:-1]:
            sums = call(add_kernel, "pair_sum", f32((quarter, width)), sums, to_partner(sums, X * mask), cost=1)
        mine = call(bind(hub_kernel, dims), "hub_sums", bf16((quarter, width)), src, sums, to_partner(sums, X * masks[0]), cost=1)
        quarters = [mine, other_side(mine), other_core(mine), other_both(mine)]
        prod = call(
            bind(score_columns_kernel, dims, flips), "score_columns", f32((n_rows, width)),
            held, far, near_across, far_across, dense, scratch=[pltpu.VMEM((n_row * VB, width), jnp.bfloat16)])
        send, keep = call(
            bind(hub_columns_kernel, dims), "hub_columns", (f32((half, width)), f32((half, width))),
            *quarters, dense, prod,
            scratch=[pltpu.VMEM((H, width), jnp.bfloat16), pltpu.VMEM((n_rows, width), jnp.float32)])
    came = other_core(send)
    parts = call(pieces_kernel, "hub_pieces", f32((n_row, piece, width)), keep, came)
    parts = lax.all_to_all(parts, "row", 0, 0)
    scores, hubs = call(bind(last_kernel, dims), "last_sums", (f32((VB, width)), f32((piece, width))),
                        src, keep, came, parts)
    return scores.reshape(1, 1, VB, width), hubs


def plain_body(tiles, tile_row, tile_col, tile_count, sources):
    slots = tiles.shape[2]
    side = tiles.shape[3]
    width = sources.shape[0]
    tiles = tiles.reshape(slots, side, side)
    rows = tile_row.reshape(slots)
    cols = tile_col.reshape(slots)
    count = tile_count.reshape(())
    n_row = lax.axis_size("row")
    n_col = lax.axis_size("col")
    devices = n_row * n_col
    r_index = lax.axis_index("row")
    c_index = lax.axis_index("col")
    hub_dev = H // devices
    block_rows = n_col * VB
    n_tile_rows = (block_rows + H) // side
    own_base = H + (r_index * n_col + c_index) * VB
    hub_start = (r_index * n_col + c_index) * hub_dev
    own_ids = jnp.arange(VB, dtype=jnp.int32) + own_base
    tele_own = (own_ids[:, None] == sources[None, :]).astype(jnp.float32)
    piece_ids = jnp.arange(hub_dev, dtype=jnp.int32) + hub_start
    tele_piece = (piece_ids[:, None] == sources[None, :]).astype(jnp.float32)
    tele_hubs = (jnp.arange(H, dtype=jnp.int32)[:, None] == sources[None, :]).astype(jnp.float32)
    column_ids = (
        H
        + (jnp.arange(n_row, dtype=jnp.int32)[:, None] * n_col + c_index) * VB
        + jnp.arange(VB, dtype=jnp.int32)[None, :]
    ).reshape(n_row * VB)
    column_panel = (column_ids[:, None] == sources[None, :]).astype(jnp.bfloat16)
    hub_panel = tele_hubs.astype(jnp.bfloat16)
    block = math.gcd(slots, 16)
    own_scores = tele_own
    hub_piece = tele_piece
    for step in range(ITERS):
        start_acc = jnp.zeros((n_tile_rows, side, width), jnp.float32)
        if step > 0:
            column_panel = lax.all_gather(
                own_scores.astype(jnp.bfloat16), "row", axis=0, tiled=True
            )
        panel = jnp.concatenate([column_panel, hub_panel], axis=0).reshape(-1, side, width)

        def step_fn(number, total):
            start = number * block
            tile_block = lax.dynamic_slice_in_dim(tiles, start, block, 0)
            col_block = lax.dynamic_slice_in_dim(cols, start, block, 0)
            row_block = lax.dynamic_slice_in_dim(rows, start, block, 0)
            pieces = jnp.take(panel, col_block, axis=0)
            prod = jnp.einsum(
                "tij,tjs->tis", tile_block, pieces, preferred_element_type=jnp.float32
            )
            live = start + jnp.arange(block, dtype=jnp.int32) < count
            prod = jnp.where(live[:, None, None], prod, 0.0)
            return total.at[row_block].add(prod)

        total = lax.fori_loop(0, slots // block, step_fn, start_acc)
        partial_value = total.reshape(n_tile_rows * side, width)
        summed_rows = lax.psum_scatter(
            partial_value[:block_rows], "col", scatter_dimension=0, tiled=True
        )
        own_scores = 0.85 * summed_rows + 0.15 * tele_own
        hub_part = partial_value[block_rows:]
        summed = lax.psum_scatter(hub_part, ("row", "col"), scatter_dimension=0, tiled=True)
        hub_piece = 0.85 * summed + 0.15 * tele_piece
        if step + 1 < ITERS:
            hub_panel = lax.all_gather(
                hub_piece.astype(jnp.bfloat16), ("row", "col"), axis=0, tiled=True
            )
    return (own_scores.reshape(1, 1, VB, width), hub_piece)


def solution(mesh):
    placed = (
        P(("groups", "row"), "col", None, None, None),
        P(("groups", "row"), "col", None),
        P(("groups", "row"), "col", None),
        P(("groups", "row"), "col"),
        P("groups"),
    )

    def body(tiles, *rest):
        n_row, n_col = mesh.shape["row"], mesh.shape["col"]
        slots, side = tiles.shape[2:4]
        blocks = (n_col * VB + H) * (n_row * VB + H) // (side * side)
        if n_col == 2 and n_row in (8, 16) and blocks <= slots and H // (n_row * n_col) % 16 == 0:
            return fast_body(tiles, *rest)
        return plain_body(tiles, *rest)

    return jax.shard_map(
        body,
        mesh=mesh,
        in_specs=placed,
        out_specs=(P(("groups", "row"), "col", None, None), P(("groups", "row", "col"), None)),
        check_vma=False,
    )
```

```python
import functools
import math

import jax
import jax.numpy as jnp
from jax import lax
from jax.experimental import pallas as pl
from jax.experimental.pallas import tpu as pltpu
from jax.sharding import PartitionSpec as P

VB = 128
H = 256
ITERS = 2
DAMP = 0.85
CHUNK = 8
X = 2
MICRO = 10 ** 9
VMEM_LIMIT = 32 * 1024 * 1024

SMEM = pl.BlockSpec(memory_space=pltpu.SMEM)
VMEM = pl.BlockSpec(memory_space=pltpu.VMEM)
HBM = pl.BlockSpec(memory_space=pltpu.HBM)


def params():
    return pltpu.CompilerParams(vmem_limit_bytes=VMEM_LIMIT)


def one_hot(first, count, src):
    ids = lax.broadcasted_iota(jnp.int32, (count, src.shape[1]), 0) + first
    return (ids == src).astype(jnp.float32)


def write_terms(dims, block, prod_ref, send_ref, keep_ref):
    n_row, n_col, side = dims
    c = lax.axis_index("col")
    for ref, col in ((keep_ref, c), (send_ref, 1 - c)):
        ref[:VB] = prod_ref[pl.ds(pl.multiple_of(col * VB, VB), VB), :]
        for k in range(H // n_col // block):
            start = n_col * VB + (k * n_col + col) * block
            ref[VB + k * block:VB + (k + 1) * block] = prod_ref[pl.ds(pl.multiple_of(start, block), block), :]


def product(dense, panel):
    prod = jnp.dot(dense, panel, preferred_element_type=jnp.float32)
    rows = prod.shape[0] // 2
    return prod[:rows] + prod[rows:]


def first_kernel(dims, tiles_ref, rows_hbm, cols_hbm, count_hbm, src_hbm, send_ref, keep_ref, dense_ref,
                 held, rows_ref, cols_ref, count_ref, src_ref, total, panel, prod, sems, small):
    n_row, n_col, side = dims
    n_rows = dense_ref.shape[0] // 2
    pairs = ((src_hbm, src_ref), (rows_hbm, rows_ref), (cols_hbm, cols_ref), (count_hbm, count_ref))
    scalars = [pltpu.make_async_copy(a, b, small.at[i]) for i, (a, b) in enumerate(pairs)]
    copies = []
    for i in range(held.shape[0] // CHUNK):
        part = pl.ds(i * CHUNK, CHUNK)
        copies.append(pltpu.make_async_copy(tiles_ref.at[part], held.at[part], sems.at[i]))
    for copy in scalars + copies:
        copy.start()
    total[...] = jnp.zeros_like(total)
    for copy in scalars:
        copy.wait()
    src = src_ref[...]
    for r in range(n_row):
        first = H + (r * n_col + lax.axis_index("col")) * VB
        panel[pl.ds(r * VB, VB), :] = one_hot(first, VB, src).astype(jnp.bfloat16)
    panel[pl.ds(n_row * VB, H), :] = one_hot(0, H, src).astype(jnp.bfloat16)
    count = count_ref[0]

    def add_tile(k, carry):
        live = k < count
        row = pl.multiple_of(jnp.where(live, rows_ref[k] * side, n_rows), side)
        col = pl.multiple_of(jnp.where(live, cols_ref[k] * side, 0), side)
        spot = (pl.ds(row, side), pl.ds(col, side))
        total[spot] += held[k].astype(jnp.float32)
        return carry

    for i, copy in enumerate(copies):
        copy.wait()
        lax.fori_loop(i * CHUNK, (i + 1) * CHUNK, add_tile, 0, unroll=4)
    for r in range(0, n_rows, side):
        whole = total[pl.ds(r, side), :]
        high = whole.astype(jnp.bfloat16)
        dense_ref[pl.ds(r, side), :] = high
        dense_ref[pl.ds(n_rows + r, side), :] = (whole - high.astype(jnp.float32)).astype(jnp.bfloat16)
    prod[...] = product(dense_ref[...], panel[...])
    write_terms(dims, H // n_col, prod, send_ref, keep_ref)


def score_columns_kernel(dims, flips, *refs):
    n_row, n_col, side = dims
    n_z = n_row // X
    blocks, (dense_ref, prod_ref, panel) = refs[:4], refs[4:]
    r = lax.axis_index("row")
    near, far = flips[:n_z // 2], flips[n_z // 2:]
    for ref, group, x in ((blocks[0], near, 0), (blocks[1], far, 0), (blocks[2], near, 1), (blocks[3], far, 1)):
        for k, flip in enumerate(group):
            owner = r ^ (X * flip + x)
            panel[pl.ds(pl.multiple_of(owner * VB, VB), VB), :] = ref[k]
    prod_ref[...] = product(dense_ref[:, :n_row * VB], panel[...])


def hub_columns_kernel(dims, *refs):
    n_row, n_col, side = dims
    quarters, (dense_ref, prod_ref, send_ref, keep_ref, panel, total) = refs[:X * n_col], refs[X * n_col:]
    r, c = lax.axis_index("row"), lax.axis_index("col")
    quarter = quarters[0].shape[0]
    for k, ref in enumerate(quarters):
        place = ((c ^ (k // X)) * X + (r % X ^ (k % X))) * quarter
        panel[pl.ds(pl.multiple_of(place, quarter), quarter), :] = ref[...]
    total[...] = prod_ref[...] + product(dense_ref[:, n_row * VB:], panel[...])
    write_terms(dims, H // (n_row * n_col), total, send_ref, keep_ref)


def own_scores(dims, src_ref, keep_ref, came_ref):
    first = H + (lax.axis_index("row") * dims[1] + lax.axis_index("col")) * VB
    tele = one_hot(first, VB, src_ref[...])
    return DAMP * (keep_ref[:VB] + came_ref[:VB]) + 0.15 * tele


def spread_kernel(dims, src_ref, keep_ref, came_ref, scores_ref, hold_ref, pass_ref):
    quarter = hold_ref.shape[0]
    x = lax.axis_index("row") % X
    for ref, place in ((hold_ref, x), (pass_ref, 1 - x)):
        spot = pl.ds(pl.multiple_of(VB + place * quarter, quarter), quarter)
        ref[...] = keep_ref[spot, :] + came_ref[spot, :]
    scores_ref[0] = own_scores(dims, src_ref, keep_ref, came_ref).astype(scores_ref.dtype)


def join_kernel(held_ref, came_ref, out_ref):
    count = held_ref.shape[0]
    out_ref[:count] = held_ref[...]
    out_ref[count:] = came_ref[...]


def add_kernel(hold_ref, came_ref, out_ref):
    out_ref[...] = hold_ref[...] + came_ref[...]


def hub_kernel(dims, src_ref, held_ref, came_ref, out_ref):
    quarter = out_ref.shape[0]
    first = (lax.axis_index("col") * X + lax.axis_index("row") % X) * quarter
    tele = one_hot(first, quarter, src_ref[...])
    out_ref[...] = (DAMP * (held_ref[...] + came_ref[...]) + 0.15 * tele).astype(out_ref.dtype)


def pieces_kernel(keep_ref, came_ref, parts_ref):
    piece = parts_ref.shape[1]
    for k in range(parts_ref.shape[0]):
        spot = slice(VB + k * piece, VB + (k + 1) * piece)
        parts_ref[k] = keep_ref[spot, :] + came_ref[spot, :]


def last_kernel(dims, src_ref, keep_ref, came_ref, parts_ref, scores_ref, hubs_ref):
    scores_ref[...] = own_scores(dims, src_ref, keep_ref, came_ref)
    piece = hubs_ref.shape[0]
    summed = parts_ref[0]
    for k in range(1, parts_ref.shape[0]):
        summed = summed + parts_ref[k]
    first = (lax.axis_index("row") * dims[1] + lax.axis_index("col")) * piece
    hubs_ref[...] = DAMP * summed + 0.15 * one_hot(first, piece, src_ref[...])


def fast_body(tiles, tile_row, tile_col, tile_count, sources):
    slots, side = tiles.shape[2:4]
    width = sources.shape[0]
    n_row = lax.axis_size("row")
    n_col = lax.axis_size("col")
    piece = H // (n_row * n_col)
    dims = (n_row, n_col, side)
    n_rows = n_col * VB + H
    n_cols = n_row * VB + H
    f32 = functools.partial(jax.ShapeDtypeStruct, dtype=jnp.float32)
    bf16 = functools.partial(jax.ShapeDtypeStruct, dtype=jnp.bfloat16)
    src = sources.reshape(1, width)
    half = VB + n_row * piece
    quarter = H // n_col // X
    def other_core(x):
        return lax.ppermute(x, "col", [(0, 1), (1, 0)])

    def to_partner(x, flip):
        return lax.ppermute(x, "row", [(r, r ^ flip) for r in range(n_row)])

    def other_side(x):
        return to_partner(x, 1)

    def other_both(x):
        devices = [(r, c) for r in range(n_row) for c in range(n_col)]
        return lax.ppermute(x, ("row", "col"), [(r * n_col + c, (r ^ 1) * n_col + 1 - c) for r, c in devices])

    def call(kernel, name, out_shape, *args, scratch=(), cost=0):
        return pl.pallas_call(
            kernel,
            out_shape=out_shape,
            in_specs=[VMEM] * len(args),
            out_specs=jax.tree.map(lambda _: VMEM, out_shape),
            scratch_shapes=scratch,
            compiler_params=params(),
            cost_estimate=pl.CostEstimate(flops=cost * MICRO, bytes_accessed=0, transcendentals=0),
            name=name,
        )(*args)

    bind = functools.partial

    in_hbm = [pltpu.with_memory_space_constraint(x, pltpu.HBM) for x in (
        tiles.reshape(slots, side, side), tile_row.reshape(slots), tile_col.reshape(slots), src)]
    send, keep, dense = pl.pallas_call(
        bind(first_kernel, dims),
        out_shape=(f32((half, width)), f32((half, width)), bf16((2 * n_rows, n_cols))),
        in_specs=[HBM] * 5,
        out_specs=[VMEM] * 3,
        scratch_shapes=[
            pltpu.VMEM((slots, side, side), jnp.bfloat16),
            pltpu.SMEM((slots,), jnp.int32),
            pltpu.SMEM((slots,), jnp.int32),
            pltpu.SMEM((1,), jnp.int32),
            pltpu.VMEM((1, width), jnp.int32),
            pltpu.VMEM((n_rows + side, n_cols), jnp.float32),
            pltpu.VMEM((n_cols, width), jnp.bfloat16),
            pltpu.VMEM((n_rows, width), jnp.float32),
            pltpu.SemaphoreType.DMA((slots // CHUNK,)),
            pltpu.SemaphoreType.DMA((4,)),
        ],
        compiler_params=params(),
        name="first_terms",
    )(*in_hbm[:3], tile_count.reshape(1), in_hbm[3])

    masks = [n_row // X - 1]
    while masks[-1] > 1:
        masks.append(masks[-1] // 2)
    for step in range(ITERS - 1):
        came = other_core(send)
        held, hold, away = call(
            bind(spread_kernel, dims), "spread",
            (bf16((1, VB, width)), f32((quarter, width)), f32((quarter, width))),
            src, keep, came, cost=2)
        away = other_side(away)
        flips = [0]
        for mask in masks[:-1]:
            far = to_partner(held, X * mask)
            held = call(join_kernel, "join_near", bf16((2 * len(flips), VB, width)), held, far, cost=3)
            flips += [flip ^ mask for flip in flips]
        far = to_partner(held, X * masks[-1])
        flips += [flip ^ masks[-1] for flip in flips]
        near_across, far_across = other_side(held), other_side(far)
        sums = call(add_kernel, "plane_sum", f32((quarter, width)), hold, away, cost=20)
        for mask in masks[:0:-1]:
            sums = call(add_kernel, "pair_sum", f32((quarter, width)), sums, to_partner(sums, X * mask), cost=1)
        mine = call(bind(hub_kernel, dims), "hub_sums", bf16((quarter, width)), src, sums, to_partner(sums, X * masks[0]), cost=1)
        quarters = [mine, other_side(mine), other_core(mine), other_both(mine)]
        prod = call(
            bind(score_columns_kernel, dims, flips), "score_columns", f32((n_rows, width)),
            held, far, near_across, far_across, dense, scratch=[pltpu.VMEM((n_row * VB, width), jnp.bfloat16)])
        send, keep = call(
            bind(hub_columns_kernel, dims), "hub_columns", (f32((half, width)), f32((half, width))),
            *quarters, dense, prod,
            scratch=[pltpu.VMEM((H, width), jnp.bfloat16), pltpu.VMEM((n_rows, width), jnp.float32)])
    came = other_core(send)
    parts = call(pieces_kernel, "hub_pieces", f32((n_row, piece, width)), keep, came)
    parts = lax.all_to_all(parts, "row", 0, 0)
    scores, hubs = call(bind(last_kernel, dims), "last_sums", (f32((VB, width)), f32((piece, width))),
                        src, keep, came, parts)
    return scores.reshape(1, 1, VB, width), hubs


def plain_body(tiles, tile_row, tile_col, tile_count, sources):
    slots = tiles.shape[2]
    side = tiles.shape[3]
    width = sources.shape[0]
    tiles = tiles.reshape(slots, side, side)
    rows = tile_row.reshape(slots)
    cols = tile_col.reshape(slots)
    count = tile_count.reshape(())
    n_row = lax.axis_size("row")
    n_col = lax.axis_size("col")
    devices = n_row * n_col
    r_index = lax.axis_index("row")
    c_index = lax.axis_index("col")
    hub_dev = H // devices
    block_rows = n_col * VB
    n_tile_rows = (block_rows + H) // side
    own_base = H + (r_index * n_col + c_index) * VB
    hub_start = (r_index * n_col + c_index) * hub_dev
    own_ids = jnp.arange(VB, dtype=jnp.int32) + own_base
    tele_own = (own_ids[:, None] == sources[None, :]).astype(jnp.float32)
    piece_ids = jnp.arange(hub_dev, dtype=jnp.int32) + hub_start
    tele_piece = (piece_ids[:, None] == sources[None, :]).astype(jnp.float32)
    tele_hubs = (jnp.arange(H, dtype=jnp.int32)[:, None] == sources[None, :]).astype(jnp.float32)
    column_ids = (
        H
        + (jnp.arange(n_row, dtype=jnp.int32)[:, None] * n_col + c_index) * VB
        + jnp.arange(VB, dtype=jnp.int32)[None, :]
    ).reshape(n_row * VB)
    column_panel = (column_ids[:, None] == sources[None, :]).astype(jnp.bfloat16)
    hub_panel = tele_hubs.astype(jnp.bfloat16)
    block = math.gcd(slots, 16)
    own_scores = tele_own
    hub_piece = tele_piece
    for step in range(ITERS):
        start_acc = jnp.zeros((n_tile_rows, side, width), jnp.float32)
        if step > 0:
            column_panel = lax.all_gather(
                own_scores.astype(jnp.bfloat16), "row", axis=0, tiled=True
            )
        panel = jnp.concatenate([column_panel, hub_panel], axis=0).reshape(-1, side, width)

        def step_fn(number, total):
            start = number * block
            tile_block = lax.dynamic_slice_in_dim(tiles, start, block, 0)
            col_block = lax.dynamic_slice_in_dim(cols, start, block, 0)
            row_block = lax.dynamic_slice_in_dim(rows, start, block, 0)
            pieces = jnp.take(panel, col_block, axis=0)
            prod = jnp.einsum(
                "tij,tjs->tis", tile_block, pieces, preferred_element_type=jnp.float32
            )
            live = start + jnp.arange(block, dtype=jnp.int32) < count
            prod = jnp.where(live[:, None, None], prod, 0.0)
            return total.at[row_block].add(prod)

        total = lax.fori_loop(0, slots // block, step_fn, start_acc)
        partial_value = total.reshape(n_tile_rows * side, width)
        summed_rows = lax.psum_scatter(
            partial_value[:block_rows], "col", scatter_dimension=0, tiled=True
        )
        own_scores = 0.85 * summed_rows + 0.15 * tele_own
        hub_part = partial_value[block_rows:]
        summed = lax.psum_scatter(hub_part, ("row", "col"), scatter_dimension=0, tiled=True)
        hub_piece = 0.85 * summed + 0.15 * tele_piece
        if step + 1 < ITERS:
            hub_panel = lax.all_gather(
                hub_piece.astype(jnp.bfloat16), ("row", "col"), axis=0, tiled=True
            )
    return (own_scores.reshape(1, 1, VB, width), hub_piece)


def solution(mesh):
    placed = (
        P(("groups", "row"), "col", None, None, None),
        P(("groups", "row"), "col", None),
        P(("groups", "row"), "col", None),
        P(("groups", "row"), "col"),
        P("groups"),
    )

    def body(tiles, *rest):
        n_row, n_col = mesh.shape["row"], mesh.shape["col"]
        slots, side = tiles.shape[2:4]
        blocks = (n_col * VB + H) * (n_row * VB + H) // (side * side)
        if n_col == 2 and n_row in (8, 16) and blocks <= slots and H // (n_row * n_col) % 16 == 0:
            return fast_body(tiles, *rest)
        return plain_body(tiles, *rest)

    return jax.shard_map(
        body,
        mesh=mesh,
        in_specs=placed,
        out_specs=(P(("groups", "row"), "col", None, None), P(("groups", "row", "col"), None)),
        check_vma=False,
    )
```

```python
import functools
import math

import jax
import jax.numpy as jnp
from jax import lax
from jax.experimental import pallas as pl
from jax.experimental.pallas import tpu as pltpu
from jax.sharding import PartitionSpec as P

VB = 128
H = 256
ITERS = 2
DAMP = 0.85
CHUNK = 8
X = 2
MICRO = 10 ** 9
VMEM_LIMIT = 32 * 1024 * 1024

SMEM = pl.BlockSpec(memory_space=pltpu.SMEM)
VMEM = pl.BlockSpec(memory_space=pltpu.VMEM)
HBM = pl.BlockSpec(memory_space=pltpu.HBM)


def params():
    return pltpu.CompilerParams(vmem_limit_bytes=VMEM_LIMIT)


def one_hot(first, count, src):
    ids = lax.broadcasted_iota(jnp.int32, (count, src.shape[1]), 0) + first
    return (ids == src).astype(jnp.float32)


def product(dense, panel):
    prod = jnp.dot(dense, panel, preferred_element_type=jnp.float32)
    rows = prod.shape[0] // 2
    return prod[:rows] + prod[rows:]


def first_kernel(dims, tiles_ref, rows_hbm, cols_hbm, count_hbm, src_hbm, send_ref, keep_ref, dense_ref,
                 held, rows_ref, cols_ref, count_ref, src_ref, total, panel, sems, small):
    n_row, n_col, side = dims
    n_rows = dense_ref.shape[0] // 2
    piece = H // (n_row * n_col)
    c = lax.axis_index("col")
    pairs = ((src_hbm, src_ref), (rows_hbm, rows_ref), (cols_hbm, cols_ref), (count_hbm, count_ref))
    scalars = [pltpu.make_async_copy(a, b, small.at[i]) for i, (a, b) in enumerate(pairs)]
    copies = []
    for i in range(held.shape[0] // CHUNK):
        part = pl.ds(i * CHUNK, CHUNK)
        copies.append(pltpu.make_async_copy(tiles_ref.at[part], held.at[part], sems.at[i]))
    for copy in scalars + copies:
        copy.start()
    total[...] = jnp.zeros_like(total)
    for copy in scalars:
        copy.wait()
    src = src_ref[...]
    for r in range(n_row):
        first = H + (r * n_col + c) * VB
        panel[pl.ds(r * VB, VB), :] = one_hot(first, VB, src).astype(jnp.bfloat16)
    panel[pl.ds(n_row * VB, H), :] = one_hot(0, H, src).astype(jnp.bfloat16)
    count = count_ref[0]

    def add_tile(k, carry):
        live = k < count
        row = pl.multiple_of(jnp.where(live, rows_ref[k] * side, n_rows), side)
        col = pl.multiple_of(jnp.where(live, cols_ref[k] * side, 0), side)
        spot = (pl.ds(row, side), pl.ds(col, side))
        total[spot] += held[k].astype(jnp.float32)
        return carry

    for i, copy in enumerate(copies):
        copy.wait()
        lax.fori_loop(i * CHUNK, (i + 1) * CHUNK, add_tile, 0, unroll=4)
    half = n_rows // n_col
    for at, out, core in ((0, keep_ref, c), (n_rows, send_ref, 1 - c)):
        chunks = [(0, core * VB, VB)]
        for r in range(n_row):
            chunks.append((VB + r * piece, n_col * VB + (r * n_col + core) * piece, piece))
        for to, start, size in chunks:
            whole = total[pl.ds(pl.multiple_of(start, size), size), :]
            high = whole.astype(jnp.bfloat16)
            dense_ref[at + to:at + to + size] = high
            dense_ref[at + half + to:at + half + to + size] = (whole - high.astype(jnp.float32)).astype(jnp.bfloat16)
        out[...] = product(dense_ref[at:at + 2 * half], panel[...])


def score_columns_kernel(dims, flips, *refs):
    n_row, n_col, side = dims
    n_z = n_row // X
    blocks, (dense_ref, send_ref, keep_ref, panel) = refs[:4], refs[4:]
    r = lax.axis_index("row")
    near, far = flips[:n_z // 2], flips[n_z // 2:]
    for ref, group, x in ((blocks[0], near, 0), (blocks[1], far, 0), (blocks[2], near, 1), (blocks[3], far, 1)):
        for k, flip in enumerate(group):
            owner = r ^ (X * flip + x)
            panel[pl.ds(pl.multiple_of(owner * VB, VB), VB), :] = ref[k]
    n_rows = dense_ref.shape[0] // 2
    keep_ref[...] = product(dense_ref[:n_rows, :n_row * VB], panel[...])
    send_ref[...] = product(dense_ref[n_rows:, :n_row * VB], panel[...])


def hub_columns_kernel(dims, *refs):
    n_row, n_col, side = dims
    n_z = n_row // X
    quarters, (dense_ref, send_part, keep_part, send_ref, keep_ref, panel) = refs[:X * n_col], refs[X * n_col:]
    r, c = lax.axis_index("row"), lax.axis_index("col")
    piece = H // (n_row * n_col)
    for k, ref in enumerate(quarters):
        for i in range(n_z):
            row = ((r % X ^ (k % X)) * n_z + i) * n_col + (c ^ (k // X))
            panel[pl.ds(pl.multiple_of(row * piece, piece), piece), :] = ref[i * piece:(i + 1) * piece]
    n_rows = dense_ref.shape[0] // 2
    send_ref[...] = send_part[...] + product(dense_ref[n_rows:, n_row * VB:], panel[...])
    keep_ref[...] = keep_part[...] + product(dense_ref[:n_rows, n_row * VB:], panel[...])


def own_scores(dims, src_ref, keep_ref, came_ref):
    first = H + (lax.axis_index("row") * dims[1] + lax.axis_index("col")) * VB
    tele = one_hot(first, VB, src_ref[...])
    return DAMP * (keep_ref[:VB] + came_ref[:VB]) + 0.15 * tele


def spread_kernel(dims, src_ref, keep_ref, came_ref, scores_ref, hold_ref, pass_ref):
    quarter = hold_ref.shape[0]
    x = lax.axis_index("row") % X
    for ref, place in ((hold_ref, x), (pass_ref, 1 - x)):
        spot = pl.ds(pl.multiple_of(VB + place * quarter, quarter), quarter)
        ref[...] = keep_ref[spot, :] + came_ref[spot, :]
    scores_ref[0] = own_scores(dims, src_ref, keep_ref, came_ref).astype(scores_ref.dtype)


def join_kernel(held_ref, came_ref, out_ref):
    count = held_ref.shape[0]
    out_ref[:count] = held_ref[...]
    out_ref[count:] = came_ref[...]


def add_kernel(hold_ref, came_ref, out_ref):
    out_ref[...] = hold_ref[...] + came_ref[...]


def hub_kernel(dims, src_ref, held_ref, came_ref, out_ref):
    n_row, n_col, side = dims
    piece = H // (n_row * n_col)
    r, c = lax.axis_index("row"), lax.axis_index("col")
    at = lax.broadcasted_iota(jnp.int32, out_ref.shape, 0)
    ids = ((r % X * (n_row // X) + at // piece) * n_col + c) * piece + at % piece
    tele = (ids == src_ref[...]).astype(jnp.float32)
    out_ref[...] = (DAMP * (held_ref[...] + came_ref[...]) + 0.15 * tele).astype(out_ref.dtype)


def pieces_kernel(keep_ref, came_ref, parts_ref):
    piece = parts_ref.shape[1]
    for k in range(parts_ref.shape[0]):
        spot = slice(VB + k * piece, VB + (k + 1) * piece)
        parts_ref[k] = keep_ref[spot, :] + came_ref[spot, :]


def last_kernel(dims, src_ref, keep_ref, came_ref, parts_ref, scores_ref, hubs_ref):
    scores_ref[...] = own_scores(dims, src_ref, keep_ref, came_ref)
    piece = hubs_ref.shape[0]
    summed = parts_ref[0]
    for k in range(1, parts_ref.shape[0]):
        summed = summed + parts_ref[k]
    first = (lax.axis_index("row") * dims[1] + lax.axis_index("col")) * piece
    hubs_ref[...] = DAMP * summed + 0.15 * one_hot(first, piece, src_ref[...])


def fast_body(tiles, tile_row, tile_col, tile_count, sources):
    slots, side = tiles.shape[2:4]
    width = sources.shape[0]
    n_row = lax.axis_size("row")
    n_col = lax.axis_size("col")
    piece = H // (n_row * n_col)
    dims = (n_row, n_col, side)
    n_rows = n_col * VB + H
    n_cols = n_row * VB + H
    f32 = functools.partial(jax.ShapeDtypeStruct, dtype=jnp.float32)
    bf16 = functools.partial(jax.ShapeDtypeStruct, dtype=jnp.bfloat16)
    src = sources.reshape(1, width)
    half = VB + n_row * piece
    quarter = H // n_col // X
    def other_core(x):
        return lax.ppermute(x, "col", [(0, 1), (1, 0)])

    def to_partner(x, flip):
        return lax.ppermute(x, "row", [(r, r ^ flip) for r in range(n_row)])

    def other_side(x):
        return to_partner(x, 1)

    def other_both(x):
        devices = [(r, c) for r in range(n_row) for c in range(n_col)]
        return lax.ppermute(x, ("row", "col"), [(r * n_col + c, (r ^ 1) * n_col + 1 - c) for r, c in devices])

    def call(kernel, name, out_shape, *args, scratch=(), cost=0):
        return pl.pallas_call(
            kernel,
            out_shape=out_shape,
            in_specs=[VMEM] * len(args),
            out_specs=jax.tree.map(lambda _: VMEM, out_shape),
            scratch_shapes=scratch,
            compiler_params=params(),
            cost_estimate=pl.CostEstimate(flops=cost * MICRO, bytes_accessed=0, transcendentals=0),
            name=name,
        )(*args)

    bind = functools.partial

    in_hbm = [pltpu.with_memory_space_constraint(x, pltpu.HBM) for x in (
        tiles.reshape(slots, side, side), tile_row.reshape(slots), tile_col.reshape(slots), src)]
    send, keep, dense = pl.pallas_call(
        bind(first_kernel, dims),
        out_shape=(f32((half, width)), f32((half, width)), bf16((2 * n_rows, n_cols))),
        in_specs=[HBM] * 5,
        out_specs=[VMEM] * 3,
        scratch_shapes=[
            pltpu.VMEM((slots, side, side), jnp.bfloat16),
            pltpu.SMEM((slots,), jnp.int32),
            pltpu.SMEM((slots,), jnp.int32),
            pltpu.SMEM((1,), jnp.int32),
            pltpu.VMEM((1, width), jnp.int32),
            pltpu.VMEM((n_rows + side, n_cols), jnp.float32),
            pltpu.VMEM((n_cols, width), jnp.bfloat16),
            pltpu.SemaphoreType.DMA((slots // CHUNK,)),
            pltpu.SemaphoreType.DMA((4,)),
        ],
        compiler_params=params(),
        name="first_terms",
    )(*in_hbm[:3], tile_count.reshape(1), in_hbm[3])

    masks = [n_row // X - 1]
    while masks[-1] > 1:
        masks.append(masks[-1] // 2)
    for step in range(ITERS - 1):
        came = other_core(send)
        held, hold, away = call(
            bind(spread_kernel, dims), "spread",
            (bf16((1, VB, width)), f32((quarter, width)), f32((quarter, width))),
            src, keep, came, cost=2)
        away = other_side(away)
        flips = [0]
        for mask in masks[:-1]:
            far = to_partner(held, X * mask)
            held = call(join_kernel, "join_near", bf16((2 * len(flips), VB, width)), held, far, cost=3)
            flips += [flip ^ mask for flip in flips]
        far = to_partner(held, X * masks[-1])
        flips += [flip ^ masks[-1] for flip in flips]
        near_across, far_across = other_side(held), other_side(far)
        sums = call(add_kernel, "plane_sum", f32((quarter, width)), hold, away, cost=20)
        for mask in masks[:0:-1]:
            sums = call(add_kernel, "pair_sum", f32((quarter, width)), sums, to_partner(sums, X * mask), cost=1)
        mine = call(bind(hub_kernel, dims), "hub_sums", bf16((quarter, width)), src, sums, to_partner(sums, X * masks[0]), cost=1)
        quarters = [mine, other_side(mine), other_core(mine), other_both(mine)]
        send, keep = call(
            bind(score_columns_kernel, dims, flips), "score_columns", (f32((half, width)),) * 2,
            held, far, near_across, far_across, dense, scratch=[pltpu.VMEM((n_row * VB, width), jnp.bfloat16)])
        send, keep = call(
            bind(hub_columns_kernel, dims), "hub_columns", (f32((half, width)),) * 2,
            *quarters, dense, send, keep, scratch=[pltpu.VMEM((H, width), jnp.bfloat16)])
    came = other_core(send)
    parts = call(pieces_kernel, "hub_pieces", f32((n_row, piece, width)), keep, came)
    parts = lax.all_to_all(parts, "row", 0, 0)
    scores, hubs = call(bind(last_kernel, dims), "last_sums", (f32((VB, width)), f32((piece, width))),
                        src, keep, came, parts)
    return scores.reshape(1, 1, VB, width), hubs


def plain_body(tiles, tile_row, tile_col, tile_count, sources):
    slots = tiles.shape[2]
    side = tiles.shape[3]
    width = sources.shape[0]
    tiles = tiles.reshape(slots, side, side)
    rows = tile_row.reshape(slots)
    cols = tile_col.reshape(slots)
    count = tile_count.reshape(())
    n_row = lax.axis_size("row")
    n_col = lax.axis_size("col")
    devices = n_row * n_col
    r_index = lax.axis_index("row")
    c_index = lax.axis_index("col")
    hub_dev = H // devices
    block_rows = n_col * VB
    n_tile_rows = (block_rows + H) // side
    own_base = H + (r_index * n_col + c_index) * VB
    hub_start = (r_index * n_col + c_index) * hub_dev
    own_ids = jnp.arange(VB, dtype=jnp.int32) + own_base
    tele_own = (own_ids[:, None] == sources[None, :]).astype(jnp.float32)
    piece_ids = jnp.arange(hub_dev, dtype=jnp.int32) + hub_start
    tele_piece = (piece_ids[:, None] == sources[None, :]).astype(jnp.float32)
    tele_hubs = (jnp.arange(H, dtype=jnp.int32)[:, None] == sources[None, :]).astype(jnp.float32)
    column_ids = (
        H
        + (jnp.arange(n_row, dtype=jnp.int32)[:, None] * n_col + c_index) * VB
        + jnp.arange(VB, dtype=jnp.int32)[None, :]
    ).reshape(n_row * VB)
    column_panel = (column_ids[:, None] == sources[None, :]).astype(jnp.bfloat16)
    hub_panel = tele_hubs.astype(jnp.bfloat16)
    block = math.gcd(slots, 16)
    own_scores = tele_own
    hub_piece = tele_piece
    for step in range(ITERS):
        start_acc = jnp.zeros((n_tile_rows, side, width), jnp.float32)
        if step > 0:
            column_panel = lax.all_gather(
                own_scores.astype(jnp.bfloat16), "row", axis=0, tiled=True
            )
        panel = jnp.concatenate([column_panel, hub_panel], axis=0).reshape(-1, side, width)

        def step_fn(number, total):
            start = number * block
            tile_block = lax.dynamic_slice_in_dim(tiles, start, block, 0)
            col_block = lax.dynamic_slice_in_dim(cols, start, block, 0)
            row_block = lax.dynamic_slice_in_dim(rows, start, block, 0)
            pieces = jnp.take(panel, col_block, axis=0)
            prod = jnp.einsum(
                "tij,tjs->tis", tile_block, pieces, preferred_element_type=jnp.float32
            )
            live = start + jnp.arange(block, dtype=jnp.int32) < count
            prod = jnp.where(live[:, None, None], prod, 0.0)
            return total.at[row_block].add(prod)

        total = lax.fori_loop(0, slots // block, step_fn, start_acc)
        partial_value = total.reshape(n_tile_rows * side, width)
        summed_rows = lax.psum_scatter(
            partial_value[:block_rows], "col", scatter_dimension=0, tiled=True
        )
        own_scores = 0.85 * summed_rows + 0.15 * tele_own
        hub_part = partial_value[block_rows:]
        summed = lax.psum_scatter(hub_part, ("row", "col"), scatter_dimension=0, tiled=True)
        hub_piece = 0.85 * summed + 0.15 * tele_piece
        if step + 1 < ITERS:
            hub_panel = lax.all_gather(
                hub_piece.astype(jnp.bfloat16), ("row", "col"), axis=0, tiled=True
            )
    return (own_scores.reshape(1, 1, VB, width), hub_piece)


def solution(mesh):
    placed = (
        P(("groups", "row"), "col", None, None, None),
        P(("groups", "row"), "col", None),
        P(("groups", "row"), "col", None),
        P(("groups", "row"), "col"),
        P("groups"),
    )

    def body(tiles, *rest):
        n_row, n_col = mesh.shape["row"], mesh.shape["col"]
        slots, side = tiles.shape[2:4]
        blocks = (n_col * VB + H) * (n_row * VB + H) // (side * side)
        if n_col == 2 and n_row in (8, 16) and blocks <= slots and H // (n_row * n_col) % 16 == 0:
            return fast_body(tiles, *rest)
        return plain_body(tiles, *rest)

    return jax.shard_map(
        body,
        mesh=mesh,
        in_specs=placed,
        out_specs=(P(("groups", "row"), "col", None, None), P(("groups", "row", "col"), None)),
        check_vma=False,
    )
```

```python
import functools
import math

import jax
import jax.numpy as jnp
from jax import lax
from jax.experimental import pallas as pl
from jax.experimental.pallas import tpu as pltpu
from jax.sharding import PartitionSpec as P

VB = 128
H = 256
ITERS = 2
DAMP = 0.85
CHUNK = 8
X = 2
MICRO = 10 ** 9
VMEM_LIMIT = 32 * 1024 * 1024

SMEM = pl.BlockSpec(memory_space=pltpu.SMEM)
VMEM = pl.BlockSpec(memory_space=pltpu.VMEM)
HBM = pl.BlockSpec(memory_space=pltpu.HBM)


def params():
    return pltpu.CompilerParams(vmem_limit_bytes=VMEM_LIMIT)


def one_hot(first, count, src):
    ids = lax.broadcasted_iota(jnp.int32, (count, src.shape[1]), 0) + first
    return (ids == src).astype(jnp.float32)


def product(dense, panel):
    prod = jnp.dot(dense, panel, preferred_element_type=jnp.float32)
    rows = prod.shape[0] // 2
    return prod[:rows] + prod[rows:]


def first_kernel(dims, tiles_ref, rows_hbm, cols_hbm, count_hbm, src_hbm, send_ref, keep_ref, dense_ref,
                 held, rows_ref, cols_ref, count_ref, src_ref, total, panel, sems, small):
    n_row, n_col, side = dims
    n_rows = dense_ref.shape[0] // 2
    piece = H // (n_row * n_col)
    c = lax.axis_index("col")
    pairs = ((src_hbm, src_ref), (rows_hbm, rows_ref), (cols_hbm, cols_ref), (count_hbm, count_ref))
    scalars = [pltpu.make_async_copy(a, b, small.at[i]) for i, (a, b) in enumerate(pairs)]
    copies = []
    for i in range(held.shape[0] // CHUNK):
        part = pl.ds(i * CHUNK, CHUNK)
        copies.append(pltpu.make_async_copy(tiles_ref.at[part], held.at[part], sems.at[i]))
    for copy in scalars + copies:
        copy.start()
    total[...] = jnp.zeros_like(total)
    for copy in scalars:
        copy.wait()
    src = src_ref[...]
    for r in range(n_row):
        first = H + (r * n_col + c) * VB
        panel[pl.ds(r * VB, VB), :] = one_hot(first, VB, src).astype(jnp.bfloat16)
    panel[pl.ds(n_row * VB, H), :] = one_hot(0, H, src).astype(jnp.bfloat16)
    count = count_ref[0]

    def add_tile(k, carry):
        live = k < count
        row = pl.multiple_of(jnp.where(live, rows_ref[k] * side, n_rows), side)
        col = pl.multiple_of(jnp.where(live, cols_ref[k] * side, 0), side)
        spot = (pl.ds(row, side), pl.ds(col, side))
        total[spot] += held[k].astype(jnp.float32)
        return carry

    for i, copy in enumerate(copies):
        copy.wait()
        lax.fori_loop(i * CHUNK, (i + 1) * CHUNK, add_tile, 0, unroll=4)
    half = n_rows // n_col
    for at, out, core in ((0, keep_ref, c), (n_rows, send_ref, 1 - c)):
        chunks = [(0, core * VB, VB)]
        for r in range(n_row):
            chunks.append((VB + r * piece, n_col * VB + (r * n_col + core) * piece, piece))
        for to, start, size in chunks:
            whole = total[pl.ds(pl.multiple_of(start, size), size), :]
            high = whole.astype(jnp.bfloat16)
            dense_ref[at + to:at + to + size] = high
            dense_ref[at + half + to:at + half + to + size] = (whole - high.astype(jnp.float32)).astype(jnp.bfloat16)
        out[...] = product(dense_ref[at:at + 2 * half], panel[...])


def score_columns_kernel(dims, flips, *refs):
    n_row, n_col, side = dims
    n_z = n_row // X
    blocks, (dense_ref, send_ref, keep_ref, panel) = refs[:4], refs[4:]
    r = lax.axis_index("row")
    near, far = flips[:n_z // 2], flips[n_z // 2:]
    for ref, group, x in ((blocks[0], near, 0), (blocks[1], far, 0), (blocks[2], near, 1), (blocks[3], far, 1)):
        for k, flip in enumerate(group):
            owner = r ^ (X * flip + x)
            panel[pl.ds(pl.multiple_of(owner * VB, VB), VB), :] = ref[k]
    n_rows = dense_ref.shape[0] // 2
    keep_ref[...] = product(dense_ref[:n_rows, :n_row * VB], panel[...])
    send_ref[...] = product(dense_ref[n_rows:, :n_row * VB], panel[...])


def hub_columns_kernel(dims, *refs):
    n_row, n_col, side = dims
    n_z = n_row // X
    quarters, (dense_ref, send_part, keep_part, send_ref, keep_ref, panel) = refs[:X * n_col], refs[X * n_col:]
    r, c = lax.axis_index("row"), lax.axis_index("col")
    piece = H // (n_row * n_col)
    for k, ref in enumerate(quarters):
        for i in range(n_z):
            row = ((r % X ^ (k % X)) * n_z + i) * n_col + (c ^ (k // X))
            panel[pl.ds(pl.multiple_of(row * piece, piece), piece), :] = ref[i * piece:(i + 1) * piece]
    n_rows = dense_ref.shape[0] // 2
    send_ref[...] = send_part[...] + product(dense_ref[n_rows:, n_row * VB:], panel[...])
    keep_ref[...] = keep_part[...] + product(dense_ref[:n_rows, n_row * VB:], panel[...])


def own_scores(dims, src_ref, keep_ref, came_ref):
    first = H + (lax.axis_index("row") * dims[1] + lax.axis_index("col")) * VB
    tele = one_hot(first, VB, src_ref[...])
    return DAMP * (keep_ref[:VB] + came_ref[:VB]) + 0.15 * tele


def spread_kernel(dims, src_ref, keep_ref, came_ref, scores_ref, hold_ref, pass_ref):
    quarter = hold_ref.shape[0]
    x = lax.axis_index("row") % X
    for ref, place in ((hold_ref, x), (pass_ref, 1 - x)):
        spot = pl.ds(pl.multiple_of(VB + place * quarter, quarter), quarter)
        ref[...] = keep_ref[spot, :] + came_ref[spot, :]
    scores_ref[0] = own_scores(dims, src_ref, keep_ref, came_ref).astype(scores_ref.dtype)


def join_kernel(held_ref, came_ref, out_ref):
    count = held_ref.shape[0]
    out_ref[:count] = held_ref[...]
    out_ref[count:] = came_ref[...]


def add_kernel(hold_ref, came_ref, out_ref):
    out_ref[...] = hold_ref[...] + came_ref[...]


def hub_kernel(dims, src_ref, held_ref, came_ref, out_ref):
    n_row, n_col, side = dims
    piece = H // (n_row * n_col)
    r, c = lax.axis_index("row"), lax.axis_index("col")
    at = lax.broadcasted_iota(jnp.int32, out_ref.shape, 0)
    ids = ((r % X * (n_row // X) + at // piece) * n_col + c) * piece + at % piece
    tele = (ids == src_ref[...]).astype(jnp.float32)
    out_ref[...] = (DAMP * (held_ref[...] + came_ref[...]) + 0.15 * tele).astype(out_ref.dtype)


def pieces_kernel(keep_ref, came_ref, parts_ref):
    piece = parts_ref.shape[1]
    for k in range(parts_ref.shape[0]):
        spot = slice(VB + k * piece, VB + (k + 1) * piece)
        parts_ref[k] = keep_ref[spot, :] + came_ref[spot, :]


def last_kernel(dims, src_ref, keep_ref, came_ref, parts_ref, scores_ref, hubs_ref):
    scores_ref[...] = own_scores(dims, src_ref, keep_ref, came_ref)
    piece = hubs_ref.shape[0]
    summed = parts_ref[0]
    for k in range(1, parts_ref.shape[0]):
        summed = summed + parts_ref[k]
    first = (lax.axis_index("row") * dims[1] + lax.axis_index("col")) * piece
    hubs_ref[...] = DAMP * summed + 0.15 * one_hot(first, piece, src_ref[...])


def fast_body(tiles, tile_row, tile_col, tile_count, sources):
    slots, side = tiles.shape[2:4]
    width = sources.shape[0]
    n_row = lax.axis_size("row")
    n_col = lax.axis_size("col")
    piece = H // (n_row * n_col)
    dims = (n_row, n_col, side)
    n_rows = n_col * VB + H
    n_cols = n_row * VB + H
    f32 = functools.partial(jax.ShapeDtypeStruct, dtype=jnp.float32)
    bf16 = functools.partial(jax.ShapeDtypeStruct, dtype=jnp.bfloat16)
    src = sources.reshape(1, width)
    half = VB + n_row * piece
    quarter = H // n_col // X
    def other_core(x):
        return lax.ppermute(x, "col", [(0, 1), (1, 0)])

    def to_partner(x, flip):
        return lax.ppermute(x, "row", [(r, r ^ flip) for r in range(n_row)])

    def other_side(x):
        return to_partner(x, 1)

    def other_both(x):
        devices = [(r, c) for r in range(n_row) for c in range(n_col)]
        return lax.ppermute(x, ("row", "col"), [(r * n_col + c, (r ^ 1) * n_col + 1 - c) for r, c in devices])

    def call(kernel, name, out_shape, *args, scratch=(), cost=0):
        return pl.pallas_call(
            kernel,
            out_shape=out_shape,
            in_specs=[VMEM] * len(args),
            out_specs=jax.tree.map(lambda _: VMEM, out_shape),
            scratch_shapes=scratch,
            compiler_params=params(),
            cost_estimate=pl.CostEstimate(flops=cost * MICRO, bytes_accessed=0, transcendentals=0),
            name=name,
        )(*args)

    bind = functools.partial

    in_hbm = [pltpu.with_memory_space_constraint(x, pltpu.HBM) for x in (
        tiles.reshape(slots, side, side), tile_row.reshape(slots), tile_col.reshape(slots), src)]
    send, keep, dense = pl.pallas_call(
        bind(first_kernel, dims),
        out_shape=(f32((half, width)), f32((half, width)), bf16((2 * n_rows, n_cols))),
        in_specs=[HBM] * 5,
        out_specs=[VMEM] * 3,
        scratch_shapes=[
            pltpu.VMEM((slots, side, side), jnp.bfloat16),
            pltpu.SMEM((slots,), jnp.int32),
            pltpu.SMEM((slots,), jnp.int32),
            pltpu.SMEM((1,), jnp.int32),
            pltpu.VMEM((1, width), jnp.int32),
            pltpu.VMEM((n_rows + side, n_cols), jnp.float32),
            pltpu.VMEM((n_cols, width), jnp.bfloat16),
            pltpu.SemaphoreType.DMA((slots // CHUNK,)),
            pltpu.SemaphoreType.DMA((4,)),
        ],
        compiler_params=params(),
        name="first_terms",
    )(*in_hbm[:3], tile_count.reshape(1), in_hbm[3])

    masks = [n_row // X // 2]
    while masks[-1] > 1:
        masks.append(masks[-1] // 2)
    for step in range(ITERS - 1):
        came = other_core(send)
        held, hold, away = call(
            bind(spread_kernel, dims), "spread",
            (bf16((1, VB, width)), f32((quarter, width)), f32((quarter, width))),
            src, keep, came, cost=2)
        away = other_side(away)
        flips = [0]
        for mask in masks[:-1]:
            far = to_partner(held, X * mask)
            held = call(join_kernel, "join_near", bf16((2 * len(flips), VB, width)), held, far, cost=3)
            flips += [flip ^ mask for flip in flips]
        far = to_partner(held, X * masks[-1])
        flips += [flip ^ masks[-1] for flip in flips]
        near_across, far_across = other_side(held), other_side(far)
        sums = call(add_kernel, "plane_sum", f32((quarter, width)), hold, away, cost=20)
        for mask in masks[:0:-1]:
            sums = call(add_kernel, "pair_sum", f32((quarter, width)), sums, to_partner(sums, X * mask), cost=1)
        mine = call(bind(hub_kernel, dims), "hub_sums", bf16((quarter, width)), src, sums, to_partner(sums, X * masks[0]), cost=1)
        quarters = [mine, other_side(mine), other_core(mine), other_both(mine)]
        send, keep = call(
            bind(score_columns_kernel, dims, flips), "score_columns", (f32((half, width)),) * 2,
            held, far, near_across, far_across, dense, scratch=[pltpu.VMEM((n_row * VB, width), jnp.bfloat16)])
        send, keep = call(
            bind(hub_columns_kernel, dims), "hub_columns", (f32((half, width)),) * 2,
            *quarters, dense, send, keep, scratch=[pltpu.VMEM((H, width), jnp.bfloat16)])
    came = other_core(send)
    parts = call(pieces_kernel, "hub_pieces", f32((n_row, piece, width)), keep, came)
    parts = lax.all_to_all(parts, "row", 0, 0)
    scores, hubs = call(bind(last_kernel, dims), "last_sums", (f32((VB, width)), f32((piece, width))),
                        src, keep, came, parts)
    return scores.reshape(1, 1, VB, width), hubs


def plain_body(tiles, tile_row, tile_col, tile_count, sources):
    slots = tiles.shape[2]
    side = tiles.shape[3]
    width = sources.shape[0]
    tiles = tiles.reshape(slots, side, side)
    rows = tile_row.reshape(slots)
    cols = tile_col.reshape(slots)
    count = tile_count.reshape(())
    n_row = lax.axis_size("row")
    n_col = lax.axis_size("col")
    devices = n_row * n_col
    r_index = lax.axis_index("row")
    c_index = lax.axis_index("col")
    hub_dev = H // devices
    block_rows = n_col * VB
    n_tile_rows = (block_rows + H) // side
    own_base = H + (r_index * n_col + c_index) * VB
    hub_start = (r_index * n_col + c_index) * hub_dev
    own_ids = jnp.arange(VB, dtype=jnp.int32) + own_base
    tele_own = (own_ids[:, None] == sources[None, :]).astype(jnp.float32)
    piece_ids = jnp.arange(hub_dev, dtype=jnp.int32) + hub_start
    tele_piece = (piece_ids[:, None] == sources[None, :]).astype(jnp.float32)
    tele_hubs = (jnp.arange(H, dtype=jnp.int32)[:, None] == sources[None, :]).astype(jnp.float32)
    column_ids = (
        H
        + (jnp.arange(n_row, dtype=jnp.int32)[:, None] * n_col + c_index) * VB
        + jnp.arange(VB, dtype=jnp.int32)[None, :]
    ).reshape(n_row * VB)
    column_panel = (column_ids[:, None] == sources[None, :]).astype(jnp.bfloat16)
    hub_panel = tele_hubs.astype(jnp.bfloat16)
    block = math.gcd(slots, 16)
    own_scores = tele_own
    hub_piece = tele_piece
    for step in range(ITERS):
        start_acc = jnp.zeros((n_tile_rows, side, width), jnp.float32)
        if step > 0:
            column_panel = lax.all_gather(
                own_scores.astype(jnp.bfloat16), "row", axis=0, tiled=True
            )
        panel = jnp.concatenate([column_panel, hub_panel], axis=0).reshape(-1, side, width)

        def step_fn(number, total):
            start = number * block
            tile_block = lax.dynamic_slice_in_dim(tiles, start, block, 0)
            col_block = lax.dynamic_slice_in_dim(cols, start, block, 0)
            row_block = lax.dynamic_slice_in_dim(rows, start, block, 0)
            pieces = jnp.take(panel, col_block, axis=0)
            prod = jnp.einsum(
                "tij,tjs->tis", tile_block, pieces, preferred_element_type=jnp.float32
            )
            live = start + jnp.arange(block, dtype=jnp.int32) < count
            prod = jnp.where(live[:, None, None], prod, 0.0)
            return total.at[row_block].add(prod)

        total = lax.fori_loop(0, slots // block, step_fn, start_acc)
        partial_value = total.reshape(n_tile_rows * side, width)
        summed_rows = lax.psum_scatter(
            partial_value[:block_rows], "col", scatter_dimension=0, tiled=True
        )
        own_scores = 0.85 * summed_rows + 0.15 * tele_own
        hub_part = partial_value[block_rows:]
        summed = lax.psum_scatter(hub_part, ("row", "col"), scatter_dimension=0, tiled=True)
        hub_piece = 0.85 * summed + 0.15 * tele_piece
        if step + 1 < ITERS:
            hub_panel = lax.all_gather(
                hub_piece.astype(jnp.bfloat16), ("row", "col"), axis=0, tiled=True
            )
    return (own_scores.reshape(1, 1, VB, width), hub_piece)


def solution(mesh):
    placed = (
        P(("groups", "row"), "col", None, None, None),
        P(("groups", "row"), "col", None),
        P(("groups", "row"), "col", None),
        P(("groups", "row"), "col"),
        P("groups"),
    )

    def body(tiles, *rest):
        n_row, n_col = mesh.shape["row"], mesh.shape["col"]
        slots, side = tiles.shape[2:4]
        blocks = (n_col * VB + H) * (n_row * VB + H) // (side * side)
        if n_col == 2 and n_row in (8, 16) and blocks <= slots and H // (n_row * n_col) % 16 == 0:
            return fast_body(tiles, *rest)
        return plain_body(tiles, *rest)

    return jax.shard_map(
        body,
        mesh=mesh,
        in_specs=placed,
        out_specs=(P(("groups", "row"), "col", None, None), P(("groups", "row", "col"), None)),
        check_vma=False,
    )
```

```python
import functools
import math

import jax
import jax.numpy as jnp
from jax import lax
from jax.experimental import pallas as pl
from jax.experimental.pallas import tpu as pltpu
from jax.sharding import PartitionSpec as P

VB = 128
H = 256
ITERS = 2
DAMP = 0.85
CHUNK = 8
X = 2
MICRO = 10 ** 9
VMEM_LIMIT = 32 * 1024 * 1024

SMEM = pl.BlockSpec(memory_space=pltpu.SMEM)
VMEM = pl.BlockSpec(memory_space=pltpu.VMEM)
HBM = pl.BlockSpec(memory_space=pltpu.HBM)


def params():
    return pltpu.CompilerParams(vmem_limit_bytes=VMEM_LIMIT)


def one_hot(first, count, src):
    ids = lax.broadcasted_iota(jnp.int32, (count, src.shape[1]), 0) + first
    return (ids == src).astype(jnp.float32)


def product(dense, panel):
    prod = jnp.dot(dense, panel, preferred_element_type=jnp.float32)
    rows = prod.shape[0] // 2
    return prod[:rows] + prod[rows:]


def first_kernel(dims, tiles_ref, rows_hbm, cols_hbm, count_hbm, src_hbm, send_ref, keep_ref, dense_ref,
                 held, rows_ref, cols_ref, count_ref, src_ref, total, panel, sems, small):
    n_row, n_col, side = dims
    n_rows = dense_ref.shape[0] // 2
    piece = H // (n_row * n_col)
    c = lax.axis_index("col")
    pairs = ((src_hbm, src_ref), (rows_hbm, rows_ref), (cols_hbm, cols_ref), (count_hbm, count_ref))
    scalars = [pltpu.make_async_copy(a, b, small.at[i]) for i, (a, b) in enumerate(pairs)]
    copies = []
    for i in range(held.shape[0] // CHUNK):
        part = pl.ds(i * CHUNK, CHUNK)
        copies.append(pltpu.make_async_copy(tiles_ref.at[part], held.at[part], sems.at[i]))
    for copy in scalars + copies:
        copy.start()
    total[...] = jnp.zeros_like(total)
    for copy in scalars:
        copy.wait()
    src = src_ref[...]
    for r in range(n_row):
        first = H + (r * n_col + c) * VB
        panel[pl.ds(r * VB, VB), :] = one_hot(first, VB, src).astype(jnp.bfloat16)
    panel[pl.ds(n_row * VB, H), :] = one_hot(0, H, src).astype(jnp.bfloat16)
    count = count_ref[0]

    def add_tile(k, carry):
        live = k < count
        row = pl.multiple_of(jnp.where(live, rows_ref[k] * side, n_rows), side)
        col = pl.multiple_of(jnp.where(live, cols_ref[k] * side, 0), side)
        spot = (pl.ds(row, side), pl.ds(col, side))
        total[spot] += held[k].astype(jnp.float32)
        return carry

    for i, copy in enumerate(copies):
        copy.wait()
        lax.fori_loop(i * CHUNK, (i + 1) * CHUNK, add_tile, 0, unroll=4)
    half = n_rows // n_col
    for at, out, core in ((0, keep_ref, c), (n_rows, send_ref, 1 - c)):
        chunks = [(0, core * VB, VB)]
        for r in range(n_row):
            chunks.append((VB + r * piece, n_col * VB + (r * n_col + core) * piece, piece))
        for to, start, size in chunks:
            whole = total[pl.ds(pl.multiple_of(start, size), size), :]
            high = whole.astype(jnp.bfloat16)
            dense_ref[at + to:at + to + size] = high
            dense_ref[at + half + to:at + half + to + size] = (whole - high.astype(jnp.float32)).astype(jnp.bfloat16)
        out[...] = product(dense_ref[at:at + 2 * half], panel[...])


def score_columns_kernel(dims, *refs):
    n_row, n_col, side = dims
    blocks, (dense_ref, send_ref, keep_ref, panel) = refs[:4], refs[4:]
    r = lax.axis_index("row")
    for ref, flip in zip(blocks, (0, 2 * X, 1, 2 * X + 1)):
        for k in range(2):
            owner = r ^ (flip + X * k)
            panel[pl.ds(pl.multiple_of(owner * VB, VB), VB), :] = ref[k]
    n_rows = dense_ref.shape[0] // 2
    keep_ref[...] = product(dense_ref[:n_rows, :n_row * VB], panel[...])
    send_ref[...] = product(dense_ref[n_rows:, :n_row * VB], panel[...])


def hub_columns_kernel(dims, *refs):
    n_row, n_col, side = dims
    n_z = n_row // X
    quarters, (dense_ref, send_part, keep_part, send_ref, keep_ref, panel) = refs[:X * n_col], refs[X * n_col:]
    r, c = lax.axis_index("row"), lax.axis_index("col")
    piece = H // (n_row * n_col)
    for k, ref in enumerate(quarters):
        for i in range(n_z):
            row = ((r % X ^ (k % X)) * n_z + i) * n_col + (c ^ (k // X))
            panel[pl.ds(pl.multiple_of(row * piece, piece), piece), :] = ref[i * piece:(i + 1) * piece]
    n_rows = dense_ref.shape[0] // 2
    send_ref[...] = send_part[...] + product(dense_ref[n_rows:, n_row * VB:], panel[...])
    keep_ref[...] = keep_part[...] + product(dense_ref[:n_rows, n_row * VB:], panel[...])


def own_scores(dims, src_ref, keep_ref, came_ref):
    first = H + (lax.axis_index("row") * dims[1] + lax.axis_index("col")) * VB
    tele = one_hot(first, VB, src_ref[...])
    return DAMP * (keep_ref[:VB] + came_ref[:VB]) + 0.15 * tele


def spread_kernel(dims, src_ref, keep_ref, came_ref, scores_ref, hold_ref, pass_ref):
    quarter = hold_ref.shape[0]
    x = lax.axis_index("row") % X
    for ref, place in ((hold_ref, x), (pass_ref, 1 - x)):
        spot = pl.ds(pl.multiple_of(VB + place * quarter, quarter), quarter)
        ref[...] = keep_ref[spot, :] + came_ref[spot, :]
    scores_ref[0] = own_scores(dims, src_ref, keep_ref, came_ref).astype(scores_ref.dtype)


def join_kernel(held_ref, came_ref, out_ref):
    count = held_ref.shape[0]
    out_ref[:count] = held_ref[...]
    out_ref[count:] = came_ref[...]


def add_kernel(hold_ref, came_ref, out_ref):
    out_ref[...] = hold_ref[...] + came_ref[...]


def hub_kernel(dims, src_ref, held_ref, came_ref, out_ref):
    n_row, n_col, side = dims
    piece = H // (n_row * n_col)
    r, c = lax.axis_index("row"), lax.axis_index("col")
    at = lax.broadcasted_iota(jnp.int32, out_ref.shape, 0)
    ids = ((r % X * (n_row // X) + at // piece) * n_col + c) * piece + at % piece
    tele = (ids == src_ref[...]).astype(jnp.float32)
    out_ref[...] = (DAMP * (held_ref[...] + came_ref[...]) + 0.15 * tele).astype(out_ref.dtype)


def pieces_kernel(keep_ref, came_ref, parts_ref):
    piece = parts_ref.shape[1]
    for k in range(parts_ref.shape[0]):
        spot = slice(VB + k * piece, VB + (k + 1) * piece)
        parts_ref[k] = keep_ref[spot, :] + came_ref[spot, :]


def last_kernel(dims, src_ref, keep_ref, came_ref, parts_ref, scores_ref, hubs_ref):
    scores_ref[...] = own_scores(dims, src_ref, keep_ref, came_ref)
    piece = hubs_ref.shape[0]
    summed = parts_ref[0]
    for k in range(1, parts_ref.shape[0]):
        summed = summed + parts_ref[k]
    first = (lax.axis_index("row") * dims[1] + lax.axis_index("col")) * piece
    hubs_ref[...] = DAMP * summed + 0.15 * one_hot(first, piece, src_ref[...])


def fast_body(tiles, tile_row, tile_col, tile_count, sources):
    slots, side = tiles.shape[2:4]
    width = sources.shape[0]
    n_row = lax.axis_size("row")
    n_col = lax.axis_size("col")
    piece = H // (n_row * n_col)
    dims = (n_row, n_col, side)
    n_rows = n_col * VB + H
    n_cols = n_row * VB + H
    f32 = functools.partial(jax.ShapeDtypeStruct, dtype=jnp.float32)
    bf16 = functools.partial(jax.ShapeDtypeStruct, dtype=jnp.bfloat16)
    src = sources.reshape(1, width)
    half = VB + n_row * piece
    quarter = H // n_col // X
    def other_core(x):
        return lax.ppermute(x, "col", [(0, 1), (1, 0)])

    def to_partner(x, flip):
        return lax.ppermute(x, "row", [(r, r ^ flip) for r in range(n_row)])

    def other_side(x):
        return to_partner(x, 1)

    def other_both(x):
        devices = [(r, c) for r in range(n_row) for c in range(n_col)]
        return lax.ppermute(x, ("row", "col"), [(r * n_col + c, (r ^ 1) * n_col + 1 - c) for r, c in devices])

    def call(kernel, name, out_shape, *args, scratch=(), cost=0):
        return pl.pallas_call(
            kernel,
            out_shape=out_shape,
            in_specs=[VMEM] * len(args),
            out_specs=jax.tree.map(lambda _: VMEM, out_shape),
            scratch_shapes=scratch,
            compiler_params=params(),
            cost_estimate=pl.CostEstimate(flops=cost * MICRO, bytes_accessed=0, transcendentals=0),
            name=name,
        )(*args)

    bind = functools.partial

    in_hbm = [pltpu.with_memory_space_constraint(x, pltpu.HBM) for x in (
        tiles.reshape(slots, side, side), tile_row.reshape(slots), tile_col.reshape(slots), src)]
    send, keep, dense = pl.pallas_call(
        bind(first_kernel, dims),
        out_shape=(f32((half, width)), f32((half, width)), bf16((2 * n_rows, n_cols))),
        in_specs=[HBM] * 5,
        out_specs=[VMEM] * 3,
        scratch_shapes=[
            pltpu.VMEM((slots, side, side), jnp.bfloat16),
            pltpu.SMEM((slots,), jnp.int32),
            pltpu.SMEM((slots,), jnp.int32),
            pltpu.SMEM((1,), jnp.int32),
            pltpu.VMEM((1, width), jnp.int32),
            pltpu.VMEM((n_rows + side, n_cols), jnp.float32),
            pltpu.VMEM((n_cols, width), jnp.bfloat16),
            pltpu.SemaphoreType.DMA((slots // CHUNK,)),
            pltpu.SemaphoreType.DMA((4,)),
        ],
        compiler_params=params(),
        name="first_terms",
    )(*in_hbm[:3], tile_count.reshape(1), in_hbm[3])

    for step in range(ITERS - 1):
        came = other_core(send)
        held, hold, away = call(
            bind(spread_kernel, dims), "spread",
            (bf16((1, VB, width)), f32((quarter, width)), f32((quarter, width))),
            src, keep, came, cost=2)
        away = other_side(away)
        pair = bf16((2, VB, width))
        next_z, far_z = to_partner(held, X), to_partner(held, 2 * X)
        near = call(join_kernel, "join_near", pair, held, next_z, cost=1)
        far = call(join_kernel, "join_far", pair, far_z, to_partner(far_z, X), cost=2)
        near_across, far_across = other_side(near), other_side(far)
        sums = call(add_kernel, "plane_sum", f32((quarter, width)), hold, away, cost=20)
        sums = call(add_kernel, "pair_sum", f32((quarter, width)), sums, to_partner(sums, X), cost=2)
        mine = call(bind(hub_kernel, dims), "hub_sums", bf16((quarter, width)), src, sums, to_partner(sums, 2 * X), cost=8)
        quarters = [mine, other_side(mine), other_core(mine), other_both(mine)]
        send, keep = call(
            bind(score_columns_kernel, dims), "score_columns", (f32((half, width)),) * 2,
            near, far, near_across, far_across, dense, scratch=[pltpu.VMEM((n_row * VB, width), jnp.bfloat16)])
        send, keep = call(
            bind(hub_columns_kernel, dims), "hub_columns", (f32((half, width)),) * 2,
            *quarters, dense, send, keep, scratch=[pltpu.VMEM((H, width), jnp.bfloat16)])
    came = other_core(send)
    parts = call(pieces_kernel, "hub_pieces", f32((n_row, piece, width)), keep, came)
    parts = lax.all_to_all(parts, "row", 0, 0)
    scores, hubs = call(bind(last_kernel, dims), "last_sums", (f32((VB, width)), f32((piece, width))),
                        src, keep, came, parts)
    return scores.reshape(1, 1, VB, width), hubs


def plain_body(tiles, tile_row, tile_col, tile_count, sources):
    slots = tiles.shape[2]
    side = tiles.shape[3]
    width = sources.shape[0]
    tiles = tiles.reshape(slots, side, side)
    rows = tile_row.reshape(slots)
    cols = tile_col.reshape(slots)
    count = tile_count.reshape(())
    n_row = lax.axis_size("row")
    n_col = lax.axis_size("col")
    devices = n_row * n_col
    r_index = lax.axis_index("row")
    c_index = lax.axis_index("col")
    hub_dev = H // devices
    block_rows = n_col * VB
    n_tile_rows = (block_rows + H) // side
    own_base = H + (r_index * n_col + c_index) * VB
    hub_start = (r_index * n_col + c_index) * hub_dev
    own_ids = jnp.arange(VB, dtype=jnp.int32) + own_base
    tele_own = (own_ids[:, None] == sources[None, :]).astype(jnp.float32)
    piece_ids = jnp.arange(hub_dev, dtype=jnp.int32) + hub_start
    tele_piece = (piece_ids[:, None] == sources[None, :]).astype(jnp.float32)
    tele_hubs = (jnp.arange(H, dtype=jnp.int32)[:, None] == sources[None, :]).astype(jnp.float32)
    column_ids = (
        H
        + (jnp.arange(n_row, dtype=jnp.int32)[:, None] * n_col + c_index) * VB
        + jnp.arange(VB, dtype=jnp.int32)[None, :]
    ).reshape(n_row * VB)
    column_panel = (column_ids[:, None] == sources[None, :]).astype(jnp.bfloat16)
    hub_panel = tele_hubs.astype(jnp.bfloat16)
    block = math.gcd(slots, 16)
    own_scores = tele_own
    hub_piece = tele_piece
    for step in range(ITERS):
        start_acc = jnp.zeros((n_tile_rows, side, width), jnp.float32)
        if step > 0:
            column_panel = lax.all_gather(
                own_scores.astype(jnp.bfloat16), "row", axis=0, tiled=True
            )
        panel = jnp.concatenate([column_panel, hub_panel], axis=0).reshape(-1, side, width)

        def step_fn(number, total):
            start = number * block
            tile_block = lax.dynamic_slice_in_dim(tiles, start, block, 0)
            col_block = lax.dynamic_slice_in_dim(cols, start, block, 0)
            row_block = lax.dynamic_slice_in_dim(rows, start, block, 0)
            pieces = jnp.take(panel, col_block, axis=0)
            prod = jnp.einsum(
                "tij,tjs->tis", tile_block, pieces, preferred_element_type=jnp.float32
            )
            live = start + jnp.arange(block, dtype=jnp.int32) < count
            prod = jnp.where(live[:, None, None], prod, 0.0)
            return total.at[row_block].add(prod)

        total = lax.fori_loop(0, slots // block, step_fn, start_acc)
        partial_value = total.reshape(n_tile_rows * side, width)
        summed_rows = lax.psum_scatter(
            partial_value[:block_rows], "col", scatter_dimension=0, tiled=True
        )
        own_scores = 0.85 * summed_rows + 0.15 * tele_own
        hub_part = partial_value[block_rows:]
        summed = lax.psum_scatter(hub_part, ("row", "col"), scatter_dimension=0, tiled=True)
        hub_piece = 0.85 * summed + 0.15 * tele_piece
        if step + 1 < ITERS:
            hub_panel = lax.all_gather(
                hub_piece.astype(jnp.bfloat16), ("row", "col"), axis=0, tiled=True
            )
    return (own_scores.reshape(1, 1, VB, width), hub_piece)


def solution(mesh):
    placed = (
        P(("groups", "row"), "col", None, None, None),
        P(("groups", "row"), "col", None),
        P(("groups", "row"), "col", None),
        P(("groups", "row"), "col"),
        P("groups"),
    )

    def body(tiles, *rest):
        n_row, n_col = mesh.shape["row"], mesh.shape["col"]
        slots, side = tiles.shape[2:4]
        blocks = (n_col * VB + H) * (n_row * VB + H) // (side * side)
        if n_col == 2 and n_row == 4 * X and blocks <= slots and H // (n_row * n_col) % 16 == 0:
            return fast_body(tiles, *rest)
        return plain_body(tiles, *rest)

    return jax.shard_map(
        body,
        mesh=mesh,
        in_specs=placed,
        out_specs=(P(("groups", "row"), "col", None, None), P(("groups", "row", "col"), None)),
        check_vma=False,
    )
```

```python
import functools
import math

import jax
import jax.numpy as jnp
from jax import lax
from jax.experimental import pallas as pl
from jax.experimental.pallas import tpu as pltpu
from jax.sharding import PartitionSpec as P

VB = 128
H = 256
ITERS = 2
DAMP = 0.85
CHUNK = 8
X = 2
MICRO = 10 ** 9
VMEM_LIMIT = 32 * 1024 * 1024

SMEM = pl.BlockSpec(memory_space=pltpu.SMEM)
VMEM = pl.BlockSpec(memory_space=pltpu.VMEM)
HBM = pl.BlockSpec(memory_space=pltpu.HBM)


def params():
    return pltpu.CompilerParams(vmem_limit_bytes=VMEM_LIMIT)


def one_hot(first, count, src):
    ids = lax.broadcasted_iota(jnp.int32, (count, src.shape[1]), 0) + first
    return (ids == src).astype(jnp.float32)


def product(dense, panel):
    prod = jnp.dot(dense, panel, preferred_element_type=jnp.float32)
    rows = prod.shape[0] // 2
    return prod[:rows] + prod[rows:]


def first_kernel(dims, tiles_ref, rows_hbm, cols_hbm, count_hbm, src_hbm, send_ref, keep_ref, dense_ref,
                 held, rows_ref, cols_ref, count_ref, src_ref, total, panel, sems, small):
    n_row, n_col, side = dims
    n_rows = dense_ref.shape[0] // 2
    piece = H // (n_row * n_col)
    c = lax.axis_index("col")
    pairs = ((src_hbm, src_ref), (rows_hbm, rows_ref), (cols_hbm, cols_ref), (count_hbm, count_ref))
    scalars = [pltpu.make_async_copy(a, b, small.at[i]) for i, (a, b) in enumerate(pairs)]
    copies = []
    for i in range(held.shape[0] // CHUNK):
        part = pl.ds(i * CHUNK, CHUNK)
        copies.append(pltpu.make_async_copy(tiles_ref.at[part], held.at[part], sems.at[i]))
    for copy in scalars + copies:
        copy.start()
    total[...] = jnp.zeros_like(total)
    for copy in scalars:
        copy.wait()
    src = src_ref[...]
    for r in range(n_row):
        first = H + (r * n_col + c) * VB
        panel[pl.ds(r * VB, VB), :] = one_hot(first, VB, src).astype(jnp.bfloat16)
    panel[pl.ds(n_row * VB, H), :] = one_hot(0, H, src).astype(jnp.bfloat16)
    count = count_ref[0]

    def add_tile(k, carry):
        live = k < count
        row = pl.multiple_of(jnp.where(live, rows_ref[k] * side, n_rows), side)
        col = pl.multiple_of(jnp.where(live, cols_ref[k] * side, 0), side)
        spot = (pl.ds(row, side), pl.ds(col, side))
        total[spot] += held[k].astype(jnp.float32)
        return carry

    for i, copy in enumerate(copies):
        copy.wait()
        lax.fori_loop(i * CHUNK, (i + 1) * CHUNK, add_tile, 0, unroll=4)
    half = n_rows // n_col
    for at, out, core in ((0, keep_ref, c), (n_rows, send_ref, 1 - c)):
        chunks = [(0, core * VB, VB)]
        for r in range(n_row):
            chunks.append((VB + r * piece, n_col * VB + (r * n_col + core) * piece, piece))
        for to, start, size in chunks:
            whole = total[pl.ds(pl.multiple_of(start, size), size), :]
            high = whole.astype(jnp.bfloat16)
            dense_ref[at + to:at + to + size] = high
            dense_ref[at + half + to:at + half + to + size] = (whole - high.astype(jnp.float32)).astype(jnp.bfloat16)
        out[...] = product(dense_ref[at:at + 2 * half], panel[...])


def score_columns_kernel(dims, *refs):
    n_row, n_col, side = dims
    blocks, (dense_ref, send_ref, keep_ref, panel) = refs[:4], refs[4:]
    r = lax.axis_index("row")
    for ref, flips in zip(blocks, ((0, X, 2 * X), (3 * X,), (1, X + 1, 2 * X + 1), (3 * X + 1,))):
        for k, flip in enumerate(flips):
            panel[pl.ds(pl.multiple_of((r ^ flip) * VB, VB), VB), :] = ref[k]
    n_rows = dense_ref.shape[0] // 2
    keep_ref[...] = product(dense_ref[:n_rows, :n_row * VB], panel[...])
    send_ref[...] = product(dense_ref[n_rows:, :n_row * VB], panel[...])


def hub_columns_kernel(dims, *refs):
    n_row, n_col, side = dims
    n_z = n_row // X
    quarters, (dense_ref, send_part, keep_part, send_ref, keep_ref, panel) = refs[:X * n_col], refs[X * n_col:]
    r, c = lax.axis_index("row"), lax.axis_index("col")
    piece = H // (n_row * n_col)
    for k, ref in enumerate(quarters):
        for i in range(n_z):
            row = ((r % X ^ (k % X)) * n_z + i) * n_col + (c ^ (k // X))
            panel[pl.ds(pl.multiple_of(row * piece, piece), piece), :] = ref[i * piece:(i + 1) * piece]
    n_rows = dense_ref.shape[0] // 2
    send_ref[...] = send_part[...] + product(dense_ref[n_rows:, n_row * VB:], panel[...])
    keep_ref[...] = keep_part[...] + product(dense_ref[:n_rows, n_row * VB:], panel[...])


def own_scores(dims, src_ref, keep_ref, came_ref):
    first = H + (lax.axis_index("row") * dims[1] + lax.axis_index("col")) * VB
    tele = one_hot(first, VB, src_ref[...])
    return DAMP * (keep_ref[:VB] + came_ref[:VB]) + 0.15 * tele


def spread_kernel(dims, src_ref, keep_ref, came_ref, scores_ref, hold_ref, pass_ref):
    quarter = hold_ref.shape[0]
    x = lax.axis_index("row") % X
    for ref, place in ((hold_ref, x), (pass_ref, 1 - x)):
        spot = pl.ds(pl.multiple_of(VB + place * quarter, quarter), quarter)
        ref[...] = keep_ref[spot, :] + came_ref[spot, :]
    scores_ref[0] = own_scores(dims, src_ref, keep_ref, came_ref).astype(scores_ref.dtype)


def join_kernel(*refs):
    for k, ref in enumerate(refs[:-1]):
        refs[-1][k] = ref[0]


def add_kernel(hold_ref, came_ref, out_ref):
    out_ref[...] = hold_ref[...] + came_ref[...]


def hub_kernel(dims, src_ref, held_ref, came_ref, out_ref):
    n_row, n_col, side = dims
    piece = H // (n_row * n_col)
    r, c = lax.axis_index("row"), lax.axis_index("col")
    at = lax.broadcasted_iota(jnp.int32, out_ref.shape, 0)
    ids = ((r % X * (n_row // X) + at // piece) * n_col + c) * piece + at % piece
    tele = (ids == src_ref[...]).astype(jnp.float32)
    out_ref[...] = (DAMP * (held_ref[...] + came_ref[...]) + 0.15 * tele).astype(out_ref.dtype)


def pieces_kernel(keep_ref, came_ref, parts_ref):
    piece = parts_ref.shape[1]
    for k in range(parts_ref.shape[0]):
        spot = slice(VB + k * piece, VB + (k + 1) * piece)
        parts_ref[k] = keep_ref[spot, :] + came_ref[spot, :]


def last_kernel(dims, src_ref, keep_ref, came_ref, parts_ref, scores_ref, hubs_ref):
    scores_ref[...] = own_scores(dims, src_ref, keep_ref, came_ref)
    piece = hubs_ref.shape[0]
    summed = parts_ref[0]
    for k in range(1, parts_ref.shape[0]):
        summed = summed + parts_ref[k]
    first = (lax.axis_index("row") * dims[1] + lax.axis_index("col")) * piece
    hubs_ref[...] = DAMP * summed + 0.15 * one_hot(first, piece, src_ref[...])


def fast_body(tiles, tile_row, tile_col, tile_count, sources):
    slots, side = tiles.shape[2:4]
    width = sources.shape[0]
    n_row = lax.axis_size("row")
    n_col = lax.axis_size("col")
    piece = H // (n_row * n_col)
    dims = (n_row, n_col, side)
    n_rows = n_col * VB + H
    n_cols = n_row * VB + H
    f32 = functools.partial(jax.ShapeDtypeStruct, dtype=jnp.float32)
    bf16 = functools.partial(jax.ShapeDtypeStruct, dtype=jnp.bfloat16)
    src = sources.reshape(1, width)
    half = VB + n_row * piece
    quarter = H // n_col // X
    def other_core(x):
        return lax.ppermute(x, "col", [(0, 1), (1, 0)])

    def to_partner(x, flip):
        return lax.ppermute(x, "row", [(r, r ^ flip) for r in range(n_row)])

    def other_side(x):
        return to_partner(x, 1)

    def other_both(x):
        devices = [(r, c) for r in range(n_row) for c in range(n_col)]
        return lax.ppermute(x, ("row", "col"), [(r * n_col + c, (r ^ 1) * n_col + 1 - c) for r, c in devices])

    def call(kernel, name, out_shape, *args, scratch=(), cost=0):
        return pl.pallas_call(
            kernel,
            out_shape=out_shape,
            in_specs=[VMEM] * len(args),
            out_specs=jax.tree.map(lambda _: VMEM, out_shape),
            scratch_shapes=scratch,
            compiler_params=params(),
            cost_estimate=pl.CostEstimate(flops=cost * MICRO, bytes_accessed=0, transcendentals=0),
            name=name,
        )(*args)

    bind = functools.partial

    in_hbm = [pltpu.with_memory_space_constraint(x, pltpu.HBM) for x in (
        tiles.reshape(slots, side, side), tile_row.reshape(slots), tile_col.reshape(slots), src)]
    send, keep, dense = pl.pallas_call(
        bind(first_kernel, dims),
        out_shape=(f32((half, width)), f32((half, width)), bf16((2 * n_rows, n_cols))),
        in_specs=[HBM] * 5,
        out_specs=[VMEM] * 3,
        scratch_shapes=[
            pltpu.VMEM((slots, side, side), jnp.bfloat16),
            pltpu.SMEM((slots,), jnp.int32),
            pltpu.SMEM((slots,), jnp.int32),
            pltpu.SMEM((1,), jnp.int32),
            pltpu.VMEM((1, width), jnp.int32),
            pltpu.VMEM((n_rows + side, n_cols), jnp.float32),
            pltpu.VMEM((n_cols, width), jnp.bfloat16),
            pltpu.SemaphoreType.DMA((slots // CHUNK,)),
            pltpu.SemaphoreType.DMA((4,)),
        ],
        compiler_params=params(),
        name="first_terms",
    )(*in_hbm[:3], tile_count.reshape(1), in_hbm[3])

    for step in range(ITERS - 1):
        came = other_core(send)
        held, hold, away = call(
            bind(spread_kernel, dims), "spread",
            (bf16((1, VB, width)), f32((quarter, width)), f32((quarter, width))),
            src, keep, came, cost=2)
        away = other_side(away)
        next_z, far_z = to_partner(held, X), to_partner(held, 2 * X)
        last = to_partner(far_z, X)
        first = call(join_kernel, "join_first", bf16((3, VB, width)), held, next_z, far_z)
        first_across, last_across = other_side(first), other_side(last)
        sums = call(add_kernel, "plane_sum", f32((quarter, width)), hold, away, cost=20)
        sums = call(add_kernel, "pair_sum", f32((quarter, width)), sums, to_partner(sums, X), cost=1)
        mine = call(bind(hub_kernel, dims), "hub_sums", bf16((quarter, width)), src, sums, to_partner(sums, 2 * X), cost=1)
        quarters = [mine, other_side(mine), other_core(mine), other_both(mine)]
        send, keep = call(
            bind(score_columns_kernel, dims), "score_columns", (f32((half, width)),) * 2,
            first, last, first_across, last_across, dense, scratch=[pltpu.VMEM((n_row * VB, width), jnp.bfloat16)])
        send, keep = call(
            bind(hub_columns_kernel, dims), "hub_columns", (f32((half, width)),) * 2,
            *quarters, dense, send, keep, scratch=[pltpu.VMEM((H, width), jnp.bfloat16)])
    came = other_core(send)
    parts = call(pieces_kernel, "hub_pieces", f32((n_row, piece, width)), keep, came)
    parts = lax.all_to_all(parts, "row", 0, 0)
    scores, hubs = call(bind(last_kernel, dims), "last_sums", (f32((VB, width)), f32((piece, width))),
                        src, keep, came, parts)
    return scores.reshape(1, 1, VB, width), hubs


def plain_body(tiles, tile_row, tile_col, tile_count, sources):
    slots = tiles.shape[2]
    side = tiles.shape[3]
    width = sources.shape[0]
    tiles = tiles.reshape(slots, side, side)
    rows = tile_row.reshape(slots)
    cols = tile_col.reshape(slots)
    count = tile_count.reshape(())
    n_row = lax.axis_size("row")
    n_col = lax.axis_size("col")
    devices = n_row * n_col
    r_index = lax.axis_index("row")
    c_index = lax.axis_index("col")
    hub_dev = H // devices
    block_rows = n_col * VB
    n_tile_rows = (block_rows + H) // side
    own_base = H + (r_index * n_col + c_index) * VB
    hub_start = (r_index * n_col + c_index) * hub_dev
    own_ids = jnp.arange(VB, dtype=jnp.int32) + own_base
    tele_own = (own_ids[:, None] == sources[None, :]).astype(jnp.float32)
    piece_ids = jnp.arange(hub_dev, dtype=jnp.int32) + hub_start
    tele_piece = (piece_ids[:, None] == sources[None, :]).astype(jnp.float32)
    tele_hubs = (jnp.arange(H, dtype=jnp.int32)[:, None] == sources[None, :]).astype(jnp.float32)
    column_ids = (
        H
        + (jnp.arange(n_row, dtype=jnp.int32)[:, None] * n_col + c_index) * VB
        + jnp.arange(VB, dtype=jnp.int32)[None, :]
    ).reshape(n_row * VB)
    column_panel = (column_ids[:, None] == sources[None, :]).astype(jnp.bfloat16)
    hub_panel = tele_hubs.astype(jnp.bfloat16)
    block = math.gcd(slots, 16)
    own_scores = tele_own
    hub_piece = tele_piece
    for step in range(ITERS):
        start_acc = jnp.zeros((n_tile_rows, side, width), jnp.float32)
        if step > 0:
            column_panel = lax.all_gather(
                own_scores.astype(jnp.bfloat16), "row", axis=0, tiled=True
            )
        panel = jnp.concatenate([column_panel, hub_panel], axis=0).reshape(-1, side, width)

        def step_fn(number, total):
            start = number * block
            tile_block = lax.dynamic_slice_in_dim(tiles, start, block, 0)
            col_block = lax.dynamic_slice_in_dim(cols, start, block, 0)
            row_block = lax.dynamic_slice_in_dim(rows, start, block, 0)
            pieces = jnp.take(panel, col_block, axis=0)
            prod = jnp.einsum(
                "tij,tjs->tis", tile_block, pieces, preferred_element_type=jnp.float32
            )
            live = start + jnp.arange(block, dtype=jnp.int32) < count
            prod = jnp.where(live[:, None, None], prod, 0.0)
            return total.at[row_block].add(prod)

        total = lax.fori_loop(0, slots // block, step_fn, start_acc)
        partial_value = total.reshape(n_tile_rows * side, width)
        summed_rows = lax.psum_scatter(
            partial_value[:block_rows], "col", scatter_dimension=0, tiled=True
        )
        own_scores = 0.85 * summed_rows + 0.15 * tele_own
        hub_part = partial_value[block_rows:]
        summed = lax.psum_scatter(hub_part, ("row", "col"), scatter_dimension=0, tiled=True)
        hub_piece = 0.85 * summed + 0.15 * tele_piece
        if step + 1 < ITERS:
            hub_panel = lax.all_gather(
                hub_piece.astype(jnp.bfloat16), ("row", "col"), axis=0, tiled=True
            )
    return (own_scores.reshape(1, 1, VB, width), hub_piece)


def solution(mesh):
    placed = (
        P(("groups", "row"), "col", None, None, None),
        P(("groups", "row"), "col", None),
        P(("groups", "row"), "col", None),
        P(("groups", "row"), "col"),
        P("groups"),
    )

    def body(tiles, *rest):
        n_row, n_col = mesh.shape["row"], mesh.shape["col"]
        slots, side = tiles.shape[2:4]
        blocks = (n_col * VB + H) * (n_row * VB + H) // (side * side)
        if n_col == 2 and n_row == 4 * X and blocks <= slots and H // (n_row * n_col) % 16 == 0:
            return fast_body(tiles, *rest)
        return plain_body(tiles, *rest)

    return jax.shard_map(
        body,
        mesh=mesh,
        in_specs=placed,
        out_specs=(P(("groups", "row"), "col", None, None), P(("groups", "row", "col"), None)),
        check_vma=False,
    )
```

```python
import functools
import math

import jax
import jax.numpy as jnp
from jax import lax
from jax.experimental import pallas as pl
from jax.experimental.pallas import tpu as pltpu
from jax.sharding import PartitionSpec as P

VB = 128
H = 256
ITERS = 2
DAMP = 0.85
CHUNK = 8
X = 2
MICRO = 10 ** 9
VMEM_LIMIT = 32 * 1024 * 1024

SMEM = pl.BlockSpec(memory_space=pltpu.SMEM)
VMEM = pl.BlockSpec(memory_space=pltpu.VMEM)
HBM = pl.BlockSpec(memory_space=pltpu.HBM)


def params():
    return pltpu.CompilerParams(vmem_limit_bytes=VMEM_LIMIT)


def one_hot(first, count, src):
    ids = lax.broadcasted_iota(jnp.int32, (count, src.shape[1]), 0) + first
    return (ids == src).astype(jnp.float32)


def hub_half():
    r = lax.axis_index("row")
    return lax.axis_index("col") ^ (r & 1) ^ (r >> 1 & 1) ^ (r >> 2 & 1)


def product(dense, panel):
    prod = jnp.dot(dense, panel, preferred_element_type=jnp.float32)
    rows = prod.shape[0] // 2
    return prod[:rows] + prod[rows:]


def first_kernel(dims, tiles_ref, rows_hbm, cols_hbm, count_hbm, src_hbm, send_ref, keep_ref, dense_ref,
                 held, rows_ref, cols_ref, count_ref, src_ref, total, panel, sems, small):
    n_row, n_col, side = dims
    n_rows = dense_ref.shape[0] // 2
    piece = H // (n_row * n_col)
    c = lax.axis_index("col")
    pairs = ((src_hbm, src_ref), (rows_hbm, rows_ref), (cols_hbm, cols_ref), (count_hbm, count_ref))
    scalars = [pltpu.make_async_copy(a, b, small.at[i]) for i, (a, b) in enumerate(pairs)]
    copies = []
    for i in range(held.shape[0] // CHUNK):
        part = pl.ds(i * CHUNK, CHUNK)
        copies.append(pltpu.make_async_copy(tiles_ref.at[part], held.at[part], sems.at[i]))
    for copy in scalars + copies:
        copy.start()
    total[...] = jnp.zeros_like(total)
    for copy in scalars:
        copy.wait()
    src = src_ref[...]
    for r in range(n_row):
        first = H + (r * n_col + c) * VB
        panel[pl.ds(r * VB, VB), :] = one_hot(first, VB, src).astype(jnp.bfloat16)
    panel[pl.ds(n_row * VB, H), :] = one_hot(0, H, src).astype(jnp.bfloat16)
    count = count_ref[0]

    def add_tile(k, carry):
        live = k < count
        row = pl.multiple_of(jnp.where(live, rows_ref[k] * side, n_rows), side)
        col = pl.multiple_of(jnp.where(live, cols_ref[k] * side, 0), side)
        spot = (pl.ds(row, side), pl.ds(col, side))
        total[spot] += held[k].astype(jnp.float32)
        return carry

    for i, copy in enumerate(copies):
        copy.wait()
        lax.fori_loop(i * CHUNK, (i + 1) * CHUNK, add_tile, 0, unroll=4)
    half = n_rows // n_col
    h = hub_half()
    for at, out, core, hubs in ((0, keep_ref, c, h), (n_rows, send_ref, 1 - c, 1 - h)):
        chunks = [(0, core * VB, VB)]
        for r in range(n_row):
            chunks.append((VB + r * piece, n_col * VB + (r * n_col + hubs) * piece, piece))
        for to, start, size in chunks:
            whole = total[pl.ds(pl.multiple_of(start, size), size), :]
            high = whole.astype(jnp.bfloat16)
            dense_ref[at + to:at + to + size] = high
            dense_ref[at + half + to:at + half + to + size] = (whole - high.astype(jnp.float32)).astype(jnp.bfloat16)
        out[...] = product(dense_ref[at:at + 2 * half], panel[...])


def score_columns_kernel(dims, *refs):
    n_row, n_col, side = dims
    blocks, (dense_ref, send_ref, keep_ref, panel) = refs[:4], refs[4:]
    r = lax.axis_index("row")
    for ref, flips in zip(blocks, ((0, X, 2 * X), (3 * X,), (1, X + 1, 2 * X + 1), (3 * X + 1,))):
        for k, flip in enumerate(flips):
            panel[pl.ds(pl.multiple_of((r ^ flip) * VB, VB), VB), :] = ref[k]
    n_rows = dense_ref.shape[0] // 2
    keep_ref[...] = product(dense_ref[:n_rows, :n_row * VB], panel[...])
    send_ref[...] = product(dense_ref[n_rows:, :n_row * VB], panel[...])


def hub_columns_kernel(dims, *refs):
    n_row, n_col, side = dims
    n_z = n_row // X
    quarters, (dense_ref, send_part, keep_part, send_ref, keep_ref, panel) = refs[:X * n_col], refs[X * n_col:]
    r, h = lax.axis_index("row"), hub_half()
    piece = H // (n_row * n_col)
    for k, ref in enumerate(quarters):
        for i in range(n_z):
            row = ((r % X ^ (k % X)) * n_z + i) * n_col + (h ^ (k % X) ^ (k // X))
            panel[pl.ds(pl.multiple_of(row * piece, piece), piece), :] = ref[i * piece:(i + 1) * piece]
    n_rows = dense_ref.shape[0] // 2
    send = send_part[...] + product(dense_ref[n_rows:, n_row * VB:], panel[...])
    keep = keep_part[...] + product(dense_ref[:n_rows, n_row * VB:], panel[...])
    same = h == lax.axis_index("col")
    send_ref[:VB] = send[:VB]
    keep_ref[:VB] = keep[:VB]
    send_ref[VB:] = jnp.where(same, send[VB:], keep[VB:])
    keep_ref[VB:] = jnp.where(same, keep[VB:], send[VB:])


def own_scores(dims, src_ref, keep_ref, came_ref):
    first = H + (lax.axis_index("row") * dims[1] + lax.axis_index("col")) * VB
    tele = one_hot(first, VB, src_ref[...])
    return DAMP * (keep_ref[:VB] + came_ref[:VB]) + 0.15 * tele


def spread_kernel(dims, src_ref, keep_ref, came_ref, scores_ref, hold_ref, pass_ref):
    quarter = hold_ref.shape[0]
    x = lax.axis_index("row") % X
    for ref, place in ((hold_ref, x), (pass_ref, 1 - x)):
        spot = pl.ds(pl.multiple_of(VB + place * quarter, quarter), quarter)
        ref[...] = keep_ref[spot, :] + came_ref[spot, :]
    scores_ref[0] = own_scores(dims, src_ref, keep_ref, came_ref).astype(scores_ref.dtype)


def join_kernel(*refs):
    for k, ref in enumerate(refs[:-1]):
        refs[-1][k] = ref[0]


def add_kernel(hold_ref, came_ref, out_ref):
    out_ref[...] = hold_ref[...] + came_ref[...]


def hub_kernel(dims, src_ref, held_ref, came_ref, out_ref):
    n_row, n_col, side = dims
    piece = H // (n_row * n_col)
    r = lax.axis_index("row")
    at = lax.broadcasted_iota(jnp.int32, out_ref.shape, 0)
    ids = ((r % X * (n_row // X) + at // piece) * n_col + hub_half()) * piece + at % piece
    tele = (ids == src_ref[...]).astype(jnp.float32)
    out_ref[...] = (DAMP * (held_ref[...] + came_ref[...]) + 0.15 * tele).astype(out_ref.dtype)


def pieces_kernel(keep_ref, came_ref, parts_ref):
    piece = parts_ref.shape[1]
    for k in range(parts_ref.shape[0]):
        spot = slice(VB + k * piece, VB + (k + 1) * piece)
        parts_ref[k] = keep_ref[spot, :] + came_ref[spot, :]


def last_kernel(dims, src_ref, keep_ref, came_ref, parts_ref, scores_ref, hubs_ref):
    scores_ref[...] = own_scores(dims, src_ref, keep_ref, came_ref)
    piece = hubs_ref.shape[0]
    summed = parts_ref[0]
    for k in range(1, parts_ref.shape[0]):
        summed = summed + parts_ref[k]
    first = (lax.axis_index("row") * dims[1] + lax.axis_index("col")) * piece
    hubs_ref[...] = DAMP * summed + 0.15 * one_hot(first, piece, src_ref[...])


def fast_body(tiles, tile_row, tile_col, tile_count, sources):
    slots, side = tiles.shape[2:4]
    width = sources.shape[0]
    n_row = lax.axis_size("row")
    n_col = lax.axis_size("col")
    piece = H // (n_row * n_col)
    dims = (n_row, n_col, side)
    n_rows = n_col * VB + H
    n_cols = n_row * VB + H
    f32 = functools.partial(jax.ShapeDtypeStruct, dtype=jnp.float32)
    bf16 = functools.partial(jax.ShapeDtypeStruct, dtype=jnp.bfloat16)
    src = sources.reshape(1, width)
    half = VB + n_row * piece
    quarter = H // n_col // X
    def other_core(x):
        return lax.ppermute(x, "col", [(0, 1), (1, 0)])

    def to_partner(x, flip):
        return lax.ppermute(x, "row", [(r, r ^ flip) for r in range(n_row)])

    def other_side(x):
        return to_partner(x, 1)

    def cross(x, flip):
        devices = [(r, c) for r in range(n_row) for c in range(n_col)]
        return lax.ppermute(x, ("row", "col"), [(r * n_col + c, (r ^ flip) * n_col + 1 - c) for r, c in devices])

    def call(kernel, name, out_shape, *args, scratch=(), cost=0):
        return pl.pallas_call(
            kernel,
            out_shape=out_shape,
            in_specs=[VMEM] * len(args),
            out_specs=jax.tree.map(lambda _: VMEM, out_shape),
            scratch_shapes=scratch,
            compiler_params=params(),
            cost_estimate=pl.CostEstimate(flops=cost * MICRO, bytes_accessed=0, transcendentals=0),
            name=name,
        )(*args)

    bind = functools.partial

    in_hbm = [pltpu.with_memory_space_constraint(x, pltpu.HBM) for x in (
        tiles.reshape(slots, side, side), tile_row.reshape(slots), tile_col.reshape(slots), src)]
    send, keep, dense = pl.pallas_call(
        bind(first_kernel, dims),
        out_shape=(f32((half, width)), f32((half, width)), bf16((2 * n_rows, n_cols))),
        in_specs=[HBM] * 5,
        out_specs=[VMEM] * 3,
        scratch_shapes=[
            pltpu.VMEM((slots, side, side), jnp.bfloat16),
            pltpu.SMEM((slots,), jnp.int32),
            pltpu.SMEM((slots,), jnp.int32),
            pltpu.SMEM((1,), jnp.int32),
            pltpu.VMEM((1, width), jnp.int32),
            pltpu.VMEM((n_rows + side, n_cols), jnp.float32),
            pltpu.VMEM((n_cols, width), jnp.bfloat16),
            pltpu.SemaphoreType.DMA((slots // CHUNK,)),
            pltpu.SemaphoreType.DMA((4,)),
        ],
        compiler_params=params(),
        name="first_terms",
    )(*in_hbm[:3], tile_count.reshape(1), in_hbm[3])

    for step in range(ITERS - 1):
        came = other_core(send)
        held, hold, away = call(
            bind(spread_kernel, dims), "spread",
            (bf16((1, VB, width)), f32((quarter, width)), f32((quarter, width))),
            src, keep, came, cost=2)
        away = cross(away, 1)
        next_z, far_z = to_partner(held, X), to_partner(held, 2 * X)
        last = to_partner(far_z, X)
        first = call(join_kernel, "join_first", bf16((3, VB, width)), held, next_z, far_z)
        first_across, last_across = other_side(first), other_side(last)
        sums = call(add_kernel, "plane_sum", f32((quarter, width)), hold, away, cost=20)
        sums = call(add_kernel, "pair_sum", f32((quarter, width)), sums, cross(sums, X), cost=1)
        mine = call(bind(hub_kernel, dims), "hub_sums", bf16((quarter, width)), src, sums, cross(sums, 2 * X), cost=1)
        quarters = [mine, other_side(mine), other_core(mine), cross(mine, 1)]
        send, keep = call(
            bind(score_columns_kernel, dims), "score_columns", (f32((half, width)),) * 2,
            first, last, first_across, last_across, dense, scratch=[pltpu.VMEM((n_row * VB, width), jnp.bfloat16)])
        send, keep = call(
            bind(hub_columns_kernel, dims), "hub_columns", (f32((half, width)),) * 2,
            *quarters, dense, send, keep, scratch=[pltpu.VMEM((H, width), jnp.bfloat16)])
    came = other_core(send)
    parts = call(pieces_kernel, "hub_pieces", f32((n_row, piece, width)), keep, came)
    parts = lax.all_to_all(parts, "row", 0, 0)
    scores, hubs = call(bind(last_kernel, dims), "last_sums", (f32((VB, width)), f32((piece, width))),
                        src, keep, came, parts)
    return scores.reshape(1, 1, VB, width), hubs


def plain_body(tiles, tile_row, tile_col, tile_count, sources):
    slots = tiles.shape[2]
    side = tiles.shape[3]
    width = sources.shape[0]
    tiles = tiles.reshape(slots, side, side)
    rows = tile_row.reshape(slots)
    cols = tile_col.reshape(slots)
    count = tile_count.reshape(())
    n_row = lax.axis_size("row")
    n_col = lax.axis_size("col")
    devices = n_row * n_col
    r_index = lax.axis_index("row")
    c_index = lax.axis_index("col")
    hub_dev = H // devices
    block_rows = n_col * VB
    n_tile_rows = (block_rows + H) // side
    own_base = H + (r_index * n_col + c_index) * VB
    hub_start = (r_index * n_col + c_index) * hub_dev
    own_ids = jnp.arange(VB, dtype=jnp.int32) + own_base
    tele_own = (own_ids[:, None] == sources[None, :]).astype(jnp.float32)
    piece_ids = jnp.arange(hub_dev, dtype=jnp.int32) + hub_start
    tele_piece = (piece_ids[:, None] == sources[None, :]).astype(jnp.float32)
    tele_hubs = (jnp.arange(H, dtype=jnp.int32)[:, None] == sources[None, :]).astype(jnp.float32)
    column_ids = (
        H
        + (jnp.arange(n_row, dtype=jnp.int32)[:, None] * n_col + c_index) * VB
        + jnp.arange(VB, dtype=jnp.int32)[None, :]
    ).reshape(n_row * VB)
    column_panel = (column_ids[:, None] == sources[None, :]).astype(jnp.bfloat16)
    hub_panel = tele_hubs.astype(jnp.bfloat16)
    block = math.gcd(slots, 16)
    own_scores = tele_own
    hub_piece = tele_piece
    for step in range(ITERS):
        start_acc = jnp.zeros((n_tile_rows, side, width), jnp.float32)
        if step > 0:
            column_panel = lax.all_gather(
                own_scores.astype(jnp.bfloat16), "row", axis=0, tiled=True
            )
        panel = jnp.concatenate([column_panel, hub_panel], axis=0).reshape(-1, side, width)

        def step_fn(number, total):
            start = number * block
            tile_block = lax.dynamic_slice_in_dim(tiles, start, block, 0)
            col_block = lax.dynamic_slice_in_dim(cols, start, block, 0)
            row_block = lax.dynamic_slice_in_dim(rows, start, block, 0)
            pieces = jnp.take(panel, col_block, axis=0)
            prod = jnp.einsum(
                "tij,tjs->tis", tile_block, pieces, preferred_element_type=jnp.float32
            )
            live = start + jnp.arange(block, dtype=jnp.int32) < count
            prod = jnp.where(live[:, None, None], prod, 0.0)
            return total.at[row_block].add(prod)

        total = lax.fori_loop(0, slots // block, step_fn, start_acc)
        partial_value = total.reshape(n_tile_rows * side, width)
        summed_rows = lax.psum_scatter(
            partial_value[:block_rows], "col", scatter_dimension=0, tiled=True
        )
        own_scores = 0.85 * summed_rows + 0.15 * tele_own
        hub_part = partial_value[block_rows:]
        summed = lax.psum_scatter(hub_part, ("row", "col"), scatter_dimension=0, tiled=True)
        hub_piece = 0.85 * summed + 0.15 * tele_piece
        if step + 1 < ITERS:
            hub_panel = lax.all_gather(
                hub_piece.astype(jnp.bfloat16), ("row", "col"), axis=0, tiled=True
            )
    return (own_scores.reshape(1, 1, VB, width), hub_piece)


def solution(mesh):
    placed = (
        P(("groups", "row"), "col", None, None, None),
        P(("groups", "row"), "col", None),
        P(("groups", "row"), "col", None),
        P(("groups", "row"), "col"),
        P("groups"),
    )

    def body(tiles, *rest):
        n_row, n_col = mesh.shape["row"], mesh.shape["col"]
        slots, side = tiles.shape[2:4]
        blocks = (n_col * VB + H) * (n_row * VB + H) // (side * side)
        if n_col == 2 and n_row == 4 * X and blocks <= slots and H // (n_row * n_col) % 16 == 0:
            return fast_body(tiles, *rest)
        return plain_body(tiles, *rest)

    return jax.shard_map(
        body,
        mesh=mesh,
        in_specs=placed,
        out_specs=(P(("groups", "row"), "col", None, None), P(("groups", "row", "col"), None)),
        check_vma=False,
    )
```

```python
import functools
import math

import jax
import jax.numpy as jnp
from jax import lax
from jax.experimental import pallas as pl
from jax.experimental.pallas import tpu as pltpu
from jax.sharding import PartitionSpec as P

VB = 128
H = 256
ITERS = 2
DAMP = 0.85
CHUNK = 8
X = 2
MICRO = 10 ** 9
VMEM_LIMIT = 32 * 1024 * 1024

SMEM = pl.BlockSpec(memory_space=pltpu.SMEM)
VMEM = pl.BlockSpec(memory_space=pltpu.VMEM)
HBM = pl.BlockSpec(memory_space=pltpu.HBM)


def params():
    return pltpu.CompilerParams(vmem_limit_bytes=VMEM_LIMIT)


def one_hot(first, count, src):
    ids = lax.broadcasted_iota(jnp.int32, (count, src.shape[1]), 0) + first
    return (ids == src).astype(jnp.float32)


def product(dense, panel):
    prod = jnp.dot(dense, panel, preferred_element_type=jnp.float32)
    rows = prod.shape[0] // 2
    return prod[:rows] + prod[rows:]


def first_kernel(dims, tiles_ref, rows_hbm, cols_hbm, count_hbm, src_hbm, send_ref, keep_ref, dense_send_ref, dense_keep_ref,
                 held, rows_ref, cols_ref, count_ref, src_ref, total, panel, sems, small):
    n_row, n_col, side = dims
    n_rows = n_col * VB + H
    piece = H // (n_row * n_col)
    c = lax.axis_index("col")
    pairs = ((src_hbm, src_ref), (rows_hbm, rows_ref), (cols_hbm, cols_ref), (count_hbm, count_ref))
    scalars = [pltpu.make_async_copy(a, b, small.at[i]) for i, (a, b) in enumerate(pairs)]
    copies = []
    for i in range(held.shape[0] // CHUNK):
        part = pl.ds(i * CHUNK, CHUNK)
        copies.append(pltpu.make_async_copy(tiles_ref.at[part], held.at[part], sems.at[i]))
    for copy in scalars + copies:
        copy.start()
    total[...] = jnp.zeros_like(total)
    for copy in scalars:
        copy.wait()
    src = src_ref[...]
    for r in range(n_row):
        first = H + (r * n_col + c) * VB
        panel[pl.ds(r * VB, VB), :] = one_hot(first, VB, src).astype(jnp.bfloat16)
    panel[pl.ds(n_row * VB, H), :] = one_hot(0, H, src).astype(jnp.bfloat16)
    count = count_ref[0]

    def add_tile(k, carry):
        live = k < count
        row = pl.multiple_of(jnp.where(live, rows_ref[k] * side, n_rows), side)
        col = pl.multiple_of(jnp.where(live, cols_ref[k] * side, 0), side)
        spot = (pl.ds(row, side), pl.ds(col, side))
        total[spot] += held[k].astype(jnp.float32)
        return carry

    for i, copy in enumerate(copies):
        copy.wait()
        lax.fori_loop(i * CHUNK, (i + 1) * CHUNK, add_tile, 0, unroll=4)
    half = n_rows // n_col
    for dense, out, core in ((dense_send_ref, send_ref, 1 - c), (dense_keep_ref, keep_ref, c)):
        chunks = [(0, core * VB, VB)]
        for r in range(n_row):
            chunks.append((VB + r * piece, n_col * VB + (r * n_col + core) * piece, piece))
        for to, start, size in chunks:
            whole = total[pl.ds(pl.multiple_of(start, size), size), :]
            high = whole.astype(jnp.bfloat16)
            dense[to:to + size] = high
            dense[half + to:half + to + size] = (whole - high.astype(jnp.float32)).astype(jnp.bfloat16)
        out[...] = product(dense[...], panel[...])


def score_columns_kernel(dims, *refs):
    n_row, n_col, side = dims
    columns = n_row * VB
    blocks, (dense_mine, dense_theirs, part_ref, panel) = refs[:4], refs[4:]
    r = lax.axis_index("row")
    for at, pair in enumerate((blocks[:2], blocks[2:])):
        for x, ref in enumerate(pair):
            for k in range(n_row // X):
                owner = r ^ (X * k + x)
                panel[at, pl.ds(pl.multiple_of(owner * VB, VB), VB), :] = ref[k]
    part_ref[...] = product(dense_mine[:, :columns], panel[0]) + product(dense_theirs[:, :columns], panel[1])


def hub_columns_kernel(dims, src_ref, mine_ref, theirs_ref, dense_mine, dense_theirs, part_ref,
                       scores_ref, parts_ref, panel):
    n_row, n_col, side = dims
    columns = n_row * VB
    piece = parts_ref.shape[1]
    r, c = lax.axis_index("row"), lax.axis_index("col")
    for ref, core in ((mine_ref, c), (theirs_ref, 1 - c)):
        for i in range(n_row):
            place = (i * n_col + core) * piece
            panel[pl.ds(pl.multiple_of(place, piece), piece), :] = ref[i * piece:(i + 1) * piece]
    total = part_ref[...] + product(dense_mine[:, columns:], panel[...]) + product(dense_theirs[:, columns:], panel[...])
    tele = one_hot(H + (r * n_col + c) * VB, VB, src_ref[...])
    scores_ref[...] = DAMP * total[:VB] + 0.15 * tele
    parts_ref[...] = total[VB:].reshape(parts_ref.shape)


def own_scores(dims, src_ref, keep_ref, came_ref):
    first = H + (lax.axis_index("row") * dims[1] + lax.axis_index("col")) * VB
    tele = one_hot(first, VB, src_ref[...])
    return DAMP * (keep_ref[:VB] + came_ref[:VB]) + 0.15 * tele


def spread_kernel(dims, src_ref, keep_ref, came_ref, scores_ref, hold_ref, pass_ref):
    quarter = hold_ref.shape[0]
    x = lax.axis_index("row") % X
    for ref, place in ((hold_ref, x), (pass_ref, 1 - x)):
        spot = pl.ds(pl.multiple_of(VB + place * quarter, quarter), quarter)
        ref[...] = keep_ref[spot, :] + came_ref[spot, :]
    scores_ref[0] = own_scores(dims, src_ref, keep_ref, came_ref).astype(scores_ref.dtype)


def join_kernel(*refs):
    at = 0
    for ref in refs[:-1]:
        refs[-1][at:at + ref.shape[0]] = ref[...]
        at += ref.shape[0]


def add_kernel(hold_ref, came_ref, out_ref):
    out_ref[...] = hold_ref[...] + came_ref[...]


def hub_kernel(dims, src_ref, held_ref, came_ref, out_ref):
    n_row, n_col, side = dims
    piece = H // (n_row * n_col)
    r, c = lax.axis_index("row"), lax.axis_index("col")
    at = lax.broadcasted_iota(jnp.int32, out_ref.shape, 0)
    ids = ((r % X * (n_row // X) + at // piece) * n_col + c) * piece + at % piece
    tele = (ids == src_ref[...]).astype(jnp.float32)
    out_ref[...] = (DAMP * (held_ref[...] + came_ref[...]) + 0.15 * tele).astype(out_ref.dtype)


def side_kernel(mine_ref, theirs_ref, out_ref):
    part = mine_ref.shape[0]
    x = lax.axis_index("row") % X
    for ref, place in ((mine_ref, x), (theirs_ref, 1 - x)):
        out_ref[pl.ds(pl.multiple_of(place * part, part), part), :] = ref[...]


def last_kernel(dims, src_ref, parts_ref, hubs_ref):
    piece = hubs_ref.shape[0]
    summed = parts_ref[0]
    for k in range(1, parts_ref.shape[0]):
        summed = summed + parts_ref[k]
    first = (lax.axis_index("row") * dims[1] + lax.axis_index("col")) * piece
    hubs_ref[...] = DAMP * summed + 0.15 * one_hot(first, piece, src_ref[...])


def fast_body(tiles, tile_row, tile_col, tile_count, sources):
    slots, side = tiles.shape[2:4]
    width = sources.shape[0]
    n_row = lax.axis_size("row")
    n_col = lax.axis_size("col")
    piece = H // (n_row * n_col)
    dims = (n_row, n_col, side)
    n_rows = n_col * VB + H
    n_cols = n_row * VB + H
    f32 = functools.partial(jax.ShapeDtypeStruct, dtype=jnp.float32)
    bf16 = functools.partial(jax.ShapeDtypeStruct, dtype=jnp.bfloat16)
    src = sources.reshape(1, width)
    half = VB + n_row * piece
    quarter = H // n_col // X
    def other_core(x):
        return lax.ppermute(x, "col", [(0, 1), (1, 0)])

    def to_partner(x, flip):
        return lax.ppermute(x, "row", [(r, r ^ flip) for r in range(n_row)])

    def other_side(x):
        return to_partner(x, 1)

    def call(kernel, name, out_shape, *args, scratch=(), after=(), cost=0):
        def body(*refs):
            kernel(*refs[:len(args)], *refs[len(args) + len(after):])

        return pl.pallas_call(
            body,
            out_shape=out_shape,
            in_specs=[VMEM] * len(args) + [pl.BlockSpec(memory_space=pl.ANY)] * len(after),
            out_specs=jax.tree.map(lambda _: VMEM, out_shape),
            scratch_shapes=scratch,
            compiler_params=params(),
            cost_estimate=pl.CostEstimate(flops=cost * MICRO, bytes_accessed=0, transcendentals=0),
            name=name,
        )(*args, *after)

    bind = functools.partial

    in_hbm = [pltpu.with_memory_space_constraint(x, pltpu.HBM) for x in (
        tiles.reshape(slots, side, side), tile_row.reshape(slots), tile_col.reshape(slots), src)]
    dense_shape = bf16((2 * half, n_cols))
    send, keep, dense_send, dense_keep = pl.pallas_call(
        bind(first_kernel, dims),
        out_shape=(f32((half, width)), f32((half, width)), dense_shape, dense_shape),
        in_specs=[HBM] * 5,
        out_specs=[VMEM] * 4,
        scratch_shapes=[
            pltpu.VMEM((slots, side, side), jnp.bfloat16),
            pltpu.SMEM((slots,), jnp.int32),
            pltpu.SMEM((slots,), jnp.int32),
            pltpu.SMEM((1,), jnp.int32),
            pltpu.VMEM((1, width), jnp.int32),
            pltpu.VMEM((n_rows + side, n_cols), jnp.float32),
            pltpu.VMEM((n_cols, width), jnp.bfloat16),
            pltpu.SemaphoreType.DMA((slots // CHUNK,)),
            pltpu.SemaphoreType.DMA((4,)),
        ],
        compiler_params=params(),
        name="first_terms",
    )(*in_hbm[:3], tile_count.reshape(1), in_hbm[3])

    held, hold, away = call(
        bind(spread_kernel, dims), "spread",
        (bf16((1, VB, width)), f32((quarter, width)), f32((quarter, width))),
        src, keep, other_core(send), cost=1)
    away = other_side(away)
    next_z, far_z = to_partner(held, X), to_partner(held, 2 * X)
    last = to_partner(far_z, X)
    first = call(join_kernel, "join_first", bf16((3, VB, width)), held, next_z, far_z, cost=3)
    first_across, last_across = other_side(first), other_side(last)
    line_shape = bf16((n_row // X, VB, width))
    dense_came = other_core(dense_send)
    sums = call(add_kernel, "plane_sum", f32((quarter, width)), hold, away, cost=8)
    sums = call(add_kernel, "pair_sum", f32((quarter, width)), sums, to_partner(sums, X), cost=8)
    line = call(join_kernel, "join_line", line_shape, first, last, cost=12)
    line_came = other_core(line)
    hubs = call(bind(hub_kernel, dims), "hub_sums", bf16((quarter, width)), src, sums, to_partner(sums, 2 * X),
                after=[dense_came], cost=1)
    across = call(join_kernel, "join_across", line_shape, first_across, last_across, after=[hubs], cost=2)
    across_came = other_core(across)
    hubs = call(side_kernel, "join_sides", bf16((H // n_col, width)), hubs, other_side(hubs), cost=12)
    part = call(
        bind(score_columns_kernel, dims), "score_columns", f32((half, width)),
        line, across, line_came, across_came, dense_keep, dense_came,
        scratch=[pltpu.VMEM((2, n_row * VB, width), jnp.bfloat16)], cost=20)
    scores, parts = call(
        bind(hub_columns_kernel, dims), "hub_columns", (f32((VB, width)), f32((n_row, piece, width))),
        src, hubs, other_core(hubs), dense_keep, dense_came, part, scratch=[pltpu.VMEM((H, width), jnp.bfloat16)])
    parts = lax.all_to_all(parts, "row", 0, 0)
    hubs = call(bind(last_kernel, dims), "last_hubs", f32((piece, width)), src, parts)
    return scores.reshape(1, 1, VB, width), hubs


def plain_body(tiles, tile_row, tile_col, tile_count, sources):
    slots = tiles.shape[2]
    side = tiles.shape[3]
    width = sources.shape[0]
    tiles = tiles.reshape(slots, side, side)
    rows = tile_row.reshape(slots)
    cols = tile_col.reshape(slots)
    count = tile_count.reshape(())
    n_row = lax.axis_size("row")
    n_col = lax.axis_size("col")
    devices = n_row * n_col
    r_index = lax.axis_index("row")
    c_index = lax.axis_index("col")
    hub_dev = H // devices
    block_rows = n_col * VB
    n_tile_rows = (block_rows + H) // side
    own_base = H + (r_index * n_col + c_index) * VB
    hub_start = (r_index * n_col + c_index) * hub_dev
    own_ids = jnp.arange(VB, dtype=jnp.int32) + own_base
    tele_own = (own_ids[:, None] == sources[None, :]).astype(jnp.float32)
    piece_ids = jnp.arange(hub_dev, dtype=jnp.int32) + hub_start
    tele_piece = (piece_ids[:, None] == sources[None, :]).astype(jnp.float32)
    tele_hubs = (jnp.arange(H, dtype=jnp.int32)[:, None] == sources[None, :]).astype(jnp.float32)
    column_ids = (
        H
        + (jnp.arange(n_row, dtype=jnp.int32)[:, None] * n_col + c_index) * VB
        + jnp.arange(VB, dtype=jnp.int32)[None, :]
    ).reshape(n_row * VB)
    column_panel = (column_ids[:, None] == sources[None, :]).astype(jnp.bfloat16)
    hub_panel = tele_hubs.astype(jnp.bfloat16)
    block = math.gcd(slots, 16)
    own_scores = tele_own
    hub_piece = tele_piece
    for step in range(ITERS):
        start_acc = jnp.zeros((n_tile_rows, side, width), jnp.float32)
        if step > 0:
            column_panel = lax.all_gather(
                own_scores.astype(jnp.bfloat16), "row", axis=0, tiled=True
            )
        panel = jnp.concatenate([column_panel, hub_panel], axis=0).reshape(-1, side, width)

        def step_fn(number, total):
            start = number * block
            tile_block = lax.dynamic_slice_in_dim(tiles, start, block, 0)
            col_block = lax.dynamic_slice_in_dim(cols, start, block, 0)
            row_block = lax.dynamic_slice_in_dim(rows, start, block, 0)
            pieces = jnp.take(panel, col_block, axis=0)
            prod = jnp.einsum(
                "tij,tjs->tis", tile_block, pieces, preferred_element_type=jnp.float32
            )
            live = start + jnp.arange(block, dtype=jnp.int32) < count
            prod = jnp.where(live[:, None, None], prod, 0.0)
            return total.at[row_block].add(prod)

        total = lax.fori_loop(0, slots // block, step_fn, start_acc)
        partial_value = total.reshape(n_tile_rows * side, width)
        summed_rows = lax.psum_scatter(
            partial_value[:block_rows], "col", scatter_dimension=0, tiled=True
        )
        own_scores = 0.85 * summed_rows + 0.15 * tele_own
        hub_part = partial_value[block_rows:]
        summed = lax.psum_scatter(hub_part, ("row", "col"), scatter_dimension=0, tiled=True)
        hub_piece = 0.85 * summed + 0.15 * tele_piece
        if step + 1 < ITERS:
            hub_panel = lax.all_gather(
                hub_piece.astype(jnp.bfloat16), ("row", "col"), axis=0, tiled=True
            )
    return (own_scores.reshape(1, 1, VB, width), hub_piece)


def solution(mesh):
    placed = (
        P(("groups", "row"), "col", None, None, None),
        P(("groups", "row"), "col", None),
        P(("groups", "row"), "col", None),
        P(("groups", "row"), "col"),
        P("groups"),
    )

    def body(tiles, *rest):
        n_row, n_col = mesh.shape["row"], mesh.shape["col"]
        slots, side = tiles.shape[2:4]
        blocks = (n_col * VB + H) * (n_row * VB + H) // (side * side)
        if ITERS == 2 and n_col == 2 and n_row == 4 * X and blocks <= slots and H // (n_row * n_col) % 16 == 0:
            return fast_body(tiles, *rest)
        return plain_body(tiles, *rest)

    return jax.shard_map(
        body,
        mesh=mesh,
        in_specs=placed,
        out_specs=(P(("groups", "row"), "col", None, None), P(("groups", "row", "col"), None)),
        check_vma=False,
    )
```

```python
import functools
import math

import jax
import jax.numpy as jnp
from jax import lax
from jax.experimental import pallas as pl
from jax.experimental.pallas import tpu as pltpu
from jax.sharding import PartitionSpec as P

VB = 128
H = 256
ITERS = 2
DAMP = 0.85
CHUNK = 8
X = 2
MICRO = 10 ** 9
VMEM_LIMIT = 32 * 1024 * 1024

SMEM = pl.BlockSpec(memory_space=pltpu.SMEM)
VMEM = pl.BlockSpec(memory_space=pltpu.VMEM)
HBM = pl.BlockSpec(memory_space=pltpu.HBM)


def params():
    return pltpu.CompilerParams(vmem_limit_bytes=VMEM_LIMIT)


def one_hot(first, count, src):
    ids = lax.broadcasted_iota(jnp.int32, (count, src.shape[1]), 0) + first
    return (ids == src).astype(jnp.float32)


def product(dense, panel):
    prod = jnp.dot(dense, panel, preferred_element_type=jnp.float32)
    rows = prod.shape[0] // 2
    return prod[:rows] + prod[rows:]


def first_kernel(dims, tiles_ref, rows_hbm, cols_hbm, count_hbm, src_hbm, send_ref, keep_ref, dense_send_ref, dense_keep_ref,
                 held, rows_ref, cols_ref, count_ref, src_ref, total, panel, sems, small):
    n_row, n_col, side = dims
    n_rows = n_col * VB + H
    piece = H // (n_row * n_col)
    c = lax.axis_index("col")
    pairs = ((src_hbm, src_ref), (rows_hbm, rows_ref), (cols_hbm, cols_ref), (count_hbm, count_ref))
    scalars = [pltpu.make_async_copy(a, b, small.at[i]) for i, (a, b) in enumerate(pairs)]
    copies = []
    for i in range(held.shape[0] // CHUNK):
        part = pl.ds(i * CHUNK, CHUNK)
        copies.append(pltpu.make_async_copy(tiles_ref.at[part], held.at[part], sems.at[i]))
    for copy in scalars + copies:
        copy.start()
    total[...] = jnp.zeros_like(total)
    for copy in scalars:
        copy.wait()
    src = src_ref[...]
    for r in range(n_row):
        first = H + (r * n_col + c) * VB
        panel[pl.ds(r * VB, VB), :] = one_hot(first, VB, src).astype(jnp.bfloat16)
    panel[pl.ds(n_row * VB, H), :] = one_hot(0, H, src).astype(jnp.bfloat16)
    count = count_ref[0]

    def add_tile(k, carry):
        live = k < count
        row = pl.multiple_of(jnp.where(live, rows_ref[k] * side, n_rows), side)
        col = pl.multiple_of(jnp.where(live, cols_ref[k] * side, 0), side)
        spot = (pl.ds(row, side), pl.ds(col, side))
        total[spot] += held[k].astype(jnp.float32)
        return carry

    for i, copy in enumerate(copies):
        copy.wait()
        lax.fori_loop(i * CHUNK, (i + 1) * CHUNK, add_tile, 0, unroll=4)
    half = n_rows // n_col
    for dense, out, core in ((dense_send_ref, send_ref, 1 - c), (dense_keep_ref, keep_ref, c)):
        chunks = [(0, core * VB, VB)]
        for r in range(n_row):
            chunks.append((VB + r * piece, n_col * VB + (r * n_col + core) * piece, piece))
        for to, start, size in chunks:
            whole = total[pl.ds(pl.multiple_of(start, size), size), :]
            high = whole.astype(jnp.bfloat16)
            dense[to:to + size] = high
            dense[half + to:half + to + size] = (whole - high.astype(jnp.float32)).astype(jnp.bfloat16)
        out[...] = product(dense[...], panel[...])


def score_columns_kernel(dims, *refs):
    n_row, n_col, side = dims
    columns = n_row * VB
    mine, theirs, dense_mine, dense_theirs, part_ref, panel = refs
    r = lax.axis_index("row")
    n_z = n_row // X
    for at, ref in enumerate((mine, theirs)):
        for k in range(n_row):
            owner = r ^ (X * (k % n_z) + k // n_z)
            panel[at, pl.ds(pl.multiple_of(owner * VB, VB), VB), :] = ref[k]
    part_ref[...] = product(dense_mine[:, :columns], panel[0]) + product(dense_theirs[:, :columns], panel[1])


def hub_columns_kernel(dims, src_ref, mine_ref, theirs_ref, dense_mine, dense_theirs, part_ref,
                       scores_ref, parts_ref, panel):
    n_row, n_col, side = dims
    columns = n_row * VB
    piece = parts_ref.shape[1]
    r, c = lax.axis_index("row"), lax.axis_index("col")
    for ref, core in ((mine_ref, c), (theirs_ref, 1 - c)):
        for i in range(n_row):
            place = (i * n_col + core) * piece
            panel[pl.ds(pl.multiple_of(place, piece), piece), :] = ref[i * piece:(i + 1) * piece]
    total = part_ref[...] + product(dense_mine[:, columns:], panel[...]) + product(dense_theirs[:, columns:], panel[...])
    tele = one_hot(H + (r * n_col + c) * VB, VB, src_ref[...])
    scores_ref[...] = DAMP * total[:VB] + 0.15 * tele
    parts_ref[...] = total[VB:].reshape(parts_ref.shape)


def own_scores(dims, src_ref, keep_ref, came_ref):
    first = H + (lax.axis_index("row") * dims[1] + lax.axis_index("col")) * VB
    tele = one_hot(first, VB, src_ref[...])
    return DAMP * (keep_ref[:VB] + came_ref[:VB]) + 0.15 * tele


def spread_kernel(dims, src_ref, keep_ref, came_ref, scores_ref, hold_ref, pass_ref):
    quarter = hold_ref.shape[0]
    x = lax.axis_index("row") % X
    for ref, place in ((hold_ref, x), (pass_ref, 1 - x)):
        spot = pl.ds(pl.multiple_of(VB + place * quarter, quarter), quarter)
        ref[...] = keep_ref[spot, :] + came_ref[spot, :]
    scores_ref[0] = own_scores(dims, src_ref, keep_ref, came_ref).astype(scores_ref.dtype)


def join_kernel(*refs):
    at = 0
    for ref in refs[:-1]:
        refs[-1][at:at + ref.shape[0]] = ref[...]
        at += ref.shape[0]


def add_kernel(hold_ref, came_ref, out_ref):
    out_ref[...] = hold_ref[...] + came_ref[...]


def hub_kernel(dims, src_ref, held_ref, came_ref, out_ref):
    n_row, n_col, side = dims
    piece = H // (n_row * n_col)
    r, c = lax.axis_index("row"), lax.axis_index("col")
    at = lax.broadcasted_iota(jnp.int32, out_ref.shape, 0)
    ids = ((r % X * (n_row // X) + at // piece) * n_col + c) * piece + at % piece
    tele = (ids == src_ref[...]).astype(jnp.float32)
    out_ref[...] = (DAMP * (held_ref[...] + came_ref[...]) + 0.15 * tele).astype(out_ref.dtype)


def side_kernel(mine_ref, theirs_ref, out_ref):
    part = mine_ref.shape[0]
    x = lax.axis_index("row") % X
    for ref, place in ((mine_ref, x), (theirs_ref, 1 - x)):
        out_ref[pl.ds(pl.multiple_of(place * part, part), part), :] = ref[...]


def last_kernel(dims, src_ref, parts_ref, hubs_ref):
    piece = hubs_ref.shape[0]
    summed = parts_ref[0]
    for k in range(1, parts_ref.shape[0]):
        summed = summed + parts_ref[k]
    first = (lax.axis_index("row") * dims[1] + lax.axis_index("col")) * piece
    hubs_ref[...] = DAMP * summed + 0.15 * one_hot(first, piece, src_ref[...])


def fast_body(tiles, tile_row, tile_col, tile_count, sources):
    slots, side = tiles.shape[2:4]
    width = sources.shape[0]
    n_row = lax.axis_size("row")
    n_col = lax.axis_size("col")
    piece = H // (n_row * n_col)
    dims = (n_row, n_col, side)
    n_rows = n_col * VB + H
    n_cols = n_row * VB + H
    f32 = functools.partial(jax.ShapeDtypeStruct, dtype=jnp.float32)
    bf16 = functools.partial(jax.ShapeDtypeStruct, dtype=jnp.bfloat16)
    src = sources.reshape(1, width)
    half = VB + n_row * piece
    quarter = H // n_col // X
    def other_core(x):
        return lax.ppermute(x, "col", [(0, 1), (1, 0)])

    def to_partner(x, flip):
        return lax.ppermute(x, "row", [(r, r ^ flip) for r in range(n_row)])

    def other_side(x):
        return to_partner(x, 1)

    def call(kernel, name, out_shape, *args, scratch=(), after=(), cost=0):
        def body(*refs):
            kernel(*refs[:len(args)], *refs[len(args) + len(after):])

        return pl.pallas_call(
            body,
            out_shape=out_shape,
            in_specs=[VMEM] * len(args) + [pl.BlockSpec(memory_space=pl.ANY)] * len(after),
            out_specs=jax.tree.map(lambda _: VMEM, out_shape),
            scratch_shapes=scratch,
            compiler_params=params(),
            cost_estimate=pl.CostEstimate(flops=cost * MICRO, bytes_accessed=0, transcendentals=0),
            name=name,
        )(*args, *after)

    bind = functools.partial

    in_hbm = [pltpu.with_memory_space_constraint(x, pltpu.HBM) for x in (
        tiles.reshape(slots, side, side), tile_row.reshape(slots), tile_col.reshape(slots), src)]
    dense_shape = bf16((2 * half, n_cols))
    send, keep, dense_send, dense_keep = pl.pallas_call(
        bind(first_kernel, dims),
        out_shape=(f32((half, width)), f32((half, width)), dense_shape, dense_shape),
        in_specs=[HBM] * 5,
        out_specs=[VMEM] * 4,
        scratch_shapes=[
            pltpu.VMEM((slots, side, side), jnp.bfloat16),
            pltpu.SMEM((slots,), jnp.int32),
            pltpu.SMEM((slots,), jnp.int32),
            pltpu.SMEM((1,), jnp.int32),
            pltpu.VMEM((1, width), jnp.int32),
            pltpu.VMEM((n_rows + side, n_cols), jnp.float32),
            pltpu.VMEM((n_cols, width), jnp.bfloat16),
            pltpu.SemaphoreType.DMA((slots // CHUNK,)),
            pltpu.SemaphoreType.DMA((4,)),
        ],
        compiler_params=params(),
        name="first_terms",
    )(*in_hbm[:3], tile_count.reshape(1), in_hbm[3])

    held, hold, away = call(
        bind(spread_kernel, dims), "spread",
        (bf16((1, VB, width)), f32((quarter, width)), f32((quarter, width))),
        src, keep, other_core(send), cost=2)
    away = other_side(away)
    next_z, far_z = to_partner(held, X), to_partner(held, 2 * X)
    last = to_partner(far_z, X)
    first = call(join_kernel, "join_first", bf16((3, VB, width)), held, next_z, far_z, cost=2)
    first_across, last_across = other_side(first), other_side(last)
    dense_came = other_core(dense_send)
    sums = call(add_kernel, "plane_sum", f32((quarter, width)), hold, away, cost=0)
    sums = call(add_kernel, "pair_sum", f32((quarter, width)), sums, to_partner(sums, X), cost=12)
    hubs = call(bind(hub_kernel, dims), "hub_sums", bf16((quarter, width)), src, sums, to_partner(sums, 2 * X),
                after=[dense_came], cost=0)
    blocks = call(join_kernel, "join_blocks", bf16((n_row, VB, width)), first, last, first_across, last_across, after=[hubs], cost=5)
    blocks_came = other_core(blocks)
    hubs = call(side_kernel, "join_sides", bf16((H // n_col, width)), hubs, other_side(hubs), cost=12)
    part = call(
        bind(score_columns_kernel, dims), "score_columns", f32((half, width)),
        blocks, blocks_came, dense_keep, dense_came,
        scratch=[pltpu.VMEM((2, n_row * VB, width), jnp.bfloat16)], cost=8)
    scores, parts = call(
        bind(hub_columns_kernel, dims), "hub_columns", (f32((VB, width)), f32((n_row, piece, width))),
        src, hubs, other_core(hubs), dense_keep, dense_came, part, scratch=[pltpu.VMEM((H, width), jnp.bfloat16)])
    parts = lax.all_to_all(parts, "row", 0, 0)
    hubs = call(bind(last_kernel, dims), "last_hubs", f32((piece, width)), src, parts)
    return scores.reshape(1, 1, VB, width), hubs


def plain_body(tiles, tile_row, tile_col, tile_count, sources):
    slots = tiles.shape[2]
    side = tiles.shape[3]
    width = sources.shape[0]
    tiles = tiles.reshape(slots, side, side)
    rows = tile_row.reshape(slots)
    cols = tile_col.reshape(slots)
    count = tile_count.reshape(())
    n_row = lax.axis_size("row")
    n_col = lax.axis_size("col")
    devices = n_row * n_col
    r_index = lax.axis_index("row")
    c_index = lax.axis_index("col")
    hub_dev = H // devices
    block_rows = n_col * VB
    n_tile_rows = (block_rows + H) // side
    own_base = H + (r_index * n_col + c_index) * VB
    hub_start = (r_index * n_col + c_index) * hub_dev
    own_ids = jnp.arange(VB, dtype=jnp.int32) + own_base
    tele_own = (own_ids[:, None] == sources[None, :]).astype(jnp.float32)
    piece_ids = jnp.arange(hub_dev, dtype=jnp.int32) + hub_start
    tele_piece = (piece_ids[:, None] == sources[None, :]).astype(jnp.float32)
    tele_hubs = (jnp.arange(H, dtype=jnp.int32)[:, None] == sources[None, :]).astype(jnp.float32)
    column_ids = (
        H
        + (jnp.arange(n_row, dtype=jnp.int32)[:, None] * n_col + c_index) * VB
        + jnp.arange(VB, dtype=jnp.int32)[None, :]
    ).reshape(n_row * VB)
    column_panel = (column_ids[:, None] == sources[None, :]).astype(jnp.bfloat16)
    hub_panel = tele_hubs.astype(jnp.bfloat16)
    block = math.gcd(slots, 16)
    own_scores = tele_own
    hub_piece = tele_piece
    for step in range(ITERS):
        start_acc = jnp.zeros((n_tile_rows, side, width), jnp.float32)
        if step > 0:
            column_panel = lax.all_gather(
                own_scores.astype(jnp.bfloat16), "row", axis=0, tiled=True
            )
        panel = jnp.concatenate([column_panel, hub_panel], axis=0).reshape(-1, side, width)

        def step_fn(number, total):
            start = number * block
            tile_block = lax.dynamic_slice_in_dim(tiles, start, block, 0)
            col_block = lax.dynamic_slice_in_dim(cols, start, block, 0)
            row_block = lax.dynamic_slice_in_dim(rows, start, block, 0)
            pieces = jnp.take(panel, col_block, axis=0)
            prod = jnp.einsum(
                "tij,tjs->tis", tile_block, pieces, preferred_element_type=jnp.float32
            )
            live = start + jnp.arange(block, dtype=jnp.int32) < count
            prod = jnp.where(live[:, None, None], prod, 0.0)
            return total.at[row_block].add(prod)

        total = lax.fori_loop(0, slots // block, step_fn, start_acc)
        partial_value = total.reshape(n_tile_rows * side, width)
        summed_rows = lax.psum_scatter(
            partial_value[:block_rows], "col", scatter_dimension=0, tiled=True
        )
        own_scores = 0.85 * summed_rows + 0.15 * tele_own
        hub_part = partial_value[block_rows:]
        summed = lax.psum_scatter(hub_part, ("row", "col"), scatter_dimension=0, tiled=True)
        hub_piece = 0.85 * summed + 0.15 * tele_piece
        if step + 1 < ITERS:
            hub_panel = lax.all_gather(
                hub_piece.astype(jnp.bfloat16), ("row", "col"), axis=0, tiled=True
            )
    return (own_scores.reshape(1, 1, VB, width), hub_piece)


def solution(mesh):
    placed = (
        P(("groups", "row"), "col", None, None, None),
        P(("groups", "row"), "col", None),
        P(("groups", "row"), "col", None),
        P(("groups", "row"), "col"),
        P("groups"),
    )

    def body(tiles, *rest):
        n_row, n_col = mesh.shape["row"], mesh.shape["col"]
        slots, side = tiles.shape[2:4]
        blocks = (n_col * VB + H) * (n_row * VB + H) // (side * side)
        if ITERS == 2 and n_col == 2 and n_row == 4 * X and blocks <= slots and H // (n_row * n_col) % 16 == 0:
            return fast_body(tiles, *rest)
        return plain_body(tiles, *rest)

    return jax.shard_map(
        body,
        mesh=mesh,
        in_specs=placed,
        out_specs=(P(("groups", "row"), "col", None, None), P(("groups", "row", "col"), None)),
        check_vma=False,
    )
```

```python
import functools
import math

import jax
import jax.numpy as jnp
from jax import lax
from jax.experimental import pallas as pl
from jax.experimental.pallas import tpu as pltpu
from jax.sharding import PartitionSpec as P

VB = 128
H = 256
ITERS = 2
DAMP = 0.85
CHUNK = 8
X = 2
MICRO = 10 ** 9
VMEM_LIMIT = 32 * 1024 * 1024

SMEM = pl.BlockSpec(memory_space=pltpu.SMEM)
VMEM = pl.BlockSpec(memory_space=pltpu.VMEM)
HBM = pl.BlockSpec(memory_space=pltpu.HBM)


def params():
    return pltpu.CompilerParams(vmem_limit_bytes=VMEM_LIMIT)


def one_hot(first, count, src):
    ids = lax.broadcasted_iota(jnp.int32, (count, src.shape[1]), 0) + first
    return (ids == src).astype(jnp.float32)


def product(dense, panel):
    prod = jnp.dot(dense, panel, preferred_element_type=jnp.float32)
    rows = prod.shape[0] // 2
    return prod[:rows] + prod[rows:]


def first_kernel(dims, tiles_ref, rows_hbm, cols_hbm, count_hbm, src_hbm, send_ref, keep_ref, dense_send_ref, dense_keep_ref,
                 held, rows_ref, cols_ref, count_ref, src_ref, total, panel, sems, small):
    n_row, n_col, side = dims
    n_rows = n_col * VB + H
    piece = H // (n_row * n_col)
    c = lax.axis_index("col")
    pairs = ((src_hbm, src_ref), (rows_hbm, rows_ref), (cols_hbm, cols_ref), (count_hbm, count_ref))
    scalars = [pltpu.make_async_copy(a, b, small.at[i]) for i, (a, b) in enumerate(pairs)]
    copies = []
    for i in range(held.shape[0] // CHUNK):
        part = pl.ds(i * CHUNK, CHUNK)
        copies.append(pltpu.make_async_copy(tiles_ref.at[part], held.at[part], sems.at[i]))
    for copy in scalars + copies:
        copy.start()
    total[...] = jnp.zeros_like(total)
    for copy in scalars:
        copy.wait()
    src = src_ref[...]
    for r in range(n_row):
        first = H + (r * n_col + c) * VB
        panel[pl.ds(r * VB, VB), :] = one_hot(first, VB, src).astype(jnp.bfloat16)
    panel[pl.ds(n_row * VB, H), :] = one_hot(0, H, src).astype(jnp.bfloat16)
    count = count_ref[0]

    def add_tile(k, carry):
        live = k < count
        row = pl.multiple_of(jnp.where(live, rows_ref[k] * side, n_rows), side)
        col = pl.multiple_of(jnp.where(live, cols_ref[k] * side, 0), side)
        spot = (pl.ds(row, side), pl.ds(col, side))
        total[spot] += held[k].astype(jnp.float32)
        return carry

    for i, copy in enumerate(copies):
        copy.wait()
        lax.fori_loop(i * CHUNK, (i + 1) * CHUNK, add_tile, 0, unroll=4)
    half = n_rows // n_col
    for dense, out, core in ((dense_send_ref, send_ref, 1 - c), (dense_keep_ref, keep_ref, c)):
        chunks = [(0, core * VB, VB)]
        for r in range(n_row):
            chunks.append((VB + r * piece, n_col * VB + (r * n_col + core) * piece, piece))
        for to, start, size in chunks:
            whole = total[pl.ds(pl.multiple_of(start, size), size), :]
            high = whole.astype(jnp.bfloat16)
            dense[to:to + size] = high
            dense[half + to:half + to + size] = (whole - high.astype(jnp.float32)).astype(jnp.bfloat16)
        out[...] = product(dense[...], panel[...])


def score_columns_kernel(dims, *refs):
    n_row, n_col, side = dims
    columns = n_row * VB
    mine, theirs, dense_mine, dense_theirs, part_ref, panel = refs
    r = lax.axis_index("row")
    n_z = n_row // X
    for at, ref in enumerate((mine, theirs)):
        for k in range(n_row):
            owner = r ^ (X * (k % n_z) + k // n_z)
            panel[at, pl.ds(pl.multiple_of(owner * VB, VB), VB), :] = ref[k]
    part_ref[...] = product(dense_mine[:, :columns], panel[0]) + product(dense_theirs[:, :columns], panel[1])


def hub_columns_kernel(dims, src_ref, mine_ref, theirs_ref, dense_mine, dense_theirs, part_ref,
                       scores_ref, parts_ref, panel):
    n_row, n_col, side = dims
    columns = n_row * VB
    piece = parts_ref.shape[1]
    r, c = lax.axis_index("row"), lax.axis_index("col")
    for ref, core in ((mine_ref, c), (theirs_ref, 1 - c)):
        for i in range(n_row):
            place = (i * n_col + core) * piece
            panel[pl.ds(pl.multiple_of(place, piece), piece), :] = ref[i * piece:(i + 1) * piece]
    total = part_ref[...] + product(dense_mine[:, columns:], panel[...]) + product(dense_theirs[:, columns:], panel[...])
    tele = one_hot(H + (r * n_col + c) * VB, VB, src_ref[...])
    scores_ref[...] = DAMP * total[:VB] + 0.15 * tele
    parts_ref[...] = total[VB:].reshape(parts_ref.shape)


def own_scores(dims, src_ref, keep_ref, came_ref):
    first = H + (lax.axis_index("row") * dims[1] + lax.axis_index("col")) * VB
    tele = one_hot(first, VB, src_ref[...])
    return DAMP * (keep_ref[:VB] + came_ref[:VB]) + 0.15 * tele


def spread_kernel(dims, src_ref, keep_ref, came_ref, scores_ref, hold_ref, pass_ref):
    quarter = hold_ref.shape[0]
    x = lax.axis_index("row") % X
    for ref, place in ((hold_ref, x), (pass_ref, 1 - x)):
        spot = pl.ds(pl.multiple_of(VB + place * quarter, quarter), quarter)
        ref[...] = keep_ref[spot, :] + came_ref[spot, :]
    scores_ref[0] = own_scores(dims, src_ref, keep_ref, came_ref).astype(scores_ref.dtype)


def join_kernel(*refs):
    at = 0
    for ref in refs[:-1]:
        refs[-1][at:at + ref.shape[0]] = ref[...]
        at += ref.shape[0]


def add_kernel(hold_ref, came_ref, out_ref):
    out_ref[...] = hold_ref[...] + came_ref[...]


def hub_kernel(dims, src_ref, held_ref, came_ref, out_ref):
    n_row, n_col, side = dims
    piece = H // (n_row * n_col)
    r, c = lax.axis_index("row"), lax.axis_index("col")
    at = lax.broadcasted_iota(jnp.int32, out_ref.shape, 0)
    ids = ((r % X * (n_row // X) + at // piece) * n_col + c) * piece + at % piece
    tele = (ids == src_ref[...]).astype(jnp.float32)
    out_ref[...] = (DAMP * (held_ref[...] + came_ref[...]) + 0.15 * tele).astype(out_ref.dtype)


def side_kernel(mine_ref, theirs_ref, out_ref):
    part = mine_ref.shape[0]
    x = lax.axis_index("row") % X
    for ref, place in ((mine_ref, x), (theirs_ref, 1 - x)):
        out_ref[pl.ds(pl.multiple_of(place * part, part), part), :] = ref[...]


def last_kernel(dims, src_ref, held_ref, parts_ref, scores_ref, hubs_ref):
    scores_ref[...] = held_ref[...]
    piece = hubs_ref.shape[0]
    summed = parts_ref[0]
    for k in range(1, parts_ref.shape[0]):
        summed = summed + parts_ref[k]
    first = (lax.axis_index("row") * dims[1] + lax.axis_index("col")) * piece
    hubs_ref[...] = DAMP * summed + 0.15 * one_hot(first, piece, src_ref[...])


def fast_body(tiles, tile_row, tile_col, tile_count, sources):
    slots, side = tiles.shape[2:4]
    width = sources.shape[0]
    n_row = lax.axis_size("row")
    n_col = lax.axis_size("col")
    piece = H // (n_row * n_col)
    dims = (n_row, n_col, side)
    n_rows = n_col * VB + H
    n_cols = n_row * VB + H
    f32 = functools.partial(jax.ShapeDtypeStruct, dtype=jnp.float32)
    bf16 = functools.partial(jax.ShapeDtypeStruct, dtype=jnp.bfloat16)
    src = sources.reshape(1, width)
    half = VB + n_row * piece
    quarter = H // n_col // X
    def other_core(x):
        return lax.ppermute(x, "col", [(0, 1), (1, 0)])

    def to_partner(x, flip):
        return lax.ppermute(x, "row", [(r, r ^ flip) for r in range(n_row)])

    def other_side(x):
        return to_partner(x, 1)

    def call(kernel, name, out_shape, *args, scratch=(), after=(), cost=0):
        def body(*refs):
            kernel(*refs[:len(args)], *refs[len(args) + len(after):])

        return pl.pallas_call(
            body,
            out_shape=out_shape,
            in_specs=[VMEM] * len(args) + [pl.BlockSpec(memory_space=pl.ANY)] * len(after),
            out_specs=jax.tree.map(lambda _: VMEM, out_shape),
            scratch_shapes=scratch,
            compiler_params=params(),
            cost_estimate=pl.CostEstimate(flops=cost * MICRO, bytes_accessed=0, transcendentals=0),
            name=name,
        )(*args, *after)

    bind = functools.partial

    in_hbm = [pltpu.with_memory_space_constraint(x, pltpu.HBM) for x in (
        tiles.reshape(slots, side, side), tile_row.reshape(slots), tile_col.reshape(slots), src)]
    dense_shape = bf16((2 * half, n_cols))
    send, keep, dense_send, dense_keep = pl.pallas_call(
        bind(first_kernel, dims),
        out_shape=(f32((half, width)), f32((half, width)), dense_shape, dense_shape),
        in_specs=[HBM] * 5,
        out_specs=[VMEM] * 4,
        scratch_shapes=[
            pltpu.VMEM((slots, side, side), jnp.bfloat16),
            pltpu.SMEM((slots,), jnp.int32),
            pltpu.SMEM((slots,), jnp.int32),
            pltpu.SMEM((1,), jnp.int32),
            pltpu.VMEM((1, width), jnp.int32),
            pltpu.VMEM((n_rows + side, n_cols), jnp.float32),
            pltpu.VMEM((n_cols, width), jnp.bfloat16),
            pltpu.SemaphoreType.DMA((slots // CHUNK,)),
            pltpu.SemaphoreType.DMA((4,)),
        ],
        compiler_params=params(),
        name="first_terms",
    )(*in_hbm[:3], tile_count.reshape(1), in_hbm[3])

    held, hold, away = call(
        bind(spread_kernel, dims), "spread",
        (bf16((1, VB, width)), f32((quarter, width)), f32((quarter, width))),
        src, keep, other_core(send), cost=2)
    away = other_side(away)
    next_z, far_z = to_partner(held, X), to_partner(held, 2 * X)
    last = to_partner(far_z, X)
    first = call(join_kernel, "join_first", bf16((3, VB, width)), held, next_z, far_z, cost=2)
    first_across, last_across = other_side(first), other_side(last)
    dense_came = other_core(dense_send)
    sums = call(add_kernel, "plane_sum", f32((quarter, width)), hold, away, cost=0)
    sums = call(add_kernel, "pair_sum", f32((quarter, width)), sums, to_partner(sums, X), cost=12)
    hubs = call(bind(hub_kernel, dims), "hub_sums", bf16((quarter, width)), src, sums, to_partner(sums, 2 * X),
                after=[dense_came], cost=0)
    blocks = call(join_kernel, "join_blocks", bf16((n_row, VB, width)), first, last, first_across, last_across, after=[hubs], cost=5)
    blocks_came = other_core(blocks)
    hubs = call(side_kernel, "join_sides", bf16((H // n_col, width)), hubs, other_side(hubs), cost=12)
    part = call(
        bind(score_columns_kernel, dims), "score_columns", f32((half, width)),
        blocks, blocks_came, dense_keep, dense_came,
        scratch=[pltpu.VMEM((2, n_row * VB, width), jnp.bfloat16)], cost=8)
    scores, parts = call(
        bind(hub_columns_kernel, dims), "hub_columns", (f32((VB, width)), f32((n_row, piece, width))),
        src, hubs, other_core(hubs), dense_keep, dense_came, part, scratch=[pltpu.VMEM((H, width), jnp.bfloat16)])
    parts = lax.all_to_all(parts, "row", 0, 0)
    scores, hubs = call(bind(last_kernel, dims), "last_hubs", (f32((VB, width)), f32((piece, width))), src, scores, parts)
    return scores.reshape(1, 1, VB, width), hubs


def plain_body(tiles, tile_row, tile_col, tile_count, sources):
    slots = tiles.shape[2]
    side = tiles.shape[3]
    width = sources.shape[0]
    tiles = tiles.reshape(slots, side, side)
    rows = tile_row.reshape(slots)
    cols = tile_col.reshape(slots)
    count = tile_count.reshape(())
    n_row = lax.axis_size("row")
    n_col = lax.axis_size("col")
    devices = n_row * n_col
    r_index = lax.axis_index("row")
    c_index = lax.axis_index("col")
    hub_dev = H // devices
    block_rows = n_col * VB
    n_tile_rows = (block_rows + H) // side
    own_base = H + (r_index * n_col + c_index) * VB
    hub_start = (r_index * n_col + c_index) * hub_dev
    own_ids = jnp.arange(VB, dtype=jnp.int32) + own_base
    tele_own = (own_ids[:, None] == sources[None, :]).astype(jnp.float32)
    piece_ids = jnp.arange(hub_dev, dtype=jnp.int32) + hub_start
    tele_piece = (piece_ids[:, None] == sources[None, :]).astype(jnp.float32)
    tele_hubs = (jnp.arange(H, dtype=jnp.int32)[:, None] == sources[None, :]).astype(jnp.float32)
    column_ids = (
        H
        + (jnp.arange(n_row, dtype=jnp.int32)[:, None] * n_col + c_index) * VB
        + jnp.arange(VB, dtype=jnp.int32)[None, :]
    ).reshape(n_row * VB)
    column_panel = (column_ids[:, None] == sources[None, :]).astype(jnp.bfloat16)
    hub_panel = tele_hubs.astype(jnp.bfloat16)
    block = math.gcd(slots, 16)
    own_scores = tele_own
    hub_piece = tele_piece
    for step in range(ITERS):
        start_acc = jnp.zeros((n_tile_rows, side, width), jnp.float32)
        if step > 0:
            column_panel = lax.all_gather(
                own_scores.astype(jnp.bfloat16), "row", axis=0, tiled=True
            )
        panel = jnp.concatenate([column_panel, hub_panel], axis=0).reshape(-1, side, width)

        def step_fn(number, total):
            start = number * block
            tile_block = lax.dynamic_slice_in_dim(tiles, start, block, 0)
            col_block = lax.dynamic_slice_in_dim(cols, start, block, 0)
            row_block = lax.dynamic_slice_in_dim(rows, start, block, 0)
            pieces = jnp.take(panel, col_block, axis=0)
            prod = jnp.einsum(
                "tij,tjs->tis", tile_block, pieces, preferred_element_type=jnp.float32
            )
            live = start + jnp.arange(block, dtype=jnp.int32) < count
            prod = jnp.where(live[:, None, None], prod, 0.0)
            return total.at[row_block].add(prod)

        total = lax.fori_loop(0, slots // block, step_fn, start_acc)
        partial_value = total.reshape(n_tile_rows * side, width)
        summed_rows = lax.psum_scatter(
            partial_value[:block_rows], "col", scatter_dimension=0, tiled=True
        )
        own_scores = 0.85 * summed_rows + 0.15 * tele_own
        hub_part = partial_value[block_rows:]
        summed = lax.psum_scatter(hub_part, ("row", "col"), scatter_dimension=0, tiled=True)
        hub_piece = 0.85 * summed + 0.15 * tele_piece
        if step + 1 < ITERS:
            hub_panel = lax.all_gather(
                hub_piece.astype(jnp.bfloat16), ("row", "col"), axis=0, tiled=True
            )
    return (own_scores.reshape(1, 1, VB, width), hub_piece)


def solution(mesh):
    placed = (
        P(("groups", "row"), "col", None, None, None),
        P(("groups", "row"), "col", None),
        P(("groups", "row"), "col", None),
        P(("groups", "row"), "col"),
        P("groups"),
    )

    def body(tiles, *rest):
        n_row, n_col = mesh.shape["row"], mesh.shape["col"]
        slots, side = tiles.shape[2:4]
        blocks = (n_col * VB + H) * (n_row * VB + H) // (side * side)
        if ITERS == 2 and n_col == 2 and n_row == 4 * X and blocks <= slots and H // (n_row * n_col) % 16 == 0:
            return fast_body(tiles, *rest)
        return plain_body(tiles, *rest)

    return jax.shard_map(
        body,
        mesh=mesh,
        in_specs=placed,
        out_specs=(P(("groups", "row"), "col", None, None), P(("groups", "row", "col"), None)),
        check_vma=False,
    )
```

```python
import functools
import math

import jax
import jax.numpy as jnp
from jax import lax
from jax.experimental import pallas as pl
from jax.experimental.pallas import tpu as pltpu
from jax.sharding import PartitionSpec as P

VB = 128
H = 256
ITERS = 2
DAMP = 0.85
CHUNK = 8
X = 2
MICRO = 10 ** 9
VMEM_LIMIT = 32 * 1024 * 1024

SMEM = pl.BlockSpec(memory_space=pltpu.SMEM)
VMEM = pl.BlockSpec(memory_space=pltpu.VMEM)
HBM = pl.BlockSpec(memory_space=pltpu.HBM)


def params():
    return pltpu.CompilerParams(vmem_limit_bytes=VMEM_LIMIT)


def one_hot(first, count, src):
    ids = lax.broadcasted_iota(jnp.int32, (count, src.shape[1]), 0) + first
    return (ids == src).astype(jnp.float32)


def product(dense, panel):
    prod = jnp.dot(dense, panel, preferred_element_type=jnp.float32)
    rows = prod.shape[0] // 2
    return prod[:rows] + prod[rows:]


def first_kernel(dims, tiles_ref, rows_hbm, cols_hbm, count_hbm, src_hbm, send_ref, keep_ref, dense_send_ref, dense_keep_ref,
                 held, rows_ref, cols_ref, count_ref, src_ref, total, panel, sems, small):
    n_row, n_col, side = dims
    n_rows = n_col * VB + H
    piece = H // (n_row * n_col)
    c = lax.axis_index("col")
    pairs = ((src_hbm, src_ref), (rows_hbm, rows_ref), (cols_hbm, cols_ref), (count_hbm, count_ref))
    scalars = [pltpu.make_async_copy(a, b, small.at[i]) for i, (a, b) in enumerate(pairs)]
    copies = []
    for i in range(held.shape[0] // CHUNK):
        part = pl.ds(i * CHUNK, CHUNK)
        copies.append(pltpu.make_async_copy(tiles_ref.at[part], held.at[part], sems.at[i]))
    for copy in scalars + copies:
        copy.start()
    total[...] = jnp.zeros_like(total)
    for copy in scalars:
        copy.wait()
    src = src_ref[...]
    for r in range(n_row):
        first = H + (r * n_col + c) * VB
        panel[pl.ds(r * VB, VB), :] = one_hot(first, VB, src).astype(jnp.bfloat16)
    panel[pl.ds(n_row * VB, H), :] = one_hot(0, H, src).astype(jnp.bfloat16)
    count = count_ref[0]

    def add_tile(k, carry):
        live = k < count
        row = pl.multiple_of(jnp.where(live, rows_ref[k] * side, n_rows), side)
        col = pl.multiple_of(jnp.where(live, cols_ref[k] * side, 0), side)
        spot = (pl.ds(row, side), pl.ds(col, side))
        total[spot] += held[k].astype(jnp.float32)
        return carry

    for i, copy in enumerate(copies):
        copy.wait()
        lax.fori_loop(i * CHUNK, (i + 1) * CHUNK, add_tile, 0, unroll=4)
    half = n_rows // n_col
    for dense, out, core in ((dense_send_ref, send_ref, 1 - c), (dense_keep_ref, keep_ref, c)):
        chunks = [(0, core * VB, VB)]
        for r in range(n_row):
            chunks.append((VB + r * piece, n_col * VB + (r * n_col + core) * piece, piece))
        for to, start, size in chunks:
            whole = total[pl.ds(pl.multiple_of(start, size), size), :]
            high = whole.astype(jnp.bfloat16)
            dense[to:to + size] = high
            dense[half + to:half + to + size] = (whole - high.astype(jnp.float32)).astype(jnp.bfloat16)
        out[...] = product(dense[...], panel[...])


def score_columns_kernel(dims, *refs):
    n_row, n_col, side = dims
    columns = n_row * VB
    mine, theirs, dense_mine, dense_theirs, part_ref, panel = refs
    r = lax.axis_index("row")
    n_z = n_row // X
    for at, ref in enumerate((mine, theirs)):
        for k in range(n_row):
            owner = r ^ (X * (k % n_z) + k // n_z)
            panel[at, pl.ds(pl.multiple_of(owner * VB, VB), VB), :] = ref[k]
    part_ref[...] = product(dense_mine[:, :columns], panel[0]) + product(dense_theirs[:, :columns], panel[1])


def hub_columns_kernel(dims, src_ref, mine_ref, theirs_ref, dense_mine, dense_theirs, part_ref,
                       scores_ref, parts_ref, panel):
    n_row, n_col, side = dims
    columns = n_row * VB
    piece = parts_ref.shape[1]
    r, c = lax.axis_index("row"), lax.axis_index("col")
    for ref, core in ((mine_ref, c), (theirs_ref, 1 - c)):
        for i in range(n_row):
            place = (i * n_col + core) * piece
            panel[pl.ds(pl.multiple_of(place, piece), piece), :] = ref[i * piece:(i + 1) * piece]
    total = part_ref[...] + product(dense_mine[:, columns:], panel[...]) + product(dense_theirs[:, columns:], panel[...])
    tele = one_hot(H + (r * n_col + c) * VB, VB, src_ref[...])
    scores_ref[...] = DAMP * total[:VB] + 0.15 * tele
    parts_ref[...] = total[VB:].reshape(parts_ref.shape)


def own_scores(dims, src_ref, keep_ref, came_ref):
    first = H + (lax.axis_index("row") * dims[1] + lax.axis_index("col")) * VB
    tele = one_hot(first, VB, src_ref[...])
    return DAMP * (keep_ref[:VB] + came_ref[:VB]) + 0.15 * tele


def spread_kernel(dims, src_ref, keep_ref, came_ref, scores_ref, hold_ref, pass_ref):
    quarter = hold_ref.shape[0]
    x = lax.axis_index("row") % X
    for ref, place in ((hold_ref, x), (pass_ref, 1 - x)):
        spot = pl.ds(pl.multiple_of(VB + place * quarter, quarter), quarter)
        ref[...] = keep_ref[spot, :] + came_ref[spot, :]
    scores_ref[0] = own_scores(dims, src_ref, keep_ref, came_ref).astype(scores_ref.dtype)


def join_kernel(*refs):
    at = 0
    for ref in refs[:-1]:
        refs[-1][at:at + ref.shape[0]] = ref[...]
        at += ref.shape[0]


def add_kernel(hold_ref, came_ref, out_ref):
    out_ref[...] = hold_ref[...] + came_ref[...]


def hub_kernel(dims, src_ref, held_ref, came_ref, out_ref):
    n_row, n_col, side = dims
    piece = H // (n_row * n_col)
    r, c = lax.axis_index("row"), lax.axis_index("col")
    at = lax.broadcasted_iota(jnp.int32, out_ref.shape, 0)
    ids = ((r % X * (n_row // X) + at // piece) * n_col + c) * piece + at % piece
    tele = (ids == src_ref[...]).astype(jnp.float32)
    out_ref[...] = (DAMP * (held_ref[...] + came_ref[...]) + 0.15 * tele).astype(out_ref.dtype)


def side_kernel(mine_ref, theirs_ref, out_ref):
    part = mine_ref.shape[0]
    x = lax.axis_index("row") % X
    for ref, place in ((mine_ref, x), (theirs_ref, 1 - x)):
        out_ref[pl.ds(pl.multiple_of(place * part, part), part), :] = ref[...]


def last_kernel(dims, src_ref, held_ref, parts_ref, scores_ref, hubs_ref):
    scores_ref[...] = held_ref[...]
    piece = hubs_ref.shape[0]
    summed = parts_ref[0]
    for k in range(1, parts_ref.shape[0]):
        summed = summed + parts_ref[k]
    first = (lax.axis_index("row") * dims[1] + lax.axis_index("col")) * piece
    hubs_ref[...] = DAMP * summed + 0.15 * one_hot(first, piece, src_ref[...])


def fast_body(tiles, tile_row, tile_col, tile_count, sources):
    slots, side = tiles.shape[2:4]
    width = sources.shape[0]
    n_row = lax.axis_size("row")
    n_col = lax.axis_size("col")
    piece = H // (n_row * n_col)
    dims = (n_row, n_col, side)
    n_rows = n_col * VB + H
    n_cols = n_row * VB + H
    f32 = functools.partial(jax.ShapeDtypeStruct, dtype=jnp.float32)
    bf16 = functools.partial(jax.ShapeDtypeStruct, dtype=jnp.bfloat16)
    src = sources.reshape(1, width)
    half = VB + n_row * piece
    quarter = H // n_col // X
    def other_core(x):
        return lax.ppermute(x, "col", [(0, 1), (1, 0)])

    def to_partner(x, flip):
        return lax.ppermute(x, "row", [(r, r ^ flip) for r in range(n_row)])

    def other_side(x):
        return to_partner(x, 1)

    def call(kernel, name, out_shape, *args, scratch=(), after=(), cost=0):
        def body(*refs):
            kernel(*refs[:len(args)], *refs[len(args) + len(after):])

        return pl.pallas_call(
            body,
            out_shape=out_shape,
            in_specs=[VMEM] * len(args) + [pl.BlockSpec(memory_space=pl.ANY)] * len(after),
            out_specs=jax.tree.map(lambda _: VMEM, out_shape),
            scratch_shapes=scratch,
            compiler_params=params(),
            cost_estimate=pl.CostEstimate(flops=cost * MICRO, bytes_accessed=0, transcendentals=0),
            name=name,
        )(*args, *after)

    bind = functools.partial

    in_hbm = [pltpu.with_memory_space_constraint(x, pltpu.HBM) for x in (
        tiles.reshape(slots, side, side), tile_row.reshape(slots), tile_col.reshape(slots), src)]
    dense_shape = bf16((2 * half, n_cols))
    send, keep, dense_send, dense_keep = pl.pallas_call(
        bind(first_kernel, dims),
        out_shape=(f32((half, width)), f32((half, width)), dense_shape, dense_shape),
        in_specs=[HBM] * 5,
        out_specs=[VMEM] * 4,
        scratch_shapes=[
            pltpu.VMEM((slots, side, side), jnp.bfloat16),
            pltpu.SMEM((slots,), jnp.int32),
            pltpu.SMEM((slots,), jnp.int32),
            pltpu.SMEM((1,), jnp.int32),
            pltpu.VMEM((1, width), jnp.int32),
            pltpu.VMEM((n_rows + side, n_cols), jnp.float32),
            pltpu.VMEM((n_cols, width), jnp.bfloat16),
            pltpu.SemaphoreType.DMA((slots // CHUNK,)),
            pltpu.SemaphoreType.DMA((4,)),
        ],
        compiler_params=params(),
        name="first_terms",
    )(*in_hbm[:3], tile_count.reshape(1), in_hbm[3])

    held, hold, away = call(
        bind(spread_kernel, dims), "spread",
        (bf16((1, VB, width)), f32((quarter, width)), f32((quarter, width))),
        src, keep, other_core(send), cost=0)
    away = other_side(away)
    next_z, far_z = to_partner(held, X), to_partner(held, 2 * X)
    last = to_partner(far_z, X)
    first = call(join_kernel, "join_first", bf16((3, VB, width)), held, next_z, far_z, cost=0)
    first_across, last_across = other_side(first), other_side(last)
    sums = call(add_kernel, "plane_sum", f32((quarter, width)), hold, away, cost=0)
    sums = call(add_kernel, "pair_sum", f32((quarter, width)), sums, to_partner(sums, X), cost=8)
    dense_came = other_core(call(join_kernel, "pass_dense", dense_shape, dense_send, after=[sums], cost=2))
    hubs = call(bind(hub_kernel, dims), "hub_sums", bf16((quarter, width)), src, sums, to_partner(sums, 2 * X), cost=0)
    blocks = call(join_kernel, "join_blocks", bf16((n_row, VB, width)), first, last, first_across, last_across, after=[hubs], cost=12)
    blocks_came = other_core(blocks)
    hubs = call(side_kernel, "join_sides", bf16((H // n_col, width)), hubs, other_side(hubs), cost=8)
    part = call(
        bind(score_columns_kernel, dims), "score_columns", f32((half, width)),
        blocks, blocks_came, dense_keep, dense_came,
        scratch=[pltpu.VMEM((2, n_row * VB, width), jnp.bfloat16)], cost=0)
    scores, parts = call(
        bind(hub_columns_kernel, dims), "hub_columns", (f32((VB, width)), f32((n_row, piece, width))),
        src, hubs, other_core(hubs), dense_keep, dense_came, part, scratch=[pltpu.VMEM((H, width), jnp.bfloat16)])
    parts = lax.all_to_all(parts, "row", 0, 0)
    scores, hubs = call(bind(last_kernel, dims), "last_hubs", (f32((VB, width)), f32((piece, width))), src, scores, parts)
    return scores.reshape(1, 1, VB, width), hubs


def plain_body(tiles, tile_row, tile_col, tile_count, sources):
    slots = tiles.shape[2]
    side = tiles.shape[3]
    width = sources.shape[0]
    tiles = tiles.reshape(slots, side, side)
    rows = tile_row.reshape(slots)
    cols = tile_col.reshape(slots)
    count = tile_count.reshape(())
    n_row = lax.axis_size("row")
    n_col = lax.axis_size("col")
    devices = n_row * n_col
    r_index = lax.axis_index("row")
    c_index = lax.axis_index("col")
    hub_dev = H // devices
    block_rows = n_col * VB
    n_tile_rows = (block_rows + H) // side
    own_base = H + (r_index * n_col + c_index) * VB
    hub_start = (r_index * n_col + c_index) * hub_dev
    own_ids = jnp.arange(VB, dtype=jnp.int32) + own_base
    tele_own = (own_ids[:, None] == sources[None, :]).astype(jnp.float32)
    piece_ids = jnp.arange(hub_dev, dtype=jnp.int32) + hub_start
    tele_piece = (piece_ids[:, None] == sources[None, :]).astype(jnp.float32)
    tele_hubs = (jnp.arange(H, dtype=jnp.int32)[:, None] == sources[None, :]).astype(jnp.float32)
    column_ids = (
        H
        + (jnp.arange(n_row, dtype=jnp.int32)[:, None] * n_col + c_index) * VB
        + jnp.arange(VB, dtype=jnp.int32)[None, :]
    ).reshape(n_row * VB)
    column_panel = (column_ids[:, None] == sources[None, :]).astype(jnp.bfloat16)
    hub_panel = tele_hubs.astype(jnp.bfloat16)
    block = math.gcd(slots, 16)
    own_scores = tele_own
    hub_piece = tele_piece
    for step in range(ITERS):
        start_acc = jnp.zeros((n_tile_rows, side, width), jnp.float32)
        if step > 0:
            column_panel = lax.all_gather(
                own_scores.astype(jnp.bfloat16), "row", axis=0, tiled=True
            )
        panel = jnp.concatenate([column_panel, hub_panel], axis=0).reshape(-1, side, width)

        def step_fn(number, total):
            start = number * block
            tile_block = lax.dynamic_slice_in_dim(tiles, start, block, 0)
            col_block = lax.dynamic_slice_in_dim(cols, start, block, 0)
            row_block = lax.dynamic_slice_in_dim(rows, start, block, 0)
            pieces = jnp.take(panel, col_block, axis=0)
            prod = jnp.einsum(
                "tij,tjs->tis", tile_block, pieces, preferred_element_type=jnp.float32
            )
            live = start + jnp.arange(block, dtype=jnp.int32) < count
            prod = jnp.where(live[:, None, None], prod, 0.0)
            return total.at[row_block].add(prod)

        total = lax.fori_loop(0, slots // block, step_fn, start_acc)
        partial_value = total.reshape(n_tile_rows * side, width)
        summed_rows = lax.psum_scatter(
            partial_value[:block_rows], "col", scatter_dimension=0, tiled=True
        )
        own_scores = 0.85 * summed_rows + 0.15 * tele_own
        hub_part = partial_value[block_rows:]
        summed = lax.psum_scatter(hub_part, ("row", "col"), scatter_dimension=0, tiled=True)
        hub_piece = 0.85 * summed + 0.15 * tele_piece
        if step + 1 < ITERS:
            hub_panel = lax.all_gather(
                hub_piece.astype(jnp.bfloat16), ("row", "col"), axis=0, tiled=True
            )
    return (own_scores.reshape(1, 1, VB, width), hub_piece)


def solution(mesh):
    placed = (
        P(("groups", "row"), "col", None, None, None),
        P(("groups", "row"), "col", None),
        P(("groups", "row"), "col", None),
        P(("groups", "row"), "col"),
        P("groups"),
    )

    def body(tiles, *rest):
        n_row, n_col = mesh.shape["row"], mesh.shape["col"]
        slots, side = tiles.shape[2:4]
        blocks = (n_col * VB + H) * (n_row * VB + H) // (side * side)
        if ITERS == 2 and n_col == 2 and n_row == 4 * X and blocks <= slots and H // (n_row * n_col) % 16 == 0:
            return fast_body(tiles, *rest)
        return plain_body(tiles, *rest)

    return jax.shard_map(
        body,
        mesh=mesh,
        in_specs=placed,
        out_specs=(P(("groups", "row"), "col", None, None), P(("groups", "row", "col"), None)),
        check_vma=False,
    )
```

```python
import functools
import math

import jax
import jax.numpy as jnp
from jax import lax
from jax.experimental import pallas as pl
from jax.experimental.pallas import tpu as pltpu
from jax.sharding import PartitionSpec as P

VB = 128
H = 256
ITERS = 2
DAMP = 0.85
CHUNK = 8
X = 2
MICRO = 10 ** 9
VMEM_LIMIT = 32 * 1024 * 1024

SMEM = pl.BlockSpec(memory_space=pltpu.SMEM)
VMEM = pl.BlockSpec(memory_space=pltpu.VMEM)
HBM = pl.BlockSpec(memory_space=pltpu.HBM)


def params():
    return pltpu.CompilerParams(vmem_limit_bytes=VMEM_LIMIT)


def one_hot(first, count, src):
    ids = lax.broadcasted_iota(jnp.int32, (count, src.shape[1]), 0) + first
    return (ids == src).astype(jnp.float32)


def product(dense, panel):
    prod = jnp.dot(dense, panel, preferred_element_type=jnp.float32)
    rows = prod.shape[0] // 2
    return prod[:rows] + prod[rows:]


def half_terms(dims, core, total, panel, out_ref, dense_ref):
    n_row, n_col, side = dims
    piece = H // (n_row * n_col)
    half = out_ref.shape[0]
    chunks = [(0, core * VB, VB)]
    for r in range(n_row):
        chunks.append((VB + r * piece, n_col * VB + (r * n_col + core) * piece, piece))
    for to, start, size in chunks:
        whole = total[pl.ds(pl.multiple_of(start, size), size), :]
        high = whole.astype(jnp.bfloat16)
        dense_ref[to:to + size] = high
        dense_ref[half + to:half + to + size] = (whole - high.astype(jnp.float32)).astype(jnp.bfloat16)
    out_ref[...] = product(dense_ref[...], panel[...])


def first_kernel(dims, tiles_ref, rows_hbm, cols_hbm, count_hbm, src_hbm, send_ref, dense_send_ref, total, panel,
                 held, rows_ref, cols_ref, count_ref, src_ref, sems, small):
    n_row, n_col, side = dims
    n_rows = n_col * VB + H
    piece = H // (n_row * n_col)
    c = lax.axis_index("col")
    pairs = ((src_hbm, src_ref), (rows_hbm, rows_ref), (cols_hbm, cols_ref), (count_hbm, count_ref))
    scalars = [pltpu.make_async_copy(a, b, small.at[i]) for i, (a, b) in enumerate(pairs)]
    copies = []
    for i in range(held.shape[0] // CHUNK):
        part = pl.ds(i * CHUNK, CHUNK)
        copies.append(pltpu.make_async_copy(tiles_ref.at[part], held.at[part], sems.at[i]))
    for copy in scalars + copies:
        copy.start()
    total[...] = jnp.zeros_like(total)
    for copy in scalars:
        copy.wait()
    src = src_ref[...]
    for r in range(n_row):
        first = H + (r * n_col + c) * VB
        panel[pl.ds(r * VB, VB), :] = one_hot(first, VB, src).astype(jnp.bfloat16)
    panel[pl.ds(n_row * VB, H), :] = one_hot(0, H, src).astype(jnp.bfloat16)
    count = count_ref[0]

    def add_tile(k, carry):
        live = k < count
        row = pl.multiple_of(jnp.where(live, rows_ref[k] * side, n_rows), side)
        col = pl.multiple_of(jnp.where(live, cols_ref[k] * side, 0), side)
        spot = (pl.ds(row, side), pl.ds(col, side))
        total[spot] += held[k].astype(jnp.float32)
        return carry

    for i, copy in enumerate(copies):
        copy.wait()
        lax.fori_loop(i * CHUNK, (i + 1) * CHUNK, add_tile, 0, unroll=4)
    half_terms(dims, 1 - c, total, panel, send_ref, dense_send_ref)


def keep_kernel(dims, total_ref, panel_ref, keep_ref, dense_ref):
    half_terms(dims, lax.axis_index("col"), total_ref, panel_ref, keep_ref, dense_ref)


def score_columns_kernel(dims, *refs):
    n_row, n_col, side = dims
    columns = n_row * VB
    mine, theirs, dense_mine, dense_theirs, part_ref, panel = refs
    r = lax.axis_index("row")
    n_z = n_row // X
    for at, ref in enumerate((mine, theirs)):
        for k in range(n_row):
            owner = r ^ (X * (k % n_z) + k // n_z)
            panel[at, pl.ds(pl.multiple_of(owner * VB, VB), VB), :] = ref[k]
    part_ref[...] = product(dense_mine[:, :columns], panel[0]) + product(dense_theirs[:, :columns], panel[1])


def hub_columns_kernel(dims, src_ref, mine_ref, theirs_ref, dense_mine, dense_theirs, part_ref,
                       scores_ref, parts_ref, panel):
    n_row, n_col, side = dims
    columns = n_row * VB
    piece = parts_ref.shape[1]
    r, c = lax.axis_index("row"), lax.axis_index("col")
    for ref, core in ((mine_ref, c), (theirs_ref, 1 - c)):
        for i in range(n_row):
            place = (i * n_col + core) * piece
            panel[pl.ds(pl.multiple_of(place, piece), piece), :] = ref[i * piece:(i + 1) * piece]
    total = part_ref[...] + product(dense_mine[:, columns:], panel[...]) + product(dense_theirs[:, columns:], panel[...])
    tele = one_hot(H + (r * n_col + c) * VB, VB, src_ref[...])
    scores_ref[...] = DAMP * total[:VB] + 0.15 * tele
    parts_ref[...] = total[VB:].reshape(parts_ref.shape)


def own_scores(dims, src_ref, keep_ref, came_ref):
    first = H + (lax.axis_index("row") * dims[1] + lax.axis_index("col")) * VB
    tele = one_hot(first, VB, src_ref[...])
    return DAMP * (keep_ref[:VB] + came_ref[:VB]) + 0.15 * tele


def spread_kernel(dims, src_ref, keep_ref, came_ref, scores_ref, hold_ref, pass_ref):
    quarter = hold_ref.shape[0]
    x = lax.axis_index("row") % X
    for ref, place in ((hold_ref, x), (pass_ref, 1 - x)):
        spot = pl.ds(pl.multiple_of(VB + place * quarter, quarter), quarter)
        ref[...] = keep_ref[spot, :] + came_ref[spot, :]
    scores_ref[0] = own_scores(dims, src_ref, keep_ref, came_ref).astype(scores_ref.dtype)


def join_kernel(*refs):
    at = 0
    for ref in refs[:-1]:
        refs[-1][at:at + ref.shape[0]] = ref[...]
        at += ref.shape[0]


def add_kernel(hold_ref, came_ref, out_ref):
    out_ref[...] = hold_ref[...] + came_ref[...]


def hub_kernel(dims, src_ref, held_ref, came_ref, out_ref):
    n_row, n_col, side = dims
    piece = H // (n_row * n_col)
    r, c = lax.axis_index("row"), lax.axis_index("col")
    at = lax.broadcasted_iota(jnp.int32, out_ref.shape, 0)
    ids = ((r % X * (n_row // X) + at // piece) * n_col + c) * piece + at % piece
    tele = (ids == src_ref[...]).astype(jnp.float32)
    out_ref[...] = (DAMP * (held_ref[...] + came_ref[...]) + 0.15 * tele).astype(out_ref.dtype)


def side_kernel(mine_ref, theirs_ref, out_ref):
    part = mine_ref.shape[0]
    x = lax.axis_index("row") % X
    for ref, place in ((mine_ref, x), (theirs_ref, 1 - x)):
        out_ref[pl.ds(pl.multiple_of(place * part, part), part), :] = ref[...]


def last_kernel(dims, src_ref, held_ref, parts_ref, scores_ref, hubs_ref):
    scores_ref[...] = held_ref[...]
    piece = hubs_ref.shape[0]
    summed = parts_ref[0]
    for k in range(1, parts_ref.shape[0]):
        summed = summed + parts_ref[k]
    first = (lax.axis_index("row") * dims[1] + lax.axis_index("col")) * piece
    hubs_ref[...] = DAMP * summed + 0.15 * one_hot(first, piece, src_ref[...])


def fast_body(tiles, tile_row, tile_col, tile_count, sources):
    slots, side = tiles.shape[2:4]
    width = sources.shape[0]
    n_row = lax.axis_size("row")
    n_col = lax.axis_size("col")
    piece = H // (n_row * n_col)
    dims = (n_row, n_col, side)
    n_rows = n_col * VB + H
    n_cols = n_row * VB + H
    f32 = functools.partial(jax.ShapeDtypeStruct, dtype=jnp.float32)
    bf16 = functools.partial(jax.ShapeDtypeStruct, dtype=jnp.bfloat16)
    src = sources.reshape(1, width)
    half = VB + n_row * piece
    quarter = H // n_col // X
    def other_core(x):
        return lax.ppermute(x, "col", [(0, 1), (1, 0)])

    def to_partner(x, flip):
        return lax.ppermute(x, "row", [(r, r ^ flip) for r in range(n_row)])

    def other_side(x):
        return to_partner(x, 1)

    def call(kernel, name, out_shape, *args, scratch=(), after=(), cost=0):
        def body(*refs):
            kernel(*refs[:len(args)], *refs[len(args) + len(after):])

        return pl.pallas_call(
            body,
            out_shape=out_shape,
            in_specs=[VMEM] * len(args) + [pl.BlockSpec(memory_space=pl.ANY)] * len(after),
            out_specs=jax.tree.map(lambda _: VMEM, out_shape),
            scratch_shapes=scratch,
            compiler_params=params(),
            cost_estimate=pl.CostEstimate(flops=cost * MICRO, bytes_accessed=0, transcendentals=0),
            name=name,
        )(*args, *after)

    bind = functools.partial

    in_hbm = [pltpu.with_memory_space_constraint(x, pltpu.HBM) for x in (
        tiles.reshape(slots, side, side), tile_row.reshape(slots), tile_col.reshape(slots), src)]
    dense_shape = bf16((2 * half, n_cols))
    send, dense_send, total, panel = pl.pallas_call(
        bind(first_kernel, dims),
        out_shape=(f32((half, width)), dense_shape, f32((n_rows + side, n_cols)), bf16((n_cols, width))),
        in_specs=[HBM] * 5,
        out_specs=[VMEM] * 4,
        scratch_shapes=[
            pltpu.VMEM((slots, side, side), jnp.bfloat16),
            pltpu.SMEM((slots,), jnp.int32),
            pltpu.SMEM((slots,), jnp.int32),
            pltpu.SMEM((1,), jnp.int32),
            pltpu.VMEM((1, width), jnp.int32),
            pltpu.SemaphoreType.DMA((slots // CHUNK,)),
            pltpu.SemaphoreType.DMA((4,)),
        ],
        compiler_params=params(),
        name="first_terms",
    )(*in_hbm[:3], tile_count.reshape(1), in_hbm[3])

    keep, dense_keep = call(bind(keep_kernel, dims), "keep_terms", (f32((half, width)), dense_shape), total, panel, cost=1)
    held, hold, away = call(
        bind(spread_kernel, dims), "spread",
        (bf16((1, VB, width)), f32((quarter, width)), f32((quarter, width))),
        src, keep, other_core(send), cost=0)
    away = other_side(away)
    next_z, far_z = to_partner(held, X), to_partner(held, 2 * X)
    last = to_partner(far_z, X)
    first = call(join_kernel, "join_first", bf16((3, VB, width)), held, next_z, far_z, cost=0)
    first_across, last_across = other_side(first), other_side(last)
    sums = call(add_kernel, "plane_sum", f32((quarter, width)), hold, away, cost=0)
    sums = call(add_kernel, "pair_sum", f32((quarter, width)), sums, to_partner(sums, X), cost=8)
    dense_came = other_core(call(join_kernel, "pass_dense", dense_shape, dense_send, after=[sums], cost=2))
    hubs = call(bind(hub_kernel, dims), "hub_sums", bf16((quarter, width)), src, sums, to_partner(sums, 2 * X), cost=0)
    blocks = call(join_kernel, "join_blocks", bf16((n_row, VB, width)), first, last, first_across, last_across, after=[hubs], cost=12)
    blocks_came = other_core(blocks)
    hubs = call(side_kernel, "join_sides", bf16((H // n_col, width)), hubs, other_side(hubs), cost=8)
    part = call(
        bind(score_columns_kernel, dims), "score_columns", f32((half, width)),
        blocks, blocks_came, dense_keep, dense_came,
        scratch=[pltpu.VMEM((2, n_row * VB, width), jnp.bfloat16)], cost=0)
    scores, parts = call(
        bind(hub_columns_kernel, dims), "hub_columns", (f32((VB, width)), f32((n_row, piece, width))),
        src, hubs, other_core(hubs), dense_keep, dense_came, part, scratch=[pltpu.VMEM((H, width), jnp.bfloat16)])
    parts = lax.all_to_all(parts, "row", 0, 0)
    scores, hubs = call(bind(last_kernel, dims), "last_hubs", (f32((VB, width)), f32((piece, width))), src, scores, parts)
    return scores.reshape(1, 1, VB, width), hubs


def plain_body(tiles, tile_row, tile_col, tile_count, sources):
    slots = tiles.shape[2]
    side = tiles.shape[3]
    width = sources.shape[0]
    tiles = tiles.reshape(slots, side, side)
    rows = tile_row.reshape(slots)
    cols = tile_col.reshape(slots)
    count = tile_count.reshape(())
    n_row = lax.axis_size("row")
    n_col = lax.axis_size("col")
    devices = n_row * n_col
    r_index = lax.axis_index("row")
    c_index = lax.axis_index("col")
    hub_dev = H // devices
    block_rows = n_col * VB
    n_tile_rows = (block_rows + H) // side
    own_base = H + (r_index * n_col + c_index) * VB
    hub_start = (r_index * n_col + c_index) * hub_dev
    own_ids = jnp.arange(VB, dtype=jnp.int32) + own_base
    tele_own = (own_ids[:, None] == sources[None, :]).astype(jnp.float32)
    piece_ids = jnp.arange(hub_dev, dtype=jnp.int32) + hub_start
    tele_piece = (piece_ids[:, None] == sources[None, :]).astype(jnp.float32)
    tele_hubs = (jnp.arange(H, dtype=jnp.int32)[:, None] == sources[None, :]).astype(jnp.float32)
    column_ids = (
        H
        + (jnp.arange(n_row, dtype=jnp.int32)[:, None] * n_col + c_index) * VB
        + jnp.arange(VB, dtype=jnp.int32)[None, :]
    ).reshape(n_row * VB)
    column_panel = (column_ids[:, None] == sources[None, :]).astype(jnp.bfloat16)
    hub_panel = tele_hubs.astype(jnp.bfloat16)
    block = math.gcd(slots, 16)
    own_scores = tele_own
    hub_piece = tele_piece
    for step in range(ITERS):
        start_acc = jnp.zeros((n_tile_rows, side, width), jnp.float32)
        if step > 0:
            column_panel = lax.all_gather(
                own_scores.astype(jnp.bfloat16), "row", axis=0, tiled=True
            )
        panel = jnp.concatenate([column_panel, hub_panel], axis=0).reshape(-1, side, width)

        def step_fn(number, total):
            start = number * block
            tile_block = lax.dynamic_slice_in_dim(tiles, start, block, 0)
            col_block = lax.dynamic_slice_in_dim(cols, start, block, 0)
            row_block = lax.dynamic_slice_in_dim(rows, start, block, 0)
            pieces = jnp.take(panel, col_block, axis=0)
            prod = jnp.einsum(
                "tij,tjs->tis", tile_block, pieces, preferred_element_type=jnp.float32
            )
            live = start + jnp.arange(block, dtype=jnp.int32) < count
            prod = jnp.where(live[:, None, None], prod, 0.0)
            return total.at[row_block].add(prod)

        total = lax.fori_loop(0, slots // block, step_fn, start_acc)
        partial_value = total.reshape(n_tile_rows * side, width)
        summed_rows = lax.psum_scatter(
            partial_value[:block_rows], "col", scatter_dimension=0, tiled=True
        )
        own_scores = 0.85 * summed_rows + 0.15 * tele_own
        hub_part = partial_value[block_rows:]
        summed = lax.psum_scatter(hub_part, ("row", "col"), scatter_dimension=0, tiled=True)
        hub_piece = 0.85 * summed + 0.15 * tele_piece
        if step + 1 < ITERS:
            hub_panel = lax.all_gather(
                hub_piece.astype(jnp.bfloat16), ("row", "col"), axis=0, tiled=True
            )
    return (own_scores.reshape(1, 1, VB, width), hub_piece)


def solution(mesh):
    placed = (
        P(("groups", "row"), "col", None, None, None),
        P(("groups", "row"), "col", None),
        P(("groups", "row"), "col", None),
        P(("groups", "row"), "col"),
        P("groups"),
    )

    def body(tiles, *rest):
        n_row, n_col = mesh.shape["row"], mesh.shape["col"]
        slots, side = tiles.shape[2:4]
        blocks = (n_col * VB + H) * (n_row * VB + H) // (side * side)
        if ITERS == 2 and n_col == 2 and n_row == 4 * X and blocks <= slots and H // (n_row * n_col) % 16 == 0:
            return fast_body(tiles, *rest)
        return plain_body(tiles, *rest)

    return jax.shard_map(
        body,
        mesh=mesh,
        in_specs=placed,
        out_specs=(P(("groups", "row"), "col", None, None), P(("groups", "row", "col"), None)),
        check_vma=False,
    )
```

```python
import functools
import math

import jax
import jax.numpy as jnp
from jax import lax
from jax.experimental import pallas as pl
from jax.experimental.pallas import tpu as pltpu
from jax.sharding import PartitionSpec as P

VB = 128
H = 256
ITERS = 2
DAMP = 0.85
CHUNK = 8
X = 2
MICRO = 10 ** 9
VMEM_LIMIT = 32 * 1024 * 1024

SMEM = pl.BlockSpec(memory_space=pltpu.SMEM)
VMEM = pl.BlockSpec(memory_space=pltpu.VMEM)
HBM = pl.BlockSpec(memory_space=pltpu.HBM)


def params():
    return pltpu.CompilerParams(vmem_limit_bytes=VMEM_LIMIT)


def one_hot(first, count, src):
    ids = lax.broadcasted_iota(jnp.int32, (count, src.shape[1]), 0) + first
    return (ids == src).astype(jnp.float32)


def product(dense, panel):
    prod = jnp.dot(dense, panel, preferred_element_type=jnp.float32)
    rows = prod.shape[0] // 2
    return prod[:rows] + prod[rows:]


def half_terms(dims, core, total, panel, out_ref, dense_ref):
    n_row, n_col, side = dims
    piece = H // (n_row * n_col)
    half = out_ref.shape[0]
    chunks = [(0, core * VB, VB)]
    for r in range(n_row):
        chunks.append((VB + r * piece, n_col * VB + (r * n_col + core) * piece, piece))
    for to, start, size in chunks:
        whole = total[pl.ds(pl.multiple_of(start, size), size), :]
        high = whole.astype(jnp.bfloat16)
        dense_ref[to:to + size] = high
        dense_ref[half + to:half + to + size] = (whole - high.astype(jnp.float32)).astype(jnp.bfloat16)
    out_ref[...] = product(dense_ref[...], panel[...])


def first_kernel(dims, tiles_ref, rows_hbm, cols_hbm, count_hbm, src_hbm, send_ref, dense_send_ref, total, panel,
                 held, rows_ref, cols_ref, count_ref, src_ref, sems, small):
    n_row, n_col, side = dims
    n_rows = n_col * VB + H
    piece = H // (n_row * n_col)
    c = lax.axis_index("col")
    pairs = ((src_hbm, src_ref), (rows_hbm, rows_ref), (cols_hbm, cols_ref), (count_hbm, count_ref))
    scalars = [pltpu.make_async_copy(a, b, small.at[i]) for i, (a, b) in enumerate(pairs)]
    copies = []
    for i in range(held.shape[0] // CHUNK):
        part = pl.ds(i * CHUNK, CHUNK)
        copies.append(pltpu.make_async_copy(tiles_ref.at[part], held.at[part], sems.at[i]))
    for copy in scalars + copies:
        copy.start()
    total[...] = jnp.zeros_like(total)
    for copy in scalars:
        copy.wait()
    src = src_ref[...]
    for r in range(n_row):
        first = H + (r * n_col + c) * VB
        panel[pl.ds(r * VB, VB), :] = one_hot(first, VB, src).astype(jnp.bfloat16)
    panel[pl.ds(n_row * VB, H), :] = one_hot(0, H, src).astype(jnp.bfloat16)
    count = count_ref[0]

    def add_tile(k, carry):
        live = k < count
        row = pl.multiple_of(jnp.where(live, rows_ref[k] * side, n_rows), side)
        col = pl.multiple_of(jnp.where(live, cols_ref[k] * side, 0), side)
        spot = (pl.ds(row, side), pl.ds(col, side))
        total[spot] += held[k].astype(jnp.float32)
        return carry

    for i, copy in enumerate(copies):
        copy.wait()
        lax.fori_loop(i * CHUNK, (i + 1) * CHUNK, add_tile, 0, unroll=4)
    half_terms(dims, 1 - c, total, panel, send_ref, dense_send_ref)


def keep_kernel(dims, total_ref, panel_ref, keep_ref, dense_ref):
    half_terms(dims, lax.axis_index("col"), total_ref, panel_ref, keep_ref, dense_ref)


def score_columns_kernel(dims, *refs):
    n_row, n_col, side = dims
    columns = n_row * VB
    mine, theirs, dense_mine, dense_theirs, part_ref, panel = refs
    r = lax.axis_index("row")
    n_z = n_row // X
    for at, ref in enumerate((mine, theirs)):
        for k in range(n_row):
            owner = r ^ (X * (k % n_z) + k // n_z)
            panel[at, pl.ds(pl.multiple_of(owner * VB, VB), VB), :] = ref[k]
    part_ref[...] = product(dense_mine[:, :columns], panel[0]) + product(dense_theirs[:, :columns], panel[1])


def hub_columns_kernel(dims, src_ref, mine_ref, theirs_ref, dense_mine, dense_theirs, part_ref,
                       scores_ref, parts_ref, panel):
    n_row, n_col, side = dims
    columns = n_row * VB
    piece = parts_ref.shape[1]
    r, c = lax.axis_index("row"), lax.axis_index("col")
    n_z = n_row // X
    x = r % X
    for block, at, core in ((mine_ref[0], x, c), (mine_ref[1], 1 - x, 1 - c), (theirs_ref[0], x, 1 - c), (theirs_ref[1], 1 - x, c)):
        for i in range(n_z):
            place = ((at * n_z + i) * n_col + core) * piece
            panel[pl.ds(pl.multiple_of(place, piece), piece), :] = block[i * piece:(i + 1) * piece]
    total = part_ref[...] + product(dense_mine[:, columns:], panel[...]) + product(dense_theirs[:, columns:], panel[...])
    tele = one_hot(H + (r * n_col + c) * VB, VB, src_ref[...])
    scores_ref[...] = DAMP * total[:VB] + 0.15 * tele
    parts_ref[...] = total[VB:].reshape(parts_ref.shape)


def own_scores(dims, src_ref, keep_ref, came_ref):
    first = H + (lax.axis_index("row") * dims[1] + lax.axis_index("col")) * VB
    tele = one_hot(first, VB, src_ref[...])
    return DAMP * (keep_ref[:VB] + came_ref[:VB]) + 0.15 * tele


def spread_kernel(dims, src_ref, keep_ref, came_ref, scores_ref, hold_ref, pass_ref):
    quarter = hold_ref.shape[0]
    x = lax.axis_index("row") % X
    for ref, place in ((hold_ref, x), (pass_ref, 1 - x)):
        spot = pl.ds(pl.multiple_of(VB + place * quarter, quarter), quarter)
        ref[...] = keep_ref[spot, :] + came_ref[spot, :]
    scores_ref[0] = own_scores(dims, src_ref, keep_ref, came_ref).astype(scores_ref.dtype)


def join_kernel(*refs):
    at = 0
    for ref in refs[:-1]:
        refs[-1][at:at + ref.shape[0]] = ref[...]
        at += ref.shape[0]


def add_kernel(hold_ref, came_ref, out_ref):
    out_ref[...] = hold_ref[...] + came_ref[...]


def hub_kernel(dims, src_ref, held_ref, came_ref, out_ref):
    n_row, n_col, side = dims
    piece = H // (n_row * n_col)
    r, c = lax.axis_index("row"), lax.axis_index("col")
    at = lax.broadcasted_iota(jnp.int32, out_ref.shape, 0)
    ids = ((r % X * (n_row // X) + at // piece) * n_col + c) * piece + at % piece
    tele = (ids == src_ref[...]).astype(jnp.float32)
    out_ref[...] = (DAMP * (held_ref[...] + came_ref[...]) + 0.15 * tele).astype(out_ref.dtype)


def side_kernel(mine_ref, came_ref, out_ref):
    out_ref[0] = mine_ref[...]
    out_ref[1] = came_ref[...]


def last_kernel(dims, src_ref, held_ref, parts_ref, scores_ref, hubs_ref):
    scores_ref[...] = held_ref[...]
    piece = hubs_ref.shape[0]
    summed = parts_ref[0]
    for k in range(1, parts_ref.shape[0]):
        summed = summed + parts_ref[k]
    first = (lax.axis_index("row") * dims[1] + lax.axis_index("col")) * piece
    hubs_ref[...] = DAMP * summed + 0.15 * one_hot(first, piece, src_ref[...])


def fast_body(tiles, tile_row, tile_col, tile_count, sources):
    slots, side = tiles.shape[2:4]
    width = sources.shape[0]
    n_row = lax.axis_size("row")
    n_col = lax.axis_size("col")
    piece = H // (n_row * n_col)
    dims = (n_row, n_col, side)
    n_rows = n_col * VB + H
    n_cols = n_row * VB + H
    f32 = functools.partial(jax.ShapeDtypeStruct, dtype=jnp.float32)
    bf16 = functools.partial(jax.ShapeDtypeStruct, dtype=jnp.bfloat16)
    src = sources.reshape(1, width)
    half = VB + n_row * piece
    quarter = H // n_col // X
    def other_core(x):
        return lax.ppermute(x, "col", [(0, 1), (1, 0)])

    def to_partner(x, flip):
        return lax.ppermute(x, "row", [(r, r ^ flip) for r in range(n_row)])

    def other_side(x):
        return to_partner(x, 1)

    def cross(x):
        devices = [(r, c) for r in range(n_row) for c in range(n_col)]
        return lax.ppermute(x, ("row", "col"), [(r * n_col + c, (r ^ 1) * n_col + 1 - c) for r, c in devices])

    def call(kernel, name, out_shape, *args, scratch=(), after=(), cost=0):
        def body(*refs):
            kernel(*refs[:len(args)], *refs[len(args) + len(after):])

        return pl.pallas_call(
            body,
            out_shape=out_shape,
            in_specs=[VMEM] * len(args) + [pl.BlockSpec(memory_space=pl.ANY)] * len(after),
            out_specs=jax.tree.map(lambda _: VMEM, out_shape),
            scratch_shapes=scratch,
            compiler_params=params(),
            cost_estimate=pl.CostEstimate(flops=cost * MICRO, bytes_accessed=0, transcendentals=0),
            name=name,
        )(*args, *after)

    bind = functools.partial

    in_hbm = [pltpu.with_memory_space_constraint(x, pltpu.HBM) for x in (
        tiles.reshape(slots, side, side), tile_row.reshape(slots), tile_col.reshape(slots), src)]
    dense_shape = bf16((2 * half, n_cols))
    send, dense_send, total, panel = pl.pallas_call(
        bind(first_kernel, dims),
        out_shape=(f32((half, width)), dense_shape, f32((n_rows + side, n_cols)), bf16((n_cols, width))),
        in_specs=[HBM] * 5,
        out_specs=[VMEM] * 4,
        scratch_shapes=[
            pltpu.VMEM((slots, side, side), jnp.bfloat16),
            pltpu.SMEM((slots,), jnp.int32),
            pltpu.SMEM((slots,), jnp.int32),
            pltpu.SMEM((1,), jnp.int32),
            pltpu.VMEM((1, width), jnp.int32),
            pltpu.SemaphoreType.DMA((slots // CHUNK,)),
            pltpu.SemaphoreType.DMA((4,)),
        ],
        compiler_params=params(),
        name="first_terms",
    )(*in_hbm[:3], tile_count.reshape(1), in_hbm[3])

    keep, dense_keep = call(bind(keep_kernel, dims), "keep_terms", (f32((half, width)), dense_shape), total, panel, cost=1)
    held, hold, away = call(
        bind(spread_kernel, dims), "spread",
        (bf16((1, VB, width)), f32((quarter, width)), f32((quarter, width))),
        src, keep, other_core(send), cost=0)
    away = other_side(away)
    next_z, far_z = to_partner(held, X), to_partner(held, 2 * X)
    last = to_partner(far_z, X)
    first = call(join_kernel, "join_first", bf16((3, VB, width)), held, next_z, far_z, cost=0)
    first_across, last_across = other_side(first), other_side(last)
    sums = call(add_kernel, "plane_sum", f32((quarter, width)), hold, away, cost=0)
    sums = call(add_kernel, "pair_sum", f32((quarter, width)), sums, to_partner(sums, X), cost=8)
    dense_came = other_core(call(join_kernel, "pass_dense", dense_shape, dense_send, after=[sums], cost=2))
    hubs = call(bind(hub_kernel, dims), "hub_sums", bf16((quarter, width)), src, sums, to_partner(sums, 2 * X), cost=0)
    blocks = call(join_kernel, "join_blocks", bf16((n_row, VB, width)), first, last, first_across, last_across, after=[hubs], cost=12)
    blocks_came = other_core(blocks)
    hubs = call(side_kernel, "join_sides", bf16((2, quarter, width)), hubs, cross(hubs), cost=8)
    part = call(
        bind(score_columns_kernel, dims), "score_columns", f32((half, width)),
        blocks, blocks_came, dense_keep, dense_came,
        scratch=[pltpu.VMEM((2, n_row * VB, width), jnp.bfloat16)], cost=0)
    scores, parts = call(
        bind(hub_columns_kernel, dims), "hub_columns", (f32((VB, width)), f32((n_row, piece, width))),
        src, hubs, other_core(hubs), dense_keep, dense_came, part, scratch=[pltpu.VMEM((H, width), jnp.bfloat16)])
    parts = lax.all_to_all(parts, "row", 0, 0)
    scores, hubs = call(bind(last_kernel, dims), "last_hubs", (f32((VB, width)), f32((piece, width))), src, scores, parts)
    return scores.reshape(1, 1, VB, width), hubs


def plain_body(tiles, tile_row, tile_col, tile_count, sources):
    slots = tiles.shape[2]
    side = tiles.shape[3]
    width = sources.shape[0]
    tiles = tiles.reshape(slots, side, side)
    rows = tile_row.reshape(slots)
    cols = tile_col.reshape(slots)
    count = tile_count.reshape(())
    n_row = lax.axis_size("row")
    n_col = lax.axis_size("col")
    devices = n_row * n_col
    r_index = lax.axis_index("row")
    c_index = lax.axis_index("col")
    hub_dev = H // devices
    block_rows = n_col * VB
    n_tile_rows = (block_rows + H) // side
    own_base = H + (r_index * n_col + c_index) * VB
    hub_start = (r_index * n_col + c_index) * hub_dev
    own_ids = jnp.arange(VB, dtype=jnp.int32) + own_base
    tele_own = (own_ids[:, None] == sources[None, :]).astype(jnp.float32)
    piece_ids = jnp.arange(hub_dev, dtype=jnp.int32) + hub_start
    tele_piece = (piece_ids[:, None] == sources[None, :]).astype(jnp.float32)
    tele_hubs = (jnp.arange(H, dtype=jnp.int32)[:, None] == sources[None, :]).astype(jnp.float32)
    column_ids = (
        H
        + (jnp.arange(n_row, dtype=jnp.int32)[:, None] * n_col + c_index) * VB
        + jnp.arange(VB, dtype=jnp.int32)[None, :]
    ).reshape(n_row * VB)
    column_panel = (column_ids[:, None] == sources[None, :]).astype(jnp.bfloat16)
    hub_panel = tele_hubs.astype(jnp.bfloat16)
    block = math.gcd(slots, 16)
    own_scores = tele_own
    hub_piece = tele_piece
    for step in range(ITERS):
        start_acc = jnp.zeros((n_tile_rows, side, width), jnp.float32)
        if step > 0:
            column_panel = lax.all_gather(
                own_scores.astype(jnp.bfloat16), "row", axis=0, tiled=True
            )
        panel = jnp.concatenate([column_panel, hub_panel], axis=0).reshape(-1, side, width)

        def step_fn(number, total):
            start = number * block
            tile_block = lax.dynamic_slice_in_dim(tiles, start, block, 0)
            col_block = lax.dynamic_slice_in_dim(cols, start, block, 0)
            row_block = lax.dynamic_slice_in_dim(rows, start, block, 0)
            pieces = jnp.take(panel, col_block, axis=0)
            prod = jnp.einsum(
                "tij,tjs->tis", tile_block, pieces, preferred_element_type=jnp.float32
            )
            live = start + jnp.arange(block, dtype=jnp.int32) < count
            prod = jnp.where(live[:, None, None], prod, 0.0)
            return total.at[row_block].add(prod)

        total = lax.fori_loop(0, slots // block, step_fn, start_acc)
        partial_value = total.reshape(n_tile_rows * side, width)
        summed_rows = lax.psum_scatter(
            partial_value[:block_rows], "col", scatter_dimension=0, tiled=True
        )
        own_scores = 0.85 * summed_rows + 0.15 * tele_own
        hub_part = partial_value[block_rows:]
        summed = lax.psum_scatter(hub_part, ("row", "col"), scatter_dimension=0, tiled=True)
        hub_piece = 0.85 * summed + 0.15 * tele_piece
        if step + 1 < ITERS:
            hub_panel = lax.all_gather(
                hub_piece.astype(jnp.bfloat16), ("row", "col"), axis=0, tiled=True
            )
    return (own_scores.reshape(1, 1, VB, width), hub_piece)


def solution(mesh):
    placed = (
        P(("groups", "row"), "col", None, None, None),
        P(("groups", "row"), "col", None),
        P(("groups", "row"), "col", None),
        P(("groups", "row"), "col"),
        P("groups"),
    )

    def body(tiles, *rest):
        n_row, n_col = mesh.shape["row"], mesh.shape["col"]
        slots, side = tiles.shape[2:4]
        blocks = (n_col * VB + H) * (n_row * VB + H) // (side * side)
        if ITERS == 2 and n_col == 2 and n_row == 4 * X and blocks <= slots and H // (n_row * n_col) % 16 == 0:
            return fast_body(tiles, *rest)
        return plain_body(tiles, *rest)

    return jax.shard_map(
        body,
        mesh=mesh,
        in_specs=placed,
        out_specs=(P(("groups", "row"), "col", None, None), P(("groups", "row", "col"), None)),
        check_vma=False,
    )
```

```python
import functools
import math

import jax
import jax.numpy as jnp
from jax import lax
from jax.experimental import pallas as pl
from jax.experimental.pallas import tpu as pltpu
from jax.sharding import PartitionSpec as P

VB = 128
H = 256
ITERS = 2
DAMP = 0.85
CHUNK = 8
X = 2
MICRO = 10 ** 9
VMEM_LIMIT = 32 * 1024 * 1024

SMEM = pl.BlockSpec(memory_space=pltpu.SMEM)
VMEM = pl.BlockSpec(memory_space=pltpu.VMEM)
HBM = pl.BlockSpec(memory_space=pltpu.HBM)


def params():
    return pltpu.CompilerParams(vmem_limit_bytes=VMEM_LIMIT)


def one_hot(first, count, src):
    ids = lax.broadcasted_iota(jnp.int32, (count, src.shape[1]), 0) + first
    return (ids == src).astype(jnp.float32)


def product(dense, panel):
    prod = jnp.dot(dense, panel, preferred_element_type=jnp.float32)
    rows = prod.shape[0] // 2
    return prod[:rows] + prod[rows:]


def half_terms(dims, core, total, panel, out_ref, dense_ref):
    n_row, n_col, side = dims
    piece = H // (n_row * n_col)
    half = out_ref.shape[0]
    chunks = [(0, core * VB, VB)]
    for r in range(n_row):
        chunks.append((VB + r * piece, n_col * VB + (r * n_col + core) * piece, piece))
    for to, start, size in chunks:
        whole = total[pl.ds(pl.multiple_of(start, size), size), :]
        high = whole.astype(jnp.bfloat16)
        dense_ref[to:to + size] = high
        dense_ref[half + to:half + to + size] = (whole - high.astype(jnp.float32)).astype(jnp.bfloat16)
    out_ref[...] = product(dense_ref[...], panel[...])


def first_kernel(dims, tiles_ref, rows_hbm, cols_hbm, count_hbm, src_hbm, send_ref, dense_send_ref, total, panel,
                 held, rows_ref, cols_ref, count_ref, src_ref, sems, small):
    n_row, n_col, side = dims
    n_rows = n_col * VB + H
    piece = H // (n_row * n_col)
    c = lax.axis_index("col")
    pairs = ((src_hbm, src_ref), (rows_hbm, rows_ref), (cols_hbm, cols_ref), (count_hbm, count_ref))
    scalars = [pltpu.make_async_copy(a, b, small.at[i]) for i, (a, b) in enumerate(pairs)]
    copies = []
    for i in range(held.shape[0] // CHUNK):
        part = pl.ds(i * CHUNK, CHUNK)
        copies.append(pltpu.make_async_copy(tiles_ref.at[part], held.at[part], sems.at[i]))
    for copy in scalars + copies:
        copy.start()
    total[...] = jnp.zeros_like(total)
    for copy in scalars:
        copy.wait()
    src = src_ref[...]
    for r in range(n_row):
        first = H + (r * n_col + c) * VB
        panel[pl.ds(r * VB, VB), :] = one_hot(first, VB, src).astype(jnp.bfloat16)
    panel[pl.ds(n_row * VB, H), :] = one_hot(0, H, src).astype(jnp.bfloat16)
    count = count_ref[0]

    def add_tile(k, carry):
        live = k < count
        row = pl.multiple_of(jnp.where(live, rows_ref[k] * side, n_rows), side)
        col = pl.multiple_of(jnp.where(live, cols_ref[k] * side, 0), side)
        spot = (pl.ds(row, side), pl.ds(col, side))
        total[spot] += held[k].astype(jnp.float32)
        return carry

    for i, copy in enumerate(copies):
        copy.wait()
        lax.fori_loop(i * CHUNK, (i + 1) * CHUNK, add_tile, 0, unroll=4)
    half_terms(dims, 1 - c, total, panel, send_ref, dense_send_ref)


def keep_kernel(dims, total_ref, panel_ref, keep_ref, dense_ref):
    half_terms(dims, lax.axis_index("col"), total_ref, panel_ref, keep_ref, dense_ref)


def score_columns_kernel(dims, blocks_ref, dense_ref, part_ref, panel):
    n_row, n_col, side = dims
    n_z = n_row // X
    r = lax.axis_index("row")
    for k in range(n_row):
        owner = r ^ (X * (k % n_z) + k // n_z)
        panel[pl.ds(pl.multiple_of(owner * VB, VB), VB), :] = blocks_ref[k]
    part_ref[...] = product(dense_ref[:, :n_row * VB], panel[...])


def other_columns_kernel(dims, blocks_ref, dense_ref, held_ref, part_ref, panel):
    score_columns_kernel(dims, blocks_ref, dense_ref, part_ref, panel)
    part_ref[...] += held_ref[...]


def hub_columns_kernel(dims, src_ref, mine_ref, theirs_ref, dense_mine, dense_theirs, part_ref,
                       scores_ref, parts_ref, panel):
    n_row, n_col, side = dims
    columns = n_row * VB
    piece = parts_ref.shape[1]
    r, c = lax.axis_index("row"), lax.axis_index("col")
    n_z = n_row // X
    x = r % X
    for block, at, core in ((mine_ref[0], x, c), (mine_ref[1], 1 - x, 1 - c), (theirs_ref[0], x, 1 - c), (theirs_ref[1], 1 - x, c)):
        for i in range(n_z):
            place = ((at * n_z + i) * n_col + core) * piece
            panel[pl.ds(pl.multiple_of(place, piece), piece), :] = block[i * piece:(i + 1) * piece]
    total = part_ref[...] + product(dense_mine[:, columns:], panel[...]) + product(dense_theirs[:, columns:], panel[...])
    tele = one_hot(H + (r * n_col + c) * VB, VB, src_ref[...])
    scores_ref[...] = DAMP * total[:VB] + 0.15 * tele
    parts_ref[...] = total[VB:].reshape(parts_ref.shape)


def own_scores(dims, src_ref, keep_ref, came_ref):
    first = H + (lax.axis_index("row") * dims[1] + lax.axis_index("col")) * VB
    tele = one_hot(first, VB, src_ref[...])
    return DAMP * (keep_ref[:VB] + came_ref[:VB]) + 0.15 * tele


def spread_kernel(dims, src_ref, keep_ref, came_ref, scores_ref, hold_ref, pass_ref):
    quarter = hold_ref.shape[0]
    x = lax.axis_index("row") % X
    for ref, place in ((hold_ref, x), (pass_ref, 1 - x)):
        spot = pl.ds(pl.multiple_of(VB + place * quarter, quarter), quarter)
        ref[...] = keep_ref[spot, :] + came_ref[spot, :]
    scores_ref[0] = own_scores(dims, src_ref, keep_ref, came_ref).astype(scores_ref.dtype)


def join_kernel(*refs):
    at = 0
    for ref in refs[:-1]:
        refs[-1][at:at + ref.shape[0]] = ref[...]
        at += ref.shape[0]


def add_kernel(hold_ref, came_ref, out_ref):
    out_ref[...] = hold_ref[...] + came_ref[...]


def hub_kernel(dims, src_ref, held_ref, came_ref, out_ref):
    n_row, n_col, side = dims
    piece = H // (n_row * n_col)
    r, c = lax.axis_index("row"), lax.axis_index("col")
    at = lax.broadcasted_iota(jnp.int32, out_ref.shape, 0)
    ids = ((r % X * (n_row // X) + at // piece) * n_col + c) * piece + at % piece
    tele = (ids == src_ref[...]).astype(jnp.float32)
    out_ref[...] = (DAMP * (held_ref[...] + came_ref[...]) + 0.15 * tele).astype(out_ref.dtype)


def side_kernel(mine_ref, came_ref, out_ref):
    out_ref[0] = mine_ref[...]
    out_ref[1] = came_ref[...]


def last_kernel(dims, src_ref, held_ref, parts_ref, scores_ref, hubs_ref):
    scores_ref[...] = held_ref[...]
    piece = hubs_ref.shape[0]
    summed = parts_ref[0]
    for k in range(1, parts_ref.shape[0]):
        summed = summed + parts_ref[k]
    first = (lax.axis_index("row") * dims[1] + lax.axis_index("col")) * piece
    hubs_ref[...] = DAMP * summed + 0.15 * one_hot(first, piece, src_ref[...])


def fast_body(tiles, tile_row, tile_col, tile_count, sources):
    slots, side = tiles.shape[2:4]
    width = sources.shape[0]
    n_row = lax.axis_size("row")
    n_col = lax.axis_size("col")
    piece = H // (n_row * n_col)
    dims = (n_row, n_col, side)
    n_rows = n_col * VB + H
    n_cols = n_row * VB + H
    f32 = functools.partial(jax.ShapeDtypeStruct, dtype=jnp.float32)
    bf16 = functools.partial(jax.ShapeDtypeStruct, dtype=jnp.bfloat16)
    src = sources.reshape(1, width)
    half = VB + n_row * piece
    quarter = H // n_col // X
    def other_core(x):
        return lax.ppermute(x, "col", [(0, 1), (1, 0)])

    def to_partner(x, flip):
        return lax.ppermute(x, "row", [(r, r ^ flip) for r in range(n_row)])

    def other_side(x):
        return to_partner(x, 1)

    def cross(x):
        devices = [(r, c) for r in range(n_row) for c in range(n_col)]
        return lax.ppermute(x, ("row", "col"), [(r * n_col + c, (r ^ 1) * n_col + 1 - c) for r, c in devices])

    def call(kernel, name, out_shape, *args, scratch=(), after=(), cost=0):
        def body(*refs):
            kernel(*refs[:len(args)], *refs[len(args) + len(after):])

        return pl.pallas_call(
            body,
            out_shape=out_shape,
            in_specs=[VMEM] * len(args) + [pl.BlockSpec(memory_space=pl.ANY)] * len(after),
            out_specs=jax.tree.map(lambda _: VMEM, out_shape),
            scratch_shapes=scratch,
            compiler_params=params(),
            cost_estimate=pl.CostEstimate(flops=cost * MICRO, bytes_accessed=0, transcendentals=0),
            name=name,
        )(*args, *after)

    bind = functools.partial

    in_hbm = [pltpu.with_memory_space_constraint(x, pltpu.HBM) for x in (
        tiles.reshape(slots, side, side), tile_row.reshape(slots), tile_col.reshape(slots), src)]
    dense_shape = bf16((2 * half, n_cols))
    send, dense_send, total, panel = pl.pallas_call(
        bind(first_kernel, dims),
        out_shape=(f32((half, width)), dense_shape, f32((n_rows + side, n_cols)), bf16((n_cols, width))),
        in_specs=[HBM] * 5,
        out_specs=[VMEM] * 4,
        scratch_shapes=[
            pltpu.VMEM((slots, side, side), jnp.bfloat16),
            pltpu.SMEM((slots,), jnp.int32),
            pltpu.SMEM((slots,), jnp.int32),
            pltpu.SMEM((1,), jnp.int32),
            pltpu.VMEM((1, width), jnp.int32),
            pltpu.SemaphoreType.DMA((slots // CHUNK,)),
            pltpu.SemaphoreType.DMA((4,)),
        ],
        compiler_params=params(),
        name="first_terms",
    )(*in_hbm[:3], tile_count.reshape(1), in_hbm[3])

    keep, dense_keep = call(bind(keep_kernel, dims), "keep_terms", (f32((half, width)), dense_shape), total, panel, cost=1)
    held, hold, away = call(
        bind(spread_kernel, dims), "spread",
        (bf16((1, VB, width)), f32((quarter, width)), f32((quarter, width))),
        src, keep, other_core(send), cost=0)
    away = other_side(away)
    next_z, far_z = to_partner(held, X), to_partner(held, 2 * X)
    last = to_partner(far_z, X)
    first = call(join_kernel, "join_first", bf16((3, VB, width)), held, next_z, far_z, cost=0)
    first_across, last_across = other_side(first), other_side(last)
    sums = call(add_kernel, "plane_sum", f32((quarter, width)), hold, away, cost=0)
    sums = call(add_kernel, "pair_sum", f32((quarter, width)), sums, to_partner(sums, X), cost=8)
    dense_came = other_core(call(join_kernel, "pass_dense", dense_shape, dense_send, after=[sums], cost=2))
    hubs = call(bind(hub_kernel, dims), "hub_sums", bf16((quarter, width)), src, sums, to_partner(sums, 2 * X), cost=0)
    blocks = call(join_kernel, "join_blocks", bf16((n_row, VB, width)), first, last, first_across, last_across, after=[hubs], cost=12)
    blocks_came = other_core(blocks)
    hubs = call(side_kernel, "join_sides", bf16((2, quarter, width)), hubs, cross(hubs), cost=8)
    column_scratch = [pltpu.VMEM((n_row * VB, width), jnp.bfloat16)]
    part = call(bind(score_columns_kernel, dims), "own_columns", f32((half, width)),
                blocks, dense_keep, scratch=column_scratch)
    part = call(bind(other_columns_kernel, dims), "other_columns", f32((half, width)),
                blocks_came, dense_came, part, scratch=column_scratch)
    scores, parts = call(
        bind(hub_columns_kernel, dims), "hub_columns", (f32((VB, width)), f32((n_row, piece, width))),
        src, hubs, other_core(hubs), dense_keep, dense_came, part, scratch=[pltpu.VMEM((H, width), jnp.bfloat16)])
    parts = lax.all_to_all(parts, "row", 0, 0)
    scores, hubs = call(bind(last_kernel, dims), "last_hubs", (f32((VB, width)), f32((piece, width))), src, scores, parts)
    return scores.reshape(1, 1, VB, width), hubs


def plain_body(tiles, tile_row, tile_col, tile_count, sources):
    slots = tiles.shape[2]
    side = tiles.shape[3]
    width = sources.shape[0]
    tiles = tiles.reshape(slots, side, side)
    rows = tile_row.reshape(slots)
    cols = tile_col.reshape(slots)
    count = tile_count.reshape(())
    n_row = lax.axis_size("row")
    n_col = lax.axis_size("col")
    devices = n_row * n_col
    r_index = lax.axis_index("row")
    c_index = lax.axis_index("col")
    hub_dev = H // devices
    block_rows = n_col * VB
    n_tile_rows = (block_rows + H) // side
    own_base = H + (r_index * n_col + c_index) * VB
    hub_start = (r_index * n_col + c_index) * hub_dev
    own_ids = jnp.arange(VB, dtype=jnp.int32) + own_base
    tele_own = (own_ids[:, None] == sources[None, :]).astype(jnp.float32)
    piece_ids = jnp.arange(hub_dev, dtype=jnp.int32) + hub_start
    tele_piece = (piece_ids[:, None] == sources[None, :]).astype(jnp.float32)
    tele_hubs = (jnp.arange(H, dtype=jnp.int32)[:, None] == sources[None, :]).astype(jnp.float32)
    column_ids = (
        H
        + (jnp.arange(n_row, dtype=jnp.int32)[:, None] * n_col + c_index) * VB
        + jnp.arange(VB, dtype=jnp.int32)[None, :]
    ).reshape(n_row * VB)
    column_panel = (column_ids[:, None] == sources[None, :]).astype(jnp.bfloat16)
    hub_panel = tele_hubs.astype(jnp.bfloat16)
    block = math.gcd(slots, 16)
    own_scores = tele_own
    hub_piece = tele_piece
    for step in range(ITERS):
        start_acc = jnp.zeros((n_tile_rows, side, width), jnp.float32)
        if step > 0:
            column_panel = lax.all_gather(
                own_scores.astype(jnp.bfloat16), "row", axis=0, tiled=True
            )
        panel = jnp.concatenate([column_panel, hub_panel], axis=0).reshape(-1, side, width)

        def step_fn(number, total):
            start = number * block
            tile_block = lax.dynamic_slice_in_dim(tiles, start, block, 0)
            col_block = lax.dynamic_slice_in_dim(cols, start, block, 0)
            row_block = lax.dynamic_slice_in_dim(rows, start, block, 0)
            pieces = jnp.take(panel, col_block, axis=0)
            prod = jnp.einsum(
                "tij,tjs->tis", tile_block, pieces, preferred_element_type=jnp.float32
            )
            live = start + jnp.arange(block, dtype=jnp.int32) < count
            prod = jnp.where(live[:, None, None], prod, 0.0)
            return total.at[row_block].add(prod)

        total = lax.fori_loop(0, slots // block, step_fn, start_acc)
        partial_value = total.reshape(n_tile_rows * side, width)
        summed_rows = lax.psum_scatter(
            partial_value[:block_rows], "col", scatter_dimension=0, tiled=True
        )
        own_scores = 0.85 * summed_rows + 0.15 * tele_own
        hub_part = partial_value[block_rows:]
        summed = lax.psum_scatter(hub_part, ("row", "col"), scatter_dimension=0, tiled=True)
        hub_piece = 0.85 * summed + 0.15 * tele_piece
        if step + 1 < ITERS:
            hub_panel = lax.all_gather(
                hub_piece.astype(jnp.bfloat16), ("row", "col"), axis=0, tiled=True
            )
    return (own_scores.reshape(1, 1, VB, width), hub_piece)


def solution(mesh):
    placed = (
        P(("groups", "row"), "col", None, None, None),
        P(("groups", "row"), "col", None),
        P(("groups", "row"), "col", None),
        P(("groups", "row"), "col"),
        P("groups"),
    )

    def body(tiles, *rest):
        n_row, n_col = mesh.shape["row"], mesh.shape["col"]
        slots, side = tiles.shape[2:4]
        blocks = (n_col * VB + H) * (n_row * VB + H) // (side * side)
        if ITERS == 2 and n_col == 2 and n_row == 4 * X and blocks <= slots and H // (n_row * n_col) % 16 == 0:
            return fast_body(tiles, *rest)
        return plain_body(tiles, *rest)

    return jax.shard_map(
        body,
        mesh=mesh,
        in_specs=placed,
        out_specs=(P(("groups", "row"), "col", None, None), P(("groups", "row", "col"), None)),
        check_vma=False,
    )
```

```python
import functools
import math

import jax
import jax.numpy as jnp
from jax import lax
from jax.experimental import pallas as pl
from jax.experimental.pallas import tpu as pltpu
from jax.sharding import PartitionSpec as P

VB = 128
H = 256
ITERS = 2
DAMP = 0.85
CHUNK = 8
X = 2
MICRO = 10 ** 9
VMEM_LIMIT = 32 * 1024 * 1024

SMEM = pl.BlockSpec(memory_space=pltpu.SMEM)
VMEM = pl.BlockSpec(memory_space=pltpu.VMEM)
HBM = pl.BlockSpec(memory_space=pltpu.HBM)


def params():
    return pltpu.CompilerParams(vmem_limit_bytes=VMEM_LIMIT)


def one_hot(first, count, src):
    ids = lax.broadcasted_iota(jnp.int32, (count, src.shape[1]), 0) + first
    return (ids == src).astype(jnp.float32)


def product(dense, panel):
    prod = jnp.dot(dense, panel, preferred_element_type=jnp.float32)
    rows = prod.shape[0] // 2
    return prod[:rows] + prod[rows:]


def half_terms(dims, core, total, panel, outs, dense_ref):
    n_row, n_col, side = dims
    piece = H // (n_row * n_col)
    half = dense_ref.shape[0] // 2
    chunks = [(0, core * VB, VB)]
    for r in range(n_row):
        chunks.append((VB + r * piece, n_col * VB + (r * n_col + core) * piece, piece))
    for to, start, size in chunks:
        whole = total[pl.ds(pl.multiple_of(start, size), size), :]
        high = whole.astype(jnp.bfloat16)
        dense_ref[to:to + size] = high
        dense_ref[half + to:half + to + size] = (whole - high.astype(jnp.float32)).astype(jnp.bfloat16)
    prod = product(dense_ref[...], panel[...])
    at = 0
    for ref in outs:
        ref[...] = prod[at:at + ref.shape[0]]
        at += ref.shape[0]


def first_kernel(dims, tiles_ref, rows_hbm, cols_hbm, count_hbm, src_hbm, send_ref, hubs_ref, dense_send_ref, total, panel,
                 held, rows_ref, cols_ref, count_ref, src_ref, sems, small):
    n_row, n_col, side = dims
    n_rows = n_col * VB + H
    piece = H // (n_row * n_col)
    c = lax.axis_index("col")
    pairs = ((src_hbm, src_ref), (rows_hbm, rows_ref), (cols_hbm, cols_ref), (count_hbm, count_ref))
    scalars = [pltpu.make_async_copy(a, b, small.at[i]) for i, (a, b) in enumerate(pairs)]
    copies = []
    for i in range(held.shape[0] // CHUNK):
        part = pl.ds(i * CHUNK, CHUNK)
        copies.append(pltpu.make_async_copy(tiles_ref.at[part], held.at[part], sems.at[i]))
    for copy in scalars + copies:
        copy.start()
    total[...] = jnp.zeros_like(total)
    for copy in scalars:
        copy.wait()
    src = src_ref[...]
    for r in range(n_row):
        first = H + (r * n_col + c) * VB
        panel[pl.ds(r * VB, VB), :] = one_hot(first, VB, src).astype(jnp.bfloat16)
    panel[pl.ds(n_row * VB, H), :] = one_hot(0, H, src).astype(jnp.bfloat16)
    count = count_ref[0]

    def add_tile(k, carry):
        live = k < count
        row = pl.multiple_of(jnp.where(live, rows_ref[k] * side, n_rows), side)
        col = pl.multiple_of(jnp.where(live, cols_ref[k] * side, 0), side)
        spot = (pl.ds(row, side), pl.ds(col, side))
        total[spot] += held[k].astype(jnp.float32)
        return carry

    for i, copy in enumerate(copies):
        copy.wait()
        lax.fori_loop(i * CHUNK, (i + 1) * CHUNK, add_tile, 0, unroll=4)
    half_terms(dims, 1 - c, total, panel, (send_ref, hubs_ref), dense_send_ref)


def keep_kernel(dims, total_ref, panel_ref, keep_ref, dense_ref):
    half_terms(dims, lax.axis_index("col"), total_ref, panel_ref, (keep_ref,), dense_ref)


def score_columns_kernel(dims, blocks_ref, dense_ref, part_ref, panel):
    n_row, n_col, side = dims
    n_z = n_row // X
    r = lax.axis_index("row")
    for k in range(n_row):
        owner = r ^ (X * (k % n_z) + k // n_z)
        panel[pl.ds(pl.multiple_of(owner * VB, VB), VB), :] = blocks_ref[k]
    part_ref[...] = product(dense_ref[:, :n_row * VB], panel[...])


def other_columns_kernel(dims, blocks_ref, dense_ref, held_ref, part_ref, panel):
    score_columns_kernel(dims, blocks_ref, dense_ref, part_ref, panel)
    part_ref[...] += held_ref[...]


def hub_columns_kernel(dims, src_ref, mine_ref, theirs_ref, dense_mine, dense_theirs, part_ref,
                       scores_ref, parts_ref, panel):
    n_row, n_col, side = dims
    columns = n_row * VB
    piece = parts_ref.shape[1]
    r, c = lax.axis_index("row"), lax.axis_index("col")
    n_z = n_row // X
    x = r % X
    for block, at, core in ((mine_ref[0], x, c), (mine_ref[1], 1 - x, 1 - c), (theirs_ref[0], x, 1 - c), (theirs_ref[1], 1 - x, c)):
        for i in range(n_z):
            place = ((at * n_z + i) * n_col + core) * piece
            panel[pl.ds(pl.multiple_of(place, piece), piece), :] = block[i * piece:(i + 1) * piece]
    total = part_ref[...] + product(dense_mine[:, columns:], panel[...]) + product(dense_theirs[:, columns:], panel[...])
    tele = one_hot(H + (r * n_col + c) * VB, VB, src_ref[...])
    scores_ref[...] = DAMP * total[:VB] + 0.15 * tele
    parts_ref[...] = total[VB:].reshape(parts_ref.shape)


def own_scores(dims, src_ref, keep_ref, came_ref):
    first = H + (lax.axis_index("row") * dims[1] + lax.axis_index("col")) * VB
    tele = one_hot(first, VB, src_ref[...])
    return DAMP * (keep_ref[:VB] + came_ref[:VB]) + 0.15 * tele


def spread_kernel(keep_ref, came_ref, hold_ref, pass_ref):
    quarter = hold_ref.shape[0]
    x = lax.axis_index("row") % X
    for ref, place in ((hold_ref, x), (pass_ref, 1 - x)):
        ref[...] = keep_ref[pl.ds(pl.multiple_of(VB + place * quarter, quarter), quarter), :] + came_ref[pl.ds(
            pl.multiple_of(place * quarter, quarter), quarter), :]


def scores_kernel(dims, src_ref, keep_ref, came_ref, scores_ref):
    first = H + (lax.axis_index("row") * dims[1] + lax.axis_index("col")) * VB
    tele = one_hot(first, VB, src_ref[...])
    scores_ref[0] = (DAMP * (keep_ref[:VB] + came_ref[...]) + 0.15 * tele).astype(scores_ref.dtype)


def join_kernel(*refs):
    at = 0
    for ref in refs[:-1]:
        refs[-1][at:at + ref.shape[0]] = ref[...]
        at += ref.shape[0]


def add_kernel(hold_ref, came_ref, out_ref):
    out_ref[...] = hold_ref[...] + came_ref[...]


def hub_kernel(dims, src_ref, held_ref, came_ref, out_ref):
    n_row, n_col, side = dims
    piece = H // (n_row * n_col)
    r, c = lax.axis_index("row"), lax.axis_index("col")
    at = lax.broadcasted_iota(jnp.int32, out_ref.shape, 0)
    ids = ((r % X * (n_row // X) + at // piece) * n_col + c) * piece + at % piece
    tele = (ids == src_ref[...]).astype(jnp.float32)
    out_ref[...] = (DAMP * (held_ref[...] + came_ref[...]) + 0.15 * tele).astype(out_ref.dtype)


def side_kernel(mine_ref, came_ref, out_ref):
    out_ref[0] = mine_ref[...]
    out_ref[1] = came_ref[...]


def last_kernel(dims, src_ref, held_ref, parts_ref, scores_ref, hubs_ref):
    scores_ref[...] = held_ref[...]
    piece = hubs_ref.shape[0]
    summed = parts_ref[0]
    for k in range(1, parts_ref.shape[0]):
        summed = summed + parts_ref[k]
    first = (lax.axis_index("row") * dims[1] + lax.axis_index("col")) * piece
    hubs_ref[...] = DAMP * summed + 0.15 * one_hot(first, piece, src_ref[...])


def fast_body(tiles, tile_row, tile_col, tile_count, sources):
    slots, side = tiles.shape[2:4]
    width = sources.shape[0]
    n_row = lax.axis_size("row")
    n_col = lax.axis_size("col")
    piece = H // (n_row * n_col)
    dims = (n_row, n_col, side)
    n_rows = n_col * VB + H
    n_cols = n_row * VB + H
    f32 = functools.partial(jax.ShapeDtypeStruct, dtype=jnp.float32)
    bf16 = functools.partial(jax.ShapeDtypeStruct, dtype=jnp.bfloat16)
    src = sources.reshape(1, width)
    half = VB + n_row * piece
    quarter = H // n_col // X
    def other_core(x):
        return lax.ppermute(x, "col", [(0, 1), (1, 0)])

    def to_partner(x, flip):
        return lax.ppermute(x, "row", [(r, r ^ flip) for r in range(n_row)])

    def other_side(x):
        return to_partner(x, 1)

    def cross(x):
        devices = [(r, c) for r in range(n_row) for c in range(n_col)]
        return lax.ppermute(x, ("row", "col"), [(r * n_col + c, (r ^ 1) * n_col + 1 - c) for r, c in devices])

    def call(kernel, name, out_shape, *args, scratch=(), after=(), cost=0):
        def body(*refs):
            kernel(*refs[:len(args)], *refs[len(args) + len(after):])

        return pl.pallas_call(
            body,
            out_shape=out_shape,
            in_specs=[VMEM] * len(args) + [pl.BlockSpec(memory_space=pl.ANY)] * len(after),
            out_specs=jax.tree.map(lambda _: VMEM, out_shape),
            scratch_shapes=scratch,
            compiler_params=params(),
            cost_estimate=pl.CostEstimate(flops=cost * MICRO, bytes_accessed=0, transcendentals=0),
            name=name,
        )(*args, *after)

    bind = functools.partial

    in_hbm = [pltpu.with_memory_space_constraint(x, pltpu.HBM) for x in (
        tiles.reshape(slots, side, side), tile_row.reshape(slots), tile_col.reshape(slots), src)]
    dense_shape = bf16((2 * half, n_cols))
    send, send_hubs, dense_send, total, panel = pl.pallas_call(
        bind(first_kernel, dims),
        out_shape=(f32((VB, width)), f32((half - VB, width)), dense_shape, f32((n_rows + side, n_cols)), bf16((n_cols, width))),
        in_specs=[HBM] * 5,
        out_specs=[VMEM] * 5,
        scratch_shapes=[
            pltpu.VMEM((slots, side, side), jnp.bfloat16),
            pltpu.SMEM((slots,), jnp.int32),
            pltpu.SMEM((slots,), jnp.int32),
            pltpu.SMEM((1,), jnp.int32),
            pltpu.VMEM((1, width), jnp.int32),
            pltpu.SemaphoreType.DMA((slots // CHUNK,)),
            pltpu.SemaphoreType.DMA((4,)),
        ],
        compiler_params=params(),
        name="first_terms",
    )(*in_hbm[:3], tile_count.reshape(1), in_hbm[3])

    keep, dense_keep = call(bind(keep_kernel, dims), "keep_terms", (f32((half, width)), dense_shape), total, panel, cost=1)
    hold, away = call(spread_kernel, "spread", (f32((quarter, width)),) * 2, keep, other_core(send_hubs), cost=2)
    away = other_side(away)
    held = call(bind(scores_kernel, dims), "scores", bf16((1, VB, width)), src, keep, other_core(send))
    next_z, far_z = to_partner(held, X), to_partner(held, 2 * X)
    last = to_partner(far_z, X)
    first = call(join_kernel, "join_first", bf16((3, VB, width)), held, next_z, far_z, cost=0)
    first_across, last_across = other_side(first), other_side(last)
    sums = call(add_kernel, "plane_sum", f32((quarter, width)), hold, away, cost=0)
    sums = call(add_kernel, "pair_sum", f32((quarter, width)), sums, to_partner(sums, X), cost=8)
    dense_came = other_core(call(join_kernel, "pass_dense", dense_shape, dense_send, after=[sums], cost=2))
    hubs = call(bind(hub_kernel, dims), "hub_sums", bf16((quarter, width)), src, sums, to_partner(sums, 2 * X), cost=0)
    blocks = call(join_kernel, "join_blocks", bf16((n_row, VB, width)), first, last, first_across, last_across, after=[hubs], cost=12)
    blocks_came = other_core(blocks)
    hubs = call(side_kernel, "join_sides", bf16((2, quarter, width)), hubs, cross(hubs), cost=8)
    column_scratch = [pltpu.VMEM((n_row * VB, width), jnp.bfloat16)]
    part = call(bind(score_columns_kernel, dims), "own_columns", f32((half, width)),
                blocks, dense_keep, scratch=column_scratch)
    part = call(bind(other_columns_kernel, dims), "other_columns", f32((half, width)),
                blocks_came, dense_came, part, scratch=column_scratch)
    scores, parts = call(
        bind(hub_columns_kernel, dims), "hub_columns", (f32((VB, width)), f32((n_row, piece, width))),
        src, hubs, other_core(hubs), dense_keep, dense_came, part, scratch=[pltpu.VMEM((H, width), jnp.bfloat16)])
    parts = lax.all_to_all(parts, "row", 0, 0)
    scores, hubs = call(bind(last_kernel, dims), "last_hubs", (f32((VB, width)), f32((piece, width))), src, scores, parts)
    return scores.reshape(1, 1, VB, width), hubs


def plain_body(tiles, tile_row, tile_col, tile_count, sources):
    slots = tiles.shape[2]
    side = tiles.shape[3]
    width = sources.shape[0]
    tiles = tiles.reshape(slots, side, side)
    rows = tile_row.reshape(slots)
    cols = tile_col.reshape(slots)
    count = tile_count.reshape(())
    n_row = lax.axis_size("row")
    n_col = lax.axis_size("col")
    devices = n_row * n_col
    r_index = lax.axis_index("row")
    c_index = lax.axis_index("col")
    hub_dev = H // devices
    block_rows = n_col * VB
    n_tile_rows = (block_rows + H) // side
    own_base = H + (r_index * n_col + c_index) * VB
    hub_start = (r_index * n_col + c_index) * hub_dev
    own_ids = jnp.arange(VB, dtype=jnp.int32) + own_base
    tele_own = (own_ids[:, None] == sources[None, :]).astype(jnp.float32)
    piece_ids = jnp.arange(hub_dev, dtype=jnp.int32) + hub_start
    tele_piece = (piece_ids[:, None] == sources[None, :]).astype(jnp.float32)
    tele_hubs = (jnp.arange(H, dtype=jnp.int32)[:, None] == sources[None, :]).astype(jnp.float32)
    column_ids = (
        H
        + (jnp.arange(n_row, dtype=jnp.int32)[:, None] * n_col + c_index) * VB
        + jnp.arange(VB, dtype=jnp.int32)[None, :]
    ).reshape(n_row * VB)
    column_panel = (column_ids[:, None] == sources[None, :]).astype(jnp.bfloat16)
    hub_panel = tele_hubs.astype(jnp.bfloat16)
    block = math.gcd(slots, 16)
    own_scores = tele_own
    hub_piece = tele_piece
    for step in range(ITERS):
        start_acc = jnp.zeros((n_tile_rows, side, width), jnp.float32)
        if step > 0:
            column_panel = lax.all_gather(
                own_scores.astype(jnp.bfloat16), "row", axis=0, tiled=True
            )
        panel = jnp.concatenate([column_panel, hub_panel], axis=0).reshape(-1, side, width)

        def step_fn(number, total):
            start = number * block
            tile_block = lax.dynamic_slice_in_dim(tiles, start, block, 0)
            col_block = lax.dynamic_slice_in_dim(cols, start, block, 0)
            row_block = lax.dynamic_slice_in_dim(rows, start, block, 0)
            pieces = jnp.take(panel, col_block, axis=0)
            prod = jnp.einsum(
                "tij,tjs->tis", tile_block, pieces, preferred_element_type=jnp.float32
            )
            live = start + jnp.arange(block, dtype=jnp.int32) < count
            prod = jnp.where(live[:, None, None], prod, 0.0)
            return total.at[row_block].add(prod)

        total = lax.fori_loop(0, slots // block, step_fn, start_acc)
        partial_value = total.reshape(n_tile_rows * side, width)
        summed_rows = lax.psum_scatter(
            partial_value[:block_rows], "col", scatter_dimension=0, tiled=True
        )
        own_scores = 0.85 * summed_rows + 0.15 * tele_own
        hub_part = partial_value[block_rows:]
        summed = lax.psum_scatter(hub_part, ("row", "col"), scatter_dimension=0, tiled=True)
        hub_piece = 0.85 * summed + 0.15 * tele_piece
        if step + 1 < ITERS:
            hub_panel = lax.all_gather(
                hub_piece.astype(jnp.bfloat16), ("row", "col"), axis=0, tiled=True
            )
    return (own_scores.reshape(1, 1, VB, width), hub_piece)


def solution(mesh):
    placed = (
        P(("groups", "row"), "col", None, None, None),
        P(("groups", "row"), "col", None),
        P(("groups", "row"), "col", None),
        P(("groups", "row"), "col"),
        P("groups"),
    )

    def body(tiles, *rest):
        n_row, n_col = mesh.shape["row"], mesh.shape["col"]
        slots, side = tiles.shape[2:4]
        blocks = (n_col * VB + H) * (n_row * VB + H) // (side * side)
        if ITERS == 2 and n_col == 2 and n_row == 4 * X and blocks <= slots and H // (n_row * n_col) % 16 == 0:
            return fast_body(tiles, *rest)
        return plain_body(tiles, *rest)

    return jax.shard_map(
        body,
        mesh=mesh,
        in_specs=placed,
        out_specs=(P(("groups", "row"), "col", None, None), P(("groups", "row", "col"), None)),
        check_vma=False,
    )
```

```python
import functools
import math

import jax
import jax.numpy as jnp
from jax import lax
from jax.experimental import pallas as pl
from jax.experimental.pallas import tpu as pltpu
from jax.sharding import PartitionSpec as P

VB = 128
H = 256
ITERS = 2
DAMP = 0.85
CHUNK = 8
X = 2
MICRO = 10 ** 9
VMEM_LIMIT = 32 * 1024 * 1024

SMEM = pl.BlockSpec(memory_space=pltpu.SMEM)
VMEM = pl.BlockSpec(memory_space=pltpu.VMEM)
HBM = pl.BlockSpec(memory_space=pltpu.HBM)


def params():
    return pltpu.CompilerParams(vmem_limit_bytes=VMEM_LIMIT)


def one_hot(first, count, src):
    ids = lax.broadcasted_iota(jnp.int32, (count, src.shape[1]), 0) + first
    return (ids == src).astype(jnp.float32)


def product(dense, panel):
    prod = jnp.dot(dense, panel, preferred_element_type=jnp.float32)
    rows = prod.shape[0] // 2
    return prod[:rows] + prod[rows:]


def half_terms(dims, core, total, panel, outs, dense_ref):
    n_row, n_col, side = dims
    piece = H // (n_row * n_col)
    half = dense_ref.shape[0] // 2
    chunks = [(0, core * VB, VB)]
    for r in range(n_row):
        chunks.append((VB + r * piece, n_col * VB + (r * n_col + core) * piece, piece))
    for to, start, size in chunks:
        whole = total[pl.ds(pl.multiple_of(start, size), size), :]
        high = whole.astype(jnp.bfloat16)
        dense_ref[to:to + size] = high
        dense_ref[half + to:half + to + size] = (whole - high.astype(jnp.float32)).astype(jnp.bfloat16)
    prod = product(dense_ref[...], panel[...])
    at = 0
    for ref in outs:
        ref[...] = prod[at:at + ref.shape[0]]
        at += ref.shape[0]


def first_kernel(dims, tiles_ref, rows_hbm, cols_hbm, count_hbm, src_hbm, send_ref, hubs_ref, dense_send_ref, total, panel,
                 held, rows_ref, cols_ref, count_ref, src_ref, sems, small):
    n_row, n_col, side = dims
    n_rows = n_col * VB + H
    piece = H // (n_row * n_col)
    c = lax.axis_index("col")
    pairs = ((src_hbm, src_ref), (rows_hbm, rows_ref), (cols_hbm, cols_ref), (count_hbm, count_ref))
    scalars = [pltpu.make_async_copy(a, b, small.at[i]) for i, (a, b) in enumerate(pairs)]
    copies = []
    for i in range(held.shape[0] // CHUNK):
        part = pl.ds(i * CHUNK, CHUNK)
        copies.append(pltpu.make_async_copy(tiles_ref.at[part], held.at[part], sems.at[i]))
    for copy in scalars + copies:
        copy.start()
    total[...] = jnp.zeros_like(total)
    for copy in scalars:
        copy.wait()
    src = src_ref[...]
    for r in range(n_row):
        first = H + (r * n_col + c) * VB
        panel[pl.ds(r * VB, VB), :] = one_hot(first, VB, src).astype(jnp.bfloat16)
    panel[pl.ds(n_row * VB, H), :] = one_hot(0, H, src).astype(jnp.bfloat16)
    count = count_ref[0]

    def add_tile(k, carry):
        live = k < count
        row = pl.multiple_of(jnp.where(live, rows_ref[k] * side, n_rows), side)
        col = pl.multiple_of(jnp.where(live, cols_ref[k] * side, 0), side)
        spot = (pl.ds(row, side), pl.ds(col, side))
        total[spot] += held[k].astype(jnp.float32)
        return carry

    for i, copy in enumerate(copies):
        copy.wait()
        lax.fori_loop(i * CHUNK, (i + 1) * CHUNK, add_tile, 0, unroll=8)
    half_terms(dims, 1 - c, total, panel, (send_ref, hubs_ref), dense_send_ref)


def keep_kernel(dims, total_ref, panel_ref, keep_ref, dense_ref):
    half_terms(dims, lax.axis_index("col"), total_ref, panel_ref, (keep_ref,), dense_ref)


def score_columns_kernel(dims, blocks_ref, dense_ref, part_ref, panel):
    n_row, n_col, side = dims
    n_z = n_row // X
    r = lax.axis_index("row")
    for k in range(n_row):
        owner = r ^ (X * (k % n_z) + k // n_z)
        panel[pl.ds(pl.multiple_of(owner * VB, VB), VB), :] = blocks_ref[k]
    part_ref[...] = product(dense_ref[:, :n_row * VB], panel[...])


def other_columns_kernel(dims, blocks_ref, dense_ref, held_ref, part_ref, panel):
    score_columns_kernel(dims, blocks_ref, dense_ref, part_ref, panel)
    part_ref[...] += held_ref[...]


def hub_columns_kernel(dims, src_ref, mine_ref, theirs_ref, dense_mine, dense_theirs, part_ref,
                       scores_ref, parts_ref, panel):
    n_row, n_col, side = dims
    columns = n_row * VB
    piece = parts_ref.shape[1]
    r, c = lax.axis_index("row"), lax.axis_index("col")
    n_z = n_row // X
    x = r % X
    for block, at, core in ((mine_ref[0], x, c), (mine_ref[1], 1 - x, 1 - c), (theirs_ref[0], x, 1 - c), (theirs_ref[1], 1 - x, c)):
        for i in range(n_z):
            place = ((at * n_z + i) * n_col + core) * piece
            panel[pl.ds(pl.multiple_of(place, piece), piece), :] = block[i * piece:(i + 1) * piece]
    total = part_ref[...] + product(dense_mine[:, columns:], panel[...]) + product(dense_theirs[:, columns:], panel[...])
    tele = one_hot(H + (r * n_col + c) * VB, VB, src_ref[...])
    scores_ref[...] = DAMP * total[:VB] + 0.15 * tele
    parts_ref[...] = total[VB:].reshape(parts_ref.shape)


def own_scores(dims, src_ref, keep_ref, came_ref):
    first = H + (lax.axis_index("row") * dims[1] + lax.axis_index("col")) * VB
    tele = one_hot(first, VB, src_ref[...])
    return DAMP * (keep_ref[:VB] + came_ref[:VB]) + 0.15 * tele


def spread_kernel(keep_ref, came_ref, hold_ref, pass_ref):
    quarter = hold_ref.shape[0]
    x = lax.axis_index("row") % X
    for ref, place in ((hold_ref, x), (pass_ref, 1 - x)):
        ref[...] = keep_ref[pl.ds(pl.multiple_of(VB + place * quarter, quarter), quarter), :] + came_ref[pl.ds(
            pl.multiple_of(place * quarter, quarter), quarter), :]


def scores_kernel(dims, src_ref, keep_ref, came_ref, scores_ref):
    first = H + (lax.axis_index("row") * dims[1] + lax.axis_index("col")) * VB
    tele = one_hot(first, VB, src_ref[...])
    scores_ref[0] = (DAMP * (keep_ref[:VB] + came_ref[...]) + 0.15 * tele).astype(scores_ref.dtype)


def join_kernel(*refs):
    at = 0
    for ref in refs[:-1]:
        refs[-1][at:at + ref.shape[0]] = ref[...]
        at += ref.shape[0]


def add_kernel(hold_ref, came_ref, out_ref):
    out_ref[...] = hold_ref[...] + came_ref[...]


def hub_kernel(dims, src_ref, held_ref, came_ref, out_ref):
    n_row, n_col, side = dims
    piece = H // (n_row * n_col)
    r, c = lax.axis_index("row"), lax.axis_index("col")
    at = lax.broadcasted_iota(jnp.int32, out_ref.shape, 0)
    ids = ((r % X * (n_row // X) + at // piece) * n_col + c) * piece + at % piece
    tele = (ids == src_ref[...]).astype(jnp.float32)
    out_ref[...] = (DAMP * (held_ref[...] + came_ref[...]) + 0.15 * tele).astype(out_ref.dtype)


def side_kernel(mine_ref, came_ref, out_ref):
    out_ref[0] = mine_ref[...]
    out_ref[1] = came_ref[...]


def last_kernel(dims, src_ref, held_ref, parts_ref, scores_ref, hubs_ref):
    scores_ref[...] = held_ref[...]
    piece = hubs_ref.shape[0]
    summed = parts_ref[0]
    for k in range(1, parts_ref.shape[0]):
        summed = summed + parts_ref[k]
    first = (lax.axis_index("row") * dims[1] + lax.axis_index("col")) * piece
    hubs_ref[...] = DAMP * summed + 0.15 * one_hot(first, piece, src_ref[...])


def fast_body(tiles, tile_row, tile_col, tile_count, sources):
    slots, side = tiles.shape[2:4]
    width = sources.shape[0]
    n_row = lax.axis_size("row")
    n_col = lax.axis_size("col")
    piece = H // (n_row * n_col)
    dims = (n_row, n_col, side)
    n_rows = n_col * VB + H
    n_cols = n_row * VB + H
    f32 = functools.partial(jax.ShapeDtypeStruct, dtype=jnp.float32)
    bf16 = functools.partial(jax.ShapeDtypeStruct, dtype=jnp.bfloat16)
    src = sources.reshape(1, width)
    half = VB + n_row * piece
    quarter = H // n_col // X
    def other_core(x):
        return lax.ppermute(x, "col", [(0, 1), (1, 0)])

    def to_partner(x, flip):
        return lax.ppermute(x, "row", [(r, r ^ flip) for r in range(n_row)])

    def other_side(x):
        return to_partner(x, 1)

    def cross(x):
        devices = [(r, c) for r in range(n_row) for c in range(n_col)]
        return lax.ppermute(x, ("row", "col"), [(r * n_col + c, (r ^ 1) * n_col + 1 - c) for r, c in devices])

    def call(kernel, name, out_shape, *args, scratch=(), after=(), cost=0):
        def body(*refs):
            kernel(*refs[:len(args)], *refs[len(args) + len(after):])

        return pl.pallas_call(
            body,
            out_shape=out_shape,
            in_specs=[VMEM] * len(args) + [pl.BlockSpec(memory_space=pl.ANY)] * len(after),
            out_specs=jax.tree.map(lambda _: VMEM, out_shape),
            scratch_shapes=scratch,
            compiler_params=params(),
            cost_estimate=pl.CostEstimate(flops=cost * MICRO, bytes_accessed=0, transcendentals=0),
            name=name,
        )(*args, *after)

    bind = functools.partial

    in_hbm = [pltpu.with_memory_space_constraint(x, pltpu.HBM) for x in (
        tiles.reshape(slots, side, side), tile_row.reshape(slots), tile_col.reshape(slots), src)]
    dense_shape = bf16((2 * half, n_cols))
    send, send_hubs, dense_send, total, panel = pl.pallas_call(
        bind(first_kernel, dims),
        out_shape=(f32((VB, width)), f32((half - VB, width)), dense_shape, f32((n_rows + side, n_cols)), bf16((n_cols, width))),
        in_specs=[HBM] * 5,
        out_specs=[VMEM] * 5,
        scratch_shapes=[
            pltpu.VMEM((slots, side, side), jnp.bfloat16),
            pltpu.SMEM((slots,), jnp.int32),
            pltpu.SMEM((slots,), jnp.int32),
            pltpu.SMEM((1,), jnp.int32),
            pltpu.VMEM((1, width), jnp.int32),
            pltpu.SemaphoreType.DMA((slots // CHUNK,)),
            pltpu.SemaphoreType.DMA((4,)),
        ],
        compiler_params=params(),
        name="first_terms",
    )(*in_hbm[:3], tile_count.reshape(1), in_hbm[3])

    keep, dense_keep = call(bind(keep_kernel, dims), "keep_terms", (f32((half, width)), dense_shape), total, panel, cost=1)
    hold, away = call(spread_kernel, "spread", (f32((quarter, width)),) * 2, keep, other_core(send_hubs), cost=2)
    away = other_side(away)
    held = call(bind(scores_kernel, dims), "scores", bf16((1, VB, width)), src, keep, other_core(send))
    next_z, far_z = to_partner(held, X), to_partner(held, 2 * X)
    last = to_partner(far_z, X)
    first = call(join_kernel, "join_first", bf16((3, VB, width)), held, next_z, far_z, cost=0)
    first_across, last_across = other_side(first), other_side(last)
    sums = call(add_kernel, "plane_sum", f32((quarter, width)), hold, away, cost=0)
    sums = call(add_kernel, "pair_sum", f32((quarter, width)), sums, to_partner(sums, X), cost=8)
    dense_came = other_core(call(join_kernel, "pass_dense", dense_shape, dense_send, after=[sums], cost=2))
    hubs = call(bind(hub_kernel, dims), "hub_sums", bf16((quarter, width)), src, sums, to_partner(sums, 2 * X), cost=0)
    blocks = call(join_kernel, "join_blocks", bf16((n_row, VB, width)), first, last, first_across, last_across, after=[hubs], cost=12)
    blocks_came = other_core(blocks)
    hubs = call(side_kernel, "join_sides", bf16((2, quarter, width)), hubs, cross(hubs), cost=8)
    column_scratch = [pltpu.VMEM((n_row * VB, width), jnp.bfloat16)]
    part = call(bind(score_columns_kernel, dims), "own_columns", f32((half, width)),
                blocks, dense_keep, scratch=column_scratch)
    part = call(bind(other_columns_kernel, dims), "other_columns", f32((half, width)),
                blocks_came, dense_came, part, scratch=column_scratch)
    scores, parts = call(
        bind(hub_columns_kernel, dims), "hub_columns", (f32((VB, width)), f32((n_row, piece, width))),
        src, hubs, other_core(hubs), dense_keep, dense_came, part, scratch=[pltpu.VMEM((H, width), jnp.bfloat16)])
    parts = lax.all_to_all(parts, "row", 0, 0)
    scores, hubs = call(bind(last_kernel, dims), "last_hubs", (f32((VB, width)), f32((piece, width))), src, scores, parts)
    return scores.reshape(1, 1, VB, width), hubs


def plain_body(tiles, tile_row, tile_col, tile_count, sources):
    slots = tiles.shape[2]
    side = tiles.shape[3]
    width = sources.shape[0]
    tiles = tiles.reshape(slots, side, side)
    rows = tile_row.reshape(slots)
    cols = tile_col.reshape(slots)
    count = tile_count.reshape(())
    n_row = lax.axis_size("row")
    n_col = lax.axis_size("col")
    devices = n_row * n_col
    r_index = lax.axis_index("row")
    c_index = lax.axis_index("col")
    hub_dev = H // devices
    block_rows = n_col * VB
    n_tile_rows = (block_rows + H) // side
    own_base = H + (r_index * n_col + c_index) * VB
    hub_start = (r_index * n_col + c_index) * hub_dev
    own_ids = jnp.arange(VB, dtype=jnp.int32) + own_base
    tele_own = (own_ids[:, None] == sources[None, :]).astype(jnp.float32)
    piece_ids = jnp.arange(hub_dev, dtype=jnp.int32) + hub_start
    tele_piece = (piece_ids[:, None] == sources[None, :]).astype(jnp.float32)
    tele_hubs = (jnp.arange(H, dtype=jnp.int32)[:, None] == sources[None, :]).astype(jnp.float32)
    column_ids = (
        H
        + (jnp.arange(n_row, dtype=jnp.int32)[:, None] * n_col + c_index) * VB
        + jnp.arange(VB, dtype=jnp.int32)[None, :]
    ).reshape(n_row * VB)
    column_panel = (column_ids[:, None] == sources[None, :]).astype(jnp.bfloat16)
    hub_panel = tele_hubs.astype(jnp.bfloat16)
    block = math.gcd(slots, 16)
    own_scores = tele_own
    hub_piece = tele_piece
    for step in range(ITERS):
        start_acc = jnp.zeros((n_tile_rows, side, width), jnp.float32)
        if step > 0:
            column_panel = lax.all_gather(
                own_scores.astype(jnp.bfloat16), "row", axis=0, tiled=True
            )
        panel = jnp.concatenate([column_panel, hub_panel], axis=0).reshape(-1, side, width)

        def step_fn(number, total):
            start = number * block
            tile_block = lax.dynamic_slice_in_dim(tiles, start, block, 0)
            col_block = lax.dynamic_slice_in_dim(cols, start, block, 0)
            row_block = lax.dynamic_slice_in_dim(rows, start, block, 0)
            pieces = jnp.take(panel, col_block, axis=0)
            prod = jnp.einsum(
                "tij,tjs->tis", tile_block, pieces, preferred_element_type=jnp.float32
            )
            live = start + jnp.arange(block, dtype=jnp.int32) < count
            prod = jnp.where(live[:, None, None], prod, 0.0)
            return total.at[row_block].add(prod)

        total = lax.fori_loop(0, slots // block, step_fn, start_acc)
        partial_value = total.reshape(n_tile_rows * side, width)
        summed_rows = lax.psum_scatter(
            partial_value[:block_rows], "col", scatter_dimension=0, tiled=True
        )
        own_scores = 0.85 * summed_rows + 0.15 * tele_own
        hub_part = partial_value[block_rows:]
        summed = lax.psum_scatter(hub_part, ("row", "col"), scatter_dimension=0, tiled=True)
        hub_piece = 0.85 * summed + 0.15 * tele_piece
        if step + 1 < ITERS:
            hub_panel = lax.all_gather(
                hub_piece.astype(jnp.bfloat16), ("row", "col"), axis=0, tiled=True
            )
    return (own_scores.reshape(1, 1, VB, width), hub_piece)


def solution(mesh):
    placed = (
        P(("groups", "row"), "col", None, None, None),
        P(("groups", "row"), "col", None),
        P(("groups", "row"), "col", None),
        P(("groups", "row"), "col"),
        P("groups"),
    )

    def body(tiles, *rest):
        n_row, n_col = mesh.shape["row"], mesh.shape["col"]
        slots, side = tiles.shape[2:4]
        blocks = (n_col * VB + H) * (n_row * VB + H) // (side * side)
        if ITERS == 2 and n_col == 2 and n_row == 4 * X and blocks <= slots and H // (n_row * n_col) % 16 == 0:
            return fast_body(tiles, *rest)
        return plain_body(tiles, *rest)

    return jax.shard_map(
        body,
        mesh=mesh,
        in_specs=placed,
        out_specs=(P(("groups", "row"), "col", None, None), P(("groups", "row", "col"), None)),
        check_vma=False,
    )
```

```python
import functools
import math

import jax
import jax.numpy as jnp
from jax import lax
from jax.experimental import pallas as pl
from jax.experimental.pallas import tpu as pltpu
from jax.sharding import PartitionSpec as P

VB = 128
H = 256
ITERS = 2
DAMP = 0.85
CHUNK = 4
X = 2
MICRO = 10 ** 9
VMEM_LIMIT = 32 * 1024 * 1024

SMEM = pl.BlockSpec(memory_space=pltpu.SMEM)
VMEM = pl.BlockSpec(memory_space=pltpu.VMEM)
HBM = pl.BlockSpec(memory_space=pltpu.HBM)


def params():
    return pltpu.CompilerParams(vmem_limit_bytes=VMEM_LIMIT)


def one_hot(first, count, src):
    ids = lax.broadcasted_iota(jnp.int32, (count, src.shape[1]), 0) + first
    return (ids == src).astype(jnp.float32)


def product(dense, panel):
    prod = jnp.dot(dense, panel, preferred_element_type=jnp.float32)
    rows = prod.shape[0] // 2
    return prod[:rows] + prod[rows:]


def half_terms(dims, core, total, panel, outs, dense_ref):
    n_row, n_col, side = dims
    piece = H // (n_row * n_col)
    half = dense_ref.shape[0] // 2
    chunks = [(0, core * VB, VB)]
    for r in range(n_row):
        chunks.append((VB + r * piece, n_col * VB + (r * n_col + core) * piece, piece))
    for to, start, size in chunks:
        whole = total[pl.ds(pl.multiple_of(start, size), size), :]
        high = whole.astype(jnp.bfloat16)
        dense_ref[to:to + size] = high
        dense_ref[half + to:half + to + size] = (whole - high.astype(jnp.float32)).astype(jnp.bfloat16)
    prod = product(dense_ref[...], panel[...])
    at = 0
    for ref in outs:
        ref[...] = prod[at:at + ref.shape[0]]
        at += ref.shape[0]


def first_kernel(dims, tiles_ref, rows_hbm, cols_hbm, count_hbm, src_hbm, send_ref, hubs_ref, dense_send_ref, total, panel,
                 held, rows_ref, cols_ref, count_ref, src_ref, sems, small):
    n_row, n_col, side = dims
    n_rows = n_col * VB + H
    piece = H // (n_row * n_col)
    c = lax.axis_index("col")
    pairs = ((src_hbm, src_ref), (rows_hbm, rows_ref), (cols_hbm, cols_ref), (count_hbm, count_ref))
    scalars = [pltpu.make_async_copy(a, b, small.at[i]) for i, (a, b) in enumerate(pairs)]
    copies = []
    for i in range(held.shape[0] // CHUNK):
        part = pl.ds(i * CHUNK, CHUNK)
        copies.append(pltpu.make_async_copy(tiles_ref.at[part], held.at[part], sems.at[i]))
    for copy in scalars + copies:
        copy.start()
    total[...] = jnp.zeros_like(total)
    for copy in scalars:
        copy.wait()
    src = src_ref[...]
    for r in range(n_row):
        first = H + (r * n_col + c) * VB
        panel[pl.ds(r * VB, VB), :] = one_hot(first, VB, src).astype(jnp.bfloat16)
    panel[pl.ds(n_row * VB, H), :] = one_hot(0, H, src).astype(jnp.bfloat16)
    count = count_ref[0]

    def add_tile(k, carry):
        live = k < count
        row = pl.multiple_of(jnp.where(live, rows_ref[k] * side, n_rows), side)
        col = pl.multiple_of(jnp.where(live, cols_ref[k] * side, 0), side)
        spot = (pl.ds(row, side), pl.ds(col, side))
        total[spot] += held[k].astype(jnp.float32)
        return carry

    for i, copy in enumerate(copies):
        copy.wait()
        lax.fori_loop(i * CHUNK, (i + 1) * CHUNK, add_tile, 0, unroll=4)
    half_terms(dims, 1 - c, total, panel, (send_ref, hubs_ref), dense_send_ref)


def keep_kernel(dims, total_ref, panel_ref, keep_ref, dense_ref):
    half_terms(dims, lax.axis_index("col"), total_ref, panel_ref, (keep_ref,), dense_ref)


def score_columns_kernel(dims, blocks_ref, dense_ref, part_ref, panel):
    n_row, n_col, side = dims
    n_z = n_row // X
    r = lax.axis_index("row")
    for k in range(n_row):
        owner = r ^ (X * (k % n_z) + k // n_z)
        panel[pl.ds(pl.multiple_of(owner * VB, VB), VB), :] = blocks_ref[k]
    part_ref[...] = product(dense_ref[:, :n_row * VB], panel[...])


def other_columns_kernel(dims, blocks_ref, dense_ref, held_ref, part_ref, panel):
    score_columns_kernel(dims, blocks_ref, dense_ref, part_ref, panel)
    part_ref[...] += held_ref[...]


def hub_columns_kernel(dims, src_ref, mine_ref, theirs_ref, dense_mine, dense_theirs, part_ref,
                       scores_ref, parts_ref, panel):
    n_row, n_col, side = dims
    columns = n_row * VB
    piece = parts_ref.shape[1]
    r, c = lax.axis_index("row"), lax.axis_index("col")
    n_z = n_row // X
    x = r % X
    for block, at, core in ((mine_ref[0], x, c), (mine_ref[1], 1 - x, 1 - c), (theirs_ref[0], x, 1 - c), (theirs_ref[1], 1 - x, c)):
        for i in range(n_z):
            place = ((at * n_z + i) * n_col + core) * piece
            panel[pl.ds(pl.multiple_of(place, piece), piece), :] = block[i * piece:(i + 1) * piece]
    total = part_ref[...] + product(dense_mine[:, columns:], panel[...]) + product(dense_theirs[:, columns:], panel[...])
    tele = one_hot(H + (r * n_col + c) * VB, VB, src_ref[...])
    scores_ref[...] = DAMP * total[:VB] + 0.15 * tele
    parts_ref[...] = total[VB:].reshape(parts_ref.shape)


def own_scores(dims, src_ref, keep_ref, came_ref):
    first = H + (lax.axis_index("row") * dims[1] + lax.axis_index("col")) * VB
    tele = one_hot(first, VB, src_ref[...])
    return DAMP * (keep_ref[:VB] + came_ref[:VB]) + 0.15 * tele


def spread_kernel(keep_ref, came_ref, hold_ref, pass_ref):
    quarter = hold_ref.shape[0]
    x = lax.axis_index("row") % X
    for ref, place in ((hold_ref, x), (pass_ref, 1 - x)):
        ref[...] = keep_ref[pl.ds(pl.multiple_of(VB + place * quarter, quarter), quarter), :] + came_ref[pl.ds(
            pl.multiple_of(place * quarter, quarter), quarter), :]


def scores_kernel(dims, src_ref, keep_ref, came_ref, scores_ref):
    first = H + (lax.axis_index("row") * dims[1] + lax.axis_index("col")) * VB
    tele = one_hot(first, VB, src_ref[...])
    scores_ref[0] = (DAMP * (keep_ref[:VB] + came_ref[...]) + 0.15 * tele).astype(scores_ref.dtype)


def join_kernel(*refs):
    at = 0
    for ref in refs[:-1]:
        refs[-1][at:at + ref.shape[0]] = ref[...]
        at += ref.shape[0]


def add_kernel(hold_ref, came_ref, out_ref):
    out_ref[...] = hold_ref[...] + came_ref[...]


def hub_kernel(dims, src_ref, held_ref, came_ref, out_ref):
    n_row, n_col, side = dims
    piece = H // (n_row * n_col)
    r, c = lax.axis_index("row"), lax.axis_index("col")
    at = lax.broadcasted_iota(jnp.int32, out_ref.shape, 0)
    ids = ((r % X * (n_row // X) + at // piece) * n_col + c) * piece + at % piece
    tele = (ids == src_ref[...]).astype(jnp.float32)
    out_ref[...] = (DAMP * (held_ref[...] + came_ref[...]) + 0.15 * tele).astype(out_ref.dtype)


def side_kernel(mine_ref, came_ref, out_ref):
    out_ref[0] = mine_ref[...]
    out_ref[1] = came_ref[...]


def last_kernel(dims, src_ref, held_ref, parts_ref, scores_ref, hubs_ref):
    scores_ref[...] = held_ref[...]
    piece = hubs_ref.shape[0]
    summed = parts_ref[0]
    for k in range(1, parts_ref.shape[0]):
        summed = summed + parts_ref[k]
    first = (lax.axis_index("row") * dims[1] + lax.axis_index("col")) * piece
    hubs_ref[...] = DAMP * summed + 0.15 * one_hot(first, piece, src_ref[...])


def fast_body(tiles, tile_row, tile_col, tile_count, sources):
    slots, side = tiles.shape[2:4]
    width = sources.shape[0]
    n_row = lax.axis_size("row")
    n_col = lax.axis_size("col")
    piece = H // (n_row * n_col)
    dims = (n_row, n_col, side)
    n_rows = n_col * VB + H
    n_cols = n_row * VB + H
    f32 = functools.partial(jax.ShapeDtypeStruct, dtype=jnp.float32)
    bf16 = functools.partial(jax.ShapeDtypeStruct, dtype=jnp.bfloat16)
    src = sources.reshape(1, width)
    half = VB + n_row * piece
    quarter = H // n_col // X
    def other_core(x):
        return lax.ppermute(x, "col", [(0, 1), (1, 0)])

    def to_partner(x, flip):
        return lax.ppermute(x, "row", [(r, r ^ flip) for r in range(n_row)])

    def other_side(x):
        return to_partner(x, 1)

    def cross(x):
        devices = [(r, c) for r in range(n_row) for c in range(n_col)]
        return lax.ppermute(x, ("row", "col"), [(r * n_col + c, (r ^ 1) * n_col + 1 - c) for r, c in devices])

    def call(kernel, name, out_shape, *args, scratch=(), after=(), cost=0):
        def body(*refs):
            kernel(*refs[:len(args)], *refs[len(args) + len(after):])

        return pl.pallas_call(
            body,
            out_shape=out_shape,
            in_specs=[VMEM] * len(args) + [pl.BlockSpec(memory_space=pl.ANY)] * len(after),
            out_specs=jax.tree.map(lambda _: VMEM, out_shape),
            scratch_shapes=scratch,
            compiler_params=params(),
            cost_estimate=pl.CostEstimate(flops=cost * MICRO, bytes_accessed=0, transcendentals=0),
            name=name,
        )(*args, *after)

    bind = functools.partial

    in_hbm = [pltpu.with_memory_space_constraint(x, pltpu.HBM) for x in (
        tiles.reshape(slots, side, side), tile_row.reshape(slots), tile_col.reshape(slots), src)]
    dense_shape = bf16((2 * half, n_cols))
    send, send_hubs, dense_send, total, panel = pl.pallas_call(
        bind(first_kernel, dims),
        out_shape=(f32((VB, width)), f32((half - VB, width)), dense_shape, f32((n_rows + side, n_cols)), bf16((n_cols, width))),
        in_specs=[HBM] * 5,
        out_specs=[VMEM] * 5,
        scratch_shapes=[
            pltpu.VMEM((slots, side, side), jnp.bfloat16),
            pltpu.SMEM((slots,), jnp.int32),
            pltpu.SMEM((slots,), jnp.int32),
            pltpu.SMEM((1,), jnp.int32),
            pltpu.VMEM((1, width), jnp.int32),
            pltpu.SemaphoreType.DMA((slots // CHUNK,)),
            pltpu.SemaphoreType.DMA((4,)),
        ],
        compiler_params=params(),
        name="first_terms",
    )(*in_hbm[:3], tile_count.reshape(1), in_hbm[3])

    keep, dense_keep = call(bind(keep_kernel, dims), "keep_terms", (f32((half, width)), dense_shape), total, panel, cost=1)
    hold, away = call(spread_kernel, "spread", (f32((quarter, width)),) * 2, keep, other_core(send_hubs), cost=2)
    away = other_side(away)
    held = call(bind(scores_kernel, dims), "scores", bf16((1, VB, width)), src, keep, other_core(send))
    next_z, far_z = to_partner(held, X), to_partner(held, 2 * X)
    last = to_partner(far_z, X)
    first = call(join_kernel, "join_first", bf16((3, VB, width)), held, next_z, far_z, cost=0)
    first_across, last_across = other_side(first), other_side(last)
    sums = call(add_kernel, "plane_sum", f32((quarter, width)), hold, away, cost=0)
    sums = call(add_kernel, "pair_sum", f32((quarter, width)), sums, to_partner(sums, X), cost=8)
    dense_came = other_core(call(join_kernel, "pass_dense", dense_shape, dense_send, after=[sums], cost=2))
    hubs = call(bind(hub_kernel, dims), "hub_sums", bf16((quarter, width)), src, sums, to_partner(sums, 2 * X), cost=0)
    blocks = call(join_kernel, "join_blocks", bf16((n_row, VB, width)), first, last, first_across, last_across, after=[hubs], cost=12)
    blocks_came = other_core(blocks)
    hubs = call(side_kernel, "join_sides", bf16((2, quarter, width)), hubs, cross(hubs), cost=8)
    column_scratch = [pltpu.VMEM((n_row * VB, width), jnp.bfloat16)]
    part = call(bind(score_columns_kernel, dims), "own_columns", f32((half, width)),
                blocks, dense_keep, scratch=column_scratch)
    part = call(bind(other_columns_kernel, dims), "other_columns", f32((half, width)),
                blocks_came, dense_came, part, scratch=column_scratch)
    scores, parts = call(
        bind(hub_columns_kernel, dims), "hub_columns", (f32((VB, width)), f32((n_row, piece, width))),
        src, hubs, other_core(hubs), dense_keep, dense_came, part, scratch=[pltpu.VMEM((H, width), jnp.bfloat16)])
    parts = lax.all_to_all(parts, "row", 0, 0)
    scores, hubs = call(bind(last_kernel, dims), "last_hubs", (f32((VB, width)), f32((piece, width))), src, scores, parts)
    return scores.reshape(1, 1, VB, width), hubs


def plain_body(tiles, tile_row, tile_col, tile_count, sources):
    slots = tiles.shape[2]
    side = tiles.shape[3]
    width = sources.shape[0]
    tiles = tiles.reshape(slots, side, side)
    rows = tile_row.reshape(slots)
    cols = tile_col.reshape(slots)
    count = tile_count.reshape(())
    n_row = lax.axis_size("row")
    n_col = lax.axis_size("col")
    devices = n_row * n_col
    r_index = lax.axis_index("row")
    c_index = lax.axis_index("col")
    hub_dev = H // devices
    block_rows = n_col * VB
    n_tile_rows = (block_rows + H) // side
    own_base = H + (r_index * n_col + c_index) * VB
    hub_start = (r_index * n_col + c_index) * hub_dev
    own_ids = jnp.arange(VB, dtype=jnp.int32) + own_base
    tele_own = (own_ids[:, None] == sources[None, :]).astype(jnp.float32)
    piece_ids = jnp.arange(hub_dev, dtype=jnp.int32) + hub_start
    tele_piece = (piece_ids[:, None] == sources[None, :]).astype(jnp.float32)
    tele_hubs = (jnp.arange(H, dtype=jnp.int32)[:, None] == sources[None, :]).astype(jnp.float32)
    column_ids = (
        H
        + (jnp.arange(n_row, dtype=jnp.int32)[:, None] * n_col + c_index) * VB
        + jnp.arange(VB, dtype=jnp.int32)[None, :]
    ).reshape(n_row * VB)
    column_panel = (column_ids[:, None] == sources[None, :]).astype(jnp.bfloat16)
    hub_panel = tele_hubs.astype(jnp.bfloat16)
    block = math.gcd(slots, 16)
    own_scores = tele_own
    hub_piece = tele_piece
    for step in range(ITERS):
        start_acc = jnp.zeros((n_tile_rows, side, width), jnp.float32)
        if step > 0:
            column_panel = lax.all_gather(
                own_scores.astype(jnp.bfloat16), "row", axis=0, tiled=True
            )
        panel = jnp.concatenate([column_panel, hub_panel], axis=0).reshape(-1, side, width)

        def step_fn(number, total):
            start = number * block
            tile_block = lax.dynamic_slice_in_dim(tiles, start, block, 0)
            col_block = lax.dynamic_slice_in_dim(cols, start, block, 0)
            row_block = lax.dynamic_slice_in_dim(rows, start, block, 0)
            pieces = jnp.take(panel, col_block, axis=0)
            prod = jnp.einsum(
                "tij,tjs->tis", tile_block, pieces, preferred_element_type=jnp.float32
            )
            live = start + jnp.arange(block, dtype=jnp.int32) < count
            prod = jnp.where(live[:, None, None], prod, 0.0)
            return total.at[row_block].add(prod)

        total = lax.fori_loop(0, slots // block, step_fn, start_acc)
        partial_value = total.reshape(n_tile_rows * side, width)
        summed_rows = lax.psum_scatter(
            partial_value[:block_rows], "col", scatter_dimension=0, tiled=True
        )
        own_scores = 0.85 * summed_rows + 0.15 * tele_own
        hub_part = partial_value[block_rows:]
        summed = lax.psum_scatter(hub_part, ("row", "col"), scatter_dimension=0, tiled=True)
        hub_piece = 0.85 * summed + 0.15 * tele_piece
        if step + 1 < ITERS:
            hub_panel = lax.all_gather(
                hub_piece.astype(jnp.bfloat16), ("row", "col"), axis=0, tiled=True
            )
    return (own_scores.reshape(1, 1, VB, width), hub_piece)


def solution(mesh):
    placed = (
        P(("groups", "row"), "col", None, None, None),
        P(("groups", "row"), "col", None),
        P(("groups", "row"), "col", None),
        P(("groups", "row"), "col"),
        P("groups"),
    )

    def body(tiles, *rest):
        n_row, n_col = mesh.shape["row"], mesh.shape["col"]
        slots, side = tiles.shape[2:4]
        blocks = (n_col * VB + H) * (n_row * VB + H) // (side * side)
        if ITERS == 2 and n_col == 2 and n_row == 4 * X and blocks <= slots and H // (n_row * n_col) % 16 == 0:
            return fast_body(tiles, *rest)
        return plain_body(tiles, *rest)

    return jax.shard_map(
        body,
        mesh=mesh,
        in_specs=placed,
        out_specs=(P(("groups", "row"), "col", None, None), P(("groups", "row", "col"), None)),
        check_vma=False,
    )
```
